128 devices in a mesh: seq: 16 (over z, y), mp: 8 (over x, core).
Axes of the slice: x: 4, y: 4, z: 4, core: 2. Of those that a mesh axis runs over, the one named last changes fastest.
Arguments:
- tokens: bfloat16 [8192, 2048], P('seq'), may hold values from -6 to 6
- group_ids: int32 [8192], P('seq'), may hold values from 0 to 128, as said below
- gain_one: float32 [2048], replicated, may hold values from 0.5 to 1.5
- lin_query: bfloat16 [2048, 256], P(None, 'mp'), may hold values from -0.1875 to 0.1875
- lin_key: bfloat16 [2048, 256], P(None, 'mp'), may hold values from -0.1875 to 0.1875
- lin_value: bfloat16 [2048, 2048], P(None, 'mp'), may hold values from -0.125 to 0.125
- lin_output: bfloat16 [2048, 2048], P('mp'), may hold values from -0.5 to 0.5
- gain_two: float32 [2048], replicated, may hold values from 0.5 to 1.5
- win_query: bfloat16 [2048, 2048], P(None, 'mp'), may hold values from -0.125 to 0.125
- win_key: bfloat16 [2048, 2048], P(None, 'mp'), may hold values from -0.125 to 0.125
- win_value: bfloat16 [2048, 2048], P(None, 'mp'), may hold values from -0.125 to 0.125
- win_output: bfloat16 [2048, 2048], P('mp'), may hold values from -0.375 to 0.375
- gain_three: float32 [2048], replicated, may hold values from 0.5 to 1.5
- mlp_gate: bfloat16 [2048, 5632], P(None, 'mp'), may hold values from -0.125 to 0.125
- mlp_up: bfloat16 [2048, 5632], P(None, 'mp'), may hold values from -0.125 to 0.125
- mlp_down: bfloat16 [5632, 2048], P('mp'), may hold values from -0.078125 to 0.078125
- out_grad: bfloat16 [8192, 2048], P('seq'), may hold values from -6 to 6
Outputs:
- result: bfloat16 [8192, 2048], P('seq')
- tokens_grad: float32 [8192, 2048], P('seq')
- gain_one_grad: float32 [2048], P('seq')
- lin_query_grad: float32 [2048, 256], P('seq', 'mp')
- lin_key_grad: float32 [2048, 256], P('seq', 'mp')
- lin_value_grad: float32 [2048, 2048], P('seq', 'mp')
- lin_output_grad: float32 [2048, 2048], P('mp', 'seq')
- gain_two_grad: float32 [2048], P('seq')
- win_query_grad: float32 [2048, 2048], P('seq', 'mp')
- win_key_grad: float32 [2048, 2048], P('seq', 'mp')
- win_value_grad: float32 [2048, 2048], P('seq', 'mp')
- win_output_grad: float32 [2048, 2048], P('mp', 'seq')
- gain_three_grad: float32 [2048], P('seq')
- mlp_gate_grad: float32 [2048, 5632], P('seq', 'mp')
- mlp_up_grad: float32 [2048, 5632], P('seq', 'mp')
- mlp_down_grad: float32 [5632, 2048], P('mp', 'seq')
The draws below stay inside these ranges and needn't reach their ends.
Inputs may be any that keep to these rules, and one draw needn't show every extreme that they name: `group_ids`: never falling, starting at 0 and rising by at most one from a token to the next; one group begins among the first 512 tokens and ends among the last 512 tokens; every draw reaches the largest value.
All inputs are finite; a program needn't handle non-finite values.
Results may differ from the reference program's by a relative error of at most 0.035.
Values may be sent and summed in bfloat16 or wider, within the bound.
A program may use at most 192 MiB of HBM per device.

```python
import jax
import jax.numpy as jnp
from jax import lax

D = 2048
HEADS = 16
HD = 128
FEAT = 16
WIN = 64
FF = 5632
TOK_SEQ = 512
EXPAND = 273
TOKENS = 8192


def draw_group_ids(key, part):
    key = jax.random.fold_in(key, 7)
    head_key, tail_key = jax.random.split(key, 2)
    extra_count = max(1, TOK_SEQ // 8)
    head_spots = jax.random.permutation(head_key, TOK_SEQ - 1)[:extra_count] + 1
    tail_spots = TOKENS - 1 - jax.random.permutation(tail_key, TOK_SEQ - 1)[:extra_count]
    marks = jnp.zeros((TOKENS,), jnp.int32)
    marks = marks.at[head_spots].set(1)
    marks = marks.at[tail_spots].set(1)
    return jnp.cumsum(marks).astype(jnp.int32)


def raised(values, own_key, source, target, parts, factor):
    owner, partner = [(jnp.arange(values.shape[position]) // (values.shape[position] // parts)).reshape([-1 if axis == position else 1 for axis in range(values.ndim)]) for position in (source, target)]
    chosen = jax.random.permutation(own_key, parts)[partner]
    strong = (owner == chosen) | (owner == (partner + parts // 2) % parts)
    return jnp.where(strong, factor * values, values)


def shard_levels(own_key, extent, cuts, smallest, largest):
    def one(dim, blocks):
        heights = jax.random.uniform(jax.random.fold_in(jax.random.fold_in(own_key, 6), dim), (blocks,), jnp.float32, smallest / len(cuts), largest / len(cuts))
        return jnp.repeat(jnp.exp(heights), extent[dim] // blocks).reshape((-1,) + (1,) * (len(extent) - dim - 1))

    gain = one(*cuts[0])
    for cut in cuts[1:]:
        gain = gain * one(*cut)
    return gain


def bell_draw(rng, extent, width, most, pieces=(), held_as=jnp.bfloat16):
    values = jax.random.normal(rng, extent, jnp.float32) * width
    if len(pieces) > 0:
        values = shard_levels(rng, extent, pieces, -0.22, 0.18) * values
    return jnp.clip(values, min=-most, max=most).astype(held_as)


def noise_with(key, dims, scale, bound, shards, heavy, kind=jnp.bfloat16):
    values = scale * jax.random.normal(key, dims, jnp.float32)
    if shards:
        values = values * shard_levels(key, dims, shards, -0.22, 0.18)
    return jnp.clip(raised(values, jax.random.fold_in(key, 3), *heavy), -bound, bound).astype(kind)


def setup_inputs(seed: int = 0) -> dict:
    splits = jax.random.split(jax.random.key(seed), 18)
    return {
        "tokens": noise_with(splits[0], (TOKENS, D), 1.0, 6.0, ((0, 16),), (0, 1, 16, 2.0)),
        "group_ids": draw_group_ids(jax.random.fold_in(splits[17], 71), 0),
        "gain_one": jnp.clip(1.0 + 0.1 * jax.random.normal(splits[2], (D,), jnp.float32), 0.5, 1.5),
        "lin_query": bell_draw(splits[3], (D, HEADS * FEAT), (D // 2) ** -0.5, 0.1875, ((1, 8),)),
        "lin_key": bell_draw(splits[4], (D, HEADS * FEAT), (D // 2) ** -0.5, 0.1875, ((1, 8),)),
        "lin_value": bell_draw(splits[5], (D, HEADS * HD), D ** -0.5, 0.125, ((1, 8),)),
        "lin_output": bell_draw(splits[6], (HEADS * HD, D), (HEADS * HD // 16) ** -0.5, 0.5, ((0, 8),)),
        "gain_two": jnp.clip(1.0 + 0.1 * jax.random.normal(splits[7], (D,), jnp.float32), 0.5, 1.5),
        "win_query": bell_draw(splits[8], (D, HEADS * HD), D ** -0.5, 0.125, ((1, 8),)),
        "win_key": bell_draw(splits[9], (D, HEADS * HD), D ** -0.5, 0.125, ((1, 8),)),
        "win_value": bell_draw(splits[10], (D, HEADS * HD), D ** -0.5, 0.125, ((1, 8),)),
        "win_output": bell_draw(splits[11], (HEADS * HD, D), (HEADS * HD // 8) ** -0.5, 0.375, ((0, 8),)),
        "gain_three": jnp.clip(1.0 + 0.1 * jax.random.normal(splits[12], (D,), jnp.float32), 0.5, 1.5),
        "mlp_gate": bell_draw(splits[13], (D, FF), D ** -0.5, 0.125, ((1, 8),)),
        "mlp_up": bell_draw(splits[14], (D, FF), D ** -0.5, 0.125, ((1, 8),)),
        "mlp_down": bell_draw(splits[15], (FF, D), FF ** -0.5, 0.078125, ((0, 8),)),
        "out_grad": noise_with(splits[16], (TOKENS, D), 1.0, 6.0, ((0, 16),), (0, 1, 16, 2.0)),
    }


EPSILON = 1e-05
PRECISE = lax.Precision.HIGHEST

@jax.custom_vjp
def low(v):
    return lax.optimization_barrier(v.astype(jnp.bfloat16)).astype(jnp.float32)

@jax.custom_vjp
def low_back(v):
    return v

def low_keep(v):
    return (low(v), None)

def low_pass(kept, grad):
    return (grad,)

def back_keep(v):
    return (v, None)

def back_low(kept, grad):
    return (low(grad),)
low.defvjp(low_keep, low_pass)
low_back.defvjp(back_keep, back_low)

def both_ways(values):
    return low(low_back(values))

def project(left_rows, weight_mat):
    return jnp.dot(left_rows, weight_mat, precision=PRECISE)

def normalize(values, gain_vec):
    factor = lax.rsqrt(lax.optimization_barrier(jnp.mean(values * values, axis=-1, keepdims=True)) + EPSILON)
    return values * factor * gain_vec

def features(values):
    lead_shape = values.shape[:-1]
    feat_width = values.shape[-1]
    outer_prod = (values[..., :, None] * values[..., None, :]).reshape(lead_shape + (feat_width * feat_width,))
    return jnp.concatenate([jnp.ones(lead_shape + (1,), values.dtype), values * feat_width ** (-0.25), outer_prod * (2.0 * feat_width) ** (-0.5)], axis=-1)

def linear_mix(query_feat, key_feat, value_all, group_ids):
    token_count = query_feat.shape[0]
    head_count = query_feat.shape[1]
    block_rows = min(512, token_count)
    local_place = jnp.arange(block_rows)
    group_float = group_ids.astype(jnp.float32)

    def one_block(carried, first_row):
        state_sum, norm_sum, prev_key = carried
        query_rows = lax.dynamic_slice_in_dim(query_feat, first_row, block_rows, 0)
        key_rows = lax.dynamic_slice_in_dim(key_feat, first_row, block_rows, 0)
        value_rows = lax.dynamic_slice_in_dim(value_all, first_row, block_rows, 0)
        row_groups = lax.dynamic_slice_in_dim(group_float, first_row, block_rows, 0)
        allowed = ((local_place[None, :] <= local_place[:, None]) & (row_groups[None, :] == row_groups[:, None])).astype(jnp.float32)
        kernel = both_ways(jnp.einsum('ihf,jhf->hij', query_rows, key_rows, precision=PRECISE) * allowed[None])
        incoming = (row_groups == prev_key).astype(jnp.float32)
        numerator = low_back(jnp.einsum('hij,jhd->ihd', kernel, value_rows, precision=PRECISE) + incoming[:, None, None] * jnp.einsum('ihf,hfd->ihd', query_rows, state_sum, precision=PRECISE))
        denominator = jnp.transpose(lax.optimization_barrier(jnp.sum(kernel, axis=2))) + incoming[:, None] * jnp.einsum('ihf,hf->ih', query_rows, norm_sum, precision=PRECISE)
        last_group = row_groups[block_rows - 1]
        in_last = (row_groups == last_group).astype(jnp.float32)
        keep_old = (prev_key == last_group).astype(jnp.float32)
        chosen_keys = key_rows * in_last[:, None, None]
        new_state = keep_old * state_sum + jnp.einsum('jhf,jhd->hfd', chosen_keys, value_rows, precision=PRECISE)
        new_norm = keep_old * norm_sum + lax.optimization_barrier(jnp.sum(chosen_keys, axis=0))
        return ((new_state, new_norm, last_group), numerator / denominator[:, :, None])
    starts = jnp.arange(token_count // block_rows, dtype=jnp.int32) * block_rows
    initial = (jnp.zeros((head_count, EXPAND, HD), jnp.float32), jnp.zeros((head_count, EXPAND), jnp.float32), jnp.array(-1.0, jnp.float32))
    final_carry, mixed = lax.scan(jax.checkpoint(one_block), initial, starts)
    return mixed.reshape(token_count, head_count, HD)

def window_mix(query_all, key_all, value_all, group_ids):
    token_count = query_all.shape[0]
    head_count = query_all.shape[1]
    block_rows = min(512, token_count)
    key_pad = jnp.concatenate([jnp.zeros((WIN,) + key_all.shape[1:], key_all.dtype), key_all], axis=0)
    value_pad = jnp.concatenate([jnp.zeros((WIN,) + value_all.shape[1:], value_all.dtype), value_all], axis=0)
    group_whole = group_ids.astype(jnp.int32)
    group_pad = jnp.concatenate([-jnp.ones((WIN,), jnp.int32), group_whole])

    def one_block(first_row):
        query_rows = lax.dynamic_slice_in_dim(query_all, first_row, block_rows, 0)
        key_rows = lax.dynamic_slice_in_dim(key_pad, first_row, block_rows + WIN, 0)
        value_rows = lax.dynamic_slice_in_dim(value_pad, first_row, block_rows + WIN, 0)
        row_groups = lax.dynamic_slice_in_dim(group_whole, first_row, block_rows, 0)
        key_groups = lax.dynamic_slice_in_dim(group_pad, first_row, block_rows + WIN, 0)
        row_place = first_row + jnp.arange(block_rows, dtype=jnp.int32)
        key_place = first_row - WIN + jnp.arange(block_rows + WIN, dtype=jnp.int32)
        allowed = (key_place[None, :] <= row_place[:, None]) & (row_place[:, None] - key_place[None, :] < WIN) & (key_groups[None, :] == row_groups[:, None])
        scores = low_back(jnp.einsum('ihd,jhd->hij', query_rows, key_rows, precision=PRECISE) * HD ** (-0.5))
        scores = jnp.where(allowed[None], scores, -1e+30)
        row_peak = lax.optimization_barrier(jnp.max(scores, axis=2, keepdims=True))
        exp_scores = jnp.exp(scores - row_peak)
        attn_probs = exp_scores / lax.optimization_barrier(jnp.sum(exp_scores, axis=2, keepdims=True))
        return jnp.einsum('hij,jhd->ihd', low(attn_probs), value_rows, precision=PRECISE)
    starts = jnp.arange(token_count // block_rows, dtype=jnp.int32) * block_rows
    mixed = lax.map(jax.checkpoint(one_block), starts)
    return mixed.reshape(token_count, head_count, HD)

def reference(tokens, group_ids, gain_one, lin_query, lin_key, lin_value, lin_output, gain_two, win_query, win_key, win_value, win_output, gain_three, mlp_gate, mlp_up, mlp_down, out_grad):

    def forward(inputs, gain_one, lin_query, lin_key, lin_value, lin_output, gain_two, win_query, win_key, win_value, win_output, gain_three, mlp_gate, mlp_up, mlp_down):
        token_count = inputs.shape[0]
        normed_one = low(normalize(inputs, gain_one))
        query_lin = low_back(project(normed_one, lin_query)).reshape(token_count, HEADS, FEAT)
        key_lin = low_back(project(normed_one, lin_key)).reshape(token_count, HEADS, FEAT)
        value_lin = both_ways(project(normed_one, lin_value)).reshape(token_count, HEADS, HD)
        mixed = linear_mix(low(features(query_lin)), low(features(key_lin)), value_lin, group_ids)
        mixed_lin = both_ways(mixed.reshape(token_count, HEADS * HD))
        resid_one = inputs + low_back(project(mixed_lin, lin_output))
        normed_two = low(normalize(resid_one, gain_two))
        query_win = both_ways(project(normed_two, win_query)).reshape(token_count, HEADS, HD)
        key_win = both_ways(project(normed_two, win_key)).reshape(token_count, HEADS, HD)
        value_win = both_ways(project(normed_two, win_value)).reshape(token_count, HEADS, HD)
        mixed_win = both_ways(window_mix(query_win, key_win, value_win, group_ids).reshape(token_count, HEADS * HD))
        resid_two = resid_one + low_back(project(mixed_win, win_output))
        normed_three = low(normalize(resid_two, gain_three))
        gate_act = low_back(project(normed_three, mlp_gate))
        up_act = low_back(project(normed_three, mlp_up))
        hidden = low(jax.nn.silu(gate_act) * up_act)
        return resid_two + low_back(project(hidden, mlp_down))
    result, pullback = jax.vjp(forward, tokens.astype(jnp.float32), gain_one.astype(jnp.float32), lin_query.astype(jnp.float32), lin_key.astype(jnp.float32), lin_value.astype(jnp.float32), lin_output.astype(jnp.float32), gain_two.astype(jnp.float32), win_query.astype(jnp.float32), win_key.astype(jnp.float32), win_value.astype(jnp.float32), win_output.astype(jnp.float32), gain_three.astype(jnp.float32), mlp_gate.astype(jnp.float32), mlp_up.astype(jnp.float32), mlp_down.astype(jnp.float32))
    grads = pullback(out_grad.astype(jnp.float32))
    return (result.astype(jnp.bfloat16), grads[0], grads[1], grads[2], grads[3], grads[4], grads[5], grads[6], grads[7], grads[8], grads[9], grads[10], grads[11], grads[12], grads[13], grads[14])
```

```python
import functools

import jax
import jax.numpy as jnp
from jax import lax
from jax.experimental import pallas as pl
from jax.experimental.pallas import tpu as pltpu
from jax.sharding import PartitionSpec as P

HD = 128
FEAT = 16
WIN = 64
D = 2048
ROWS = 512
HALF_ROWS = 256
OWN = 64
PIECE = 32

EPSILON = 1e-05
PRECISE = lax.Precision.HIGHEST
MESH = pl.DeviceIdType.MESH
BF = jnp.bfloat16
F32 = jnp.float32
VMEM_LIMIT = 60 * 1024 * 1024


class Place:
    def __init__(self):
        self.seq = lax.axis_index("seq")
        self.mp = lax.axis_index("mp")
        self.z, self.y = self.seq // 4, self.seq % 4
        self.x, self.core = self.mp // 2, self.mp % 2

    def peer(self):
        return (self.seq, self.x * 2 + (1 - self.core))

    def on_x(self, step):
        return (self.seq, ((self.x + step) % 4) * 2 + self.core)

    def on_y(self, step):
        return (self.z * 4 + (self.y + step) % 4, self.mp)

    def on_z(self, step):
        return (((self.z + step) % 4) * 4 + self.y, self.mp)


class Copies:
    def __init__(self, send_sems, recv_sems):
        self.send_sems, self.recv_sems, self.count, self.started = send_sems, recv_sems, 0, []

    def make(self, src, dst, device):
        k = self.count
        self.count += 1
        return pltpu.make_async_remote_copy(
            src_ref=src,
            dst_ref=dst,
            send_sem=self.send_sems.at[k],
            recv_sem=self.recv_sems.at[k],
            device_id=device,
            device_id_type=MESH,
        )

    def start(self, src, dst, device):
        copy = self.make(src, dst, device)
        copy.start()
        self.started.append(copy)
        return copy

    def finish(self):
        for copy in self.started:
            copy.wait_send()


def greet(devices):
    barrier = pltpu.get_barrier_semaphore()
    for device in devices:
        pl.semaphore_signal(barrier, inc=1, device_id=device, device_id_type=MESH)
    pl.semaphore_wait(barrier, len(devices))


def rows_at(start, size):
    return pl.ds(pl.multiple_of(start, 16), size)


def sum_over_mp(place, copies, part, from_peer, send_opp, send_right, send_left, fwd, comb, direct, own):
    x, core = place.x, place.core
    peer, right, left = place.peer(), place.on_x(1), place.on_x(3)
    mine, other = core * HALF_ROWS, (1 - core) * HALF_ROWS
    order = [(x + 2) % 4, (x + 1) % 4, (x + 3) % 4, x]
    exchange = [
        copies.start(
            part.at[rows_at(other + at * OWN, OWN)], from_peer.at[rows_at(at * OWN, OWN)], peer
        )
        for at in order
    ]

    def chip_sum(at, low, size):
        return part[rows_at(mine + at * OWN + low, size)].astype(F32) + from_peer[
            rows_at(at * OWN + low, size)
        ].astype(F32)

    exchange[0].wait_recv()
    send_opp[...] = chip_sum(order[0], 0, OWN).astype(BF)
    to_right = copies.start(send_opp.at[0:PIECE], fwd.at[0], right)
    to_left = copies.start(send_opp.at[PIECE:OWN], fwd.at[1], left)
    exchange[1].wait_recv()
    send_right[0] = chip_sum(order[1], PIECE, PIECE).astype(BF)
    direct_right = copies.start(send_right.at[0], direct.at[1], right)
    exchange[2].wait_recv()
    send_left[0] = chip_sum(order[2], 0, PIECE).astype(BF)
    direct_left = copies.start(send_left.at[0], direct.at[0], left)
    to_right.wait_recv()
    send_right[1] = (chip_sum(order[1], 0, PIECE) + fwd[0].astype(F32)).astype(BF)
    comb_right = copies.start(send_right.at[1], comb.at[0], right)
    to_left.wait_recv()
    send_left[1] = (chip_sum(order[2], PIECE, PIECE) + fwd[1].astype(F32)).astype(BF)
    comb_left = copies.start(send_left.at[1], comb.at[1], left)
    exchange[3].wait_recv()
    own[...] = chip_sum(order[3], 0, OWN)
    direct_left.wait_recv()
    own[0:PIECE] += direct[0].astype(F32)
    direct_right.wait_recv()
    own[PIECE:OWN] += direct[1].astype(F32)
    comb_right.wait_recv()
    own[0:PIECE] += comb[0].astype(F32)
    comb_left.wait_recv()
    own[PIECE:OWN] += comb[1].astype(F32)


def gather_over_mp(place, copies, full):
    x, core = place.x, place.core
    peer, right, left = place.peer(), place.on_x(1), place.on_x(3)
    base, other = core * HALF_ROWS, (1 - core) * HALF_ROWS

    def block(at, low, size):
        return full.at[rows_at(base + at * OWN + low, size)]

    def send(at, low, size, device):
        return copies.start(block(at, low, size), block(at, low, size), device)

    def expect(at, low, size, copy):
        copy.wait_recv()

    right_at, left_at, opp_at = (x + 1) % 4, (x + 3) % 4, (x + 2) % 4
    right_low = send(x, 0, PIECE, right)
    left_high = send(x, PIECE, PIECE, left)
    right_high = send(x, PIECE, PIECE, right)
    left_low = send(x, 0, PIECE, left)
    peers = [send(x, 0, OWN, peer)]
    right_low.wait_recv()
    fwd_right = send(left_at, 0, PIECE, right)
    left_high.wait_recv()
    fwd_left = send(right_at, PIECE, PIECE, left)
    right_high.wait_recv()
    peers.append(send(left_at, 0, OWN, peer))
    left_low.wait_recv()
    peers.append(send(right_at, 0, OWN, peer))
    fwd_right.wait_recv()
    peers.append(send(opp_at, 0, PIECE, peer))
    fwd_left.wait_recv()
    peers.append(send(opp_at, PIECE, PIECE, peer))
    for copy in peers:
        copy.wait_recv()


MP_COPIES = 4 + 6 + 6 + 5


def mp_scratch():
    return [
        pltpu.VMEM((HALF_ROWS, D), BF),
        pltpu.VMEM((OWN, D), BF),
        pltpu.VMEM((2, PIECE, D), BF),
        pltpu.VMEM((2, PIECE, D), BF),
        pltpu.VMEM((2, PIECE, D), BF),
        pltpu.VMEM((2, PIECE, D), BF),
        pltpu.VMEM((2, PIECE, D), BF),
        pltpu.VMEM((OWN, D), F32),
        pltpu.SemaphoreType.DMA((MP_COPIES,)),
        pltpu.SemaphoreType.DMA((MP_COPIES,)),
    ]


def own_start(place):
    return place.core * HALF_ROWS + place.x * OWN


def mp_forward_kernel(part, resid, gain, full, resid_out, *scratch):
    place = Place()
    *bufs, own, send_sems, recv_sems = scratch
    copies = Copies(send_sems, recv_sems)
    greet([place.peer(), place.on_x(1), place.on_x(3)])
    sum_over_mp(place, copies, part, *bufs, own)
    rows = own[...] + resid[...]
    resid_out[...] = rows
    factor = lax.rsqrt(jnp.mean(rows * rows, axis=-1, keepdims=True) + EPSILON)
    full[rows_at(own_start(place), OWN)] = (rows * factor * gain[...]).astype(BF)
    gather_over_mp(place, copies, full)
    copies.finish()


def mp_plain_kernel(part, resid, full, *scratch):
    place = Place()
    *bufs, own, send_sems, recv_sems = scratch
    copies = Copies(send_sems, recv_sems)
    greet([place.peer(), place.on_x(1), place.on_x(3)])
    sum_over_mp(place, copies, part, *bufs, own)
    full[rows_at(own_start(place), OWN)] = (own[...] + resid[...]).astype(BF)
    gather_over_mp(place, copies, full)
    copies.finish()


def mp_backward_kernel(part, resid, gain, grad, full, grad_out, gain_out, *scratch):
    place = Place()
    *bufs, own, send_sems, recv_sems = scratch
    copies = Copies(send_sems, recv_sems)
    greet([place.peer(), place.on_x(1), place.on_x(3)])
    sum_over_mp(place, copies, part, *bufs, own)
    rows, normed_grad = resid[...], own[...]
    factor = lax.rsqrt(jnp.mean(rows * rows, axis=-1, keepdims=True) + EPSILON)
    normed = rows * factor
    scaled = normed_grad * gain[...]
    total = grad[...] + factor * (
        scaled - normed * jnp.mean(scaled * normed, axis=-1, keepdims=True)
    )
    grad_out[...] = total
    gain_out[...] = jnp.sum(normed_grad * normed, axis=0, keepdims=True)
    full[rows_at(own_start(place), OWN)] = total.astype(BF)
    gather_over_mp(place, copies, full)
    copies.finish()


def vmem(count):
    return [pl.BlockSpec(memory_space=pltpu.VMEM)] * count


def call(kernel, outs, scratch, collective_id, *args):
    return pl.pallas_call(
        kernel,
        out_shape=outs,
        in_specs=vmem(len(args)),
        out_specs=vmem(len(outs)),
        scratch_shapes=scratch,
        compiler_params=pltpu.CompilerParams(
            collective_id=collective_id, has_side_effects=True, vmem_limit_bytes=VMEM_LIMIT
        ),
    )(*args)


def shape(dims, kind):
    return jax.ShapeDtypeStruct(dims, kind)


def mp_forward(part, resid, gain):
    return call(
        mp_forward_kernel,
        (shape((ROWS, D), BF), shape((OWN, D), F32)),
        mp_scratch(),
        0,
        part.astype(BF),
        resid,
        gain.reshape(1, D),
    )


def mp_plain(part, resid):
    return call(mp_plain_kernel, (shape((ROWS, D), BF),), mp_scratch(), 1, part.astype(BF), resid)[0]


def mp_backward(part, resid, gain, grad):
    return call(
        mp_backward_kernel,
        (shape((ROWS, D), BF), shape((OWN, D), F32), shape((1, D), F32)),
        mp_scratch(),
        2,
        part.astype(BF),
        resid,
        gain.reshape(1, D),
        grad,
    )


STATE_ROWS = 576
STATE_HALF = 288


def ring_gather(copies, right, left, held):
    low, high = pl.ds(0, STATE_HALF), pl.ds(STATE_HALF, STATE_HALF)
    right_low = copies.start(held.at[0, low], held.at[1, low], right)
    left_high = copies.start(held.at[0, high], held.at[3, high], left)
    right_high = copies.start(held.at[0, high], held.at[1, high], right)
    left_low = copies.start(held.at[0, low], held.at[3, low], left)
    right_low.wait_recv()
    fwd_right = copies.start(held.at[1, low], held.at[2, low], right)
    left_high.wait_recv()
    fwd_left = copies.start(held.at[3, high], held.at[2, high], left)
    for copy in (right_high, left_low, fwd_right, fwd_left):
        copy.wait_recv()


def state_kernel(reverse, state, out, held_y, held_z, send_sems, recv_sems):
    place = Place()
    copies = Copies(send_sems, recv_sems)
    right_y, left_y = place.on_y(1), place.on_y(3)
    right_z, left_z = place.on_z(1), place.on_z(3)
    greet([right_y, left_y, right_z, left_z])
    held_y[0] = state[...]
    ring_gather(copies, right_y, left_y, held_y)
    parts = [held_y[k].astype(F32) for k in range(4)]
    held_z[0] = (parts[0] + parts[1] + parts[2] + parts[3]).astype(BF)

    def counted(position, step):
        at = (position - step + 4) % 4
        reached = at > position if reverse else at < position
        return jnp.where(reached, 1.0, 0.0)

    total = jnp.zeros((STATE_ROWS, HD), F32)
    for step in range(1, 4):
        total = total + counted(place.y, step) * parts[step]
    out[...] = total
    ring_gather(copies, right_z, left_z, held_z)
    total = out[...]
    for step in range(1, 4):
        total = total + counted(place.z, step) * held_z[step].astype(F32)
    out[...] = total
    copies.finish()


def state_scan(state, norm, reverse):
    heads, width = norm.shape
    flat = jnp.concatenate(
        [
            state.reshape(heads * width, HD),
            jnp.pad(norm.reshape(-1), (0, 5 * HD - heads * width)).reshape(5, HD),
        ]
    ).astype(BF)
    flat = jnp.pad(flat, ((0, STATE_ROWS - flat.shape[0]), (0, 0)))
    out = call(
        functools.partial(state_kernel, reverse),
        (shape((STATE_ROWS, HD), F32),),
        [
            pltpu.VMEM((4, STATE_ROWS, HD), BF),
            pltpu.VMEM((4, STATE_ROWS, HD), BF),
            pltpu.SemaphoreType.DMA((12,)),
            pltpu.SemaphoreType.DMA((12,)),
        ],
        4 if reverse else 3,
        flat,
    )[0]
    count = heads * width
    return (
        out[:count].reshape(heads, width, HD),
        out[count : count + 5].reshape(-1)[:count].reshape(heads, width),
    )


COLS = 3712


class Ring:
    def __init__(self, copies, right, left, pick, bufs):
        self.copies, self.right, self.left, self.pick = copies, right, left, pick
        self.fwd, self.direct, self.comb, self.out = bufs

    def first(self):
        copies, pick = self.copies, self.pick
        self.fwd_right = copies.start(pick(2, 0), self.fwd.at[0], self.right)
        self.fwd_left = copies.start(pick(2, 1), self.fwd.at[1], self.left)
        self.direct_right = copies.start(pick(1, 1), self.direct.at[1], self.right)
        self.direct_left = copies.start(pick(3, 0), self.direct.at[0], self.left)

    def second(self):
        self.fwd_right.wait_recv()
        self.out[0] = (self.pick(1, 0)[...].astype(F32) + self.fwd[0].astype(F32)).astype(BF)
        self.comb_right = self.copies.start(self.out.at[0], self.comb.at[0], self.right)
        self.fwd_left.wait_recv()
        self.out[1] = (self.pick(3, 1)[...].astype(F32) + self.fwd[1].astype(F32)).astype(BF)
        self.comb_left = self.copies.start(self.out.at[1], self.comb.at[1], self.left)

    def total(self, half):
        (self.direct_left if half == 0 else self.direct_right).wait_recv()
        (self.comb_right if half == 0 else self.comb_left).wait_recv()
        return (
            self.pick(0, half)[...].astype(F32)
            + self.direct[half].astype(F32)
            + self.comb[half].astype(F32)
        )


SPLITS = ((0, 1024), (1024, 1024), (2048, 896), (2944, 768))


def seq_kernel(grads, gains, out, gains_out, *scratch):
    place = Place()
    send_sems, recv_sems = scratch[-2:]
    gain_y, gain_z, gain_zz, gain_x, gain_xx, gain_p, gain_pp = scratch[-9:-2]
    bufs = scratch[:-9]
    copies = Copies(send_sems, recv_sems)
    z, y = place.z, place.y
    ring_y, ring_z = (place.on_y(1), place.on_y(3)), (place.on_z(1), place.on_z(3))
    greet(
        [place.on_y(k) for k in (1, 2, 3)]
        + [place.on_z(k) for k in (1, 2, 3)]
        + [place.on_x(k) for k in (1, 2, 3)]
        + [place.peer()]
    )
    stages = []
    for number, (at, width) in enumerate(SPLITS):
        cols = pl.ds(at, width)
        mine = bufs[number * 10 : number * 10 + 10]

        def pick_a(k, half, cols=cols):
            return grads.at[:, (y + k) % 4, pl.ds(half * 32, 32), cols]

        def pick_b(k, half, cols=cols):
            return grads.at[(z + k) % 4, :, pl.ds(64 + half * 32, 32), cols]

        first_a = Ring(copies, *ring_y, pick_a, mine[0:4])
        first_b = Ring(copies, *ring_z, pick_b, mine[4:8])
        sum_a, sum_b = mine[8], mine[9]

        stages.append((number, cols, width, first_a, first_b, sum_a, sum_b))
    for stage in stages:
        stage[3].first()
        stage[4].first()
    for number, cols, width, first_a, first_b, sum_a, sum_b in stages:
        first_a.second()
        first_b.second()
    second = []
    offset = len(SPLITS) * 10
    for number, cols, width, first_a, first_b, sum_a, sum_b in stages:
        for half in range(2):
            sum_a[:, half] = first_a.total(half).astype(BF)
            sum_b[:, half] = first_b.total(half).astype(BF)

        def pick_c(k, half, ref=sum_a):
            return ref.at[(z + k) % 4, half]

        def pick_d(k, half, ref=sum_b):
            return ref.at[(y + k) % 4, half]

        extra = bufs[offset + number * 8 : offset + number * 8 + 8]
        second_a = Ring(copies, *ring_z, pick_c, extra[0:4])
        second_b = Ring(copies, *ring_y, pick_d, extra[4:8])
        second_a.first()
        second_b.first()
        second.append((cols, second_a, second_b))
    for cols, second_a, second_b in second:
        second_a.second()
        second_b.second()
    over_y = [
        copies.start(gains.at[:, (y + k) % 4], gain_y.at[k - 1], place.on_y(k)) for k in (1, 2, 3)
    ]
    total = gains[:, pl.ds(y, 1)][:, 0].astype(F32)
    for k, copy in enumerate(over_y):
        copy.wait_recv()
        total = total + gain_y[k].astype(F32)
    gain_z[...] = total.astype(BF)
    over_z = [
        copies.start(gain_z.at[(z + k) % 4], gain_zz.at[k - 1], place.on_z(k)) for k in (1, 2, 3)
    ]
    total = gain_z[z].astype(F32)
    for k, copy in enumerate(over_z):
        copy.wait_recv()
        total = total + gain_zz[k].astype(F32)
    gain_x[...] = total.astype(BF)
    over_x = [copies.start(gain_x, gain_xx.at[k - 1], place.on_x(k)) for k in (1, 2, 3)]
    total = gain_x[...].astype(F32)
    for k, copy in enumerate(over_x):
        copy.wait_recv()
        total = total + gain_xx[k].astype(F32)
    gain_p[...] = total.astype(BF)
    over_p = copies.start(gain_p, gain_pp, place.peer())
    over_p.wait_recv()
    gains_out[...] = gain_p[...].astype(F32) + gain_pp[...].astype(F32)
    for cols, second_a, second_b in second:
        for half in range(2):
            out[pl.ds(half * 32, 32), cols] = second_a.total(half)
            out[pl.ds(64 + half * 32, 32), cols] = second_b.total(half)
    copies.finish()


def seq_reduce(grads, gains):
    grads = grads.reshape(4, 4, 128, COLS)
    gains = gains.reshape(4, 4, 16, HD)
    bufs = []
    for at, width in SPLITS:
        bufs += [pltpu.VMEM((2, 4, 32, width), BF)] * 8
        bufs += [pltpu.VMEM((4, 2, 32, width), BF)] * 2
    for at, width in SPLITS:
        bufs += [pltpu.VMEM((2, 32, width), BF)] * 8
    bufs += [
        pltpu.VMEM((3, 4, 16, HD), BF),
        pltpu.VMEM((4, 16, HD), BF),
        pltpu.VMEM((3, 16, HD), BF),
        pltpu.VMEM((16, HD), BF),
        pltpu.VMEM((3, 16, HD), BF),
        pltpu.VMEM((16, HD), BF),
        pltpu.VMEM((16, HD), BF),
    ]
    count = len(SPLITS) * 24 + 10
    return call(
        seq_kernel,
        (shape((128, COLS), F32), shape((16, HD), F32)),
        bufs + [pltpu.SemaphoreType.DMA((count,)), pltpu.SemaphoreType.DMA((count,))],
        5,
        grads,
        gains,
    )


def shifted(shard, axis, by):
    size = lax.axis_size(axis)
    pairs = [(i, i + by) for i in range(size) if 0 <= i + by < size]
    return lax.ppermute(shard, axis, pairs)


def normalize(values, gain_vec):
    factor = lax.rsqrt(jnp.mean(values * values, axis=-1, keepdims=True) + EPSILON)
    return values * factor * gain_vec


def features(values):
    lead_shape = values.shape[:-1]
    feat_width = values.shape[-1]
    outer_prod = (values[..., :, None] * values[..., None, :]).reshape(
        lead_shape + (feat_width * feat_width,)
    )
    return jnp.concatenate(
        [
            jnp.ones(lead_shape + (1,), values.dtype),
            values * feat_width ** (-0.25),
            outer_prod * (2.0 * feat_width) ** (-0.5),
        ],
        axis=-1,
    )


def weight_grad(left_rows, right_rows):
    return jnp.einsum("ta,tb->ab", left_rows, right_rows, preferred_element_type=jnp.float32)


def input_grad(right_rows, weight_mat):
    return jnp.einsum("tb,ab->ta", right_rows, weight_mat, preferred_element_type=jnp.float32)


def local(
    tokens,
    group_ids,
    gain_one,
    lin_query,
    lin_key,
    lin_value,
    lin_output,
    gain_two,
    win_query,
    win_key,
    win_value,
    win_output,
    gain_three,
    mlp_gate,
    mlp_up,
    mlp_down,
    out_grad,
):
    row_count = tokens.shape[0]
    heads_lin = lin_query.shape[1] // FEAT
    heads_win = win_query.shape[1] // HD
    inputs = tokens.astype(jnp.float32)
    group_float = group_ids.astype(jnp.float32)
    positions = jnp.arange(row_count)
    causal_mask = (
        (positions[None, :] <= positions[:, None]) & (group_ids[None, :] == group_ids[:, None])
    ).astype(jnp.float32)
    last_group = (group_ids == group_ids[row_count - 1]).astype(jnp.float32)
    normed_one = normalize(inputs, gain_one).astype(jnp.bfloat16)
    query_lin = jnp.dot(normed_one, lin_query, preferred_element_type=jnp.float32).reshape(
        row_count, heads_lin, FEAT
    )
    key_lin = jnp.dot(normed_one, lin_key, preferred_element_type=jnp.float32).reshape(
        row_count, heads_lin, FEAT
    )
    value_lin = (
        jnp.dot(normed_one, lin_value, preferred_element_type=jnp.float32)
        .astype(jnp.bfloat16)
        .reshape(row_count, heads_lin, HD)
    )
    query_feat = features(query_lin).astype(jnp.bfloat16)
    key_feat = features(key_lin).astype(jnp.bfloat16)
    query_full = query_feat.astype(jnp.float32)
    key_full = key_feat.astype(jnp.float32)
    value_full = value_lin.astype(jnp.float32)
    kernel_low = (
        jnp.einsum("ihf,jhf->hij", query_feat, key_feat, preferred_element_type=jnp.float32)
        * causal_mask[None]
    ).astype(jnp.bfloat16)
    local_state = jnp.einsum(
        "jhf,jhd->hfd",
        key_feat * last_group.astype(jnp.bfloat16)[:, None, None],
        value_lin,
        preferred_element_type=jnp.float32,
    )
    local_norm = jnp.sum(key_full * last_group[:, None, None], axis=0)
    carried_state, carried_norm = state_scan(local_state, local_norm, False)
    prev_key = jnp.where(lax.axis_index("seq") > 0, group_float[0:1], -1.0)
    incoming = (group_float == prev_key[0]).astype(jnp.float32)
    numerator = jnp.einsum(
        "hij,jhd->ihd", kernel_low, value_lin, preferred_element_type=jnp.float32
    ) + incoming[:, None, None] * jnp.einsum(
        "ihf,hfd->ihd", query_full, carried_state, precision=PRECISE
    )
    denominator = jnp.transpose(jnp.sum(kernel_low.astype(jnp.float32), axis=2)) + incoming[
        :, None
    ] * jnp.einsum("ihf,hf->ih", query_full, carried_norm, precision=PRECISE)
    quotient = numerator / denominator[:, :, None]
    mixed_lin = quotient.astype(jnp.bfloat16).reshape(row_count, heads_lin * HD)
    own_at = (lax.axis_index("mp") % 2) * HALF_ROWS + (lax.axis_index("mp") // 2) * OWN
    own_tokens = lax.dynamic_slice_in_dim(tokens, own_at, OWN, 0).astype(F32)
    own_out_grad = lax.dynamic_slice_in_dim(out_grad, own_at, OWN, 0).astype(F32)
    normed_two, resid_one = mp_forward(
        jnp.dot(mixed_lin, lin_output, preferred_element_type=jnp.float32), own_tokens, gain_two
    )
    query_win = (
        jnp.dot(normed_two, win_query, preferred_element_type=jnp.float32)
        .astype(jnp.bfloat16)
        .reshape(row_count, heads_win, HD)
    )
    key_win = (
        jnp.dot(normed_two, win_key, preferred_element_type=jnp.float32)
        .astype(jnp.bfloat16)
        .reshape(row_count, heads_win, HD)
    )
    value_win = (
        jnp.dot(normed_two, win_value, preferred_element_type=jnp.float32)
        .astype(jnp.bfloat16)
        .reshape(row_count, heads_win, HD)
    )
    tail_flag = last_group[row_count - WIN :].astype(jnp.bfloat16)
    halo_key, halo_value, halo_flag = shifted(
        (key_win[row_count - WIN :], value_win[row_count - WIN :], tail_flag), "seq", 1
    )
    keys_all = jnp.concatenate([halo_key, key_win], axis=0)
    values_all = jnp.concatenate([halo_value, value_win], axis=0)
    key_groups = jnp.concatenate(
        [jnp.where(halo_flag.astype(jnp.float32) > 0.5, prev_key[0], -2.0), group_float]
    )
    key_place = jnp.arange(row_count + WIN) - WIN
    window_mask = (
        (key_place[None, :] <= positions[:, None])
        & (positions[:, None] - key_place[None, :] < WIN)
        & (key_groups[None, :] == group_float[:, None])
    )
    score_scale = HD ** (-0.5)
    scores = (
        jnp.einsum("ihd,jhd->hij", query_win, keys_all, preferred_element_type=jnp.float32)
        * score_scale
    )
    scores = jnp.where(window_mask[None], scores, -1e30)
    row_peak = jnp.max(scores, axis=2, keepdims=True)
    exp_scores = jnp.exp(scores - row_peak)
    attn_probs = exp_scores / jnp.sum(exp_scores, axis=2, keepdims=True)
    probs_low = attn_probs.astype(jnp.bfloat16)
    mixed_win = (
        jnp.einsum("hij,jhd->ihd", probs_low, values_all, preferred_element_type=jnp.float32)
        .astype(jnp.bfloat16)
        .reshape(row_count, heads_win * HD)
    )
    normed_three, resid_two = mp_forward(
        jnp.dot(mixed_win, win_output, preferred_element_type=jnp.float32), resid_one, gain_three
    )
    gate_act = jnp.dot(normed_three, mlp_gate, preferred_element_type=jnp.float32)
    up_act = jnp.dot(normed_three, mlp_up, preferred_element_type=jnp.float32)
    hidden = (jax.nn.silu(gate_act) * up_act).astype(jnp.bfloat16)
    result = mp_plain(jnp.dot(hidden, mlp_down, preferred_element_type=jnp.float32), resid_two)
    down_grad = weight_grad(out_grad, hidden)
    hidden_grad = input_grad(out_grad, mlp_down)
    act_value, act_back = jax.vjp(
        lambda gate_in, up_in: jax.nn.silu(gate_in) * up_in, gate_act, up_act
    )
    gate_grad, up_grad = act_back(hidden_grad)
    gate_low = gate_grad.astype(jnp.bfloat16)
    up_low = up_grad.astype(jnp.bfloat16)
    gate_wgrad = weight_grad(normed_three, gate_low)
    up_wgrad = weight_grad(normed_three, up_low)
    win_low, grad_two, gain_three_grad = mp_backward(
        input_grad(gate_low, mlp_gate) + input_grad(up_low, mlp_up),
        resid_two,
        gain_three,
        own_out_grad,
    )
    win_output_grad = weight_grad(win_low, mixed_win)
    mixed_grad = (
        input_grad(win_low, win_output).astype(jnp.bfloat16).reshape(row_count, heads_win, HD)
    )
    probs_grad = jnp.einsum(
        "ihd,jhd->hij", mixed_grad, values_all, preferred_element_type=jnp.float32
    )
    values_grad = jnp.einsum(
        "hij,ihd->jhd", probs_low, mixed_grad, preferred_element_type=jnp.float32
    )
    score_grad = attn_probs * (probs_grad - jnp.sum(probs_grad * attn_probs, axis=2, keepdims=True))
    score_low = score_grad.astype(jnp.bfloat16)
    query_grad = (
        jnp.einsum("hij,jhd->ihd", score_low, keys_all, preferred_element_type=jnp.float32)
        * score_scale
    )
    keys_grad = (
        jnp.einsum("hij,ihd->jhd", score_low, query_win, preferred_element_type=jnp.float32)
        * score_scale
    )
    back_key, back_value = (
        shifted(keys_grad[:WIN].astype(jnp.bfloat16), "seq", -1).astype(jnp.float32),
        shifted(values_grad[:WIN].astype(jnp.bfloat16), "seq", -1).astype(jnp.float32),
    )
    key_own = keys_grad[WIN:].at[row_count - WIN :].add(back_key)
    value_own = values_grad[WIN:].at[row_count - WIN :].add(back_value)
    query_win_low = query_grad.astype(jnp.bfloat16).reshape(row_count, heads_win * HD)
    key_win_low = key_own.astype(jnp.bfloat16).reshape(row_count, heads_win * HD)
    value_win_low = value_own.astype(jnp.bfloat16).reshape(row_count, heads_win * HD)
    win_query_grad = weight_grad(normed_two, query_win_low)
    win_key_grad = weight_grad(normed_two, key_win_low)
    win_value_grad = weight_grad(normed_two, value_win_low)
    lin_low, grad_one, gain_two_grad = mp_backward(
        input_grad(query_win_low, win_query)
        + input_grad(key_win_low, win_key)
        + input_grad(value_win_low, win_value),
        resid_one,
        gain_two,
        grad_two,
    )
    lin_output_grad = weight_grad(lin_low, mixed_lin)
    mix_grad = (
        lax.optimization_barrier(input_grad(lin_low, lin_output).astype(jnp.bfloat16))
        .astype(jnp.float32)
        .reshape(row_count, heads_lin, HD)
    )
    numer_low = (mix_grad / denominator[:, :, None]).astype(jnp.bfloat16)
    numer_grad = numer_low.astype(jnp.float32)
    denom_grad = -jnp.sum(mix_grad * quotient, axis=2) / denominator
    kernel_grad = (
        (
            jnp.einsum("ihd,jhd->hij", numer_low, value_lin, preferred_element_type=jnp.float32)
            + jnp.transpose(denom_grad)[:, :, None]
        )
        * causal_mask[None]
    ).astype(jnp.bfloat16)
    value_sum = jnp.einsum(
        "hij,ihd->jhd", kernel_low, numer_low, preferred_element_type=jnp.float32
    )
    query_feat_grad = jnp.einsum(
        "hij,jhf->ihf", kernel_grad, key_feat, preferred_element_type=jnp.float32
    ) + incoming[:, None, None] * (
        jnp.einsum("ihd,hfd->ihf", numer_grad, carried_state, precision=PRECISE)
        + denom_grad[:, :, None] * carried_norm[None]
    )
    key_feat_grad = jnp.einsum(
        "hij,ihf->jhf", kernel_grad, query_feat, preferred_element_type=jnp.float32
    )
    query_used = query_full * incoming[:, None, None]
    state_in_grad = jnp.einsum("ihf,ihd->hfd", query_used, numer_grad, precision=PRECISE)
    norm_in_grad = jnp.einsum("ihf,ih->hf", query_used, denom_grad, precision=PRECISE)
    summary_state, summary_norm = state_scan(state_in_grad, norm_in_grad, True)
    key_feat_grad = key_feat_grad + last_group[:, None, None] * (
        jnp.einsum("jhd,hfd->jhf", value_full, summary_state, precision=PRECISE)
        + summary_norm[None]
    )
    value_sum = value_sum + last_group[:, None, None] * jnp.einsum(
        "jhf,hfd->jhd", key_full, summary_state, precision=PRECISE
    )
    feat_value, query_back = jax.vjp(features, query_lin)
    feat_value_two, key_back = jax.vjp(features, key_lin)
    query_low = (
        query_back(query_feat_grad)[0].astype(jnp.bfloat16).reshape(row_count, heads_lin * FEAT)
    )
    key_low = key_back(key_feat_grad)[0].astype(jnp.bfloat16).reshape(row_count, heads_lin * FEAT)
    value_low = value_sum.astype(jnp.bfloat16).reshape(row_count, heads_lin * HD)
    lin_query_grad = weight_grad(normed_one, query_low)
    lin_key_grad = weight_grad(normed_one, key_low)
    lin_value_grad = weight_grad(normed_one, value_low)
    tokens_low, tokens_grad_own, gain_one_grad = mp_backward(
        input_grad(query_low, lin_query)
        + input_grad(key_low, lin_key)
        + input_grad(value_low, lin_value),
        own_tokens,
        gain_one,
        grad_one,
    )
    grads = jnp.concatenate(
        [
            part.astype(BF)
            for part in (
                lin_query_grad,
                lin_key_grad,
                lin_value_grad,
                lin_output_grad,
                win_query_grad,
                win_key_grad,
                win_value_grad,
                win_output_grad,
                gate_wgrad,
                up_wgrad,
                down_grad,
            )
        ],
        axis=1,
    )
    gains = jnp.concatenate([gain_one_grad, gain_two_grad, gain_three_grad]).reshape(3, 16, HD)
    gains = jnp.pad(jnp.transpose(gains, (1, 0, 2)), ((0, 0), (0, 13), (0, 0))).astype(BF)
    sums, gain_sums = seq_reduce(grads, gains)
    cuts = [0, 32, 64, 320, 576, 832, 1088, 1344, 1600, 2304, 3008, 3712]
    pieces = [sums[:, a:b] for a, b in zip(cuts[:-1], cuts[1:])]
    return (
        result,
        tokens_low.astype(F32),
        gain_sums[0],
        pieces[0],
        pieces[1],
        pieces[2],
        pieces[3].T,
        gain_sums[1],
        pieces[4],
        pieces[5],
        pieces[6],
        pieces[7].T,
        gain_sums[2],
        pieces[8],
        pieces[9],
        pieces[10].T,
    )


def solution(mesh):
    return jax.shard_map(
        local,
        mesh=mesh,
        in_specs=(
            P("seq", None),
            P("seq"),
            P(),
            P(None, "mp"),
            P(None, "mp"),
            P(None, "mp"),
            P("mp", None),
            P(),
            P(None, "mp"),
            P(None, "mp"),
            P(None, "mp"),
            P("mp", None),
            P(),
            P(None, "mp"),
            P(None, "mp"),
            P("mp", None),
            P("seq", None),
        ),
        out_specs=(
            P("seq", None),
            P("seq", None),
            P("seq"),
            P("seq", "mp"),
            P("seq", "mp"),
            P("seq", "mp"),
            P("mp", "seq"),
            P("seq"),
            P("seq", "mp"),
            P("seq", "mp"),
            P("seq", "mp"),
            P("mp", "seq"),
            P("seq"),
            P("seq", "mp"),
            P("seq", "mp"),
            P("mp", "seq"),
        ),
        check_vma=False,
    )
```

```python
import functools

import jax
import jax.numpy as jnp
import numpy as np
from jax import lax
from jax.experimental import pallas as pl
from jax.experimental.pallas import tpu as pltpu
from jax.sharding import PartitionSpec as P

D = 2048
HD = 128
FEAT = 16
WIN = 64
FF = 704
ROWS = 512
TILE = 128
WIDE = 256
STATE = 144

CHUNKS = 4
CHUNK = ROWS // CHUNKS
HALF = CHUNK // 2
PIECE = CHUNK // 8
OWN = 64
COLS = D // 2

EPSILON = 1e-05
MESH = pl.DeviceIdType.MESH
BF = jnp.bfloat16
F32 = jnp.float32
VMEM_LIMIT = 62 * 1024 * 1024


class Place:
    def __init__(self):
        self.seq = lax.axis_index("seq")
        self.mp = lax.axis_index("mp")
        self.z, self.y = self.seq // 4, self.seq % 4
        self.x, self.core = self.mp // 2, self.mp % 2

    def peer(self):
        return (self.seq, self.x * 2 + (1 - self.core))

    def on_x(self, step):
        return (self.seq, ((self.x + step) % 4) * 2 + self.core)

    def on_y(self, step):
        return (self.z * 4 + (self.y + step) % 4, self.mp)

    def on_z(self, step):
        return (((self.z + step) % 4) * 4 + self.y, self.mp)

    def along(self, step):
        return ((self.seq + step) % 16, self.mp)


class Copies:
    def __init__(self, send_sems, recv_sems):
        self.send_sems, self.recv_sems = send_sems, recv_sems
        self.count, self.started = 0, []

    def start(self, src, dst, device):
        k = self.count
        self.count += 1
        copy = pltpu.make_async_remote_copy(
            src_ref=src,
            dst_ref=dst,
            send_sem=self.send_sems.at[k],
            recv_sem=self.recv_sems.at[k],
            device_id=device,
            device_id_type=MESH,
        )
        copy.start()
        self.started.append(copy)
        return copy

    def finish(self):
        for copy in self.started:
            copy.wait_send()
        self.count, self.started = 0, []


class Locals:
    def __init__(self, sems):
        self.sems, self.count = sems, 0

    def start(self, src, dst):
        copy = pltpu.make_async_copy(src, dst, self.sems.at[self.count])
        self.count += 1
        copy.start()
        return copy


def greet(devices):
    barrier = pltpu.get_barrier_semaphore()
    for device in devices:
        pl.semaphore_signal(barrier, inc=1, device_id=device, device_id_type=MESH)
    pl.semaphore_wait(barrier, len(devices))


def rows_at(start, size):
    return pl.ds(pl.multiple_of(start, 16), size)


def dot(left, right):
    return lax.dot_general(left, right, (((1,), (0,)), ((), ())), preferred_element_type=F32)


def dot_nt(left, right):
    return lax.dot_general(left, right, (((1,), (1,)), ((), ())), preferred_element_type=F32)


def dot_tn(left, right):
    return lax.dot_general(left, right, (((0,), (0,)), ((), ())), preferred_element_type=F32)


def halves(values):
    high = values.astype(BF)
    return high, (values - high.astype(F32)).astype(BF)


class MpSum:
    def __init__(self, place, copies, part, full, own, bufs):
        self.place, self.copies, self.part, self.full, self.own = place, copies, part, full, own
        (self.from_peer, self.send_opp, self.send_right, self.send_left) = bufs[:4]
        (self.fwd, self.direct, self.comb) = bufs[4:]
        x = place.x
        self.order = [(x + 2) % 4, (x + 1) % 4, (x + 3) % 4, x]
        self.peer, self.right, self.left = place.peer(), place.on_x(1), place.on_x(3)
        self.live = [{} for _ in range(CHUNKS)]

    def rows(self, j, core, x):
        return rows_at(j * CHUNK + core * HALF + x * PIECE, PIECE)

    def own_rows(self, j):
        return self.rows(j, self.place.core, self.place.x)

    def chip_sum(self, j, slot, low, size):
        cols = pl.ds(low, size)
        return self.part[self.rows(j, self.place.core, self.order[slot]), cols].astype(
            F32
        ) + self.from_peer[j, slot, :, cols].astype(F32)

    def exchange(self, j):
        self.live[j]["ex"] = [
            self.copies.start(
                self.part.at[self.rows(j, 1 - self.place.core, at)],
                self.from_peer.at[j, slot],
                self.peer,
            )
            for slot, at in enumerate(self.order)
        ]

    def first(self, j):
        live, copies = self.live[j], self.copies
        low, high = pl.ds(0, COLS), pl.ds(COLS, COLS)
        live["ex"][0].wait_recv()
        self.send_opp[j] = self.chip_sum(j, 0, 0, D).astype(BF)
        live["fr"] = copies.start(self.send_opp.at[j, :, low], self.fwd.at[j, 0], self.right)
        live["fl"] = copies.start(self.send_opp.at[j, :, high], self.fwd.at[j, 1], self.left)
        live["ex"][1].wait_recv()
        self.send_right[j, 0] = self.chip_sum(j, 1, COLS, COLS).astype(BF)
        live["dr"] = copies.start(self.send_right.at[j, 0], self.direct.at[j, 1], self.right)
        live["ex"][2].wait_recv()
        self.send_left[j, 0] = self.chip_sum(j, 2, 0, COLS).astype(BF)
        live["dl"] = copies.start(self.send_left.at[j, 0], self.direct.at[j, 0], self.left)

    def second(self, j):
        live, copies = self.live[j], self.copies
        live["fr"].wait_recv()
        self.send_right[j, 1] = (
            self.chip_sum(j, 1, 0, COLS) + self.fwd[j, 0].astype(F32)
        ).astype(BF)
        live["cr"] = copies.start(self.send_right.at[j, 1], self.comb.at[j, 0], self.right)
        live["fl"].wait_recv()
        self.send_left[j, 1] = (
            self.chip_sum(j, 2, COLS, COLS) + self.fwd[j, 1].astype(F32)
        ).astype(BF)
        live["cl"] = copies.start(self.send_left.at[j, 1], self.comb.at[j, 1], self.left)

    def total(self, j):
        live, mine = self.live[j], pl.ds(j * PIECE, PIECE)
        live["ex"][3].wait_recv()
        live["dl"].wait_recv()
        live["cr"].wait_recv()
        self.own[mine, 0:COLS] = (
            self.chip_sum(j, 3, 0, COLS)
            + self.direct[j, 0].astype(F32)
            + self.comb[j, 0].astype(F32)
        )
        live["dr"].wait_recv()
        live["cl"].wait_recv()
        self.own[mine, COLS:D] = (
            self.chip_sum(j, 3, COLS, COLS)
            + self.direct[j, 1].astype(F32)
            + self.comb[j, 1].astype(F32)
        )

    def send(self, j, at, low, size, device):
        block = self.full.at[self.rows(j, self.place.core, at), pl.ds(low, size)]
        return self.copies.start(block, block, device)

    def spread(self, j):
        live, x = self.live[j], self.place.x
        live["rl"] = self.send(j, x, 0, COLS, self.right)
        live["lh"] = self.send(j, x, COLS, COLS, self.left)
        live["rh"] = self.send(j, x, COLS, COLS, self.right)
        live["ll"] = self.send(j, x, 0, COLS, self.left)
        live["pp"] = [self.send(j, x, 0, D, self.peer)]

    def relay(self, j):
        live, x = self.live[j], self.place.x
        live["rl"].wait_recv()
        live["gr"] = self.send(j, (x + 3) % 4, 0, COLS, self.right)
        live["lh"].wait_recv()
        live["gl"] = self.send(j, (x + 1) % 4, COLS, COLS, self.left)
        live["rh"].wait_recv()
        live["pp"].append(self.send(j, (x + 3) % 4, 0, D, self.peer))
        live["ll"].wait_recv()
        live["pp"].append(self.send(j, (x + 1) % 4, 0, D, self.peer))

    def last(self, j):
        live, x = self.live[j], self.place.x
        live["gr"].wait_recv()
        live["pp"].append(self.send(j, (x + 2) % 4, 0, COLS, self.peer))
        live["gl"].wait_recv()
        live["pp"].append(self.send(j, (x + 2) % 4, COLS, COLS, self.peer))

    def arrived(self, j):
        for copy in self.live[j]["pp"]:
            copy.wait_recv()

    def slots(self, produce, finish, ready=None):
        for slot in range(CHUNKS + 7):
            for j in range(CHUNKS):
                stage = slot - j
                if stage == 0:
                    produce(j)
                    self.exchange(j)
                elif stage == 1:
                    self.first(j)
                elif stage == 2:
                    self.second(j)
                elif stage == 3:
                    self.total(j)
                    finish(j)
                    self.spread(j)
                elif stage == 4:
                    self.relay(j)
                elif stage == 5:
                    self.last(j)
                elif stage == 6:
                    self.arrived(j)
                    if ready is not None:
                        ready(j)
            yield slot
        self.copies.finish()


MP_COPIES = CHUNKS * 21


def mp_scratch():
    return [
        pltpu.VMEM((CHUNKS, 4, PIECE, D), BF),
        pltpu.VMEM((CHUNKS, PIECE, D), BF),
        pltpu.VMEM((CHUNKS, 2, PIECE, COLS), BF),
        pltpu.VMEM((CHUNKS, 2, PIECE, COLS), BF),
        pltpu.VMEM((CHUNKS, 2, PIECE, COLS), BF),
        pltpu.VMEM((CHUNKS, 2, PIECE, COLS), BF),
        pltpu.VMEM((CHUNKS, 2, PIECE, COLS), BF),
    ]


def run(slots):
    for _ in slots:
        pass


def interleave(slots, blocks):
    blocks = list(blocks)
    for _ in slots:
        if blocks:
            blocks.pop(0)()
    for block in blocks:
        block()


def ring_gather(copies, right, left, held):
    first = copies.start(held.at[0, 0], held.at[1, 0], right)
    second = copies.start(held.at[0, 1], held.at[3, 1], left)
    third = copies.start(held.at[0, 1], held.at[1, 1], right)
    fourth = copies.start(held.at[0, 0], held.at[3, 0], left)
    yield
    first.wait_recv()
    fifth = copies.start(held.at[1, 0], held.at[2, 0], right)
    second.wait_recv()
    sixth = copies.start(held.at[3, 1], held.at[2, 1], left)
    yield
    for copy in (third, fourth, fifth, sixth):
        copy.wait_recv()
    yield


def state_scan(place, copies, held_y, held_z, out, reverse):
    def counted(position, step):
        at = (position - step + 4) % 4
        reached = at > position if reverse else at < position
        return jnp.where(reached, 1.0, 0.0)

    yield from ring_gather(copies, place.on_y(1), place.on_y(3), held_y)
    for head in range(2):
        parts = [held_y[k, head].astype(F32) for k in range(4)]
        held_z[0, head] = (parts[0] + parts[1] + parts[2] + parts[3]).astype(BF)
    gather = ring_gather(copies, place.on_z(1), place.on_z(3), held_z)
    next(gather)
    for head in range(2):
        total = counted(place.y, 1) * held_y[1, head].astype(F32)
        for step in range(2, 4):
            total = total + counted(place.y, step) * held_y[step, head].astype(F32)
        out[head] = total
    yield
    yield from gather
    for head in range(2):
        total = out[head]
        for step in range(1, 4):
            total = total + counted(place.z, step) * held_z[step, head].astype(F32)
        out[head] = total
    yield


def feature_tables():
    pairs = [(a, b) for a in range(FEAT) for b in range(a, FEAT)]
    first = np.zeros((2, 2 * FEAT, WIDE), np.float32)
    second = np.zeros((2, 2 * FEAT, WIDE), np.float32)
    vectors = np.zeros((8, WIDE), np.float32)
    vectors[0, 0] = vectors[1, 0] = vectors[2, 0] = 1.0
    for a in range(FEAT):
        vectors[1, 1 + a] = 1.0
        vectors[2, 1 + a] = FEAT ** (-0.25)
        for h in range(2):
            first[h, h * FEAT + a, 1 + a] = 1.0
    for number, (a, b) in enumerate(pairs):
        at = 1 + FEAT + number
        vectors[2, at] = (1.0 if a == b else 2.0**0.5) * (2.0 * FEAT) ** (-0.5)
        for h in range(2):
            first[h, h * FEAT + a, at] = 1.0
            second[h, h * FEAT + b, at] = 1.0
    return jnp.asarray(first, BF), jnp.asarray(second, BF), jnp.asarray(vectors, F32)


def factors(head, values, first, second, vectors):
    high, low = values
    left = dot(high, first[head]) + dot(low, first[head]) + vectors[0:1]
    right = dot(high, second[head]) + dot(low, second[head]) + vectors[1:2]
    return left, right


def of_head(values, head):
    lane = lax.broadcasted_iota(jnp.int32, values.shape, 1)
    return jnp.where((lane >= head * FEAT) & (lane < (head + 1) * FEAT), values, jnp.zeros_like(values))


def products(head, query, key, rows, count):
    high, low = (of_head(part[rows], head) for part in query)
    key_high, key_low = (part[0:count] for part in key)
    return dot_nt(high, key_high) + dot_nt(low, key_high) + dot_nt(high, key_low)


def shape(dims, kind):
    return jax.ShapeDtypeStruct(dims, kind)


def normed(rows, gain):
    factor = lax.rsqrt(jnp.mean(rows * rows, axis=-1, keepdims=True) + EPSILON)
    return rows * factor * gain


FORWARD_SAVED = (
    ("normed_one", (ROWS, D), BF),
    ("query", (2, ROWS, 2 * FEAT), BF),
    ("key", (2, ROWS, 2 * FEAT), BF),
    ("value", (ROWS, WIDE), BF),
    ("query_feat", (2, ROWS, WIDE), BF),
    ("key_feat", (2, ROWS, WIDE), BF),
    ("kernel", (2, ROWS, ROWS), BF),
    ("carried", (2, STATE, WIDE), F32),
    ("quotient", (ROWS, WIDE), F32),
    ("denominator", (2, ROWS, 1), F32),
    ("mixed_lin", (ROWS, WIDE), BF),
    ("resid_one", (OWN, D), F32),
    ("normed_two", (ROWS, D), BF),
    ("query_win", (ROWS, WIDE), BF),
    ("keys_all", (ROWS + WIN, WIDE), BF),
    ("values_all", (ROWS + WIN, WIDE), BF),
    ("probs", (2, ROWS, TILE), F32),
    ("mixed_win", (ROWS, WIDE), BF),
    ("resid_two", (OWN, D), F32),
    ("part_four", (ROWS, D), BF),
    ("gate_sum", (16, TILE, FF), BF),
    ("up_sum", (16, TILE, FF), BF),
    ("down_sum", (16, TILE, FF), BF),
    ("result", (ROWS, D), BF),
)
FORWARD_WEIGHTS = (
    ("w_query", (D, 2 * FEAT)),
    ("w_key", (D, 2 * FEAT)),
    ("w_value", (D, WIDE)),
    ("w_out", (WIDE, D)),
    ("win_q", (D, WIDE)),
    ("win_k", (D, WIDE)),
    ("win_v", (D, WIDE)),
    ("win_out", (WIDE, D)),
    ("w_gate", (D, FF)),
    ("w_up", (D, FF)),
    ("w_down", (FF, D)),
)
FORWARD_INPUTS = (
    ("tokens", "group_col", "group_row", "key_groups", "tail_flag", "gain_one", "gain_two", "gain_three")
    + ("first", "second", "vectors")
    + ("out_grad",)
)


def forward_kernel(*refs):
    take = list(refs)

    def pop(names):
        found = {name: take.pop(0) for name in names}
        return found

    inputs = pop(FORWARD_INPUTS)
    hbm_weights = pop([name for name, _ in FORWARD_WEIGHTS])
    hbm_saved = pop([name for name, _, _ in FORWARD_SAVED])
    weights = pop([name for name, _ in FORWARD_WEIGHTS])
    saved = pop([name for name, _, _ in FORWARD_SAVED])
    (og, part, own, halo_flag, normed_three, hidden, gate_low, up_low, gate_act, up_act) = (
        take.pop(0) for _ in range(10)
    )
    held_y, held_z = take.pop(0), take.pop(0)
    bufs = [take.pop(0) for _ in range(7)]
    send_sems, recv_sems, state_send, state_recv, halo_send, halo_recv, local_sems = take

    place = Place()
    local = Locals(local_sems)
    loads = {name: local.start(hbm_weights[name], weights[name]) for name, _ in FORWARD_WEIGHTS}
    og_load = local.start(inputs["out_grad"], og)
    saves = []

    def save(name):
        saves.append(local.start(saved[name], hbm_saved[name]))

    greet(
        [place.peer()]
        + [place.on_x(k) for k in (1, 3)]
        + [place.on_y(k) for k in (1, 3)]
        + [place.on_z(k) for k in (1, 3)]
        + [place.along(1), place.along(15)]
    )
    tokens = inputs["tokens"]
    first, second, vectors = (inputs[k] for k in ("first", "second", "vectors"))
    scale = vectors[2:3]
    gain_one, gain_two, gain_three = (inputs["gain_" + k] for k in ("one", "two", "three"))
    group_col, group_row = inputs["group_col"], inputs["group_row"]
    normed_one = saved["normed_one"]

    def norm_rows(i, _):
        rows = rows_at(i * 32, 32)
        normed_one[rows] = normed(tokens[rows].astype(F32), gain_one[...]).astype(BF)
        return 0

    lax.fori_loop(0, ROWS // 32, norm_rows, 0)
    save("normed_one")
    query, key, value = saved["query"], saved["key"], saved["value"]
    for name, held in (("w_query", query), ("w_key", key)):
        loads[name].wait()
        held[0], held[1] = halves(dot(normed_one[...], weights[name][...]))
    loads["w_value"].wait()
    value[...] = dot(normed_one[...], weights["w_value"][...]).astype(BF)
    save("query")
    save("key")
    save("value")

    in_last = (group_col[...] == group_row[0:1, ROWS - 1 : ROWS]).astype(F32)
    query_feat, key_feat = saved["query_feat"], saved["key_feat"]
    for head in range(2):
        left, right = factors(head, (key[0], key[1]), first, second, vectors)
        feat = (left * right * scale).astype(BF)
        key_feat[head] = feat
        kept = feat.astype(F32) * in_last
        held_y[0, head, 0:HD] = dot_tn(value[:, head * HD : (head + 1) * HD], kept.astype(BF)).astype(BF)
        held_y[0, head, HD:STATE] = jnp.broadcast_to(
            jnp.sum(kept, axis=0, keepdims=True), (STATE - HD, WIDE)
        ).astype(BF)
    save("key_feat")
    copies_state = Copies(state_send, state_recv)
    scan = state_scan(place, copies_state, held_y, held_z, saved["carried"], False)
    next(scan)
    kernel, quotient, denominator = (saved[k] for k in ("kernel", "quotient", "denominator"))
    for head in range(2):
        left, right = factors(head, (query[0], query[1]), first, second, vectors)
        query_feat[head] = (left * right * scale).astype(BF)
    save("query_feat")
    next(scan)
    for tile in range(ROWS // TILE):
        rows, count = pl.ds(tile * TILE, TILE), (tile + 1) * TILE
        place_row = lax.broadcasted_iota(jnp.int32, (TILE, count), 0) + tile * TILE
        place_col = lax.broadcasted_iota(jnp.int32, (TILE, count), 1)
        kept = (place_col <= place_row) & (group_col[rows] == group_row[0:1, 0:count])
        for head in range(2):
            inner = products(head, (query.at[0], query.at[1]), (key.at[0], key.at[1]), rows, count)
            block = jnp.where(kept, 1.0 + inner * 0.25 + inner * inner * 0.03125, 0.0).astype(BF)
            kernel[head, rows, 0:count] = block
            denominator[head, rows] = jnp.sum(block.astype(F32), axis=1, keepdims=True)
            quotient[rows, head * HD : (head + 1) * HD] = dot(
                block, value[0:count, head * HD : (head + 1) * HD]
            )
        next(scan)
    for _ in scan:
        pass
    copies_state.finish()
    save("kernel")
    save("carried")
    incoming = (group_col[...] == group_row[0:1, 0:1]).astype(F32) * jnp.where(place.seq > 0, 1.0, 0.0)
    carried, mixed_lin = saved["carried"], saved["mixed_lin"]
    for head in range(2):
        lanes = slice(head * HD, (head + 1) * HD)
        feat = query_feat[head]
        numer = quotient[:, lanes] + incoming * dot_nt(feat, carried[head, 0:HD].astype(BF))
        denom = denominator[head] + incoming * jnp.sum(
            feat.astype(F32) * carried[head, HD : HD + 1], axis=1, keepdims=True
        )
        ratio = numer / denom
        denominator[head] = denom
        quotient[:, lanes] = ratio
        mixed_lin[:, lanes] = ratio.astype(BF)
    save("quotient")
    save("denominator")
    save("mixed_lin")

    copies = Copies(send_sems, recv_sems)
    resid_one, resid_two = saved["resid_one"], saved["resid_two"]
    normed_two = saved["normed_two"]
    loads["w_out"].wait()
    sum_one = MpSum(place, copies, part, normed_two, own, bufs)

    def produce_one(j):
        rows = pl.ds(j * CHUNK, CHUNK)
        part[rows] = dot(mixed_lin[rows], weights["w_out"][...]).astype(BF)

    def finish_one(j):
        mine = pl.ds(j * PIECE, PIECE)
        rows = own[mine] + tokens[sum_one.own_rows(j)].astype(F32)
        resid_one[mine] = rows
        normed_two[sum_one.own_rows(j)] = normed(rows, gain_two[...]).astype(BF)

    run(sum_one.slots(produce_one, finish_one))
    save("resid_one")
    save("normed_two")

    query_win, keys_all, values_all = (saved[k] for k in ("query_win", "keys_all", "values_all"))
    loads["win_k"].wait()
    keys_all[WIN : WIN + ROWS] = dot(normed_two[...], weights["win_k"][...]).astype(BF)
    loads["win_v"].wait()
    values_all[WIN : WIN + ROWS] = dot(normed_two[...], weights["win_v"][...]).astype(BF)
    copies_halo = Copies(halo_send, halo_recv)
    halo = [
        copies_halo.start(ref.at[pl.ds(ROWS, WIN)], ref.at[pl.ds(0, WIN)], place.along(1))
        for ref in (keys_all, values_all)
    ]
    halo.append(copies_halo.start(inputs["tail_flag"], halo_flag, place.along(1)))
    loads["win_q"].wait()
    query_win[...] = dot(normed_two[...], weights["win_q"][...]).astype(BF)
    save("query_win")
    probs, mixed_win = saved["probs"], saved["mixed_win"]
    tile_row = lax.broadcasted_iota(jnp.int32, (WIN, TILE), 0)
    tile_col = lax.broadcasted_iota(jnp.int32, (WIN, TILE), 1)
    near = (tile_col > tile_row) & (tile_col <= tile_row + WIN)
    score_scale = HD ** (-0.5)

    def window_tile(t):
        rows = pl.ds(t * WIN, WIN)
        groups = inputs["key_groups"][t : t + 1]
        if t == 0:
            flag = jnp.where(place.seq > 0, halo_flag[0:1].astype(F32), 0.0)
            column = lax.broadcasted_iota(jnp.int32, (1, TILE), 1)
            halo_group = jnp.where(flag > 0.5, group_row[0:1, 0:1], -2)
            groups = jnp.where(column < WIN, halo_group, groups)
        kept = near & (group_col[rows] == groups)
        for head in range(2):
            lanes = slice(head * HD, (head + 1) * HD)
            scores = dot_nt(query_win[rows, lanes], keys_all[t * WIN : t * WIN + TILE, lanes])
            scores = jnp.where(kept, scores * score_scale, -1e30)
            exp_scores = jnp.exp(scores - jnp.max(scores, axis=1, keepdims=True))
            found = exp_scores / jnp.sum(exp_scores, axis=1, keepdims=True)
            probs[head, rows] = found
            mixed_win[rows, lanes] = dot(
                found.astype(BF), values_all[t * WIN : t * WIN + TILE, lanes]
            ).astype(BF)

    for t in range(1, 8):
        window_tile(t)
    for copy in halo:
        copy.wait_recv()
    window_tile(0)
    copies_halo.finish()
    for name in ("keys_all", "values_all", "probs", "mixed_win"):
        save(name)

    loads["win_out"].wait()
    sum_two = MpSum(place, copies, part, normed_three, own, bufs)

    def produce_two(j):
        rows = pl.ds(j * CHUNK, CHUNK)
        part[rows] = dot(mixed_win[rows], weights["win_out"][...]).astype(BF)

    def finish_two(j):
        mine = pl.ds(j * PIECE, PIECE)
        rows = own[mine] + resid_one[mine]
        resid_two[mine] = rows
        normed_three[sum_two.own_rows(j)] = normed(rows, gain_three[...]).astype(BF)

    run(sum_two.slots(produce_two, finish_two))
    save("resid_two")

    w_gate, w_up, w_down = (weights[k] for k in ("w_gate", "w_up", "w_down"))
    for name in ("w_gate", "w_up", "w_down"):
        loads[name].wait()
    og_load.wait()
    gate_act[...] = dot(normed_three[...], w_gate[...])
    up_act[...] = dot(normed_three[...], w_up[...])
    for tile in range(4):
        rows = pl.ds(tile * TILE, TILE)
        gate = gate_act[rows]
        hidden[rows] = (gate / (1.0 + jnp.exp(-gate)) * up_act[rows]).astype(BF)
    result = saved["result"]
    sum_three = MpSum(place, copies, part, result, own, bufs)

    def produce_three(j):
        rows = pl.ds(j * CHUNK, CHUNK)
        part[rows] = dot(hidden[rows], w_down[...]).astype(BF)

    def finish_three(j):
        mine = pl.ds(j * PIECE, PIECE)
        result[sum_three.own_rows(j)] = (own[mine] + resid_two[mine]).astype(BF)

    part_four = saved["part_four"]

    def hidden_back(quarter):
        rows = pl.ds(quarter * TILE, TILE)
        hidden_grad = dot_nt(og[rows], w_down[...])
        gate = gate_act[rows]
        sigmoid = 1.0 / (1.0 + jnp.exp(-gate))
        act = gate * sigmoid
        up_low[rows] = (hidden_grad * act).astype(BF)
        gate_low[rows] = (
            hidden_grad * up_act[rows] * (sigmoid + act * (1.0 - sigmoid))
        ).astype(BF)

    def input_back(quarter):
        cols = pl.ds(quarter * 512, 512)
        part_four[:, cols] = (
            dot_nt(gate_low[...], w_gate[cols]) + dot_nt(up_low[...], w_up[cols])
        ).astype(BF)
        if quarter == 3:
            save("part_four")

    def weight_back(name, rows_ref, right, quarter):
        cols = pl.ds(quarter * 512, 512)
        block = dot_tn(rows_ref[:, cols], right[...]).astype(BF)
        saved[name][quarter * 4 : quarter * 4 + 4] = block.reshape(4, TILE, FF)
        if quarter == 3:
            save(name)

    blocks = [functools.partial(hidden_back, k) for k in range(4)]
    blocks += [functools.partial(input_back, k) for k in range(4)]
    for name, rows_ref, right in (
        ("gate_sum", normed_three, gate_low),
        ("up_sum", normed_three, up_low),
        ("down_sum", og, hidden),
    ):
        blocks += [functools.partial(weight_back, name, rows_ref, right, k) for k in range(4)]
    pairs = [blocks[k : k + 2] for k in range(0, len(blocks), 2)]

    def both(pair):
        for block in pair:
            block()

    interleave(
        sum_three.slots(produce_three, finish_three),
        [functools.partial(both, pair) for pair in pairs],
    )
    save("result")
    for copy in saves:
        copy.wait()


def forward(inputs, weights):
    scratch = [pltpu.VMEM(dims, BF) for _, dims in FORWARD_WEIGHTS]
    scratch += [pltpu.VMEM(dims, kind) for _, dims, kind in FORWARD_SAVED]
    scratch += [
        pltpu.VMEM((ROWS, D), BF),
        pltpu.VMEM((ROWS, D), BF),
        pltpu.VMEM((OWN, D), F32),
        pltpu.VMEM((16, TILE), BF),
        pltpu.VMEM((ROWS, D), BF),
        pltpu.VMEM((ROWS, FF), BF),
        pltpu.VMEM((ROWS, FF), BF),
        pltpu.VMEM((ROWS, FF), BF),
        pltpu.VMEM((ROWS, FF), F32),
        pltpu.VMEM((ROWS, FF), F32),
        pltpu.VMEM((4, 2, STATE, WIDE), BF),
        pltpu.VMEM((4, 2, STATE, WIDE), BF),
    ]
    scratch += mp_scratch()
    scratch += [pltpu.SemaphoreType.DMA((MP_COPIES,))] * 2
    scratch += [pltpu.SemaphoreType.DMA((12,))] * 2
    scratch += [pltpu.SemaphoreType.DMA((3,))] * 2
    scratch += [pltpu.SemaphoreType.DMA((len(FORWARD_WEIGHTS) + len(FORWARD_SAVED) + 1,))]
    hbm = pl.BlockSpec(memory_space=pl.ANY)
    inside = pl.BlockSpec(memory_space=pltpu.VMEM)
    outs = pl.pallas_call(
        forward_kernel,
        out_shape=[shape(dims, kind) for _, dims, kind in FORWARD_SAVED],
        in_specs=[inside] * (len(FORWARD_INPUTS) - 1) + [hbm] * (len(FORWARD_WEIGHTS) + 1),
        out_specs=[hbm] * len(FORWARD_SAVED),
        scratch_shapes=scratch,
        compiler_params=pltpu.CompilerParams(
            collective_id=0, has_side_effects=True, vmem_limit_bytes=VMEM_LIMIT
        ),
    )(*[inputs[name] for name in FORWARD_INPUTS], *[weights[name] for name, _ in FORWARD_WEIGHTS])
    return dict(zip([name for name, _, _ in FORWARD_SAVED], outs))


class SeqSum:
    def __init__(self, place, copies, blocks, out, bufs):
        self.place, self.copies, self.blocks, self.out = place, copies, blocks, out
        self.one, self.two, self.three, self.four = bufs[0:3], bufs[3:6], bufs[6:9], bufs[9:12]
        z, y = place.z, place.y
        ring_y, ring_z = (place.on_y(1), place.on_y(3)), (place.on_z(1), place.on_z(3))

        def pick_one(k, half):
            return blocks.at[:, (y + k) % 4, pl.ds(half * 32, 32)]

        def pick_two(k, half):
            return blocks.at[(z + k) % 4, :, pl.ds(64 + half * 32, 32)]

        def pick_three(k, half):
            return blocks.at[(z + k) % 4, y, pl.ds(half * 32, 32)]

        def pick_four(k, half):
            return blocks.at[z, (y + k) % 4, pl.ds(64 + half * 32, 32)]

        self.early = ((ring_y, pick_one, self.one, {}), (ring_z, pick_two, self.two, {}))
        self.late = ((ring_z, pick_three, self.three, {}), (ring_y, pick_four, self.four, {}))

    def begin(self, rings):
        for (right, left), pick, (fwd, direct, comb), live in rings:
            live["fr"] = self.copies.start(pick(2, 0), fwd.at[0], right)
            live["fl"] = self.copies.start(pick(2, 1), fwd.at[1], left)
            live["dr"] = self.copies.start(pick(1, 1), direct.at[1], right)
            live["dl"] = self.copies.start(pick(3, 0), direct.at[0], left)

    def join(self, rings):
        for (right, left), pick, (fwd, direct, comb), live in rings:
            live["fr"].wait_recv()
            block = pick(1, 0)
            block[...] = (block[...].astype(F32) + fwd[0].astype(F32)).astype(BF)
            live["cr"] = self.copies.start(block, comb.at[0], right)
            live["fl"].wait_recv()
            block = pick(3, 1)
            block[...] = (block[...].astype(F32) + fwd[1].astype(F32)).astype(BF)
            live["cl"] = self.copies.start(block, comb.at[1], left)

    def total(self, ring, half):
        _, pick, (fwd, direct, comb), live = ring
        live["dl" if half == 0 else "dr"].wait_recv()
        live["cr" if half == 0 else "cl"].wait_recv()
        return (
            pick(0, half)[...].astype(F32) + direct[half].astype(F32) + comb[half].astype(F32)
        )

    def step(self, number):
        if number == 0:
            self.begin(self.early)
        elif number == 1:
            self.join(self.early)
        elif number == 2:
            for ring in self.early:
                for half in range(2):
                    block = ring[1](0, half)
                    block[...] = self.total(ring, half).astype(BF)
            self.begin(self.late)
        elif number == 3:
            self.join(self.late)
        else:
            for half in range(2):
                self.out[pl.ds(half * 32, 32)] = self.total(self.late[0], half)
                self.out[pl.ds(64 + half * 32, 32)] = self.total(self.late[1], half)


def seq_scratch(width):
    early, late = (2, 4, 32, width), (2, 32, width)
    return [pltpu.VMEM(early, BF)] * 6 + [pltpu.VMEM(late, BF)] * 6


GROUPS = (
    ("gate_sum", FF),
    ("up_sum", FF),
    ("down_sum", FF),
    ("win_out_sum", WIDE),
    ("win_sum", 3 * WIDE),
    ("out_sum", WIDE),
    ("lin_sum", WIDE + TILE),
)
BACKWARD_FROM = (
    "query",
    "key",
    "value",
    "query_feat",
    "key_feat",
    "kernel",
    "carried",
    "quotient",
    "denominator",
    "mixed_lin",
    "resid_one",
    "query_win",
    "keys_all",
    "values_all",
    "probs",
    "mixed_win",
    "resid_two",
)
BACKWARD_INPUTS = ("group_col", "group_row", "gain_one", "gain_two", "gain_three", "first", "second", "vectors")
BACKWARD_INPUTS += ("placing",)
BACKWARD_HBM = ("part_four", "out_grad", "tokens", "normed_one", "normed_two", "gate_sum", "up_sum", "down_sum")
BACKWARD_HBM += ("w_query", "w_key", "w_value", "w_out", "win_q", "win_k", "win_v", "win_out")
SAVED_SHAPES = {name: (dims, kind) for name, dims, kind in FORWARD_SAVED}


def backward_kernel(*refs):
    take = list(refs)

    def pop(names):
        return {name: take.pop(0) for name in names}

    inputs = pop(BACKWARD_INPUTS)
    hbm = pop(BACKWARD_HBM)
    hbm_saved = pop(BACKWARD_FROM)
    tokens_low, gains_out = take.pop(0), take.pop(0)
    sums = pop([name for name, _ in GROUPS])
    saved = pop(BACKWARD_FROM)
    blocks = pop([name for name, _ in GROUPS])
    seq_bufs = {name: [take.pop(0) for _ in range(12)] for name, _ in GROUPS}
    part, other_full, own, grad_own, token_own = (take.pop(0) for _ in range(5))
    normed_low, w_query, w_key, w_out, win_out = (take.pop(0) for _ in range(5))
    mixed_grad, keys_sum, values_sum, back_key, back_value, win_grads = (take.pop(0) for _ in range(6))
    numer_low, denom_grad, query_sum, key_sum, value_sum, lin_grads = (take.pop(0) for _ in range(6))
    gain_sums, gain_low, gain_z, gain_zz, gain_y, gain_x, gain_xx, gain_p, gain_pp = (
        take.pop(0) for _ in range(9)
    )
    held_y, held_z, later = (take.pop(0) for _ in range(3))
    bufs = [take.pop(0) for _ in range(7)]
    (send_sems, recv_sems, seq_send, seq_recv, few_send, few_recv, local_sems) = take

    place = Place()
    z, y = place.z, place.y
    local = Locals(local_sems)
    copies = Copies(send_sems, recv_sems)
    sum_four = MpSum(place, copies, part, tokens_low, own, bufs)
    sum_five = MpSum(place, copies, part, other_full, own, bufs)
    sum_six = MpSum(place, copies, part, tokens_low, own, bufs)
    loads = {}

    def load(name, src, dst):
        loads.setdefault(name, []).append(local.start(src, dst))

    def need(*names):
        for name in names:
            for copy in loads.pop(name, []):
                copy.wait()

    load("part_four", hbm["part_four"], part)
    for name in ("gate_sum", "up_sum", "down_sum"):
        load(name, hbm[name], blocks[name])
    load("resid_two", hbm_saved["resid_two"], saved["resid_two"])
    for j in range(CHUNKS):
        mine = pl.ds(j * PIECE, PIECE)
        load("grad_own", hbm["out_grad"].at[sum_four.own_rows(j)], token_own.at[mine])
    load("win_out", hbm["win_out"], win_out)
    for name in BACKWARD_FROM[::-1]:
        if name != "resid_two":
            load(name, hbm_saved[name], saved[name])
    win_blocks, lin_blocks = blocks["win_sum"], blocks["lin_sum"]
    for k, name in enumerate(("win_q", "win_k", "win_v")):
        load("win", hbm[name], win_blocks.at[:, :, :, pl.ds(k * WIDE, WIDE)])
    load("normed_two", hbm["normed_two"], normed_low)
    load("w_value", hbm["w_value"], lin_blocks.at[:, :, :, pl.ds(0, WIDE)])
    load("w_query", hbm["w_query"], w_query)
    load("w_key", hbm["w_key"], w_key)
    load("w_out", hbm["w_out"], w_out)

    greet(
        [place.peer()]
        + [place.on_x(k) for k in (1, 2, 3)]
        + [place.on_y(k) for k in (1, 2, 3)]
        + [place.on_z(k) for k in (1, 2, 3)]
        + [place.along(1), place.along(15)]
    )
    seq_copies = Copies(seq_send, seq_recv)
    few = Copies(few_send, few_recv)
    gain_sums[...] = jnp.zeros_like(gain_sums)
    seq_sums = {
        name: SeqSum(place, seq_copies, blocks[name], sums[name], seq_bufs[name])
        for name, _ in GROUPS
    }
    queue = []

    def step(name, number):
        if number == 0:
            need(name)
        seq_sums[name].step(number)

    def pump(count=1):
        for _ in range(count):
            if queue:
                queue.pop(0)()

    def plan(*tasks):
        queue.extend(functools.partial(step, name, number) for name, number in tasks)

    first, second, vectors = (inputs[k] for k in ("first", "second", "vectors"))
    scale = vectors[2:3]
    group_col, group_row = inputs["group_col"], inputs["group_row"]
    in_last = (group_col[...] == group_row[0:1, ROWS - 1 : ROWS]).astype(F32)
    incoming = (group_col[...] == group_row[0:1, 0:1]).astype(F32) * jnp.where(place.seq > 0, 1.0, 0.0)

    def back_through_norm(mp_sum, number, resid, gain, grad, to, j):
        mine = pl.ds(j * PIECE, PIECE)
        rows, normed_grad = resid[mine].astype(F32), own[mine]
        factor = lax.rsqrt(jnp.mean(rows * rows, axis=-1, keepdims=True) + EPSILON)
        unit = rows * factor
        scaled = normed_grad * gain[...]
        total = grad[mine].astype(F32) + factor * (
            scaled - unit * jnp.mean(scaled * unit, axis=-1, keepdims=True)
        )
        here = jnp.sum(normed_grad * unit, axis=0, keepdims=True)
        gain_sums[number : number + 1] = here if j == 0 else gain_sums[number : number + 1] + here
        if number > 0:
            grad_own[mine] = total
        to[mp_sum.own_rows(j)] = total.astype(BF)

    need("part_four", "resid_two", "grad_own")
    plan(("gate_sum", 0), ("up_sum", 0), ("down_sum", 0))

    def finish_four(j):
        back_through_norm(sum_four, 2, saved["resid_two"], inputs["gain_three"], token_own, tokens_low, j)

    def ready_four(j):
        if j == 0:
            need("win_out")
        rows = pl.ds(j * CHUNK, CHUNK)
        mixed_grad[rows] = dot_nt(tokens_low[rows], win_out[...]).astype(BF)

    for slot in sum_four.slots(lambda j: None, finish_four, ready_four):
        pump()
        if slot == 5:
            plan(("gate_sum", 1))
        if slot == 8:
            plan(("up_sum", 1))

    need("probs", "query_win", "keys_all", "values_all", "mixed_win")
    probs, query_win, keys_all, values_all = (
        saved[k] for k in ("probs", "query_win", "keys_all", "values_all")
    )
    score_scale = HD ** (-0.5)
    back = []
    for t in range(8):
        rows, window = pl.ds(t * WIN, WIN), pl.ds(t * WIN, TILE)
        for head in range(2):
            lanes = slice(head * HD, (head + 1) * HD)
            grad_tile, held = mixed_grad[rows, lanes], probs[head, rows]
            probs_grad = dot_nt(grad_tile, values_all[window, lanes])
            score_low = (
                held * (probs_grad - jnp.sum(probs_grad * held, axis=1, keepdims=True))
            ).astype(BF)
            win_grads[rows, lanes] = (dot(score_low, keys_all[window, lanes]) * score_scale).astype(BF)
            for ref, found in (
                (keys_sum, dot_tn(score_low, query_win[rows, lanes]) * score_scale),
                (values_sum, dot_tn(held.astype(BF), grad_tile)),
            ):
                if t == 0:
                    ref[window, lanes] = found
                else:
                    ref[rows, lanes] += found[:WIN]
                    ref[pl.ds(t * WIN + WIN, WIN), lanes] = found[WIN:]
        if t == 0:
            for k, ref in enumerate((keys_sum, values_sum)):
                to_send = back_key if k == 0 else back_value
                to_send[0] = ref[0:WIN].astype(BF)
                back.append(few.start(to_send.at[0], to_send.at[1], place.along(15)))
        if t == 4:
            plan(("down_sum", 1))
            pump()
    most = slice(0, ROWS - WIN)
    for k, (ref, got) in enumerate(((keys_sum, back_key), (values_sum, back_value))):
        lanes = slice((k + 1) * WIDE, (k + 2) * WIDE)
        win_grads[most, lanes] = ref[WIN:ROWS].astype(BF)
        back[k].wait_recv()
        win_grads[ROWS - WIN : ROWS, lanes] = (
            ref[ROWS : ROWS + WIN] + got[1].astype(F32)
        ).astype(BF)
    need("win")

    def produce_five(j):
        rows = pl.ds(j * CHUNK, CHUNK)
        for k in range(4):
            part[rows, k * 512 : (k + 1) * 512] = dot_nt(
                win_grads[rows], win_blocks[k].reshape(512, 3 * WIDE)
            ).astype(BF)

    def weight_back(name, left, right, quarter):
        blocks[name][quarter] = dot_tn(
            left[:, quarter * 512 : (quarter + 1) * 512], right[...]
        ).astype(BF).reshape(4, TILE, right.shape[1])

    def finish_five(j):
        back_through_norm(sum_five, 1, saved["resid_one"], inputs["gain_two"], grad_own, other_full, j)

    def ready_five(j):
        rows = pl.ds(j * CHUNK, CHUNK)
        if j == 0:
            need("w_out", "denominator", "quotient")
        mixed = dot_nt(other_full[rows], w_out[...]).astype(BF).astype(F32)
        for head in range(2):
            lanes = slice(head * HD, (head + 1) * HD)
            denom = saved["denominator"][head, rows]
            numer_low[rows, lanes] = (mixed[:, lanes] / denom).astype(BF)
            denom_grad[head, rows] = (
                -jnp.sum(mixed[:, lanes] * saved["quotient"][rows, lanes], axis=1, keepdims=True) / denom
            )

    need("resid_one", "normed_two")
    work = [functools.partial(weight_back, "win_out_sum", tokens_low, saved["mixed_win"], k) for k in range(4)]
    work.append(functools.partial(step, "win_out_sum", 0))

    def win_weights(quarter):
        weight_back("win_sum", normed_low, win_grads, quarter)

    late_work = [functools.partial(win_weights, k) for k in range(4)]
    late_work.append(functools.partial(step, "win_sum", 0))
    for slot in sum_five.slots(produce_five, finish_five, ready_five):
        if slot < CHUNKS - 1:
            continue
        for _ in range(2):
            if work:
                work.pop(0)()
            elif late_work:
                late_work.pop(0)()
        if slot == CHUNKS + 1:
            plan(("gate_sum", 2), ("up_sum", 2))
        if slot == CHUNKS + 4:
            plan(("down_sum", 2))
        pump()
    for block in work + late_work:
        block()
    load("normed_one", hbm["normed_one"], normed_low)

    need("query", "key", "value", "query_feat", "key_feat", "kernel", "carried", "mixed_lin")
    query, key, value = (saved[k] for k in ("query", "key", "value"))
    query_feat, key_feat, kernel, carried = (
        saved[k] for k in ("query_feat", "key_feat", "kernel", "carried")
    )
    for head in range(2):
        lanes = slice(head * HD, (head + 1) * HD)
        used = query_feat[head].astype(F32) * incoming
        held_y[0, head, 0:HD] = dot_tn(numer_low[:, lanes], used.astype(BF)).astype(BF)
        held_y[0, head, HD:STATE] = jnp.broadcast_to(
            jnp.sum(used * denom_grad[head], axis=0, keepdims=True), (STATE - HD, WIDE)
        ).astype(BF)
    scan = state_scan(place, few, held_y, held_z, later, True)
    next(scan)

    def through_features(head, values, grad):
        left, right = factors(head, (values[0], values[1]), first, second, vectors)
        scaled = grad * scale
        return dot_nt((scaled * right).astype(BF), first[head]) + dot_nt(
            (scaled * left).astype(BF), second[head]
        )

    for head in range(2):
        lanes = slice(head * HD, (head + 1) * HD)
        grad = incoming * (
            dot(numer_low[:, lanes], carried[head, 0:HD].astype(BF))
            + denom_grad[head] * carried[head, HD : HD + 1]
        )
        found = through_features(head, query, grad)
        query_sum[...] = found if head == 0 else query_sum[...] + found
    next(scan)
    for tile in range(ROWS // TILE):
        rows, count = pl.ds(tile * TILE, TILE), (tile + 1) * TILE
        place_row = lax.broadcasted_iota(jnp.int32, (TILE, count), 0) + tile * TILE
        place_col = lax.broadcasted_iota(jnp.int32, (TILE, count), 1)
        kept = (place_col <= place_row) & (group_col[rows] == group_row[0:1, 0:count])
        key_new, values_new = [], []
        for head in range(2):
            lanes = slice(head * HD, (head + 1) * HD)
            inner = products(head, (query.at[0], query.at[1]), (key.at[0], key.at[1]), rows, count)
            grad = dot_nt(numer_low[rows, lanes], value[0:count, lanes]) + denom_grad[head, rows]
            grad = jnp.where(kept, grad, 0.0).astype(BF).astype(F32)
            inner_grad = (grad * (0.25 + inner * 0.0625)).astype(BF)
            query_sum[rows] += of_head(dot(inner_grad, key[0, 0:count]), head)
            key_new.append(of_head(dot_tn(inner_grad, query[0, rows]), head))
            values_new.append(dot_tn(kernel[head, rows, 0:count], numer_low[rows, lanes]))
        found = key_new[0] + key_new[1]
        before = count - TILE
        if tile > 0:
            key_sum[0:before] += found[0:before]
        key_sum[before:count] = found[before:count]
        for head in range(2):
            lanes = slice(head * HD, (head + 1) * HD)
            if tile > 0:
                value_sum[0:before, lanes] += values_new[head][0:before]
            value_sum[before:count, lanes] = values_new[head][before:count]
        next(scan)
    for _ in scan:
        pass
    for k in range(4):
        weight_back("out_sum", other_full, saved["mixed_lin"], k)
    plan(("out_sum", 0), ("gate_sum", 3), ("win_out_sum", 1), ("up_sum", 3), ("win_sum", 1))
    pump(2)
    for head in range(2):
        lanes = slice(head * HD, (head + 1) * HD)
        state = later[head, 0:HD].astype(BF)
        grad = in_last * (dot(value[:, lanes], state) + later[head, HD : HD + 1])
        key_sum[...] += through_features(head, key, grad)
        value_sum[:, lanes] += in_last * dot_nt(key_feat[head], state)
    need("w_value", "w_query", "w_key")
    placing = inputs["placing"]
    lin_grads[:, 0:WIDE] = value_sum[...].astype(BF)
    lin_grads[:, WIDE : WIDE + TILE] = (
        dot(query_sum[...].astype(BF), placing[0]) + dot(key_sum[...].astype(BF), placing[1])
    ).astype(BF)
    packed = (dot(w_query[...], placing[0]) + dot(w_key[...], placing[1])).astype(BF)
    lin_blocks[:, :, :, WIDE : WIDE + TILE] = packed.reshape(4, 4, TILE, TILE)

    def produce_six(j):
        rows = pl.ds(j * CHUNK, CHUNK)
        for k in range(4):
            part[rows, k * 512 : (k + 1) * 512] = dot_nt(
                lin_grads[rows], lin_blocks[k].reshape(512, WIDE + TILE)
            ).astype(BF)

    for j in range(CHUNKS):
        mine = pl.ds(j * PIECE, PIECE)
        load("token_own", hbm["tokens"].at[sum_six.own_rows(j)], token_own.at[mine])
    need("token_own", "normed_one")

    def finish_six(j):
        back_through_norm(sum_six, 0, token_own, inputs["gain_one"], grad_own, tokens_low, j)

    def gains():
        gain_low[...] = gain_sums[...].astype(BF)

        def block(ref, at, size):
            return ref.at[:, pl.ds(pl.multiple_of(at * size, TILE), size)]

        over = [
            few.start(block(gain_low, (z + k) % 4, 512), gain_z.at[k - 1], place.on_z(k))
            for k in (1, 2, 3)
        ]
        yield
        total = block(gain_low, z, 512)[...].astype(F32)
        for k, copy in enumerate(over):
            copy.wait_recv()
            total = total + gain_z[k].astype(F32)
        gain_zz[...] = total.astype(BF)
        over = [
            few.start(block(gain_zz, (y + k) % 4, TILE), gain_y.at[k - 1], place.on_y(k))
            for k in (1, 2, 3)
        ]
        yield
        total = block(gain_zz, y, TILE)[...].astype(F32)
        for k, copy in enumerate(over):
            copy.wait_recv()
            total = total + gain_y[k].astype(F32)
        gain_x[...] = total.astype(BF)
        over = [few.start(gain_x, gain_xx.at[k - 1], place.on_x(k)) for k in (1, 2, 3)]
        yield
        total = gain_x[...].astype(F32)
        for k, copy in enumerate(over):
            copy.wait_recv()
            total = total + gain_xx[k].astype(F32)
        gain_p[...] = total.astype(BF)
        copy = few.start(gain_p, gain_pp, place.peer())
        yield
        copy.wait_recv()
        gains_out[...] = gain_p[...].astype(F32) + gain_pp[...].astype(F32)

    work = [functools.partial(weight_back, "lin_sum", normed_low, lin_grads, k) for k in range(4)]
    work.append(functools.partial(step, "lin_sum", 0))
    plan(("down_sum", 3), ("out_sum", 1), ("gate_sum", 4), ("up_sum", 4), ("win_out_sum", 2))
    gain_steps = gains()
    for slot in sum_six.slots(produce_six, finish_six):
        if slot < CHUNKS - 1:
            continue
        for _ in range(2):
            if work:
                work.pop(0)()
        pump()
        if slot >= CHUNKS + 2:
            next(gain_steps, None)
    plan(("win_sum", 2), ("lin_sum", 1), ("down_sum", 4), ("out_sum", 2), ("win_out_sum", 3))
    plan(("win_sum", 3), ("lin_sum", 2), ("out_sum", 3), ("win_out_sum", 4), ("win_sum", 4))
    plan(("lin_sum", 3), ("out_sum", 4), ("lin_sum", 4))
    pump(len(queue))
    for _ in gain_steps:
        pass
    seq_copies.finish()
    few.finish()


def backward(saved, inputs, weights):
    hbm = dict(weights)
    for name in ("part_four", "normed_one", "normed_two"):
        hbm[name] = saved[name]
    for name in ("gate_sum", "up_sum", "down_sum"):
        hbm[name] = saved[name].reshape(4, 4, TILE, FF)
    for name in ("win_q", "win_k", "win_v", "w_value"):
        hbm[name] = weights[name].reshape(4, 4, TILE, WIDE)
    hbm["tokens"], hbm["out_grad"] = inputs["tokens"], inputs["out_grad"]
    placing = np.zeros((2, 2 * FEAT, TILE), np.float32)
    for a in range(2 * FEAT):
        placing[0, a, a] = placing[1, a, 2 * FEAT + a] = 1.0
    inputs = dict(inputs, placing=jnp.asarray(placing, BF))
    scratch = [pltpu.VMEM(*SAVED_SHAPES[name]) for name in BACKWARD_FROM]
    scratch += [pltpu.VMEM((4, 4, TILE, width), BF) for _, width in GROUPS]
    for _, width in GROUPS:
        scratch += seq_scratch(width)
    scratch += [
        pltpu.VMEM((ROWS, D), BF),
        pltpu.VMEM((ROWS, D), BF),
        pltpu.VMEM((OWN, D), F32),
        pltpu.VMEM((OWN, D), F32),
        pltpu.VMEM((OWN, D), BF),
        pltpu.VMEM((ROWS, D), BF),
        pltpu.VMEM((D, 2 * FEAT), BF),
        pltpu.VMEM((D, 2 * FEAT), BF),
        pltpu.VMEM((WIDE, D), BF),
        pltpu.VMEM((WIDE, D), BF),
        pltpu.VMEM((ROWS, WIDE), BF),
        pltpu.VMEM((ROWS + WIN, WIDE), F32),
        pltpu.VMEM((ROWS + WIN, WIDE), F32),
        pltpu.VMEM((2, WIN, WIDE), BF),
        pltpu.VMEM((2, WIN, WIDE), BF),
        pltpu.VMEM((ROWS, 3 * WIDE), BF),
        pltpu.VMEM((ROWS, WIDE), BF),
        pltpu.VMEM((2, ROWS, 1), F32),
        pltpu.VMEM((ROWS, 2 * FEAT), F32),
        pltpu.VMEM((ROWS, 2 * FEAT), F32),
        pltpu.VMEM((ROWS, WIDE), F32),
        pltpu.VMEM((ROWS, WIDE + TILE), BF),
        pltpu.VMEM((16, D), F32),
        pltpu.VMEM((16, D), BF),
        pltpu.VMEM((3, 16, 512), BF),
        pltpu.VMEM((16, 512), BF),
        pltpu.VMEM((3, 16, TILE), BF),
        pltpu.VMEM((16, TILE), BF),
        pltpu.VMEM((3, 16, TILE), BF),
        pltpu.VMEM((16, TILE), BF),
        pltpu.VMEM((16, TILE), BF),
        pltpu.VMEM((4, 2, STATE, WIDE), BF),
        pltpu.VMEM((4, 2, STATE, WIDE), BF),
        pltpu.VMEM((2, STATE, WIDE), F32),
    ]
    scratch += mp_scratch()
    scratch += [pltpu.SemaphoreType.DMA((MP_COPIES,))] * 2
    scratch += [pltpu.SemaphoreType.DMA((24 * len(GROUPS),))] * 2
    scratch += [pltpu.SemaphoreType.DMA((24,))] * 2
    scratch += [pltpu.SemaphoreType.DMA((64,))]
    anywhere = pl.BlockSpec(memory_space=pl.ANY)
    inside = pl.BlockSpec(memory_space=pltpu.VMEM)
    outs = pl.pallas_call(
        backward_kernel,
        out_shape=[shape((ROWS, D), BF), shape((16, TILE), F32)]
        + [shape((TILE, width), F32) for _, width in GROUPS],
        in_specs=[inside] * len(BACKWARD_INPUTS)
        + [anywhere] * (len(BACKWARD_HBM) + len(BACKWARD_FROM)),
        out_specs=[inside] * (2 + len(GROUPS)),
        scratch_shapes=scratch,
        compiler_params=pltpu.CompilerParams(
            collective_id=1, has_side_effects=True, vmem_limit_bytes=VMEM_LIMIT
        ),
    )(
        *[inputs[name] for name in BACKWARD_INPUTS],
        *[hbm[name] for name in BACKWARD_HBM],
        *[saved[name] for name in BACKWARD_FROM],
    )
    return outs[0], outs[1], dict(zip([name for name, _ in GROUPS], outs[2:]))


def prepare(tokens, group_ids, gains, out_grad):
    ids = group_ids.reshape(8, WIN)
    before = jnp.concatenate([jnp.full((1, WIN), -2, jnp.int32), ids[:7]])
    flag = (group_ids[ROWS - WIN :] == group_ids[ROWS - 1]).astype(BF)
    first, second, vectors = feature_tables()
    return {
        "tokens": tokens,
        "group_col": group_ids.reshape(ROWS, 1),
        "group_row": group_ids.reshape(1, ROWS),
        "key_groups": jnp.concatenate([before, ids], axis=1),
        "tail_flag": jnp.zeros((16, TILE), BF).at[0, :WIN].set(flag),
        "gain_one": gains[0].reshape(1, D),
        "gain_two": gains[1].reshape(1, D),
        "gain_three": gains[2].reshape(1, D),
        "first": first,
        "second": second,
        "vectors": vectors,
        "out_grad": out_grad,
    }


def local(
    tokens,
    group_ids,
    gain_one,
    lin_query,
    lin_key,
    lin_value,
    lin_output,
    gain_two,
    win_query,
    win_key,
    win_value,
    win_output,
    gain_three,
    mlp_gate,
    mlp_up,
    mlp_down,
    out_grad,
):
    inputs = prepare(tokens, group_ids, (gain_one, gain_two, gain_three), out_grad)
    weights = {
        "w_query": lin_query,
        "w_key": lin_key,
        "w_value": lin_value,
        "w_out": lin_output,
        "win_q": win_query,
        "win_k": win_key,
        "win_v": win_value,
        "win_out": win_output,
        "w_gate": mlp_gate,
        "w_up": mlp_up,
        "w_down": mlp_down,
    }
    saved = forward(inputs, weights)
    tokens_low, gains, sums = backward(saved, inputs, weights)
    win, lin = sums["win_sum"], sums["lin_sum"]
    return (
        saved["result"],
        tokens_low.astype(F32),
        gains[0],
        lin[:, WIDE : WIDE + 2 * FEAT],
        lin[:, WIDE + 2 * FEAT : WIDE + 4 * FEAT],
        lin[:, :WIDE],
        sums["out_sum"].T,
        gains[1],
        win[:, :WIDE],
        win[:, WIDE : 2 * WIDE],
        win[:, 2 * WIDE :],
        sums["win_out_sum"].T,
        gains[2],
        sums["gate_sum"],
        sums["up_sum"],
        sums["down_sum"].T,
    )


def solution(mesh):
    return jax.shard_map(
        local,
        mesh=mesh,
        in_specs=(
            P("seq", None),
            P("seq"),
            P(),
            P(None, "mp"),
            P(None, "mp"),
            P(None, "mp"),
            P("mp", None),
            P(),
            P(None, "mp"),
            P(None, "mp"),
            P(None, "mp"),
            P("mp", None),
            P(),
            P(None, "mp"),
            P(None, "mp"),
            P("mp", None),
            P("seq", None),
        ),
        out_specs=(
            P("seq", None),
            P("seq", None),
            P("seq"),
            P("seq", "mp"),
            P("seq", "mp"),
            P("seq", "mp"),
            P("mp", "seq"),
            P("seq"),
            P("seq", "mp"),
            P("seq", "mp"),
            P("seq", "mp"),
            P("mp", "seq"),
            P("seq"),
            P("seq", "mp"),
            P("seq", "mp"),
            P("mp", "seq"),
        ),
        check_vma=False,
    )
```

```python
import functools
import types
from typing import Any, NamedTuple

import jax
import jax.numpy as jnp
import numpy as np
from jax import lax
from jax.experimental import pallas as pl
from jax.experimental.pallas import tpu as pltpu
from jax.sharding import PartitionSpec as P

D = 2048
HD = 128
FEAT = 16
WIN = 64
FF = 704
FF_PAD = 768
ROWS = 512
TILE = 128
WIDE = 256
STATE = 144

CHUNKS = 4
CHUNK = ROWS // CHUNKS
HALF = CHUNK // 2
PIECE = CHUNK // 8
OWN = 64
COLS = D // 2
PER_CHUNK = 21

EPSILON = 1e-05
MESH = pl.DeviceIdType.MESH
BF = jnp.bfloat16
F32 = jnp.float32
VMEM_LIMIT = 62 * 1024 * 1024


class Place:
    def __init__(self):
        self.seq = lax.axis_index("seq")
        self.mp = lax.axis_index("mp")
        self.z, self.y = self.seq // 4, self.seq % 4
        self.x, self.core = self.mp // 2, self.mp % 2

    def peer(self):
        return (self.seq, self.x * 2 + (1 - self.core))

    def on_x(self, step):
        return (self.seq, ((self.x + step) % 4) * 2 + self.core)

    def on_y(self, step):
        return (self.z * 4 + (self.y + step) % 4, self.mp)

    def on_z(self, step):
        return (((self.z + step) % 4) * 4 + self.y, self.mp)

    def along(self, step):
        return ((self.seq + step) % 16, self.mp)


class Copies:
    def __init__(self, send_sems, recv_sems):
        self.send_sems, self.recv_sems = send_sems, recv_sems
        self.count, self.started = 0, []

    def start(self, src, dst, device):
        k = self.count
        self.count += 1
        copy = pltpu.make_async_remote_copy(
            src_ref=src,
            dst_ref=dst,
            send_sem=self.send_sems.at[k],
            recv_sem=self.recv_sems.at[k],
            device_id=device,
            device_id_type=MESH,
        )
        copy.start()
        self.started.append(copy)
        return copy

    def finish(self):
        for copy in self.started:
            copy.wait_send()


class Locals:
    def __init__(self, sems):
        self.sems, self.count = sems, 0

    def start(self, src, dst):
        copy = pltpu.make_async_copy(src, dst, self.sems.at[self.count])
        self.count += 1
        copy.start()
        return copy


def greet(devices):
    barrier = pltpu.get_barrier_semaphore()
    for device in devices:
        pl.semaphore_signal(barrier, inc=1, device_id=device, device_id_type=MESH)
    pl.semaphore_wait(barrier, len(devices))


def rows_at(start, size):
    return pl.ds(pl.multiple_of(start, 16), size)


def dot(left, right):
    return lax.dot_general(left, right, (((1,), (0,)), ((), ())), preferred_element_type=F32)


def dot_nt(left, right):
    return lax.dot_general(left, right, (((1,), (1,)), ((), ())), preferred_element_type=F32)


def dot_tn(left, right):
    return lax.dot_general(left, right, (((0,), (0,)), ((), ())), preferred_element_type=F32)


def halves(values):
    high = values.astype(BF)
    return high, (values - high.astype(F32)).astype(BF)


class MpSum:
    def __init__(self, place, sems, part, full, own, bufs, order=tuple(range(CHUNKS))):
        self.place, self.part, self.full, self.own, self.order = place, part, full, own, order
        self.send_sems, self.recv_sems = sems
        (self.from_peer, self.send_opp, self.send_right, self.send_left) = bufs[:4]
        (self.fwd, self.direct, self.comb) = bufs[4:]
        x = place.x
        self.turn = [(x + 2) % 4, (x + 1) % 4, (x + 3) % 4, x]
        self.peer, self.right, self.left = place.peer(), place.on_x(1), place.on_x(3)
        self.live = [types.SimpleNamespace(sent=[]) for _ in range(CHUNKS)]

    def start(self, j, src, dst, device):
        k = j * PER_CHUNK + len(self.live[j].sent)
        copy = pltpu.make_async_remote_copy(
            src_ref=src,
            dst_ref=dst,
            send_sem=self.send_sems.at[k],
            recv_sem=self.recv_sems.at[k],
            device_id=device,
            device_id_type=MESH,
        )
        copy.start()
        self.live[j].sent.append(copy)
        return copy

    def rows(self, j, core, x):
        return rows_at(j * CHUNK + core * HALF + x * PIECE, PIECE)

    def own_rows(self, j):
        return self.rows(j, self.place.core, self.place.x)

    def chip_sum(self, j, slot, low, size):
        cols = pl.ds(low, size)
        return self.part[self.rows(j, self.place.core, self.turn[slot]), cols].astype(
            F32
        ) + self.from_peer[j, slot, :, cols].astype(F32)

    def exchange(self, j):
        self.live[j].ex = [
            self.start(
                j,
                self.part.at[self.rows(j, 1 - self.place.core, at)],
                self.from_peer.at[j, slot],
                self.peer,
            )
            for slot, at in enumerate(self.turn)
        ]

    def first(self, j):
        live = self.live[j]
        low, high = pl.ds(0, COLS), pl.ds(COLS, COLS)
        live.ex[0].wait_recv()
        self.send_opp[j] = self.chip_sum(j, 0, 0, D).astype(BF)
        live.fr = self.start(j, self.send_opp.at[j, :, low], self.fwd.at[j, 0], self.right)
        live.fl = self.start(j, self.send_opp.at[j, :, high], self.fwd.at[j, 1], self.left)
        live.ex[1].wait_recv()
        self.send_right[j, 0] = self.chip_sum(j, 1, COLS, COLS).astype(BF)
        live.dr = self.start(j, self.send_right.at[j, 0], self.direct.at[j, 1], self.right)
        live.ex[2].wait_recv()
        self.send_left[j, 0] = self.chip_sum(j, 2, 0, COLS).astype(BF)
        live.dl = self.start(j, self.send_left.at[j, 0], self.direct.at[j, 0], self.left)

    def second(self, j):
        live = self.live[j]
        live.fr.wait_recv()
        self.send_right[j, 1] = (
            self.chip_sum(j, 1, 0, COLS) + self.fwd[j, 0].astype(F32)
        ).astype(BF)
        live.cr = self.start(j, self.send_right.at[j, 1], self.comb.at[j, 0], self.right)
        live.fl.wait_recv()
        self.send_left[j, 1] = (
            self.chip_sum(j, 2, COLS, COLS) + self.fwd[j, 1].astype(F32)
        ).astype(BF)
        live.cl = self.start(j, self.send_left.at[j, 1], self.comb.at[j, 1], self.left)

    def total(self, j):
        live, mine = self.live[j], pl.ds(j * PIECE, PIECE)
        live.ex[3].wait_recv()
        live.dl.wait_recv()
        live.cr.wait_recv()
        self.own[mine, 0:COLS] = (
            self.chip_sum(j, 3, 0, COLS)
            + self.direct[j, 0].astype(F32)
            + self.comb[j, 0].astype(F32)
        )
        live.dr.wait_recv()
        live.cl.wait_recv()
        self.own[mine, COLS:D] = (
            self.chip_sum(j, 3, COLS, COLS)
            + self.direct[j, 1].astype(F32)
            + self.comb[j, 1].astype(F32)
        )

    def send(self, j, at, low, size, device):
        block = self.full.at[self.rows(j, self.place.core, at), pl.ds(low, size)]
        return self.start(j, block, block, device)

    def spread(self, j):
        live, x = self.live[j], self.place.x
        live.rl = self.send(j, x, 0, COLS, self.right)
        live.lh = self.send(j, x, COLS, COLS, self.left)
        live.rh = self.send(j, x, COLS, COLS, self.right)
        live.ll = self.send(j, x, 0, COLS, self.left)
        live.peers = [self.send(j, x, 0, D, self.peer)]

    def relay(self, j):
        live, x = self.live[j], self.place.x
        live.rl.wait_recv()
        live.gr = self.send(j, (x + 3) % 4, 0, COLS, self.right)
        live.lh.wait_recv()
        live.gl = self.send(j, (x + 1) % 4, COLS, COLS, self.left)
        live.rh.wait_recv()
        live.peers.append(self.send(j, (x + 3) % 4, 0, D, self.peer))
        live.ll.wait_recv()
        live.peers.append(self.send(j, (x + 1) % 4, 0, D, self.peer))

    def last(self, j):
        live, x = self.live[j], self.place.x
        live.gr.wait_recv()
        live.peers.append(self.send(j, (x + 2) % 4, 0, COLS, self.peer))
        live.gl.wait_recv()
        live.peers.append(self.send(j, (x + 2) % 4, COLS, COLS, self.peer))

    def arrived(self, j):
        for copy in self.live[j].peers:
            copy.wait_recv()
        for copy in self.live[j].sent:
            copy.wait_send()

    def slots(self, produce, finish, ready=None):
        for slot in range(CHUNKS + 6):
            for position, j in enumerate(self.order):
                stage = slot - position
                if stage == 0:
                    produce(j)
                    self.exchange(j)
                elif stage == 1:
                    self.first(j)
                elif stage == 2:
                    self.second(j)
                elif stage == 3:
                    self.total(j)
                    finish(j)
                    self.spread(j)
                elif stage == 4:
                    self.relay(j)
                elif stage == 5:
                    self.last(j)
                elif stage == 6:
                    self.arrived(j)
                    if ready is not None:
                        ready(j)
            yield slot


def mp_scratch():
    ring = pltpu.VMEM((CHUNKS, 2, PIECE, COLS), BF)
    return [pltpu.VMEM((CHUNKS, 4, PIECE, D), BF), pltpu.VMEM((CHUNKS, PIECE, D), BF)] + [ring] * 5


def dma(count):
    return pltpu.SemaphoreType.DMA((count,))


def run(slots):
    for _ in slots:
        pass


def ring_gather(copies, right, left, held):
    first = copies.start(held.at[0, 0], held.at[1, 0], right)
    second = copies.start(held.at[0, 1], held.at[3, 1], left)
    third = copies.start(held.at[0, 1], held.at[1, 1], right)
    fourth = copies.start(held.at[0, 0], held.at[3, 0], left)
    yield
    first.wait_recv()
    fifth = copies.start(held.at[1, 0], held.at[2, 0], right)
    second.wait_recv()
    sixth = copies.start(held.at[3, 1], held.at[2, 1], left)
    yield
    for copy in (third, fourth, fifth, sixth):
        copy.wait_recv()
    yield


def state_scan(place, copies, held_y, held_z, out, reverse):
    def counted(position, step):
        at = (position - step + 4) % 4
        reached = at > position if reverse else at < position
        return jnp.where(reached, 1.0, 0.0)

    yield from ring_gather(copies, place.on_y(1), place.on_y(3), held_y)
    for head in range(2):
        parts = [held_y[k, head].astype(F32) for k in range(4)]
        held_z[0, head] = (parts[0] + parts[1] + parts[2] + parts[3]).astype(BF)
    gather = ring_gather(copies, place.on_z(1), place.on_z(3), held_z)
    next(gather)
    for head in range(2):
        total = counted(place.y, 1) * held_y[1, head].astype(F32)
        for step in range(2, 4):
            total = total + counted(place.y, step) * held_y[step, head].astype(F32)
        out[head] = total
    yield
    yield from gather
    for head in range(2):
        total = out[head]
        for step in range(1, 4):
            total = total + counted(place.z, step) * held_z[step, head].astype(F32)
        out[head] = total
    yield


def feature_tables():
    pairs = [(a, b) for a in range(FEAT) for b in range(a, FEAT)]
    first = np.zeros((2, 2 * FEAT, WIDE), np.float32)
    second = np.zeros((2, 2 * FEAT, WIDE), np.float32)
    vectors = np.zeros((8, WIDE), np.float32)
    vectors[0, 0] = vectors[1, 0] = vectors[2, 0] = 1.0
    for a in range(FEAT):
        vectors[1, 1 + a] = 1.0
        vectors[2, 1 + a] = FEAT ** (-0.25)
        for h in range(2):
            first[h, h * FEAT + a, 1 + a] = 1.0
    for number, (a, b) in enumerate(pairs):
        at = 1 + FEAT + number
        vectors[2, at] = (1.0 if a == b else 2.0**0.5) * (2.0 * FEAT) ** (-0.5)
        for h in range(2):
            first[h, h * FEAT + a, at] = 1.0
            second[h, h * FEAT + b, at] = 1.0
    return jnp.asarray(first, BF), jnp.asarray(second, BF), jnp.asarray(vectors, F32)


def factors(head, values, first, second, vectors):
    high, low = values
    left = dot(high, first[head]) + dot(low, first[head]) + vectors[0:1]
    right = dot(high, second[head]) + dot(low, second[head]) + vectors[1:2]
    return left, right


def of_head(values, head):
    lane = lax.broadcasted_iota(jnp.int32, values.shape, 1)
    return jnp.where((lane >= head * FEAT) & (lane < (head + 1) * FEAT), values, jnp.zeros_like(values))


def products(head, query, key, rows, count):
    high, low = (of_head(part[rows], head) for part in query)
    key_high, key_low = (part[0:count] for part in key)
    return dot_nt(high, key_high) + dot_nt(low, key_high) + dot_nt(high, key_low)


def shape(dims, kind):
    return jax.ShapeDtypeStruct(dims, kind)


def normed(rows, gain):
    factor = lax.rsqrt(jnp.mean(rows * rows, axis=-1, keepdims=True) + EPSILON)
    return rows * factor * gain


def column(group_row, held):
    for k in range(ROWS // TILE):
        block = group_row[0:1, k * TILE : (k + 1) * TILE].astype(F32)
        held[k * TILE : (k + 1) * TILE] = jnp.broadcast_to(block, (TILE, TILE)).T


def kept_pairs(group_col, group_row, tile):
    count = (tile + 1) * TILE
    row = lax.broadcasted_iota(jnp.int32, (TILE, count), 0) + tile * TILE
    col = lax.broadcasted_iota(jnp.int32, (TILE, count), 1)
    groups = group_col[tile * TILE : (tile + 1) * TILE, 0:1]
    return (col <= row) & (groups == group_row[0:1, 0:count].astype(F32))


def weight_block(into, left_t, right, quarter):
    count = into.shape[2]
    block = dot(left_t[0:count], right[:, quarter * 512 : (quarter + 1) * 512]).astype(BF)
    for k in range(4):
        into[quarter, k] = block[:, k * TILE : (k + 1) * TILE]


class Inputs(NamedTuple):
    tokens: Any
    group_row: Any
    gain_one: Any
    gain_two: Any
    gain_three: Any
    first: Any
    second: Any
    vectors: Any


class Weights(NamedTuple):
    out_grad: Any = ((ROWS, D), BF)
    w_query: Any = ((2 * FEAT, D), BF)
    w_key: Any = ((2 * FEAT, D), BF)
    w_value: Any = ((D, WIDE), BF)
    w_out: Any = ((WIDE, D), BF)
    win_k: Any = ((D, WIDE), BF)
    win_v: Any = ((D, WIDE), BF)
    win_q: Any = ((D, WIDE), BF)
    win_out: Any = ((WIDE, D), BF)
    w_gate: Any = ((FF_PAD, D), BF)
    w_up: Any = ((FF_PAD, D), BF)
    w_down: Any = ((FF_PAD, D), BF)


class Saved(NamedTuple):
    normed_one: Any = ((ROWS, D), BF)
    query: Any = ((2, ROWS, 2 * FEAT), BF)
    key: Any = ((2, ROWS, 2 * FEAT), BF)
    value: Any = ((ROWS, WIDE), BF)
    carried: Any = ((2, STATE, WIDE), F32)
    quotient: Any = ((ROWS, WIDE), F32)
    denominator: Any = ((2, ROWS, 1), F32)
    mixed_lin: Any = ((ROWS, WIDE), BF)
    resid_one: Any = ((OWN, D), F32)
    normed_two: Any = ((ROWS, D), BF)
    query_win: Any = ((ROWS, WIDE), BF)
    keys_all: Any = ((ROWS + WIN, WIDE), BF)
    values_all: Any = ((ROWS + WIN, WIDE), BF)
    probs: Any = ((2, ROWS, TILE), F32)
    mixed_win: Any = ((ROWS, WIDE), BF)
    resid_two: Any = ((OWN, D), F32)
    part_four: Any = ((ROWS, D), BF)
    gate_sum: Any = ((4, 4, FF, TILE), BF)
    up_sum: Any = ((4, 4, FF, TILE), BF)
    down_sum: Any = ((4, 4, FF, TILE), BF)
    result: Any = ((ROWS, D), BF)


class ForwardWork(NamedTuple):
    part: Any = ((ROWS, D), BF)
    own: Any = ((OWN, D), F32)
    group_col: Any = ((ROWS, TILE), F32)
    tail_flag: Any = ((16, TILE), BF)
    halo_flag: Any = ((16, TILE), BF)
    query_feat: Any = ((2, ROWS, WIDE), BF)
    key_feat: Any = ((2, ROWS, WIDE), BF)
    normed_three: Any = ((ROWS, D), BF)
    gate_act: Any = ((ROWS, FF_PAD), F32)
    up_act: Any = ((ROWS, FF_PAD), F32)
    hidden: Any = ((ROWS, FF_PAD), BF)
    gate_low: Any = ((ROWS, FF_PAD), BF)
    up_low: Any = ((ROWS, FF_PAD), BF)
    flipped: Any = ((FF_PAD, ROWS), BF)
    held_y: Any = ((4, 2, STATE, WIDE), BF)
    held_z: Any = ((4, 2, STATE, WIDE), BF)


def taker(refs):
    refs = list(refs)

    def take(kind):
        return kind(*[refs.pop(0) for _ in kind._fields])

    def some(count):
        return [refs.pop(0) for _ in range(count)]

    return take, some


def vmem(kind):
    return [pltpu.VMEM(*entry) for entry in kind()]


def forward_kernel(*refs):
    take, some = taker(refs)
    inputs, hbm_weights, hbm_saved = take(Inputs), take(Weights), take(Saved)
    weights, saved, work = take(Weights), take(Saved), take(ForwardWork)
    bufs = some(7)
    mp_sems, (state_send, state_recv), (halo_send, halo_recv), (local_sems,) = (
        some(2),
        some(2),
        some(2),
        some(1),
    )
    place = Place()
    local = Locals(local_sems)
    loads = []
    for src, dst in zip(hbm_weights[1:], weights[1:]):
        loads.append(local.start(src, dst if src.shape == dst.shape else dst.at[pl.ds(0, FF)]))
    loads = Weights(local.start(hbm_weights.out_grad, weights.out_grad), *loads)
    saves = []

    def save(*pairs):
        for src, dst in pairs:
            saves.append(local.start(src, dst))

    greet(
        [place.peer()]
        + [place.on_x(k) for k in (1, 3)]
        + [place.on_y(k) for k in (1, 3)]
        + [place.on_z(k) for k in (1, 3)]
        + [place.along(1), place.along(15)]
    )
    for ref in (weights.w_gate, weights.w_up, weights.w_down):
        ref[FF:FF_PAD] = jnp.zeros((FF_PAD - FF, D), BF)
    tokens, group_row, group_col = inputs.tokens, inputs.group_row, work.group_col
    first, second, vectors = inputs.first, inputs.second, inputs.vectors
    scale = vectors[2:3]
    normed_one = saved.normed_one

    def norm_rows(i, _):
        rows = rows_at(i * 32, 32)
        normed_one[rows] = normed(tokens[rows].astype(F32), inputs.gain_one[...]).astype(BF)
        return 0

    lax.fori_loop(0, ROWS // 32, norm_rows, 0)
    save((normed_one, hbm_saved.normed_one))
    column(group_row, group_col)
    query, key, value = saved.query, saved.key, saved.value
    for load, weight, held in (
        (loads.w_key, weights.w_key, key),
        (loads.w_query, weights.w_query, query),
    ):
        load.wait()
        held[0], held[1] = halves(dot_nt(normed_one[...], weight[...]))
    loads.w_value.wait()
    value[...] = dot(normed_one[...], weights.w_value[...]).astype(BF)

    last = group_row[0:1, ROWS - 1 : ROWS].astype(F32)
    in_last = (group_col[:, 0:1] == last).astype(F32)
    query_feat, key_feat, held_y = work.query_feat, work.key_feat, work.held_y
    for head in range(2):
        left, right = factors(head, (key[0], key[1]), first, second, vectors)
        feat = (left * right * scale).astype(BF)
        key_feat[head] = feat
        kept = feat.astype(F32) * in_last
        held_y[0, head, 0:HD] = dot_tn(value[:, head * HD : (head + 1) * HD], kept.astype(BF)).astype(BF)
        held_y[0, head, HD:STATE] = jnp.broadcast_to(
            jnp.sum(kept, axis=0, keepdims=True), (STATE - HD, WIDE)
        ).astype(BF)
    copies_state = Copies(state_send, state_recv)
    scan = state_scan(place, copies_state, held_y, work.held_z, saved.carried, False)
    next(scan)
    save((query, hbm_saved.query), (key, hbm_saved.key), (value, hbm_saved.value))
    quotient, denominator = saved.quotient, saved.denominator
    for head in range(2):
        left, right = factors(head, (query[0], query[1]), first, second, vectors)
        query_feat[head] = (left * right * scale).astype(BF)
    next(scan)
    for tile in range(ROWS // TILE):
        rows, count = pl.ds(tile * TILE, TILE), (tile + 1) * TILE
        kept = kept_pairs(group_col, group_row, tile)
        for head in range(2):
            inner = products(head, (query.at[0], query.at[1]), (key.at[0], key.at[1]), rows, count)
            block = jnp.where(kept, 1.0 + inner * 0.25 + inner * inner * 0.03125, 0.0).astype(BF)
            denominator[head, rows] = jnp.sum(block.astype(F32), axis=1, keepdims=True)
            quotient[rows, head * HD : (head + 1) * HD] = dot(
                block, value[0:count, head * HD : (head + 1) * HD]
            )
        next(scan)
    for _ in scan:
        pass
    copies_state.finish()
    first_group = group_row[0:1, 0:1].astype(F32)
    incoming = (group_col[:, 0:1] == first_group).astype(F32) * jnp.where(place.seq > 0, 1.0, 0.0)
    carried, mixed_lin = saved.carried, saved.mixed_lin
    save((carried, hbm_saved.carried))
    for head in range(2):
        lanes = slice(head * HD, (head + 1) * HD)
        feat = query_feat[head]
        numer = quotient[:, lanes] + incoming * dot_nt(feat, carried[head, 0:HD].astype(BF))
        denom = denominator[head] + incoming * jnp.sum(
            feat.astype(F32) * carried[head, HD : HD + 1], axis=1, keepdims=True
        )
        ratio = numer / denom
        denominator[head] = denom
        quotient[:, lanes] = ratio
        mixed_lin[:, lanes] = ratio.astype(BF)
    save(
        (quotient, hbm_saved.quotient),
        (denominator, hbm_saved.denominator),
        (mixed_lin, hbm_saved.mixed_lin),
    )
    loads.w_out.wait()

    part, own = work.part, work.own
    resid_one, resid_two = saved.resid_one, saved.resid_two
    normed_two, normed_three = saved.normed_two, work.normed_three
    sum_one = MpSum(place, mp_sems, part, normed_two, own, bufs, (3, 0, 1, 2))
    sum_two = MpSum(place, mp_sems, part, normed_three, own, bufs)
    sum_three = MpSum(place, mp_sems, part, saved.result, own, bufs)

    def produce_one(j):
        rows = pl.ds(j * CHUNK, CHUNK)
        part[rows] = dot(mixed_lin[rows], weights.w_out[...]).astype(BF)

    def finish_one(j):
        mine = pl.ds(j * PIECE, PIECE)
        rows = own[mine] + tokens[sum_one.own_rows(j)].astype(F32)
        resid_one[mine] = rows
        normed_two[sum_one.own_rows(j)] = normed(rows, inputs.gain_two[...]).astype(BF)

    query_win, keys_all, values_all = saved.query_win, saved.keys_all, saved.values_all
    copies_halo = Copies(halo_send, halo_recv)
    lane = lax.broadcasted_iota(jnp.int32, (1, TILE), 1)
    group_blocks = [group_row[0:1, k * TILE : (k + 1) * TILE].astype(F32) for k in range(4)]
    turned = [pltpu.roll(block, WIN, 1) for block in group_blocks]
    work.tail_flag[...] = jnp.broadcast_to((turned[3] == last).astype(F32), (16, TILE)).astype(BF)
    halo = []

    def ready_one(j):
        rows = pl.ds(j * CHUNK, CHUNK)
        below = pl.ds(WIN + j * CHUNK, CHUNK)
        if j == 3:
            for load in (loads.win_k, loads.win_v, loads.win_q):
                load.wait()
        keys_all[below] = dot(normed_two[rows], weights.win_k[...]).astype(BF)
        values_all[below] = dot(normed_two[rows], weights.win_v[...]).astype(BF)
        if j == 3:
            for ref in (keys_all, values_all):
                halo.append(
                    copies_halo.start(ref.at[pl.ds(ROWS, WIN)], ref.at[pl.ds(0, WIN)], place.along(1))
                )
            halo.append(copies_halo.start(work.tail_flag, work.halo_flag, place.along(1)))
        query_win[rows] = dot(normed_two[rows], weights.win_q[...]).astype(BF)

    probs, mixed_win = saved.probs, saved.mixed_win
    tile_row = lax.broadcasted_iota(jnp.int32, (WIN, TILE), 0)
    tile_col = lax.broadcasted_iota(jnp.int32, (WIN, TILE), 1)
    near = (tile_col > tile_row) & (tile_col <= tile_row + WIN)
    score_scale = HD ** (-0.5)

    def window_tile(t):
        rows = pl.ds(t * WIN, WIN)
        if t == 0:
            flag = jnp.where(place.seq > 0, work.halo_flag[0:1].astype(F32), 0.0)
            groups = jnp.where(lane < WIN, jnp.where(flag > 0.5, first_group, -2.0), turned[0])
        elif t % 2 == 1:
            groups = group_blocks[t // 2]
        else:
            groups = jnp.where(lane < WIN, turned[t // 2 - 1], turned[t // 2])
        kept = near & (group_col[rows] == groups)
        for head in range(2):
            lanes = slice(head * HD, (head + 1) * HD)
            scores = dot_nt(query_win[rows, lanes], keys_all[t * WIN : t * WIN + TILE, lanes])
            scores = jnp.where(kept, scores * score_scale, -1e30)
            exp_scores = jnp.exp(scores - jnp.max(scores, axis=1, keepdims=True))
            found = exp_scores / jnp.sum(exp_scores, axis=1, keepdims=True)
            probs[head, rows] = found
            mixed_win[rows, lanes] = dot(
                found.astype(BF), values_all[t * WIN : t * WIN + TILE, lanes]
            ).astype(BF)

    def produce_two(j):
        if j == 0:
            for copy in halo:
                copy.wait_recv()
            loads.win_out.wait()
        window_tile(2 * j)
        window_tile(2 * j + 1)
        rows = pl.ds(j * CHUNK, CHUNK)
        part[rows] = dot(mixed_win[rows], weights.win_out[...]).astype(BF)

    def finish_two(j):
        mine = pl.ds(j * PIECE, PIECE)
        rows = own[mine] + resid_one[mine]
        resid_two[mine] = rows
        normed_three[sum_two.own_rows(j)] = normed(rows, inputs.gain_three[...]).astype(BF)

    w_gate, w_up, w_down, og = weights.w_gate, weights.w_up, weights.w_down, weights.out_grad
    gate_act, up_act, hidden = work.gate_act, work.up_act, work.hidden
    gate_low, up_low = work.gate_low, work.up_low

    def ready_two(j):
        if j % 2 == 0:
            return
        if j == 1:
            for load in (loads.w_gate, loads.w_up, loads.w_down):
                load.wait()
        rows = pl.ds((j - 1) * CHUNK, 2 * CHUNK)
        gate = dot_nt(normed_three[rows], w_gate[...])
        gate_act[rows] = gate
        up = dot_nt(normed_three[rows], w_up[...])
        up_act[rows] = up
        hidden[rows] = (gate / (1.0 + jnp.exp(-gate)) * up).astype(BF)

    def produce_three(j):
        rows = pl.ds(j * CHUNK, CHUNK)
        part[rows] = dot(hidden[rows], w_down[...]).astype(BF)

    def finish_three(j):
        mine = pl.ds(j * PIECE, PIECE)
        saved.result[sum_three.own_rows(j)] = (own[mine] + resid_two[mine]).astype(BF)

    one = sum_one.slots(produce_one, finish_one, ready_one)
    two = sum_two.slots(produce_two, finish_two, ready_two)
    three = sum_three.slots(produce_three, finish_three)
    for slot in one:
        if slot >= 7:
            next(two)
    copies_halo.finish()
    save(
        (resid_one, hbm_saved.resid_one),
        (normed_two, hbm_saved.normed_two),
        (query_win, hbm_saved.query_win),
        (keys_all, hbm_saved.keys_all),
        (values_all, hbm_saved.values_all),
    )
    for slot in two:
        if slot >= 7:
            next(three)
    save(
        (probs, hbm_saved.probs), (mixed_win, hbm_saved.mixed_win), (resid_two, hbm_saved.resid_two)
    )
    loads.out_grad.wait()

    def hidden_back(half):
        rows = pl.ds(half * 256, 256)
        hidden_grad = dot_nt(og[rows], w_down[...])
        gate = gate_act[rows]
        sigmoid = 1.0 / (1.0 + jnp.exp(-gate))
        act = gate * sigmoid
        up_low[rows] = (hidden_grad * act).astype(BF)
        gate_low[rows] = (
            hidden_grad * up_act[rows] * (sigmoid + act * (1.0 - sigmoid))
        ).astype(BF)

    def input_back(half):
        cols = pl.ds(half * 1024, 1024)
        saved.part_four[:, cols] = (
            dot(gate_low[...], w_gate[:, cols]) + dot(up_low[...], w_up[:, cols])
        ).astype(BF)
        if half == 1:
            save((saved.part_four, hbm_saved.part_four))

    def weight_back(into, to_hbm, left, right, quarter):
        if quarter == 0:
            work.flipped[...] = left[...].T
        weight_block(into, work.flipped, right, quarter)
        if quarter == 3:
            save((into, to_hbm))

    blocks = [functools.partial(hidden_back, k) for k in range(2)]
    blocks += [functools.partial(input_back, k) for k in range(2)]
    for into, to_hbm, left, right in (
        (saved.gate_sum, hbm_saved.gate_sum, gate_low, normed_three),
        (saved.up_sum, hbm_saved.up_sum, up_low, normed_three),
        (saved.down_sum, hbm_saved.down_sum, hidden, og),
    ):
        blocks += [functools.partial(weight_back, into, to_hbm, left, right, k) for k in range(4)]
    for _ in three:
        for _ in range(2):
            if blocks:
                blocks.pop(0)()
    save((saved.result, hbm_saved.result))
    for block in blocks:
        block()
    for copy in saves:
        copy.wait()


HBM = pl.BlockSpec(memory_space=pl.ANY)
INSIDE = pl.BlockSpec(memory_space=pltpu.VMEM)


def forward(inputs, weights):
    scratch = vmem(Weights) + vmem(Saved) + vmem(ForwardWork) + mp_scratch()
    scratch += [dma(CHUNKS * PER_CHUNK)] * 2 + [dma(12)] * 2 + [dma(3)] * 2
    scratch += [dma(len(Weights._fields) + len(Saved._fields))]
    return Saved(
        *pl.pallas_call(
            forward_kernel,
            out_shape=[shape(dims, kind) for dims, kind in Saved()],
            in_specs=[INSIDE] * len(inputs) + [HBM] * len(weights),
            out_specs=[HBM] * len(Saved._fields),
            scratch_shapes=scratch,
            compiler_params=pltpu.CompilerParams(
                collective_id=0, has_side_effects=True, vmem_limit_bytes=VMEM_LIMIT
            ),
        )(*inputs, *weights)
    )


class SeqSum:
    def __init__(self, place, copies, blocks, out, bufs):
        self.place, self.copies, self.blocks, self.out = place, copies, blocks, out
        z, y = place.z, place.y
        quarter = self.quarter = blocks.shape[2] // 4
        ring_y, ring_z = (place.on_y(1), place.on_y(3)), (place.on_z(1), place.on_z(3))

        def pick_one(k, half):
            return blocks.at[:, (y + k) % 4, pl.ds(half * quarter, quarter)]

        def pick_two(k, half):
            return blocks.at[(z + k) % 4, :, pl.ds((2 + half) * quarter, quarter)]

        def pick_three(k, half):
            return blocks.at[(z + k) % 4, y, pl.ds(half * quarter, quarter)]

        def pick_four(k, half):
            return blocks.at[z, (y + k) % 4, pl.ds((2 + half) * quarter, quarter)]

        live = [types.SimpleNamespace() for _ in range(4)]
        self.early = ((ring_y, pick_one, bufs[0:3], live[0]), (ring_z, pick_two, bufs[3:6], live[1]))
        self.late = ((ring_z, pick_three, bufs[6:9], live[2]), (ring_y, pick_four, bufs[9:12], live[3]))

    def begin(self, rings):
        for (right, left), pick, (fwd, direct, comb), live in rings:
            live.fr = self.copies.start(pick(2, 0), fwd.at[0], right)
            live.fl = self.copies.start(pick(2, 1), fwd.at[1], left)
            live.dr = self.copies.start(pick(1, 1), direct.at[1], right)
            live.dl = self.copies.start(pick(3, 0), direct.at[0], left)

    def join(self, rings):
        for (right, left), pick, (fwd, direct, comb), live in rings:
            live.fr.wait_recv()
            block = pick(1, 0)
            block[...] = (block[...].astype(F32) + fwd[0].astype(F32)).astype(BF)
            live.cr = self.copies.start(block, comb.at[0], right)
            live.fl.wait_recv()
            block = pick(3, 1)
            block[...] = (block[...].astype(F32) + fwd[1].astype(F32)).astype(BF)
            live.cl = self.copies.start(block, comb.at[1], left)

    def total(self, ring, half):
        _, pick, (fwd, direct, comb), live = ring
        (live.dl if half == 0 else live.dr).wait_recv()
        (live.cr if half == 0 else live.cl).wait_recv()
        return (
            pick(0, half)[...].astype(F32) + direct[half].astype(F32) + comb[half].astype(F32)
        )

    def step(self, number):
        if number == 0:
            self.begin(self.early)
        elif number == 1:
            self.join(self.early)
        elif number == 2:
            for ring in self.early:
                for half in range(2):
                    block = ring[1](0, half)
                    block[...] = self.total(ring, half).astype(BF)
            self.begin(self.late)
        elif number == 3:
            self.join(self.late)
        else:
            size = self.quarter
            for half in range(2):
                self.out[pl.ds(half * size, size)] = self.total(self.late[0], half)
                self.out[pl.ds((2 + half) * size, size)] = self.total(self.late[1], half)


def seq_scratch(width):
    early, late = (2, 4, width // 4, TILE), (2, width // 4, TILE)
    return [pltpu.VMEM(early, BF)] * 6 + [pltpu.VMEM(late, BF)] * 6


class Groups(NamedTuple):
    gate: Any = FF
    up: Any = FF
    down: Any = FF
    win_out: Any = WIDE
    win: Any = 3 * WIDE
    out: Any = WIDE
    lin: Any = WIDE + 4 * FEAT


class BackInputs(NamedTuple):
    group_row: Any
    gain_one: Any
    gain_two: Any
    gain_three: Any
    first: Any
    second: Any
    vectors: Any


class BackHbm(NamedTuple):
    part_four: Any
    out_grad: Any
    tokens: Any
    normed_one: Any
    normed_two: Any
    gate_sum: Any
    up_sum: Any
    down_sum: Any
    w_query: Any
    w_key: Any
    w_value: Any
    w_out: Any
    win_q: Any
    win_k: Any
    win_v: Any
    win_out: Any


SPECS = Saved()


class BackSaved(NamedTuple):
    query: Any = SPECS.query
    key: Any = SPECS.key
    value: Any = SPECS.value
    carried: Any = SPECS.carried
    quotient: Any = SPECS.quotient
    denominator: Any = SPECS.denominator
    mixed_lin: Any = SPECS.mixed_lin
    resid_one: Any = SPECS.resid_one
    query_win: Any = SPECS.query_win
    keys_all: Any = SPECS.keys_all
    values_all: Any = SPECS.values_all
    probs: Any = SPECS.probs
    mixed_win: Any = SPECS.mixed_win
    resid_two: Any = SPECS.resid_two


class BackOuts(NamedTuple):
    tokens_low: Any = ((ROWS, D), BF)
    gain_one: Any = ((1, TILE), F32)
    gain_two: Any = ((1, TILE), F32)
    gain_three: Any = ((1, TILE), F32)
    gate: Any = ((FF, TILE), F32)
    up: Any = ((FF, TILE), F32)
    down: Any = ((FF, TILE), F32)
    win_out: Any = ((WIDE, TILE), F32)
    out: Any = ((WIDE, TILE), F32)
    win_q: Any = ((TILE, WIDE), F32)
    win_k: Any = ((TILE, WIDE), F32)
    win_v: Any = ((TILE, WIDE), F32)
    value: Any = ((TILE, WIDE), F32)
    query: Any = ((2 * FEAT, TILE), F32)
    key: Any = ((2 * FEAT, TILE), F32)


class BackWork(NamedTuple):
    part: Any = ((ROWS, D), BF)
    other_full: Any = ((ROWS, D), BF)
    own: Any = ((OWN, D), F32)
    grad_own: Any = ((OWN, D), F32)
    token_own: Any = ((OWN, D), BF)
    group_col: Any = ((ROWS, TILE), F32)
    normed_low: Any = ((ROWS, D), BF)
    w_query: Any = ((2 * FEAT, D), BF)
    w_key: Any = ((2 * FEAT, D), BF)
    w_out: Any = ((WIDE, D), BF)
    win_out: Any = ((WIDE, D), BF)
    w_win: Any = ((D, 3 * WIDE), BF)
    mixed_grad: Any = ((ROWS, WIDE), BF)
    keys_sum: Any = ((ROWS + WIN, WIDE), F32)
    values_sum: Any = ((ROWS + WIN, WIDE), F32)
    back_key: Any = ((2, WIN, WIDE), BF)
    back_value: Any = ((2, WIN, WIDE), BF)
    win_grads: Any = ((ROWS, 3 * WIDE), BF)
    flipped: Any = ((3 * WIDE, ROWS), BF)
    numer_low: Any = ((ROWS, WIDE), BF)
    query_sum: Any = ((ROWS, 2 * FEAT), F32)
    key_sum: Any = ((ROWS, 2 * FEAT), F32)
    value_sum: Any = ((ROWS, WIDE), F32)
    query_low: Any = ((ROWS, 2 * FEAT), BF)
    key_low: Any = ((ROWS, 2 * FEAT), BF)
    value_low: Any = ((ROWS, WIDE), BF)
    state_sum: Any = ((2, STATE, WIDE), F32)
    gain_sums: Any = ((16, D), F32)
    gain_low: Any = ((16, D), BF)
    gain_z: Any = ((3, 16, 512), BF)
    gain_zz: Any = ((16, 512), BF)
    gain_y: Any = ((3, 16, TILE), BF)
    gain_x: Any = ((16, TILE), BF)
    gain_xx: Any = ((3, 16, TILE), BF)
    gain_p: Any = ((16, TILE), BF)
    gain_pp: Any = ((16, TILE), BF)
    sum_win: Any = ((3 * WIDE, TILE), F32)
    sum_lin: Any = ((WIDE + 4 * FEAT, TILE), F32)
    held_y: Any = ((4, 2, STATE, WIDE), BF)
    held_z: Any = ((4, 2, STATE, WIDE), BF)
    later: Any = ((2, STATE, WIDE), F32)


def backward_kernel(*refs):
    take, some = taker(refs)
    inputs, hbm, hbm_saved, outs = take(BackInputs), take(BackHbm), take(BackSaved), take(BackOuts)
    saved, blocks, work = take(BackSaved), take(Groups), take(BackWork)
    seq_bufs = [some(12) for _ in Groups._fields]
    bufs = some(7)
    mp_sems, (seq_send, seq_recv), (few_send, few_recv), (local_sems,) = (
        some(2),
        some(2),
        some(2),
        some(1),
    )
    place = Place()
    z, y = place.z, place.y
    local = Locals(local_sems)
    part, own, other_full, tokens_low = work.part, work.own, work.other_full, outs.tokens_low
    sum_four = MpSum(place, mp_sems, part, tokens_low, own, bufs)
    sum_five = MpSum(place, mp_sems, part, other_full, own, bufs)
    sum_six = MpSum(place, mp_sems, part, tokens_low, own, bufs)

    load_part = local.start(hbm.part_four, part)
    mlp_loads = [
        local.start(src, dst)
        for src, dst in ((hbm.gate_sum, blocks.gate), (hbm.up_sum, blocks.up), (hbm.down_sum, blocks.down))
    ]
    load_grad = [
        local.start(hbm.out_grad.at[sum_four.own_rows(j)], work.token_own.at[pl.ds(j * PIECE, PIECE)])
        for j in range(CHUNKS)
    ]
    load_saved = BackSaved(*[local.start(src, dst) for src, dst in zip(hbm_saved, saved)])
    load_win_out = local.start(hbm.win_out, work.win_out)
    load_win = [
        local.start(src, work.w_win.at[:, pl.ds(k * WIDE, WIDE)])
        for k, src in enumerate((hbm.win_q, hbm.win_k, hbm.win_v))
    ]
    load_normed = local.start(hbm.normed_two, work.normed_low)
    load_lin = [
        local.start(src, dst)
        for src, dst in ((hbm.w_query, work.w_query), (hbm.w_key, work.w_key), (hbm.w_out, work.w_out))
    ]

    greet(
        [place.peer()]
        + [place.on_x(k) for k in (1, 2, 3)]
        + [place.on_y(k) for k in (1, 2, 3)]
        + [place.on_z(k) for k in (1, 2, 3)]
        + [place.along(1), place.along(15)]
    )
    seq_copies = Copies(seq_send, seq_recv)
    few = Copies(few_send, few_recv)
    finished = Groups(outs.gate, outs.up, outs.down, outs.win_out, work.sum_win, outs.out, work.sum_lin)
    seq_sums = Groups(
        *[
            SeqSum(place, seq_copies, block, out, bufs_here)
            for block, out, bufs_here in zip(blocks, finished, seq_bufs)
        ]
    )
    queue = []

    def pump(count=1):
        for _ in range(count):
            if queue:
                group, number = queue.pop(0)
                group.step(number)

    first, second, vectors = inputs.first, inputs.second, inputs.vectors
    scale = vectors[2:3]
    group_row, group_col = inputs.group_row, work.group_col
    column(group_row, group_col)
    last_group = group_row[0:1, ROWS - 1 : ROWS].astype(F32)
    first_group = group_row[0:1, 0:1].astype(F32)
    in_last = (group_col[:, 0:1] == last_group).astype(F32)
    after_first = jnp.where(place.seq > 0, 1.0, 0.0)
    work.gain_sums[...] = jnp.zeros_like(work.gain_sums)

    def back_through_norm(mp_sum, number, resid, gain, grad, to, j):
        mine = pl.ds(j * PIECE, PIECE)
        rows, normed_grad = resid[mine].astype(F32), own[mine]
        factor = lax.rsqrt(jnp.mean(rows * rows, axis=-1, keepdims=True) + EPSILON)
        unit = rows * factor
        scaled = normed_grad * gain[...]
        total = grad[mine].astype(F32) + factor * (
            scaled - unit * jnp.mean(scaled * unit, axis=-1, keepdims=True)
        )
        work.gain_sums[number : number + 1] += jnp.sum(normed_grad * unit, axis=0, keepdims=True)
        if number > 0:
            work.grad_own[mine] = total
        to[mp_sum.own_rows(j)] = total.astype(BF)

    load_part.wait()
    mixed_grad, keys_sum, values_sum, win_grads = (
        work.mixed_grad,
        work.keys_sum,
        work.values_sum,
        work.win_grads,
    )
    probs, query_win, keys_all, values_all = (
        saved.probs,
        saved.query_win,
        saved.keys_all,
        saved.values_all,
    )
    score_scale = HD ** (-0.5)
    back = []

    def finish_four(j):
        if j == 0:
            load_saved.resid_two.wait()
            for load in load_grad:
                load.wait()
        back_through_norm(sum_four, 2, saved.resid_two, inputs.gain_three, work.token_own, tokens_low, j)

    def window_back(t):
        rows, window = pl.ds(t * WIN, WIN), pl.ds(t * WIN, TILE)
        for head in range(2):
            lanes = slice(head * HD, (head + 1) * HD)
            grad_tile, held = mixed_grad[rows, lanes], probs[head, rows]
            probs_grad = dot_nt(grad_tile, values_all[window, lanes])
            score_low = (
                held * (probs_grad - jnp.sum(probs_grad * held, axis=1, keepdims=True))
            ).astype(BF)
            win_grads[rows, lanes] = (dot(score_low, keys_all[window, lanes]) * score_scale).astype(BF)
            for ref, found in (
                (keys_sum, dot_tn(score_low, query_win[rows, lanes]) * score_scale),
                (values_sum, dot_tn(held.astype(BF), grad_tile)),
            ):
                if t == 0:
                    ref[window, lanes] = found
                else:
                    ref[rows, lanes] += found[:WIN]
                    ref[pl.ds(t * WIN + WIN, WIN), lanes] = found[WIN:]
        if t == 0:
            for ref, to_send in ((keys_sum, work.back_key), (values_sum, work.back_value)):
                to_send[0] = ref[0:WIN].astype(BF)
                back.append(few.start(to_send.at[0], to_send.at[1], place.along(15)))

    def ready_four(j):
        if j == 0:
            load_win_out.wait()
            for load in (load_saved.probs, load_saved.query_win, load_saved.keys_all, load_saved.values_all):
                load.wait()
        rows = pl.ds(j * CHUNK, CHUNK)
        mixed_grad[rows] = dot_nt(tokens_low[rows], work.win_out[...]).astype(BF)
        window_back(2 * j)
        window_back(2 * j + 1)

    def produce_five(j):
        if j == 0:
            for load in load_win:
                load.wait()
        rows = pl.ds(j * CHUNK, CHUNK)
        for k, (ref, got) in enumerate(((keys_sum, work.back_key), (values_sum, work.back_value))):
            lanes = slice((k + 1) * WIDE, (k + 2) * WIDE)
            if j < CHUNKS - 1:
                win_grads[rows, lanes] = ref[WIN + j * CHUNK : WIN + (j + 1) * CHUNK].astype(BF)
            else:
                win_grads[j * CHUNK : ROWS - WIN, lanes] = ref[WIN + j * CHUNK : ROWS].astype(BF)
                back[k].wait_recv()
                win_grads[ROWS - WIN : ROWS, lanes] = (
                    ref[ROWS : ROWS + WIN] + got[1].astype(F32)
                ).astype(BF)
        part[rows] = dot_nt(win_grads[rows], work.w_win[...]).astype(BF)

    def finish_five(j):
        if j == 0:
            load_saved.resid_one.wait()
        back_through_norm(sum_five, 1, saved.resid_one, inputs.gain_two, work.grad_own, other_full, j)

    query, key, value, carried = saved.query, saved.key, saved.value, saved.carried
    numer_low, query_sum, key_sum, value_sum = (
        work.numer_low,
        work.query_sum,
        work.key_sum,
        work.value_sum,
    )

    def through_features(head, parts, grad):
        left, right = parts
        scaled = grad * scale
        return dot_nt((scaled * right).astype(BF), first[head]) + dot_nt(
            (scaled * left).astype(BF), second[head]
        )

    def ready_five(j):
        rows, count = pl.ds(j * CHUNK, CHUNK), (j + 1) * CHUNK
        if j == 0:
            for load in load_lin:
                load.wait()
            for load in (
                load_saved.denominator,
                load_saved.quotient,
                load_saved.query,
                load_saved.key,
                load_saved.value,
                load_saved.carried,
            ):
                load.wait()
        mixed = dot_nt(other_full[rows], work.w_out[...]).astype(BF).astype(F32)
        incoming = (group_col[rows, 0:1] == first_group).astype(F32) * after_first
        kept = kept_pairs(group_col, group_row, j)
        key_new = []
        for head in range(2):
            lanes = slice(head * HD, (head + 1) * HD)
            denom = saved.denominator[head, rows]
            numer = (mixed[:, lanes] / denom).astype(BF)
            numer_low[rows, lanes] = numer
            denom_grad = (
                -jnp.sum(mixed[:, lanes] * saved.quotient[rows, lanes], axis=1, keepdims=True) / denom
            )
            parts = factors(head, (query[0, rows], query[1, rows]), first, second, vectors)
            used = (parts[0] * parts[1] * scale).astype(BF).astype(F32) * incoming
            state = dot_tn(numer, used.astype(BF))
            norm = jnp.broadcast_to(jnp.sum(used * denom_grad, axis=0, keepdims=True), (STATE - HD, WIDE))
            if j == 0:
                work.state_sum[head, 0:HD] = state
                work.state_sum[head, HD:STATE] = norm
            else:
                work.state_sum[head, 0:HD] += state
                work.state_sum[head, HD:STATE] += norm
            grad = incoming * (
                dot(numer, carried[head, 0:HD].astype(BF)) + denom_grad * carried[head, HD : HD + 1]
            )
            query_new = through_features(head, parts, grad)
            inner = products(head, (query.at[0], query.at[1]), (key.at[0], key.at[1]), rows, count)
            kernel = jnp.where(kept, 1.0 + inner * 0.25 + inner * inner * 0.03125, 0.0).astype(BF)
            grad = dot_nt(numer, value[0:count, lanes]) + denom_grad
            grad = jnp.where(kept, grad, 0.0).astype(BF).astype(F32)
            inner_grad = (grad * (0.25 + inner * 0.0625)).astype(BF)
            query_new = query_new + of_head(dot(inner_grad, key[0, 0:count]), head)
            if head == 0:
                query_sum[rows] = query_new
            else:
                query_sum[rows] += query_new
            key_new.append(of_head(dot_tn(inner_grad, query[0, rows]), head))
            found = dot_tn(kernel, numer)
            if j > 0:
                value_sum[0 : count - CHUNK, lanes] += found[0 : count - CHUNK]
            value_sum[count - CHUNK : count, lanes] = found[count - CHUNK : count]
        found = key_new[0] + key_new[1]
        if j > 0:
            key_sum[0 : count - CHUNK] += found[0 : count - CHUNK]
        key_sum[count - CHUNK : count] = found[count - CHUNK : count]
        if j == CHUNKS - 1:
            for head in range(2):
                work.held_y[0, head] = work.state_sum[head].astype(BF)

    def weight_task(block, right, quarter):
        weight_block(block, work.flipped, right, quarter)

    def begin(group):
        group.step(0)

    def turn_mixed(ref, load):
        load.wait()
        work.flipped[0:WIDE] = ref[...].T

    def turn_win():
        load_normed.wait()
        for k in range(3):
            rows = slice(k * WIDE, (k + 1) * WIDE)
            work.flipped[rows] = win_grads[:, rows].T

    late_work = [functools.partial(turn_mixed, saved.mixed_win, load_saved.mixed_win)]
    late_work += [functools.partial(weight_task, blocks.win_out, tokens_low, k) for k in range(4)]
    late_work += [functools.partial(begin, seq_sums.win_out), turn_win]
    late_work += [functools.partial(weight_task, blocks.win, work.normed_low, k) for k in range(4)]
    late_work += [functools.partial(begin, seq_sums.win)]

    four = sum_four.slots(lambda j: None, finish_four, ready_four)
    five = sum_five.slots(produce_five, finish_five, ready_five)
    for slot in four:
        if slot < 3:
            mlp_loads[slot].wait()
            seq_sums[slot].step(0)
        if slot == 6:
            seq_sums.gate.step(1)
        if slot == 8:
            seq_sums.up.step(1)
        if slot >= 7:
            next(five)
    seq_sums.down.step(1)
    queue += [(seq_sums.gate, 2), (seq_sums.up, 2), (seq_sums.down, 2), (seq_sums.gate, 3)]
    for slot in five:
        for _ in range(2):
            if slot >= CHUNKS and late_work:
                late_work.pop(0)()
        if slot >= 5:
            pump()
    scan = state_scan(place, few, work.held_y, work.held_z, work.later, True)
    next(scan)
    for block in late_work:
        block()
    load_normed_one = local.start(hbm.normed_one, work.normed_low)
    load_value = local.start(hbm.w_value, work.w_win.at[:, pl.ds(0, WIDE)])
    load_token = [
        local.start(hbm.tokens.at[sum_six.own_rows(j)], work.token_own.at[pl.ds(j * PIECE, PIECE)])
        for j in range(CHUNKS)
    ]
    next(scan)
    turn_mixed(saved.mixed_lin, load_saved.mixed_lin)
    weight_task(blocks.out, other_full, 0)
    weight_task(blocks.out, other_full, 1)
    next(scan)
    weight_task(blocks.out, other_full, 2)
    weight_task(blocks.out, other_full, 3)
    for _ in scan:
        pass
    queue += [(seq_sums.out, 0), (seq_sums.up, 3), (seq_sums.win_out, 1), (seq_sums.win, 1)]
    pump()
    for head in range(2):
        lanes = slice(head * HD, (head + 1) * HD)
        state = work.later[head, 0:HD].astype(BF)
        parts = factors(head, (key[0], key[1]), first, second, vectors)
        feat = (parts[0] * parts[1] * scale).astype(BF)
        grad = in_last * (dot(value[:, lanes], state) + work.later[head, HD : HD + 1])
        key_sum[...] += through_features(head, parts, grad)
        value_sum[:, lanes] += in_last * dot_nt(feat, state)
    work.query_low[...] = query_sum[...].astype(BF)
    work.key_low[...] = key_sum[...].astype(BF)
    work.value_low[...] = value_sum[...].astype(BF)
    load_value.wait()

    def produce_six(j):
        rows = pl.ds(j * CHUNK, CHUNK)
        part[rows] = (
            dot_nt(work.value_low[rows], work.w_win[:, 0:WIDE])
            + dot(work.query_low[rows], work.w_query[...])
            + dot(work.key_low[rows], work.w_key[...])
        ).astype(BF)

    for load in load_token:
        load.wait()

    def finish_six(j):
        back_through_norm(sum_six, 0, work.token_own, inputs.gain_one, work.grad_own, tokens_low, j)

    def gains():
        work.gain_low[...] = work.gain_sums[...].astype(BF)

        def block(ref, at, size):
            return ref.at[:, pl.ds(pl.multiple_of(at * size, TILE), size)]

        over = [
            few.start(block(work.gain_low, (z + k) % 4, 512), work.gain_z.at[k - 1], place.on_z(k))
            for k in (1, 2, 3)
        ]
        yield
        total = block(work.gain_low, z, 512)[...].astype(F32)
        for k, copy in enumerate(over):
            copy.wait_recv()
            total = total + work.gain_z[k].astype(F32)
        work.gain_zz[...] = total.astype(BF)
        over = [
            few.start(block(work.gain_zz, (y + k) % 4, TILE), work.gain_y.at[k - 1], place.on_y(k))
            for k in (1, 2, 3)
        ]
        yield
        total = block(work.gain_zz, y, TILE)[...].astype(F32)
        for k, copy in enumerate(over):
            copy.wait_recv()
            total = total + work.gain_y[k].astype(F32)
        work.gain_x[...] = total.astype(BF)
        over = [few.start(work.gain_x, work.gain_xx.at[k - 1], place.on_x(k)) for k in (1, 2, 3)]
        yield
        total = work.gain_x[...].astype(F32)
        for k, copy in enumerate(over):
            copy.wait_recv()
            total = total + work.gain_xx[k].astype(F32)
        work.gain_p[...] = total.astype(BF)
        copy = few.start(work.gain_p, work.gain_pp, place.peer())
        yield
        copy.wait_recv()
        total = work.gain_p[...].astype(F32) + work.gain_pp[...].astype(F32)
        for k, ref in enumerate((outs.gain_one, outs.gain_two, outs.gain_three)):
            ref[...] = total[k : k + 1]

    def turn_lin():
        load_normed_one.wait()
        work.flipped[0:WIDE] = work.value_low[...].T
        for k, ref in enumerate((query_sum, key_sum)):
            at = WIDE + 2 * FEAT * k
            wide = jnp.concatenate([ref[...], jnp.zeros((ROWS, TILE - 2 * FEAT), F32)], axis=1)
            work.flipped[at : at + 2 * FEAT] = wide.T[0 : 2 * FEAT].astype(BF)

    tasks = [turn_lin]
    tasks += [functools.partial(weight_task, blocks.lin, work.normed_low, k) for k in range(4)]
    tasks += [functools.partial(begin, seq_sums.lin)]
    queue += [(seq_sums.down, 3), (seq_sums.out, 1), (seq_sums.gate, 4), (seq_sums.win_out, 2)]
    queue += [(seq_sums.up, 4)]
    gain_steps = gains()
    for slot in sum_six.slots(produce_six, finish_six):
        if slot < CHUNKS - 1:
            continue
        for _ in range(2):
            if tasks:
                tasks.pop(0)()
        pump()
        if slot >= CHUNKS + 2:
            next(gain_steps, None)
    queue += [(seq_sums.win, 2), (seq_sums.lin, 1), (seq_sums.down, 4), (seq_sums.out, 2)]
    queue += [(seq_sums.win_out, 3), (seq_sums.win, 3), (seq_sums.lin, 2), (seq_sums.out, 3)]
    queue += [(seq_sums.win_out, 4), (seq_sums.win, 4), (seq_sums.lin, 3), (seq_sums.out, 4)]
    queue += [(seq_sums.lin, 4)]
    pump(len(queue))
    for k, ref in enumerate((outs.win_q, outs.win_k, outs.win_v)):
        ref[...] = work.sum_win[k * WIDE : (k + 1) * WIDE].T
    outs.value[...] = work.sum_lin[0:WIDE].T
    outs.query[...] = work.sum_lin[WIDE : WIDE + 2 * FEAT]
    outs.key[...] = work.sum_lin[WIDE + 2 * FEAT : WIDE + 4 * FEAT]
    for _ in gain_steps:
        pass
    seq_copies.finish()
    few.finish()


def backward(saved, inputs, weights):
    back_inputs = BackInputs(*inputs[1:])
    hbm = BackHbm(
        part_four=saved.part_four,
        out_grad=weights.out_grad,
        tokens=inputs.tokens,
        normed_one=saved.normed_one,
        normed_two=saved.normed_two,
        gate_sum=saved.gate_sum,
        up_sum=saved.up_sum,
        down_sum=saved.down_sum,
        w_query=weights.w_query,
        w_key=weights.w_key,
        w_value=weights.w_value,
        w_out=weights.w_out,
        win_q=weights.win_q,
        win_k=weights.win_k,
        win_v=weights.win_v,
        win_out=weights.win_out,
    )
    held = BackSaved(*[getattr(saved, name) for name in BackSaved._fields])
    scratch = vmem(BackSaved) + [pltpu.VMEM((4, 4, width, TILE), BF) for width in Groups()]
    scratch += vmem(BackWork)
    for width in Groups():
        scratch += seq_scratch(width)
    scratch += mp_scratch()
    scratch += [dma(CHUNKS * PER_CHUNK)] * 2 + [dma(24 * len(Groups._fields))] * 2 + [dma(24)] * 2
    scratch += [dma(64)]
    return BackOuts(
        *pl.pallas_call(
            backward_kernel,
            out_shape=[shape(dims, kind) for dims, kind in BackOuts()],
            in_specs=[INSIDE] * len(back_inputs) + [HBM] * (len(hbm) + len(held)),
            out_specs=[INSIDE] * len(BackOuts._fields),
            scratch_shapes=scratch,
            compiler_params=pltpu.CompilerParams(
                collective_id=1, has_side_effects=True, vmem_limit_bytes=VMEM_LIMIT
            ),
        )(*back_inputs, *hbm, *held)
    )


def hand_over_kernel(*refs):
    count = (len(refs) - 3) // 2
    ins, outs, (low, wide, sems) = refs[:count], refs[count : 2 * count], refs[2 * count :]
    block = ROWS // 4
    local = Locals(sems)
    loads = []
    for k in range(4):
        rows = pl.ds(k * block, block)
        loads.append(local.start(ins[0].at[rows], low.at[rows]))
    copies = [local.start(src, dst) for src, dst in zip(ins[1:], outs[1:])]
    for k in range(4):
        rows = pl.ds(k * block, block)
        loads[k].wait()
        wide[rows] = low[rows].astype(F32)
        copies.append(local.start(wide.at[rows], outs[0].at[rows]))
    for copy in copies:
        copy.wait()


def hand_over(arrays):
    kinds = [F32] + [array.dtype for array in arrays[1:]]
    return pl.pallas_call(
        hand_over_kernel,
        out_shape=[shape(array.shape, kind) for array, kind in zip(arrays, kinds)],
        in_specs=[HBM] * len(arrays),
        out_specs=[HBM] * len(arrays),
        scratch_shapes=[
            pltpu.VMEM((ROWS, D), BF),
            pltpu.VMEM((ROWS, D), F32),
            dma(len(arrays) + 7),
        ],
        compiler_params=pltpu.CompilerParams(vmem_limit_bytes=VMEM_LIMIT),
    )(*arrays)


def local(
    tokens,
    group_ids,
    gain_one,
    lin_query,
    lin_key,
    lin_value,
    lin_output,
    gain_two,
    win_query,
    win_key,
    win_value,
    win_output,
    gain_three,
    mlp_gate,
    mlp_up,
    mlp_down,
    out_grad,
):
    first, second, vectors = feature_tables()
    inputs = Inputs(
        tokens=tokens,
        group_row=group_ids.reshape(1, ROWS),
        gain_one=gain_one.reshape(1, D),
        gain_two=gain_two.reshape(1, D),
        gain_three=gain_three.reshape(1, D),
        first=first,
        second=second,
        vectors=vectors,
    )
    weights = Weights(
        out_grad=out_grad,
        w_query=lin_query.T,
        w_key=lin_key.T,
        w_value=lin_value,
        w_out=lin_output,
        win_k=win_key,
        win_v=win_value,
        win_q=win_query,
        win_out=win_output,
        w_gate=mlp_gate.T,
        w_up=mlp_up.T,
        w_down=mlp_down,
    )
    saved = forward(inputs, weights)
    outs = BackOuts(*backward(saved, inputs, weights))
    done = hand_over([*outs, saved.result])
    outs, result = BackOuts(*done[:-1]), done[-1]
    return (
        result,
        outs.tokens_low,
        outs.gain_one.reshape(TILE),
        outs.query.T,
        outs.key.T,
        outs.value,
        outs.out,
        outs.gain_two.reshape(TILE),
        outs.win_q,
        outs.win_k,
        outs.win_v,
        outs.win_out,
        outs.gain_three.reshape(TILE),
        outs.gate.T,
        outs.up.T,
        outs.down,
    )


def solution(mesh):
    return jax.shard_map(
        local,
        mesh=mesh,
        in_specs=(
            P("seq", None),
            P("seq"),
            P(),
            P(None, "mp"),
            P(None, "mp"),
            P(None, "mp"),
            P("mp", None),
            P(),
            P(None, "mp"),
            P(None, "mp"),
            P(None, "mp"),
            P("mp", None),
            P(),
            P(None, "mp"),
            P(None, "mp"),
            P("mp", None),
            P("seq", None),
        ),
        out_specs=(
            P("seq", None),
            P("seq", None),
            P("seq"),
            P("seq", "mp"),
            P("seq", "mp"),
            P("seq", "mp"),
            P("mp", "seq"),
            P("seq"),
            P("seq", "mp"),
            P("seq", "mp"),
            P("seq", "mp"),
            P("mp", "seq"),
            P("seq"),
            P("seq", "mp"),
            P("seq", "mp"),
            P("mp", "seq"),
        ),
        check_vma=False,
    )
```

```python
import functools
import types
from typing import Any, NamedTuple

import jax
import jax.numpy as jnp
import numpy as np
from jax import lax
from jax.experimental import pallas as pl
from jax.experimental.pallas import tpu as pltpu
from jax.sharding import PartitionSpec as P

D = 2048
HD = 128
FEAT = 16
WIN = 64
FF = 704
FF_PAD = 768
ROWS = 512
TILE = 128
WIDE = 256
FEATURES = 160
STATE = FEATURES + 16

CHUNKS = 4
CHUNK = ROWS // CHUNKS
HALF = CHUNK // 2
PIECE = CHUNK // 8
OWN = 64
COLS = D // 2
PER_CHUNK = 21

EPSILON = 1e-05
MESH = pl.DeviceIdType.MESH
BF = jnp.bfloat16
F32 = jnp.float32
VMEM_LIMIT = 62 * 1024 * 1024


class Place:
    def __init__(self):
        self.seq = lax.axis_index("seq")
        self.mp = lax.axis_index("mp")
        self.z, self.y = self.seq // 4, self.seq % 4
        self.x, self.core = self.mp // 2, self.mp % 2

    def peer(self):
        return (self.seq, self.x * 2 + (1 - self.core))

    def on_x(self, step):
        return (self.seq, ((self.x + step) % 4) * 2 + self.core)

    def on_y(self, step):
        return (self.z * 4 + (self.y + step) % 4, self.mp)

    def on_z(self, step):
        return (((self.z + step) % 4) * 4 + self.y, self.mp)

    def along(self, step):
        return ((self.seq + step) % 16, self.mp)


class Copies:
    def __init__(self, send_sems, recv_sems):
        self.send_sems, self.recv_sems = send_sems, recv_sems
        self.count, self.started = 0, []

    def start(self, src, dst, device):
        k = self.count
        self.count += 1
        copy = pltpu.make_async_remote_copy(
            src_ref=src,
            dst_ref=dst,
            send_sem=self.send_sems.at[k],
            recv_sem=self.recv_sems.at[k],
            device_id=device,
            device_id_type=MESH,
        )
        copy.start()
        self.started.append(copy)
        return copy

    def finish(self):
        for copy in self.started:
            copy.wait_send()


class Locals:
    def __init__(self, sems):
        self.sems, self.count = sems, 0

    def start(self, src, dst):
        copy = pltpu.make_async_copy(src, dst, self.sems.at[self.count])
        self.count += 1
        copy.start()
        return copy


def greet(devices):
    barrier = pltpu.get_barrier_semaphore()
    for device in devices:
        pl.semaphore_signal(barrier, inc=1, device_id=device, device_id_type=MESH)


def meet(count):
    pl.semaphore_wait(pltpu.get_barrier_semaphore(), count)


def rows_at(start, size):
    return pl.ds(pl.multiple_of(start, 16), size)


def dot(left, right):
    return lax.dot_general(left, right, (((1,), (0,)), ((), ())), preferred_element_type=F32)


def dot_nt(left, right):
    return lax.dot_general(left, right, (((1,), (1,)), ((), ())), preferred_element_type=F32)


def dot_tn(left, right):
    return lax.dot_general(left, right, (((0,), (0,)), ((), ())), preferred_element_type=F32)


def halves(values):
    high = values.astype(BF)
    return high, (values - high.astype(F32)).astype(BF)


class MpSum:
    def __init__(self, place, sems, part, full, own, bufs, lag=0, order=tuple(range(CHUNKS))):
        self.place, self.part, self.full, self.own = place, part, full, own
        self.lag, self.order = lag, order
        self.send_sems, self.recv_sems = sems
        (self.from_peer, self.send_opp, self.send_right, self.send_left) = bufs[:4]
        (self.fwd, self.direct, self.comb) = bufs[4:]
        x = place.x
        self.turn = [(x + 2) % 4, (x + 1) % 4, (x + 3) % 4, x]
        self.peer, self.right, self.left = place.peer(), place.on_x(1), place.on_x(3)
        self.live = [types.SimpleNamespace(sent=[]) for _ in range(CHUNKS)]

    def start(self, j, src, dst, device):
        k = j * PER_CHUNK + len(self.live[j].sent)
        copy = pltpu.make_async_remote_copy(
            src_ref=src,
            dst_ref=dst,
            send_sem=self.send_sems.at[k],
            recv_sem=self.recv_sems.at[k],
            device_id=device,
            device_id_type=MESH,
        )
        copy.start()
        self.live[j].sent.append(copy)
        return copy

    def rows(self, j, core, x):
        return rows_at(j * CHUNK + core * HALF + x * PIECE, PIECE)

    def own_rows(self, j):
        return self.rows(j, self.place.core, self.place.x)

    def chip_sum(self, j, slot, low, size):
        cols = pl.ds(low, size)
        return self.part[self.rows(j, self.place.core, self.turn[slot]), cols].astype(
            F32
        ) + self.from_peer[j, slot, :, cols].astype(F32)

    def exchange(self, j):
        self.live[j].ex = [
            self.start(
                j,
                self.part.at[self.rows(j, 1 - self.place.core, at)],
                self.from_peer.at[j, slot],
                self.peer,
            )
            for slot, at in enumerate(self.turn)
        ]

    def first(self, j):
        live = self.live[j]
        low, high = pl.ds(0, COLS), pl.ds(COLS, COLS)
        live.ex[0].wait_recv()
        self.send_opp[j] = self.chip_sum(j, 0, 0, D).astype(BF)
        live.fr = self.start(j, self.send_opp.at[j, :, low], self.fwd.at[j, 0], self.right)
        live.fl = self.start(j, self.send_opp.at[j, :, high], self.fwd.at[j, 1], self.left)
        live.ex[1].wait_recv()
        self.send_right[j, 0] = self.chip_sum(j, 1, COLS, COLS).astype(BF)
        live.dr = self.start(j, self.send_right.at[j, 0], self.direct.at[j, 1], self.right)
        live.ex[2].wait_recv()
        self.send_left[j, 0] = self.chip_sum(j, 2, 0, COLS).astype(BF)
        live.dl = self.start(j, self.send_left.at[j, 0], self.direct.at[j, 0], self.left)

    def second(self, j):
        live = self.live[j]
        live.fr.wait_recv()
        self.send_right[j, 1] = (
            self.chip_sum(j, 1, 0, COLS) + self.fwd[j, 0].astype(F32)
        ).astype(BF)
        live.cr = self.start(j, self.send_right.at[j, 1], self.comb.at[j, 0], self.right)
        live.fl.wait_recv()
        self.send_left[j, 1] = (
            self.chip_sum(j, 2, COLS, COLS) + self.fwd[j, 1].astype(F32)
        ).astype(BF)
        live.cl = self.start(j, self.send_left.at[j, 1], self.comb.at[j, 1], self.left)

    def total(self, j):
        live, mine = self.live[j], pl.ds(j * PIECE, PIECE)
        live.ex[3].wait_recv()
        live.dl.wait_recv()
        live.cr.wait_recv()
        self.own[mine, 0:COLS] = (
            self.chip_sum(j, 3, 0, COLS)
            + self.direct[j, 0].astype(F32)
            + self.comb[j, 0].astype(F32)
        )
        live.dr.wait_recv()
        live.cl.wait_recv()
        self.own[mine, COLS:D] = (
            self.chip_sum(j, 3, COLS, COLS)
            + self.direct[j, 1].astype(F32)
            + self.comb[j, 1].astype(F32)
        )

    def send(self, j, at, low, size, device):
        block = self.full.at[self.rows(j, self.place.core, at), pl.ds(low, size)]
        return self.start(j, block, block, device)

    def spread(self, j):
        live, x = self.live[j], self.place.x
        live.rl = self.send(j, x, 0, COLS, self.right)
        live.lh = self.send(j, x, COLS, COLS, self.left)
        live.rh = self.send(j, x, COLS, COLS, self.right)
        live.ll = self.send(j, x, 0, COLS, self.left)
        live.peers = [self.send(j, x, 0, D, self.peer)]

    def relay(self, j):
        live, x = self.live[j], self.place.x
        live.rl.wait_recv()
        live.gr = self.send(j, (x + 3) % 4, 0, COLS, self.right)
        live.lh.wait_recv()
        live.gl = self.send(j, (x + 1) % 4, COLS, COLS, self.left)
        live.rh.wait_recv()
        live.peers.append(self.send(j, (x + 3) % 4, 0, D, self.peer))
        live.ll.wait_recv()
        live.peers.append(self.send(j, (x + 1) % 4, 0, D, self.peer))

    def last(self, j):
        live, x = self.live[j], self.place.x
        live.gr.wait_recv()
        live.peers.append(self.send(j, (x + 2) % 4, 0, COLS, self.peer))
        live.gl.wait_recv()
        live.peers.append(self.send(j, (x + 2) % 4, COLS, COLS, self.peer))

    def arrived(self, j):
        for copy in self.live[j].peers:
            copy.wait_recv()
        for copy in self.live[j].sent:
            copy.wait_send()

    def slots(self, produce, finish, ready=None):
        for slot in range((CHUNKS - 1) * self.lag + 7):
            for position, j in enumerate(self.order):
                stage = slot - position * self.lag
                if stage == 0:
                    produce(j)
                    self.exchange(j)
                elif stage == 1:
                    self.first(j)
                elif stage == 2:
                    self.second(j)
                elif stage == 3:
                    self.total(j)
                    finish(j)
                    self.spread(j)
                elif stage == 4:
                    self.relay(j)
                elif stage == 5:
                    self.last(j)
                elif stage == 6:
                    self.arrived(j)
                    if ready is not None:
                        ready(j)
            yield slot


def mp_scratch():
    ring = pltpu.VMEM((CHUNKS, 2, PIECE, COLS), BF)
    return [pltpu.VMEM((CHUNKS, 4, PIECE, D), BF), pltpu.VMEM((CHUNKS, PIECE, D), BF)] + [ring] * 5


def dma(count):
    return pltpu.SemaphoreType.DMA((count,))


def run(slots):
    for _ in slots:
        pass


def norm_rows_of(total):
    row = lax.broadcasted_iota(jnp.int32, (16, TILE), 0)
    return jnp.where(row == 0, total[:, 0:TILE], jnp.where(row == 1, total[:, TILE:WIDE], 0.0))


class StateScan(NamedTuple):
    mine: Any = ((2, STATE, HD), BF)
    early: Any = ((2, 3, STATE, HD), BF)
    sent: Any = ((2, 2, STATE, HD), BF)
    late: Any = ((2, 3, STATE, HD), BF)


def state_scan(place, copies, bufs, states, norms, reverse):
    def counted(position, step):
        at = (position - step + 4) % 4
        reached = at > position if reverse else at < position
        return jnp.where(reached, 1.0, 0.0)

    def wider(step):
        to = (place.y + step) % 4
        return (to < place.y if reverse else to > place.y).astype(jnp.int32)

    def put(head, total):
        states[head, 0:FEATURES] = total[0:FEATURES]
        states[head, FEATURES:WIDE] = jnp.zeros((WIDE - FEATURES, HD), F32)
        norms[head, 0:1, 0:TILE] = total[FEATURES : FEATURES + 1]
        norms[head, 0:1, TILE:WIDE] = total[FEATURES + 1 : FEATURES + 2]

    steps = (1, 2, 3)
    over = [copies.start(bufs.mine.at[0], bufs.early.at[0, k - 1], place.on_y(k)) for k in steps]
    across = [copies.start(bufs.mine.at[1], bufs.early.at[1, k - 1], place.on_z(k)) for k in steps]
    yield
    total, before = bufs.mine[0].astype(F32), jnp.zeros((STATE, HD), F32)
    for k, copy in zip(steps, over):
        copy.wait_recv()
        part = bufs.early[0, k - 1].astype(F32)
        total, before = total + part, before + counted(place.y, k) * part
    bufs.sent[0, 0] = total.astype(BF)
    over = [copies.start(bufs.sent.at[0, 0], bufs.late.at[0, k - 1], place.on_z(k)) for k in steps]
    put(0, before)
    before = jnp.zeros((STATE, HD), F32)
    for k, copy in zip(steps, across):
        copy.wait_recv()
        before = before + counted(place.z, k) * bufs.early[1, k - 1].astype(F32)
    bufs.sent[1, 0] = before.astype(BF)
    bufs.sent[1, 1] = (before + bufs.mine[1].astype(F32)).astype(BF)
    across = [
        copies.start(bufs.sent.at[1, wider(k)], bufs.late.at[1, k - 1], place.on_y(k)) for k in steps
    ]
    put(1, before)
    yield
    for head, sent in enumerate((over, across)):
        total = jnp.zeros((STATE, HD), F32)
        for k, copy in zip(steps, sent):
            copy.wait_recv()
            part = bufs.late[head, k - 1].astype(F32)
            total = total + (counted(place.z, k) * part if head == 0 else part)
        states[head, 0:FEATURES] += total[0:FEATURES]
        norms[head, 0:1, 0:TILE] += total[FEATURES : FEATURES + 1]
        norms[head, 0:1, TILE:WIDE] += total[FEATURES + 1 : FEATURES + 2]
    yield


def feature_tables():
    pairs = [(a, b) for a in range(FEAT) for b in range(a, FEAT)]
    first = np.zeros((2, 2 * FEAT, WIDE), np.float32)
    second = np.zeros((2, 2 * FEAT, WIDE), np.float32)
    vectors = np.zeros((8, WIDE), np.float32)
    vectors[0, 0] = vectors[1, 0] = vectors[2, 0] = 1.0
    for a in range(FEAT):
        vectors[1, 1 + a] = 1.0
        vectors[2, 1 + a] = FEAT ** (-0.25)
        for h in range(2):
            first[h, h * FEAT + a, 1 + a] = 1.0
    for number, (a, b) in enumerate(pairs):
        at = 1 + FEAT + number
        vectors[2, at] = (1.0 if a == b else 2.0**0.5) * (2.0 * FEAT) ** (-0.5)
        for h in range(2):
            first[h, h * FEAT + a, at] = 1.0
            second[h, h * FEAT + b, at] = 1.0
    return jnp.asarray(first, BF), jnp.asarray(second, BF), jnp.asarray(vectors, F32)


def factors(head, values, first, second, vectors):
    high, low = values
    left = dot(high, first[head]) + dot(low, first[head]) + vectors[0:1]
    right = dot(high, second[head]) + dot(low, second[head]) + vectors[1:2]
    return left, right


def of_head(values, head):
    lane = lax.broadcasted_iota(jnp.int32, values.shape, 1)
    return jnp.where((lane >= head * FEAT) & (lane < (head + 1) * FEAT), values, jnp.zeros_like(values))


def products(head, query, key, rows, count):
    high, low = (of_head(part[rows], head) for part in query)
    key_high, key_low = (part[0:count] for part in key)
    return dot_nt(high, key_high) + dot_nt(low, key_high) + dot_nt(high, key_low)


def shape(dims, kind):
    return jax.ShapeDtypeStruct(dims, kind)


def normed(rows, gain):
    factor = lax.rsqrt(jnp.mean(rows * rows, axis=-1, keepdims=True) + EPSILON)
    return rows * factor * gain


def column(group_row, held):
    for k in range(ROWS // TILE):
        block = group_row[0:1, k * TILE : (k + 1) * TILE].astype(F32)
        held[k * TILE : (k + 1) * TILE] = jnp.broadcast_to(block, (TILE, TILE)).T


def kept_pairs(group_col, group_row, tile):
    count = (tile + 1) * TILE
    row = lax.broadcasted_iota(jnp.int32, (TILE, count), 0) + tile * TILE
    col = lax.broadcasted_iota(jnp.int32, (TILE, count), 1)
    groups = group_col[tile * TILE : (tile + 1) * TILE, 0:1]
    return (col <= row) & (groups == group_row[0:1, 0:count].astype(F32))


def weight_block(into, left_t, right, quarter):
    count = into.shape[2]
    block = dot(left_t[0:count], right[:, quarter * 512 : (quarter + 1) * 512]).astype(BF)
    for k in range(4):
        into[quarter, k] = block[:, k * TILE : (k + 1) * TILE]


class Inputs(NamedTuple):
    tokens: Any
    group_row: Any
    gain_one: Any
    gain_two: Any
    gain_three: Any
    first: Any
    second: Any
    vectors: Any


class Weights(NamedTuple):
    out_grad: Any = ((ROWS, D), BF)
    w_query: Any = ((2 * FEAT, D), BF)
    w_key: Any = ((2 * FEAT, D), BF)
    w_value: Any = ((D, WIDE), BF)
    w_out: Any = ((WIDE, D), BF)
    win_k: Any = ((D, WIDE), BF)
    win_v: Any = ((D, WIDE), BF)
    win_q: Any = ((D, WIDE), BF)
    win_out: Any = ((WIDE, D), BF)
    w_gate: Any = ((FF_PAD, D), BF)
    w_up: Any = ((FF_PAD, D), BF)
    w_down: Any = ((FF_PAD, D), BF)


class Saved(NamedTuple):
    normed_one: Any = ((ROWS, D), BF)
    query: Any = ((2, ROWS, 2 * FEAT), BF)
    key: Any = ((2, ROWS, 2 * FEAT), BF)
    value: Any = ((ROWS, WIDE), BF)
    carried: Any = ((2, WIDE, HD), F32)
    carried_norm: Any = ((2, 1, WIDE), F32)
    quotient: Any = ((ROWS, WIDE), F32)
    denominator: Any = ((2, ROWS, 1), F32)
    mixed_lin: Any = ((ROWS, WIDE), BF)
    resid_one: Any = ((OWN, D), F32)
    normed_two: Any = ((ROWS, D), BF)
    query_win: Any = ((ROWS, WIDE), BF)
    keys_all: Any = ((ROWS + WIN, WIDE), BF)
    values_all: Any = ((ROWS + WIN, WIDE), BF)
    probs: Any = ((2, ROWS, TILE), F32)
    mixed_win: Any = ((ROWS, WIDE), BF)
    resid_two: Any = ((OWN, D), F32)
    part_four: Any = ((ROWS, D), BF)
    gate_sum: Any = ((4, 4, FF, TILE), BF)
    up_sum: Any = ((4, 4, FF, TILE), BF)
    down_sum: Any = ((4, 4, FF, TILE), BF)
    result: Any = ((ROWS, D), BF)


class ForwardWork(NamedTuple):
    part: Any = ((ROWS, D), BF)
    own: Any = ((OWN, D), F32)
    group_col: Any = ((ROWS, TILE), F32)
    tail_flag: Any = ((16, TILE), BF)
    halo_flag: Any = ((16, TILE), BF)
    query_feat: Any = ((2, ROWS, WIDE), BF)
    key_feat: Any = ((2, ROWS, WIDE), BF)
    normed_three: Any = ((ROWS, D), BF)
    gate_act: Any = ((ROWS, FF_PAD), F32)
    up_act: Any = ((ROWS, FF_PAD), F32)
    hidden: Any = ((ROWS, FF_PAD), BF)
    gate_low: Any = ((ROWS, FF_PAD), BF)
    up_low: Any = ((ROWS, FF_PAD), BF)
    flipped: Any = ((FF_PAD, ROWS), BF)


def taker(refs):
    refs = list(refs)

    def take(kind):
        return kind(*[refs.pop(0) for _ in kind._fields])

    def some(count):
        return [refs.pop(0) for _ in range(count)]

    return take, some


def vmem(kind):
    return [pltpu.VMEM(*entry) for entry in kind()]


def forward_kernel(*refs):
    take, some = taker(refs)
    inputs, hbm_weights, hbm_saved = take(Inputs), take(Weights), take(Saved)
    weights, saved, work, scan_bufs = take(Weights), take(Saved), take(ForwardWork), take(StateScan)
    bufs = some(7)
    mp_sems, (state_send, state_recv), (halo_send, halo_recv), (local_sems,) = (
        some(2),
        some(2),
        some(2),
        some(1),
    )
    place = Place()
    local = Locals(local_sems)
    loads = []
    for src, dst in zip(hbm_weights[1:], weights[1:]):
        loads.append(local.start(src, dst if src.shape == dst.shape else dst.at[pl.ds(0, FF)]))
    loads = Weights(local.start(hbm_weights.out_grad, weights.out_grad), *loads)
    saves = []

    def save(*pairs):
        for src, dst in pairs:
            saves.append(local.start(src, dst))

    greet(
        [place.peer()]
        + [place.on_x(k) for k in (1, 3)]
        + [place.on_y(k) for k in (1, 2, 3)]
        + [place.on_z(k) for k in (1, 2, 3)]
        + [place.along(1), place.along(15)]
    )
    for ref in (weights.w_gate, weights.w_up, weights.w_down):
        ref[FF:FF_PAD] = jnp.zeros((FF_PAD - FF, D), BF)
    tokens, group_row, group_col = inputs.tokens, inputs.group_row, work.group_col
    first, second, vectors = inputs.first, inputs.second, inputs.vectors
    scale = vectors[2:3]
    normed_one = saved.normed_one

    def norm_rows(i, _):
        rows = rows_at(i * 32, 32)
        normed_one[rows] = normed(tokens[rows].astype(F32), inputs.gain_one[...]).astype(BF)
        return 0

    lax.fori_loop(0, ROWS // 32, norm_rows, 0)
    save((normed_one, hbm_saved.normed_one))
    column(group_row, group_col)
    query, key, value = saved.query, saved.key, saved.value
    for load, weight, held in (
        (loads.w_key, weights.w_key, key),
        (loads.w_query, weights.w_query, query),
    ):
        load.wait()
        held[0], held[1] = halves(dot_nt(normed_one[...], weight[...]))
    loads.w_value.wait()
    value[...] = dot(normed_one[...], weights.w_value[...]).astype(BF)

    last = group_row[0:1, ROWS - 1 : ROWS].astype(F32)
    in_last = (group_col[:, 0:1] == last).astype(F32)
    query_feat, key_feat, mine = work.query_feat, work.key_feat, scan_bufs.mine
    for head in range(2):
        left, right = factors(head, (key[0], key[1]), first, second, vectors)
        feat = (left * right * scale).astype(BF)
        key_feat[head] = feat
        kept = feat.astype(F32) * in_last
        state = dot_tn(kept.astype(BF), value[:, head * HD : (head + 1) * HD])
        mine[head, 0:FEATURES] = state[0:FEATURES].astype(BF)
        mine[head, FEATURES:STATE] = norm_rows_of(jnp.sum(kept, axis=0, keepdims=True)).astype(BF)
    meet(11)
    copies_state = Copies(state_send, state_recv)
    scan = state_scan(place, copies_state, scan_bufs, saved.carried, saved.carried_norm, False)
    next(scan)
    save((query, hbm_saved.query), (key, hbm_saved.key), (value, hbm_saved.value))
    quotient, denominator = saved.quotient, saved.denominator
    for head in range(2):
        left, right = factors(head, (query[0], query[1]), first, second, vectors)
        query_feat[head] = (left * right * scale).astype(BF)
    for tile in range(ROWS // TILE):
        rows, count = pl.ds(tile * TILE, TILE), (tile + 1) * TILE
        kept = kept_pairs(group_col, group_row, tile)
        for head in range(2):
            inner = products(head, (query.at[0], query.at[1]), (key.at[0], key.at[1]), rows, count)
            block = jnp.where(kept, 1.0 + inner * 0.25 + inner * inner * 0.03125, 0.0).astype(BF)
            denominator[head, rows] = jnp.sum(block.astype(F32), axis=1, keepdims=True)
            quotient[rows, head * HD : (head + 1) * HD] = dot(
                block, value[0:count, head * HD : (head + 1) * HD]
            )
        if tile == 1:
            next(scan)
    for _ in scan:
        pass
    copies_state.finish()
    first_group = group_row[0:1, 0:1].astype(F32)
    incoming = (group_col[:, 0:1] == first_group).astype(F32) * jnp.where(place.seq > 0, 1.0, 0.0)
    carried, carried_norm, mixed_lin = saved.carried, saved.carried_norm, saved.mixed_lin
    save((carried, hbm_saved.carried), (carried_norm, hbm_saved.carried_norm))
    for head in range(2):
        lanes = slice(head * HD, (head + 1) * HD)
        feat = query_feat[head]
        numer = quotient[:, lanes] + incoming * dot(feat, carried[head].astype(BF))
        denom = denominator[head] + incoming * jnp.sum(
            feat.astype(F32) * carried_norm[head], axis=1, keepdims=True
        )
        ratio = numer / denom
        denominator[head] = denom
        quotient[:, lanes] = ratio
        mixed_lin[:, lanes] = ratio.astype(BF)
    save(
        (quotient, hbm_saved.quotient),
        (denominator, hbm_saved.denominator),
        (mixed_lin, hbm_saved.mixed_lin),
    )
    loads.w_out.wait()

    part, own = work.part, work.own
    resid_one, resid_two = saved.resid_one, saved.resid_two
    normed_two, normed_three = saved.normed_two, work.normed_three
    sum_one = MpSum(place, mp_sems, part, normed_two, own, bufs, 0, (3, 0, 1, 2))
    sum_two = MpSum(place, mp_sems, part, normed_three, own, bufs, 1)
    sum_three = MpSum(place, mp_sems, part, saved.result, own, bufs)

    def produce_one(j):
        rows = pl.ds(j * CHUNK, CHUNK)
        part[rows] = dot(mixed_lin[rows], weights.w_out[...]).astype(BF)

    def finish_one(j):
        mine = pl.ds(j * PIECE, PIECE)
        rows = own[mine] + tokens[sum_one.own_rows(j)].astype(F32)
        resid_one[mine] = rows
        normed_two[sum_one.own_rows(j)] = normed(rows, inputs.gain_two[...]).astype(BF)

    query_win, keys_all, values_all = saved.query_win, saved.keys_all, saved.values_all
    copies_halo = Copies(halo_send, halo_recv)
    lane = lax.broadcasted_iota(jnp.int32, (1, TILE), 1)
    group_blocks = [group_row[0:1, k * TILE : (k + 1) * TILE].astype(F32) for k in range(4)]
    turned = [pltpu.roll(block, WIN, 1) for block in group_blocks]
    work.tail_flag[...] = jnp.broadcast_to((turned[3] == last).astype(F32), (16, TILE)).astype(BF)
    halo = []

    def ready_one(j):
        rows = pl.ds(j * CHUNK, CHUNK)
        below = pl.ds(WIN + j * CHUNK, CHUNK)
        if j == 3:
            for load in (loads.win_k, loads.win_v, loads.win_q):
                load.wait()
        keys_all[below] = dot(normed_two[rows], weights.win_k[...]).astype(BF)
        values_all[below] = dot(normed_two[rows], weights.win_v[...]).astype(BF)
        if j == 3:
            for ref in (keys_all, values_all):
                halo.append(
                    copies_halo.start(ref.at[pl.ds(ROWS, WIN)], ref.at[pl.ds(0, WIN)], place.along(1))
                )
            halo.append(copies_halo.start(work.tail_flag, work.halo_flag, place.along(1)))
        query_win[rows] = dot(normed_two[rows], weights.win_q[...]).astype(BF)
        if j != 3:
            next(two)

    probs, mixed_win = saved.probs, saved.mixed_win
    tile_row = lax.broadcasted_iota(jnp.int32, (WIN, TILE), 0)
    tile_col = lax.broadcasted_iota(jnp.int32, (WIN, TILE), 1)
    near = (tile_col > tile_row) & (tile_col <= tile_row + WIN)
    score_scale = HD ** (-0.5)

    def window_tile(t):
        rows = pl.ds(t * WIN, WIN)
        if t == 0:
            flag = jnp.where(place.seq > 0, work.halo_flag[0:1].astype(F32), 0.0)
            groups = jnp.where(lane < WIN, jnp.where(flag > 0.5, first_group, -2.0), turned[0])
        elif t % 2 == 1:
            groups = group_blocks[t // 2]
        else:
            groups = jnp.where(lane < WIN, turned[t // 2 - 1], turned[t // 2])
        kept = near & (group_col[rows] == groups)
        for head in range(2):
            lanes = slice(head * HD, (head + 1) * HD)
            scores = dot_nt(query_win[rows, lanes], keys_all[t * WIN : t * WIN + TILE, lanes])
            scores = jnp.where(kept, scores * score_scale, -1e30)
            exp_scores = jnp.exp(scores - jnp.max(scores, axis=1, keepdims=True))
            found = exp_scores / jnp.sum(exp_scores, axis=1, keepdims=True)
            probs[head, rows] = found
            mixed_win[rows, lanes] = dot(
                found.astype(BF), values_all[t * WIN : t * WIN + TILE, lanes]
            ).astype(BF)

    def produce_two(j):
        if j == 0:
            for copy in halo:
                copy.wait_recv()
            loads.win_out.wait()
        window_tile(2 * j)
        window_tile(2 * j + 1)
        rows = pl.ds(j * CHUNK, CHUNK)
        part[rows] = dot(mixed_win[rows], weights.win_out[...]).astype(BF)

    def finish_two(j):
        mine = pl.ds(j * PIECE, PIECE)
        rows = own[mine] + resid_one[mine]
        resid_two[mine] = rows
        normed_three[sum_two.own_rows(j)] = normed(rows, inputs.gain_three[...]).astype(BF)

    w_gate, w_up, w_down, og = weights.w_gate, weights.w_up, weights.w_down, weights.out_grad
    gate_act, up_act, hidden = work.gate_act, work.up_act, work.hidden
    gate_low, up_low = work.gate_low, work.up_low

    def ready_two(j):
        if j % 2 == 0:
            return
        if j == 1:
            for load in (loads.w_gate, loads.w_up, loads.w_down):
                load.wait()
        rows = pl.ds((j - 1) * CHUNK, 2 * CHUNK)
        gate = dot_nt(normed_three[rows], w_gate[...])
        gate_act[rows] = gate
        up = dot_nt(normed_three[rows], w_up[...])
        up_act[rows] = up
        hidden[rows] = (gate / (1.0 + jnp.exp(-gate)) * up).astype(BF)

    def produce_three(j):
        rows = pl.ds(j * CHUNK, CHUNK)
        part[rows] = dot(hidden[rows], w_down[...]).astype(BF)

    def finish_three(j):
        mine = pl.ds(j * PIECE, PIECE)
        saved.result[sum_three.own_rows(j)] = (own[mine] + resid_two[mine]).astype(BF)

    one = sum_one.slots(produce_one, finish_one, ready_one)
    two = sum_two.slots(produce_two, finish_two, ready_two)
    three = sum_three.slots(produce_three, finish_three)
    run(one)
    copies_halo.finish()
    save(
        (resid_one, hbm_saved.resid_one),
        (normed_two, hbm_saved.normed_two),
        (query_win, hbm_saved.query_win),
        (keys_all, hbm_saved.keys_all),
        (values_all, hbm_saved.values_all),
    )
    run(two)
    save(
        (probs, hbm_saved.probs), (mixed_win, hbm_saved.mixed_win), (resid_two, hbm_saved.resid_two)
    )
    loads.out_grad.wait()

    def hidden_back(half):
        rows = pl.ds(half * 256, 256)
        hidden_grad = dot_nt(og[rows], w_down[...])
        gate = gate_act[rows]
        sigmoid = 1.0 / (1.0 + jnp.exp(-gate))
        act = gate * sigmoid
        up_low[rows] = (hidden_grad * act).astype(BF)
        gate_low[rows] = (
            hidden_grad * up_act[rows] * (sigmoid + act * (1.0 - sigmoid))
        ).astype(BF)

    def input_back(half):
        cols = pl.ds(half * 1024, 1024)
        saved.part_four[:, cols] = (
            dot(gate_low[...], w_gate[:, cols]) + dot(up_low[...], w_up[:, cols])
        ).astype(BF)
        if half == 1:
            save((saved.part_four, hbm_saved.part_four))

    def weight_back(into, to_hbm, left, right, quarter):
        if quarter == 0:
            work.flipped[...] = left[...].T
        weight_block(into, work.flipped, right, quarter)
        if quarter == 3:
            save((into, to_hbm))

    blocks = [functools.partial(hidden_back, k) for k in range(2)]
    blocks += [functools.partial(input_back, k) for k in range(2)]
    for into, to_hbm, left, right in (
        (saved.gate_sum, hbm_saved.gate_sum, gate_low, normed_three),
        (saved.up_sum, hbm_saved.up_sum, up_low, normed_three),
        (saved.down_sum, hbm_saved.down_sum, hidden, og),
    ):
        blocks += [functools.partial(weight_back, into, to_hbm, left, right, k) for k in range(4)]
    for _ in three:
        for _ in range(3):
            if blocks:
                blocks.pop(0)()
    save((saved.result, hbm_saved.result))
    for block in blocks:
        block()
    for copy in saves:
        copy.wait()


HBM = pl.BlockSpec(memory_space=pl.ANY)
INSIDE = pl.BlockSpec(memory_space=pltpu.VMEM)


def forward(inputs, weights):
    scratch = vmem(Weights) + vmem(Saved) + vmem(ForwardWork) + vmem(StateScan) + mp_scratch()
    scratch += [dma(CHUNKS * PER_CHUNK)] * 2 + [dma(12)] * 2 + [dma(3)] * 2
    scratch += [dma(len(Weights._fields) + len(Saved._fields))]
    return Saved(
        *pl.pallas_call(
            forward_kernel,
            out_shape=[shape(dims, kind) for dims, kind in Saved()],
            in_specs=[INSIDE] * len(inputs) + [HBM] * len(weights),
            out_specs=[HBM] * len(Saved._fields),
            scratch_shapes=scratch,
            compiler_params=pltpu.CompilerParams(
                collective_id=0, has_side_effects=True, vmem_limit_bytes=VMEM_LIMIT
            ),
        )(*inputs, *weights)
    )


class SeqSum:
    def __init__(self, place, copies, blocks, out, bufs):
        self.place, self.copies, self.blocks, self.out = place, copies, blocks, out
        z, y = place.z, place.y
        quarter = self.quarter = blocks.shape[2] // 4
        ring_y, ring_z = (place.on_y(1), place.on_y(3)), (place.on_z(1), place.on_z(3))

        def pick_one(k, half):
            return blocks.at[:, (y + k) % 4, pl.ds(half * quarter, quarter)]

        def pick_two(k, half):
            return blocks.at[(z + k) % 4, :, pl.ds((2 + half) * quarter, quarter)]

        def pick_three(k, half):
            return blocks.at[(z + k) % 4, y, pl.ds(half * quarter, quarter)]

        def pick_four(k, half):
            return blocks.at[z, (y + k) % 4, pl.ds((2 + half) * quarter, quarter)]

        live = [types.SimpleNamespace() for _ in range(4)]
        self.early = ((ring_y, pick_one, bufs[0:3], live[0]), (ring_z, pick_two, bufs[3:6], live[1]))
        self.late = ((ring_z, pick_three, bufs[6:9], live[2]), (ring_y, pick_four, bufs[9:12], live[3]))

    def begin(self, rings):
        for (right, left), pick, (fwd, direct, comb), live in rings:
            live.fr = self.copies.start(pick(2, 0), fwd.at[0], right)
            live.fl = self.copies.start(pick(2, 1), fwd.at[1], left)
            live.dr = self.copies.start(pick(1, 1), direct.at[1], right)
            live.dl = self.copies.start(pick(3, 0), direct.at[0], left)

    def join(self, rings):
        for (right, left), pick, (fwd, direct, comb), live in rings:
            live.fr.wait_recv()
            block = pick(1, 0)
            block[...] = (block[...].astype(F32) + fwd[0].astype(F32)).astype(BF)
            live.cr = self.copies.start(block, comb.at[0], right)
            live.fl.wait_recv()
            block = pick(3, 1)
            block[...] = (block[...].astype(F32) + fwd[1].astype(F32)).astype(BF)
            live.cl = self.copies.start(block, comb.at[1], left)

    def total(self, ring, half):
        _, pick, (fwd, direct, comb), live = ring
        (live.dl if half == 0 else live.dr).wait_recv()
        (live.cr if half == 0 else live.cl).wait_recv()
        return (
            pick(0, half)[...].astype(F32) + direct[half].astype(F32) + comb[half].astype(F32)
        )

    def step(self, number):
        if number == 0:
            self.begin(self.early)
        elif number == 1:
            self.join(self.early)
        elif number == 2:
            for ring in self.early:
                for half in range(2):
                    block = ring[1](0, half)
                    block[...] = self.total(ring, half).astype(BF)
            self.begin(self.late)
        elif number == 3:
            self.join(self.late)
        else:
            size = self.quarter
            for half in range(2):
                self.out[pl.ds(half * size, size)] = self.total(self.late[0], half)
                self.out[pl.ds((2 + half) * size, size)] = self.total(self.late[1], half)


def seq_scratch(width):
    early, late = (2, 4, width // 4, TILE), (2, width // 4, TILE)
    return [pltpu.VMEM(early, BF)] * 6 + [pltpu.VMEM(late, BF)] * 6


class Groups(NamedTuple):
    gate: Any = FF
    up: Any = FF
    down: Any = FF
    win_out: Any = WIDE
    win: Any = 3 * WIDE
    out: Any = WIDE
    lin: Any = WIDE + 4 * FEAT


class BackInputs(NamedTuple):
    group_row: Any
    gain_one: Any
    gain_two: Any
    gain_three: Any
    first: Any
    second: Any
    vectors: Any


class BackHbm(NamedTuple):
    part_four: Any
    out_grad: Any
    tokens: Any
    normed_one: Any
    normed_two: Any
    gate_sum: Any
    up_sum: Any
    down_sum: Any
    w_query: Any
    w_key: Any
    w_value: Any
    w_out: Any
    win_q: Any
    win_k: Any
    win_v: Any
    win_out: Any


SPECS = Saved()


class BackSaved(NamedTuple):
    query: Any = SPECS.query
    key: Any = SPECS.key
    value: Any = SPECS.value
    carried: Any = SPECS.carried
    carried_norm: Any = SPECS.carried_norm
    quotient: Any = SPECS.quotient
    denominator: Any = SPECS.denominator
    mixed_lin: Any = SPECS.mixed_lin
    resid_one: Any = SPECS.resid_one
    query_win: Any = SPECS.query_win
    keys_all: Any = SPECS.keys_all
    values_all: Any = SPECS.values_all
    probs: Any = SPECS.probs
    mixed_win: Any = SPECS.mixed_win
    resid_two: Any = SPECS.resid_two


class BackOuts(NamedTuple):
    tokens_low: Any = ((ROWS, D), BF)
    gain_one: Any = ((1, TILE), F32)
    gain_two: Any = ((1, TILE), F32)
    gain_three: Any = ((1, TILE), F32)
    gate: Any = ((FF, TILE), F32)
    up: Any = ((FF, TILE), F32)
    down: Any = ((FF, TILE), F32)
    win_out: Any = ((WIDE, TILE), F32)
    out: Any = ((WIDE, TILE), F32)
    win_q: Any = ((TILE, WIDE), F32)
    win_k: Any = ((TILE, WIDE), F32)
    win_v: Any = ((TILE, WIDE), F32)
    value: Any = ((TILE, WIDE), F32)
    query: Any = ((2 * FEAT, TILE), F32)
    key: Any = ((2 * FEAT, TILE), F32)


class BackWork(NamedTuple):
    part: Any = ((ROWS, D), BF)
    other_full: Any = ((ROWS, D), BF)
    own: Any = ((OWN, D), F32)
    grad_own: Any = ((OWN, D), F32)
    token_own: Any = ((OWN, D), BF)
    group_col: Any = ((ROWS, TILE), F32)
    normed_low: Any = ((ROWS, D), BF)
    w_query: Any = ((2 * FEAT, D), BF)
    w_key: Any = ((2 * FEAT, D), BF)
    w_out: Any = ((WIDE, D), BF)
    win_out: Any = ((WIDE, D), BF)
    w_win: Any = ((D, 3 * WIDE), BF)
    mixed_grad: Any = ((ROWS, WIDE), BF)
    keys_sum: Any = ((ROWS + WIN, WIDE), F32)
    values_sum: Any = ((ROWS + WIN, WIDE), F32)
    back_key: Any = ((2, WIN, WIDE), BF)
    back_value: Any = ((2, WIN, WIDE), BF)
    win_grads: Any = ((ROWS, 3 * WIDE), BF)
    flipped: Any = ((3 * WIDE, ROWS), BF)
    numer_low: Any = ((ROWS, WIDE), BF)
    query_sum: Any = ((ROWS, 2 * FEAT), F32)
    key_sum: Any = ((ROWS, 2 * FEAT), F32)
    value_sum: Any = ((ROWS, WIDE), F32)
    query_low: Any = ((ROWS, 2 * FEAT), BF)
    key_low: Any = ((ROWS, 2 * FEAT), BF)
    value_low: Any = ((ROWS, WIDE), BF)
    state_sum: Any = ((2, WIDE, HD), F32)
    norm_sum: Any = ((2, 1, WIDE), F32)
    gain_sums: Any = ((16, D), F32)
    gain_low: Any = ((16, D), BF)
    gain_z: Any = ((3, 16, 512), BF)
    gain_zz: Any = ((16, 512), BF)
    gain_y: Any = ((3, 16, TILE), BF)
    gain_x: Any = ((16, TILE), BF)
    gain_xx: Any = ((3, 16, TILE), BF)
    gain_p: Any = ((16, TILE), BF)
    gain_pp: Any = ((16, TILE), BF)
    sum_win: Any = ((3 * WIDE, TILE), F32)
    sum_lin: Any = ((WIDE + 4 * FEAT, TILE), F32)
    later: Any = ((2, WIDE, HD), F32)
    later_norm: Any = ((2, 1, WIDE), F32)


def backward_kernel(*refs):
    take, some = taker(refs)
    inputs, hbm, hbm_saved, outs = take(BackInputs), take(BackHbm), take(BackSaved), take(BackOuts)
    saved, blocks, work, scan_bufs = take(BackSaved), take(Groups), take(BackWork), take(StateScan)
    seq_bufs = [some(12) for _ in Groups._fields]
    bufs = some(7)
    mp_sems, (seq_send, seq_recv), (few_send, few_recv), (local_sems,) = (
        some(2),
        some(2),
        some(2),
        some(1),
    )
    place = Place()
    z, y = place.z, place.y
    local = Locals(local_sems)
    part, own, other_full, tokens_low = work.part, work.own, work.other_full, outs.tokens_low
    sum_four = MpSum(place, mp_sems, part, tokens_low, own, bufs)
    sum_five = MpSum(place, mp_sems, part, other_full, own, bufs, 1)
    sum_six = MpSum(place, mp_sems, part, tokens_low, own, bufs)

    load_part = local.start(hbm.part_four, part)
    load_grad = [
        local.start(hbm.out_grad.at[sum_four.own_rows(j)], work.token_own.at[pl.ds(j * PIECE, PIECE)])
        for j in range(CHUNKS)
    ]
    greet(
        [place.peer()]
        + [place.on_x(k) for k in (1, 2, 3)]
        + [place.on_y(k) for k in (1, 2, 3)]
        + [place.on_z(k) for k in (1, 2, 3)]
        + [place.along(1), place.along(15)]
    )
    seq_copies = Copies(seq_send, seq_recv)
    few = Copies(few_send, few_recv)
    finished = Groups(outs.gate, outs.up, outs.down, outs.win_out, work.sum_win, outs.out, work.sum_lin)
    seq_sums = Groups(
        *[
            SeqSum(place, seq_copies, block, out, bufs_here)
            for block, out, bufs_here in zip(blocks, finished, seq_bufs)
        ]
    )
    queue = []

    def pump(count=1):
        for _ in range(count):
            if queue:
                group, number = queue.pop(0)
                group.step(number)

    first, second, vectors = inputs.first, inputs.second, inputs.vectors
    scale = vectors[2:3]
    group_row, group_col = inputs.group_row, work.group_col
    column(group_row, group_col)
    last_group = group_row[0:1, ROWS - 1 : ROWS].astype(F32)
    first_group = group_row[0:1, 0:1].astype(F32)
    in_last = (group_col[:, 0:1] == last_group).astype(F32)
    after_first = jnp.where(place.seq > 0, 1.0, 0.0)
    work.gain_sums[...] = jnp.zeros_like(work.gain_sums)

    def back_through_norm(mp_sum, number, resid, gain, grad, to, j):
        mine = pl.ds(j * PIECE, PIECE)
        rows, normed_grad = resid[mine].astype(F32), own[mine]
        factor = lax.rsqrt(jnp.mean(rows * rows, axis=-1, keepdims=True) + EPSILON)
        unit = rows * factor
        scaled = normed_grad * gain[...]
        total = grad[mine].astype(F32) + factor * (
            scaled - unit * jnp.mean(scaled * unit, axis=-1, keepdims=True)
        )
        work.gain_sums[number : number + 1] += jnp.sum(normed_grad * unit, axis=0, keepdims=True)
        if number > 0:
            work.grad_own[mine] = total
        to[mp_sum.own_rows(j)] = total.astype(BF)

    mixed_grad, keys_sum, values_sum, win_grads = (
        work.mixed_grad,
        work.keys_sum,
        work.values_sum,
        work.win_grads,
    )
    probs, query_win, keys_all, values_all = (
        saved.probs,
        saved.query_win,
        saved.keys_all,
        saved.values_all,
    )
    score_scale = HD ** (-0.5)
    back = []

    def finish_four(j):
        if j == 0:
            load_saved.resid_two.wait()
            for load in load_grad:
                load.wait()
        back_through_norm(sum_four, 2, saved.resid_two, inputs.gain_three, work.token_own, tokens_low, j)

    def window_back(t):
        rows, window = pl.ds(t * WIN, WIN), pl.ds(t * WIN, TILE)
        for head in range(2):
            lanes = slice(head * HD, (head + 1) * HD)
            grad_tile, held = mixed_grad[rows, lanes], probs[head, rows]
            probs_grad = dot_nt(grad_tile, values_all[window, lanes])
            score_low = (
                held * (probs_grad - jnp.sum(probs_grad * held, axis=1, keepdims=True))
            ).astype(BF)
            win_grads[rows, lanes] = (dot(score_low, keys_all[window, lanes]) * score_scale).astype(BF)
            for ref, found in (
                (keys_sum, dot_tn(score_low, query_win[rows, lanes]) * score_scale),
                (values_sum, dot_tn(held.astype(BF), grad_tile)),
            ):
                if t == 0:
                    ref[window, lanes] = found
                else:
                    ref[rows, lanes] += found[:WIN]
                    ref[pl.ds(t * WIN + WIN, WIN), lanes] = found[WIN:]
        if t == 0:
            for ref, to_send in ((keys_sum, work.back_key), (values_sum, work.back_value)):
                to_send[0] = ref[0:WIN].astype(BF)
                back.append(few.start(to_send.at[0], to_send.at[1], place.along(15)))

    def ready_four(j):
        if j == 0:
            load_win_out.wait()
            for load in (load_saved.probs, load_saved.query_win, load_saved.keys_all, load_saved.values_all):
                load.wait()
        rows = pl.ds(j * CHUNK, CHUNK)
        mixed_grad[rows] = dot_nt(tokens_low[rows], work.win_out[...]).astype(BF)
        window_back(2 * j)
        window_back(2 * j + 1)
        if j > 0:
            next(five)

    def produce_five(j):
        if j == 0:
            for load in load_win:
                load.wait()
        rows = pl.ds(j * CHUNK, CHUNK)
        for k, (ref, got) in enumerate(((keys_sum, work.back_key), (values_sum, work.back_value))):
            lanes = slice((k + 1) * WIDE, (k + 2) * WIDE)
            if j < CHUNKS - 1:
                win_grads[rows, lanes] = ref[WIN + j * CHUNK : WIN + (j + 1) * CHUNK].astype(BF)
            else:
                win_grads[j * CHUNK : ROWS - WIN, lanes] = ref[WIN + j * CHUNK : ROWS].astype(BF)
                back[k].wait_recv()
                win_grads[ROWS - WIN : ROWS, lanes] = (
                    ref[ROWS : ROWS + WIN] + got[1].astype(F32)
                ).astype(BF)
        part[rows] = dot_nt(win_grads[rows], work.w_win[...]).astype(BF)

    def finish_five(j):
        if j == 0:
            load_saved.resid_one.wait()
        back_through_norm(sum_five, 1, saved.resid_one, inputs.gain_two, work.grad_own, other_full, j)

    query, key, value, carried = saved.query, saved.key, saved.value, saved.carried
    numer_low, query_sum, key_sum, value_sum = (
        work.numer_low,
        work.query_sum,
        work.key_sum,
        work.value_sum,
    )

    def through_features(head, parts, grad):
        left, right = parts
        scaled = grad * scale
        return dot_nt((scaled * right).astype(BF), first[head]) + dot_nt(
            (scaled * left).astype(BF), second[head]
        )

    def ready_five(j):
        rows, count = pl.ds(j * CHUNK, CHUNK), (j + 1) * CHUNK
        if j == 0:
            for load in load_lin:
                load.wait()
            for load in (
                load_saved.denominator,
                load_saved.quotient,
                load_saved.query,
                load_saved.key,
                load_saved.value,
                load_saved.carried,
                load_saved.carried_norm,
            ):
                load.wait()
        mixed = dot_nt(other_full[rows], work.w_out[...]).astype(BF).astype(F32)
        incoming = (group_col[rows, 0:1] == first_group).astype(F32) * after_first
        kept = kept_pairs(group_col, group_row, j)
        key_new = []
        for head in range(2):
            lanes = slice(head * HD, (head + 1) * HD)
            denom = saved.denominator[head, rows]
            numer = (mixed[:, lanes] / denom).astype(BF)
            numer_low[rows, lanes] = numer
            denom_grad = (
                -jnp.sum(mixed[:, lanes] * saved.quotient[rows, lanes], axis=1, keepdims=True) / denom
            )
            parts = factors(head, (query[0, rows], query[1, rows]), first, second, vectors)
            used = (parts[0] * parts[1] * scale).astype(BF).astype(F32) * incoming
            state = dot_tn(used.astype(BF), numer)
            norm = jnp.sum(used * denom_grad, axis=0, keepdims=True)
            if j == 0:
                work.state_sum[head], work.norm_sum[head] = state, norm
            else:
                work.state_sum[head] += state
                work.norm_sum[head] += norm
            grad = incoming * (
                dot_nt(numer, carried[head].astype(BF)) + denom_grad * saved.carried_norm[head]
            )
            query_new = through_features(head, parts, grad)
            inner = products(head, (query.at[0], query.at[1]), (key.at[0], key.at[1]), rows, count)
            kernel = jnp.where(kept, 1.0 + inner * 0.25 + inner * inner * 0.03125, 0.0).astype(BF)
            grad = dot_nt(numer, value[0:count, lanes]) + denom_grad
            grad = jnp.where(kept, grad, 0.0).astype(BF).astype(F32)
            inner_grad = (grad * (0.25 + inner * 0.0625)).astype(BF)
            query_new = query_new + of_head(dot(inner_grad, key[0, 0:count]), head)
            if head == 0:
                query_sum[rows] = query_new
            else:
                query_sum[rows] += query_new
            key_new.append(of_head(dot_tn(inner_grad, query[0, rows]), head))
            found = dot_tn(kernel, numer)
            if j > 0:
                value_sum[0 : count - CHUNK, lanes] += found[0 : count - CHUNK]
            value_sum[count - CHUNK : count, lanes] = found[count - CHUNK : count]
        found = key_new[0] + key_new[1]
        if j > 0:
            key_sum[0 : count - CHUNK] += found[0 : count - CHUNK]
        key_sum[count - CHUNK : count] = found[count - CHUNK : count]
        if j == CHUNKS - 1:
            for head in range(2):
                scan_bufs.mine[head, 0:FEATURES] = work.state_sum[head, 0:FEATURES].astype(BF)
                scan_bufs.mine[head, FEATURES:STATE] = norm_rows_of(work.norm_sum[head]).astype(BF)

    def weight_task(block, right, quarter):
        weight_block(block, work.flipped, right, quarter)

    def begin(group):
        group.step(0)

    def turn_mixed(ref, load):
        load.wait()
        work.flipped[0:WIDE] = ref[...].T

    def turn_win():
        load_normed.wait()
        for k in range(3):
            rows = slice(k * WIDE, (k + 1) * WIDE)
            work.flipped[rows] = win_grads[:, rows].T

    late_work = [lambda: turn_mixed(saved.mixed_win, load_saved.mixed_win)]
    late_work += [functools.partial(weight_task, blocks.win_out, tokens_low, k) for k in range(4)]
    late_work += [functools.partial(begin, seq_sums.win_out), turn_win]
    late_work += [functools.partial(weight_task, blocks.win, work.normed_low, k) for k in range(4)]
    late_work += [functools.partial(begin, seq_sums.win)]

    four = sum_four.slots(lambda j: None, finish_four, ready_four)
    five = sum_five.slots(produce_five, finish_five, ready_five)
    meet(12)
    load_part.wait()
    next(four)
    mlp_loads = [
        local.start(src, dst)
        for src, dst in ((hbm.gate_sum, blocks.gate), (hbm.up_sum, blocks.up), (hbm.down_sum, blocks.down))
    ]
    load_saved = BackSaved(*[local.start(src, dst) for src, dst in zip(hbm_saved, saved)])
    load_win_out = local.start(hbm.win_out, work.win_out)
    load_win = [
        local.start(src, work.w_win.at[:, pl.ds(k * WIDE, WIDE)])
        for k, src in enumerate((hbm.win_q, hbm.win_k, hbm.win_v))
    ]
    load_normed = local.start(hbm.normed_two, work.normed_low)
    load_lin = [
        local.start(src, dst)
        for src, dst in ((hbm.w_query, work.w_query), (hbm.w_key, work.w_key), (hbm.w_out, work.w_out))
    ]

    for slot in four:
        if 1 <= slot < 4:
            mlp_loads[slot - 1].wait()
            seq_sums[slot - 1].step(0)
        if slot == 5:
            seq_sums.gate.step(1)
    queue += [(seq_sums.up, 1), (seq_sums.down, 1), (seq_sums.gate, 2), (seq_sums.up, 2)]
    queue += [(seq_sums.down, 2)]
    for slot in five:
        for _ in range(2):
            if late_work:
                late_work.pop(0)()
        pump()
    for block in late_work:
        block()
    pump(len(queue))
    scan = state_scan(place, few, scan_bufs, work.later, work.later_norm, True)
    next(scan)
    load_normed_one = local.start(hbm.normed_one, work.normed_low)
    load_value = local.start(hbm.w_value, work.w_win.at[:, pl.ds(0, WIDE)])
    load_token = [
        local.start(hbm.tokens.at[sum_six.own_rows(j)], work.token_own.at[pl.ds(j * PIECE, PIECE)])
        for j in range(CHUNKS)
    ]
    turn_mixed(saved.mixed_lin, load_saved.mixed_lin)
    weight_task(blocks.out, other_full, 0)
    weight_task(blocks.out, other_full, 1)
    next(scan)
    weight_task(blocks.out, other_full, 2)
    weight_task(blocks.out, other_full, 3)
    queue += [(seq_sums.out, 0), (seq_sums.gate, 3), (seq_sums.win_out, 1)]
    pump(2)
    for _ in scan:
        pass
    for head in range(2):
        lanes = slice(head * HD, (head + 1) * HD)
        state = work.later[head].astype(BF)
        parts = factors(head, (key[0], key[1]), first, second, vectors)
        feat = (parts[0] * parts[1] * scale).astype(BF)
        grad = in_last * (dot_nt(value[:, lanes], state) + work.later_norm[head])
        key_sum[...] += through_features(head, parts, grad)
        value_sum[:, lanes] += in_last * dot(feat, state)
    work.query_low[...] = query_sum[...].astype(BF)
    work.key_low[...] = key_sum[...].astype(BF)
    work.value_low[...] = value_sum[...].astype(BF)
    load_value.wait()

    def produce_six(j):
        rows = pl.ds(j * CHUNK, CHUNK)
        part[rows] = (
            dot_nt(work.value_low[rows], work.w_win[:, 0:WIDE])
            + dot(work.query_low[rows], work.w_query[...])
            + dot(work.key_low[rows], work.w_key[...])
        ).astype(BF)

    for load in load_token:
        load.wait()

    def finish_six(j):
        back_through_norm(sum_six, 0, work.token_own, inputs.gain_one, work.grad_own, tokens_low, j)

    def gains():
        work.gain_low[...] = work.gain_sums[...].astype(BF)

        def block(ref, at, size):
            return ref.at[:, pl.ds(pl.multiple_of(at * size, TILE), size)]

        over = [
            few.start(block(work.gain_low, (z + k) % 4, 512), work.gain_z.at[k - 1], place.on_z(k))
            for k in (1, 2, 3)
        ]
        yield
        total = block(work.gain_low, z, 512)[...].astype(F32)
        for k, copy in enumerate(over):
            copy.wait_recv()
            total = total + work.gain_z[k].astype(F32)
        work.gain_zz[...] = total.astype(BF)
        over = [
            few.start(block(work.gain_zz, (y + k) % 4, TILE), work.gain_y.at[k - 1], place.on_y(k))
            for k in (1, 2, 3)
        ]
        yield
        total = block(work.gain_zz, y, TILE)[...].astype(F32)
        for k, copy in enumerate(over):
            copy.wait_recv()
            total = total + work.gain_y[k].astype(F32)
        work.gain_x[...] = total.astype(BF)
        over = [few.start(work.gain_x, work.gain_xx.at[k - 1], place.on_x(k)) for k in (1, 2, 3)]
        yield
        total = work.gain_x[...].astype(F32)
        for k, copy in enumerate(over):
            copy.wait_recv()
            total = total + work.gain_xx[k].astype(F32)
        work.gain_p[...] = total.astype(BF)
        copy = few.start(work.gain_p, work.gain_pp, place.peer())
        yield
        copy.wait_recv()
        total = work.gain_p[...].astype(F32) + work.gain_pp[...].astype(F32)
        for k, ref in enumerate((outs.gain_one, outs.gain_two, outs.gain_three)):
            ref[...] = total[k : k + 1]

    def turn_lin():
        load_normed_one.wait()
        work.flipped[0:WIDE] = work.value_low[...].T
        for k, ref in enumerate((query_sum, key_sum)):
            at = WIDE + 2 * FEAT * k
            wide = jnp.concatenate([ref[...], jnp.zeros((ROWS, TILE - 2 * FEAT), F32)], axis=1)
            work.flipped[at : at + 2 * FEAT] = wide.T[0 : 2 * FEAT].astype(BF)

    six = sum_six.slots(produce_six, finish_six)
    next(six)
    turn_lin()
    for k in range(4):
        weight_task(blocks.lin, work.normed_low, k)
    queue += [(seq_sums.lin, 0), (seq_sums.up, 3), (seq_sums.win, 1), (seq_sums.down, 3)]
    queue += [(seq_sums.out, 1), (seq_sums.gate, 4), (seq_sums.win_out, 2), (seq_sums.lin, 1)]
    queue += [(seq_sums.win, 2), (seq_sums.up, 4), (seq_sums.down, 4), (seq_sums.out, 2)]
    gain_steps = gains()
    for slot in six:
        pump(2)
        if slot >= 3:
            next(gain_steps, None)
    pump(len(queue))
    queue += [(seq_sums.win_out, 3), (seq_sums.win, 3), (seq_sums.lin, 2), (seq_sums.out, 3)]
    queue += [(seq_sums.win_out, 4), (seq_sums.win, 4), (seq_sums.lin, 3), (seq_sums.out, 4)]
    queue += [(seq_sums.lin, 4)]
    pump(len(queue))
    for k, ref in enumerate((outs.win_q, outs.win_k, outs.win_v)):
        ref[...] = work.sum_win[k * WIDE : (k + 1) * WIDE].T
    outs.value[...] = work.sum_lin[0:WIDE].T
    outs.query[...] = work.sum_lin[WIDE : WIDE + 2 * FEAT]
    outs.key[...] = work.sum_lin[WIDE + 2 * FEAT : WIDE + 4 * FEAT]
    for _ in gain_steps:
        pass
    seq_copies.finish()
    few.finish()


def backward(saved, inputs, weights):
    back_inputs = BackInputs(*inputs[1:])
    hbm = BackHbm(
        part_four=saved.part_four,
        out_grad=weights.out_grad,
        tokens=inputs.tokens,
        normed_one=saved.normed_one,
        normed_two=saved.normed_two,
        gate_sum=saved.gate_sum,
        up_sum=saved.up_sum,
        down_sum=saved.down_sum,
        w_query=weights.w_query,
        w_key=weights.w_key,
        w_value=weights.w_value,
        w_out=weights.w_out,
        win_q=weights.win_q,
        win_k=weights.win_k,
        win_v=weights.win_v,
        win_out=weights.win_out,
    )
    held = BackSaved(*[getattr(saved, name) for name in BackSaved._fields])
    scratch = vmem(BackSaved) + [pltpu.VMEM((4, 4, width, TILE), BF) for width in Groups()]
    scratch += vmem(BackWork) + vmem(StateScan)
    for width in Groups():
        scratch += seq_scratch(width)
    scratch += mp_scratch()
    scratch += [dma(CHUNKS * PER_CHUNK)] * 2 + [dma(24 * len(Groups._fields))] * 2 + [dma(24)] * 2
    scratch += [dma(64)]
    return BackOuts(
        *pl.pallas_call(
            backward_kernel,
            out_shape=[shape(dims, kind) for dims, kind in BackOuts()],
            in_specs=[INSIDE] * len(back_inputs) + [HBM] * (len(hbm) + len(held)),
            out_specs=[INSIDE] * len(BackOuts._fields),
            scratch_shapes=scratch,
            compiler_params=pltpu.CompilerParams(
                collective_id=1, has_side_effects=True, vmem_limit_bytes=VMEM_LIMIT
            ),
        )(*back_inputs, *hbm, *held)
    )


def hand_over_kernel(*refs):
    count = (len(refs) - 2) // 3
    ins, outs, held = refs[:count], refs[count : 2 * count], refs[2 * count : 3 * count]
    wide, sems = refs[3 * count :]
    block = ROWS // 4
    local = Locals(sems)
    parts = [pl.ds(k * block, block) for k in range(4)]
    loads = [local.start(ins[0].at[rows], held[0].at[rows]) for rows in parts]
    others = [local.start(src, dst) for src, dst in zip(ins[1:], held[1:])]
    copies = []
    for load, rows in zip(loads, parts):
        load.wait()
        wide[rows] = held[0][rows].astype(F32)
        copies.append(local.start(wide.at[rows], outs[0].at[rows]))
    for load, src, dst in zip(others, held[1:], outs[1:]):
        load.wait()
        copies.append(local.start(src, dst))
    for copy in copies:
        copy.wait()


def hand_over(arrays):
    kinds = [F32] + [array.dtype for array in arrays[1:]]
    return pl.pallas_call(
        hand_over_kernel,
        out_shape=[shape(array.shape, kind) for array, kind in zip(arrays, kinds)],
        in_specs=[HBM] * len(arrays),
        out_specs=[HBM] * len(arrays),
        scratch_shapes=[pltpu.VMEM(array.shape, array.dtype) for array in arrays]
        + [pltpu.VMEM((ROWS, D), F32), dma(2 * len(arrays) + 6)],
        compiler_params=pltpu.CompilerParams(vmem_limit_bytes=VMEM_LIMIT),
    )(*arrays)


def local(
    tokens,
    group_ids,
    gain_one,
    lin_query,
    lin_key,
    lin_value,
    lin_output,
    gain_two,
    win_query,
    win_key,
    win_value,
    win_output,
    gain_three,
    mlp_gate,
    mlp_up,
    mlp_down,
    out_grad,
):
    first, second, vectors = feature_tables()
    inputs = Inputs(
        tokens=tokens,
        group_row=group_ids.reshape(1, ROWS),
        gain_one=gain_one.reshape(1, D),
        gain_two=gain_two.reshape(1, D),
        gain_three=gain_three.reshape(1, D),
        first=first,
        second=second,
        vectors=vectors,
    )
    weights = Weights(
        out_grad=out_grad,
        w_query=lin_query.T,
        w_key=lin_key.T,
        w_value=lin_value,
        w_out=lin_output,
        win_k=win_key,
        win_v=win_value,
        win_q=win_query,
        win_out=win_output,
        w_gate=mlp_gate.T,
        w_up=mlp_up.T,
        w_down=mlp_down,
    )
    saved = forward(inputs, weights)
    outs = BackOuts(*backward(saved, inputs, weights))
    done = hand_over([*outs, saved.result])
    outs, result = BackOuts(*done[:-1]), done[-1]
    return (
        result,
        outs.tokens_low,
        outs.gain_one.reshape(TILE),
        outs.query.T,
        outs.key.T,
        outs.value,
        outs.out,
        outs.gain_two.reshape(TILE),
        outs.win_q,
        outs.win_k,
        outs.win_v,
        outs.win_out,
        outs.gain_three.reshape(TILE),
        outs.gate.T,
        outs.up.T,
        outs.down,
    )


def solution(mesh):
    return jax.shard_map(
        local,
        mesh=mesh,
        in_specs=(
            P("seq", None),
            P("seq"),
            P(),
            P(None, "mp"),
            P(None, "mp"),
            P(None, "mp"),
            P("mp", None),
            P(),
            P(None, "mp"),
            P(None, "mp"),
            P(None, "mp"),
            P("mp", None),
            P(),
            P(None, "mp"),
            P(None, "mp"),
            P("mp", None),
            P("seq", None),
        ),
        out_specs=(
            P("seq", None),
            P("seq", None),
            P("seq"),
            P("seq", "mp"),
            P("seq", "mp"),
            P("seq", "mp"),
            P("mp", "seq"),
            P("seq"),
            P("seq", "mp"),
            P("seq", "mp"),
            P("seq", "mp"),
            P("mp", "seq"),
            P("seq"),
            P("seq", "mp"),
            P("seq", "mp"),
            P("mp", "seq"),
        ),
        check_vma=False,
    )
```

```python
import functools
import types
from typing import Any, NamedTuple

import jax
import jax.numpy as jnp
import numpy as np
from jax import lax
from jax.experimental import pallas as pl
from jax.experimental.pallas import tpu as pltpu
from jax.sharding import PartitionSpec as P

D = 2048
HD = 128
FEAT = 16
WIN = 64
FF = 704
FF_PAD = 768
ROWS = 512
TILE = 128
WIDE = 256
FEATURES = 160
STATE = FEATURES + 16

CHUNKS = 4
CHUNK = ROWS // CHUNKS
HALF = CHUNK // 2
PIECE = CHUNK // 8
OWN = 64
COLS = D // 2
PER_CHUNK = 21

EPSILON = 1e-05
MESH = pl.DeviceIdType.MESH
BF = jnp.bfloat16
F32 = jnp.float32
VMEM_LIMIT = 63 * 1024 * 1024 + 512 * 1024


class Place:
    def __init__(self):
        self.seq = lax.axis_index("seq")
        self.mp = lax.axis_index("mp")
        self.z, self.y = self.seq // 4, self.seq % 4
        self.x, self.core = self.mp // 2, self.mp % 2

    def peer(self):
        return (self.seq, self.x * 2 + (1 - self.core))

    def on_x(self, step):
        return (self.seq, ((self.x + step) % 4) * 2 + self.core)

    def on_y(self, step):
        return (self.z * 4 + (self.y + step) % 4, self.mp)

    def on_z(self, step):
        return (((self.z + step) % 4) * 4 + self.y, self.mp)

    def along(self, step):
        return ((self.seq + step) % 16, self.mp)


class Copies:
    def __init__(self, send_sems, recv_sems):
        self.send_sems, self.recv_sems = send_sems, recv_sems
        self.count, self.started = 0, []

    def start(self, src, dst, device):
        k = self.count
        self.count += 1
        copy = pltpu.make_async_remote_copy(
            src_ref=src,
            dst_ref=dst,
            send_sem=self.send_sems.at[k],
            recv_sem=self.recv_sems.at[k],
            device_id=device,
            device_id_type=MESH,
        )
        copy.start()
        self.started.append(copy)
        return copy

    def finish(self):
        for copy in self.started:
            copy.wait_send()


class Locals:
    def __init__(self, sems):
        self.sems, self.count = sems, 0

    def start(self, src, dst):
        copy = pltpu.make_async_copy(src, dst, self.sems.at[self.count])
        self.count += 1
        copy.start()
        return copy


def greet(devices):
    barrier = pltpu.get_barrier_semaphore()
    for device in devices:
        pl.semaphore_signal(barrier, inc=1, device_id=device, device_id_type=MESH)


def meet(count):
    pl.semaphore_wait(pltpu.get_barrier_semaphore(), count)


def rows_at(start, size):
    return pl.ds(pl.multiple_of(start, 16), size)


def dot(left, right):
    return lax.dot_general(left, right, (((1,), (0,)), ((), ())), preferred_element_type=F32)


def dot_nt(left, right):
    return lax.dot_general(left, right, (((1,), (1,)), ((), ())), preferred_element_type=F32)


def dot_tn(left, right):
    return lax.dot_general(left, right, (((0,), (0,)), ((), ())), preferred_element_type=F32)


def halves(values):
    high = values.astype(BF)
    return high, (values - high.astype(F32)).astype(BF)


class MpSum:
    def __init__(self, place, sems, part, full, own, bufs, lag=0, order=tuple(range(CHUNKS)), hold=False):
        self.place, self.part, self.full, self.own = place, part, full, own
        self.lag, self.order, self.hold = lag, order, hold
        self.send_sems, self.recv_sems = sems
        (self.from_peer, self.send_opp, self.send_right, self.send_left) = bufs[:4]
        (self.fwd, self.direct, self.comb) = bufs[4:]
        x = place.x
        self.turn = [(x + 2) % 4, (x + 1) % 4, (x + 3) % 4, x]
        self.peer, self.right, self.left = place.peer(), place.on_x(1), place.on_x(3)
        self.live = [types.SimpleNamespace(sent=[]) for _ in range(CHUNKS)]

    def start(self, j, src, dst, device):
        k = j * PER_CHUNK + len(self.live[j].sent)
        copy = pltpu.make_async_remote_copy(
            src_ref=src,
            dst_ref=dst,
            send_sem=self.send_sems.at[k],
            recv_sem=self.recv_sems.at[k],
            device_id=device,
            device_id_type=MESH,
        )
        copy.start()
        self.live[j].sent.append(copy)
        return copy

    def rows(self, j, core, x):
        return rows_at(j * CHUNK + core * HALF + x * PIECE, PIECE)

    def own_rows(self, j):
        return self.rows(j, self.place.core, self.place.x)

    def chip_sum(self, j, slot, low, size):
        cols = pl.ds(low, size)
        return self.part[self.rows(j, self.place.core, self.turn[slot]), cols].astype(
            F32
        ) + self.from_peer[j, slot, :, cols].astype(F32)

    def exchange(self, j):
        self.live[j].ex = [
            self.start(
                j,
                self.part.at[self.rows(j, 1 - self.place.core, at)],
                self.from_peer.at[j, slot],
                self.peer,
            )
            for slot, at in enumerate(self.turn)
        ]

    def first(self, j):
        live = self.live[j]
        low, high = pl.ds(0, COLS), pl.ds(COLS, COLS)
        live.ex[0].wait_recv()
        self.send_opp[j] = self.chip_sum(j, 0, 0, D).astype(BF)
        live.fr = self.start(j, self.send_opp.at[j, :, low], self.fwd.at[j, 0], self.right)
        live.fl = self.start(j, self.send_opp.at[j, :, high], self.fwd.at[j, 1], self.left)
        live.ex[1].wait_recv()
        self.send_right[j, 0] = self.chip_sum(j, 1, COLS, COLS).astype(BF)
        live.dr = self.start(j, self.send_right.at[j, 0], self.direct.at[j, 1], self.right)
        live.ex[2].wait_recv()
        self.send_left[j, 0] = self.chip_sum(j, 2, 0, COLS).astype(BF)
        live.dl = self.start(j, self.send_left.at[j, 0], self.direct.at[j, 0], self.left)

    def second(self, j):
        live = self.live[j]
        live.fr.wait_recv()
        self.send_right[j, 1] = (
            self.chip_sum(j, 1, 0, COLS) + self.fwd[j, 0].astype(F32)
        ).astype(BF)
        live.cr = self.start(j, self.send_right.at[j, 1], self.comb.at[j, 0], self.right)
        live.fl.wait_recv()
        self.send_left[j, 1] = (
            self.chip_sum(j, 2, COLS, COLS) + self.fwd[j, 1].astype(F32)
        ).astype(BF)
        live.cl = self.start(j, self.send_left.at[j, 1], self.comb.at[j, 1], self.left)

    def total(self, j):
        live, mine = self.live[j], pl.ds(j * PIECE, PIECE)
        live.ex[3].wait_recv()
        live.dl.wait_recv()
        live.cr.wait_recv()
        self.own[mine, 0:COLS] = (
            self.chip_sum(j, 3, 0, COLS)
            + self.direct[j, 0].astype(F32)
            + self.comb[j, 0].astype(F32)
        )
        live.dr.wait_recv()
        live.cl.wait_recv()
        self.own[mine, COLS:D] = (
            self.chip_sum(j, 3, COLS, COLS)
            + self.direct[j, 1].astype(F32)
            + self.comb[j, 1].astype(F32)
        )
        for copy in live.ex:
            copy.wait_send()

    def send(self, j, at, low, size, device):
        block = self.full.at[self.rows(j, self.place.core, at), pl.ds(low, size)]
        return self.start(j, block, block, device)

    def spread(self, j):
        live, x = self.live[j], self.place.x
        live.rl = self.send(j, x, 0, COLS, self.right)
        live.lh = self.send(j, x, COLS, COLS, self.left)
        live.rh = self.send(j, x, COLS, COLS, self.right)
        live.ll = self.send(j, x, 0, COLS, self.left)
        live.peers = [self.send(j, x, 0, D, self.peer)]

    def relay(self, j):
        live, x = self.live[j], self.place.x
        live.rl.wait_recv()
        live.gr = self.send(j, (x + 3) % 4, 0, COLS, self.right)
        live.lh.wait_recv()
        live.gl = self.send(j, (x + 1) % 4, COLS, COLS, self.left)
        live.rh.wait_recv()
        live.peers.append(self.send(j, (x + 3) % 4, 0, D, self.peer))
        live.ll.wait_recv()
        live.peers.append(self.send(j, (x + 1) % 4, 0, D, self.peer))

    def last(self, j):
        live, x = self.live[j], self.place.x
        live.gr.wait_recv()
        live.peers.append(self.send(j, (x + 2) % 4, 0, COLS, self.peer))
        live.gl.wait_recv()
        live.peers.append(self.send(j, (x + 2) % 4, COLS, COLS, self.peer))

    def arrived(self, j):
        for copy in self.live[j].peers:
            copy.wait_recv()
        for copy in self.live[j].sent[4:]:
            copy.wait_send()

    def slots(self, produce, finish, ready=None):
        for slot in range((CHUNKS - 1) * self.lag + (8 if self.hold else 7)):
            for position, j in enumerate(self.order):
                stage = slot - position * self.lag
                if self.hold and stage >= 4:
                    if stage == 4:
                        self.spread(j)
                        continue
                    stage -= 1
                if stage == 0:
                    produce(j)
                    self.exchange(j)
                elif stage == 1:
                    self.first(j)
                elif stage == 2:
                    self.second(j)
                elif stage == 3:
                    self.total(j)
                    finish(j)
                    if not self.hold:
                        self.spread(j)
                elif stage == 4:
                    self.relay(j)
                elif stage == 5:
                    self.last(j)
                elif stage == 6:
                    self.arrived(j)
                    if ready is not None:
                        ready(j)
            yield slot


def mp_scratch():
    ring = pltpu.VMEM((CHUNKS, 2, PIECE, COLS), BF)
    return [pltpu.VMEM((CHUNKS, 4, PIECE, D), BF), pltpu.VMEM((CHUNKS, PIECE, D), BF)] + [ring] * 5


def dma(count):
    return pltpu.SemaphoreType.DMA((count,))


def run(slots):
    for _ in slots:
        pass


def norm_rows_of(total):
    row = lax.broadcasted_iota(jnp.int32, (16, TILE), 0)
    return jnp.where(row == 0, total[:, 0:TILE], jnp.where(row == 1, total[:, TILE:WIDE], 0.0))


class StateScan(NamedTuple):
    mine: Any = ((2, STATE, HD), BF)
    early: Any = ((2, 3, STATE, HD), BF)
    sent: Any = ((2, 2, STATE, HD), BF)
    late: Any = ((2, 3, STATE, HD), BF)


def state_scan(place, copies, bufs, states, norms, reverse):
    def counted(position, step):
        at = (position - step + 4) % 4
        reached = at > position if reverse else at < position
        return jnp.where(reached, 1.0, 0.0)

    def wider(step):
        to = (place.y + step) % 4
        return (to < place.y if reverse else to > place.y).astype(jnp.int32)

    def put(head, total):
        states[head, 0:FEATURES] = total[0:FEATURES]
        states[head, FEATURES:WIDE] = jnp.zeros((WIDE - FEATURES, HD), F32)
        norms[head, 0:1, 0:TILE] = total[FEATURES : FEATURES + 1]
        norms[head, 0:1, TILE:WIDE] = total[FEATURES + 1 : FEATURES + 2]

    steps = (1, 2, 3)
    over = [copies.start(bufs.mine.at[0], bufs.early.at[0, k - 1], place.on_y(k)) for k in steps]
    across = [copies.start(bufs.mine.at[1], bufs.early.at[1, k - 1], place.on_z(k)) for k in steps]
    yield
    total, before = bufs.mine[0].astype(F32), jnp.zeros((STATE, HD), F32)
    for k, copy in zip(steps, over):
        copy.wait_recv()
        part = bufs.early[0, k - 1].astype(F32)
        total, before = total + part, before + counted(place.y, k) * part
    bufs.sent[0, 0] = total.astype(BF)
    over = [copies.start(bufs.sent.at[0, 0], bufs.late.at[0, k - 1], place.on_z(k)) for k in steps]
    put(0, before)
    before = jnp.zeros((STATE, HD), F32)
    for k, copy in zip(steps, across):
        copy.wait_recv()
        before = before + counted(place.z, k) * bufs.early[1, k - 1].astype(F32)
    bufs.sent[1, 0] = before.astype(BF)
    bufs.sent[1, 1] = (before + bufs.mine[1].astype(F32)).astype(BF)
    across = [
        copies.start(bufs.sent.at[1, wider(k)], bufs.late.at[1, k - 1], place.on_y(k)) for k in steps
    ]
    put(1, before)
    yield
    for head, sent in enumerate((over, across)):
        total = jnp.zeros((STATE, HD), F32)
        for k, copy in zip(steps, sent):
            copy.wait_recv()
            part = bufs.late[head, k - 1].astype(F32)
            total = total + (counted(place.z, k) * part if head == 0 else part)
        states[head, 0:FEATURES] += total[0:FEATURES]
        norms[head, 0:1, 0:TILE] += total[FEATURES : FEATURES + 1]
        norms[head, 0:1, TILE:WIDE] += total[FEATURES + 1 : FEATURES + 2]
    yield


def feature_tables():
    pairs = [(a, b) for a in range(FEAT) for b in range(a, FEAT)]
    first = np.zeros((2, 2 * FEAT, WIDE), np.float32)
    second = np.zeros((2, 2 * FEAT, WIDE), np.float32)
    vectors = np.zeros((8, WIDE), np.float32)
    vectors[0, 0] = vectors[1, 0] = vectors[2, 0] = 1.0
    for a in range(FEAT):
        vectors[1, 1 + a] = 1.0
        vectors[2, 1 + a] = FEAT ** (-0.25)
        for h in range(2):
            first[h, h * FEAT + a, 1 + a] = 1.0
    for number, (a, b) in enumerate(pairs):
        at = 1 + FEAT + number
        vectors[2, at] = (1.0 if a == b else 2.0**0.5) * (2.0 * FEAT) ** (-0.5)
        for h in range(2):
            first[h, h * FEAT + a, at] = 1.0
            second[h, h * FEAT + b, at] = 1.0
    return jnp.asarray(first, BF), jnp.asarray(second, BF), jnp.asarray(vectors, F32)


def factors(head, values, first, second, vectors):
    high, low = values
    left = dot(high, first[head]) + dot(low, first[head]) + vectors[0:1]
    right = dot(high, second[head]) + dot(low, second[head]) + vectors[1:2]
    return left, right


def of_head(values, head):
    lane = lax.broadcasted_iota(jnp.int32, values.shape, 1)
    return jnp.where((lane >= head * FEAT) & (lane < (head + 1) * FEAT), values, jnp.zeros_like(values))


def products(head, query, key, rows, count):
    high, low = (of_head(part[rows], head) for part in query)
    key_high, key_low = (part[0:count] for part in key)
    return dot_nt(high, key_high) + dot_nt(low, key_high) + dot_nt(high, key_low)


def shape(dims, kind):
    return jax.ShapeDtypeStruct(dims, kind)


def normed(rows, gain):
    factor = lax.rsqrt(jnp.mean(rows * rows, axis=-1, keepdims=True) + EPSILON)
    return rows * factor * gain


def column(group_row, held):
    for k in range(ROWS // TILE):
        block = group_row[0:1, k * TILE : (k + 1) * TILE].astype(F32)
        held[k * TILE : (k + 1) * TILE] = jnp.broadcast_to(block, (TILE, TILE)).T


def kept_pairs(group_col, group_row, tile):
    count = (tile + 1) * TILE
    row = lax.broadcasted_iota(jnp.int32, (TILE, count), 0) + tile * TILE
    col = lax.broadcasted_iota(jnp.int32, (TILE, count), 1)
    groups = group_col[tile * TILE : (tile + 1) * TILE, 0:1]
    return (col <= row) & (groups == group_row[0:1, 0:count].astype(F32))


def weight_block(into, left_t, right, quarter):
    count = into.shape[2]
    block = dot(left_t[0:count], right[:, quarter * 512 : (quarter + 1) * 512]).astype(BF)
    for k in range(4):
        into[quarter, k] = block[:, k * TILE : (k + 1) * TILE]


def back_through_norm(resid, grad, normed_grad, gain):
    factor = lax.rsqrt(jnp.mean(resid * resid, axis=-1, keepdims=True) + EPSILON)
    unit = resid * factor
    scaled = normed_grad * gain
    total = grad + factor * (scaled - unit * jnp.mean(scaled * unit, axis=-1, keepdims=True))
    return total, jnp.sum(normed_grad * unit, axis=0, keepdims=True)


class Inputs(NamedTuple):
    tokens: Any
    group_row: Any
    gain_one: Any
    gain_two: Any
    gain_three: Any
    first: Any
    second: Any
    vectors: Any


class Weights(NamedTuple):
    out_grad: Any = ((ROWS, D), BF)
    w_query: Any = ((2 * FEAT, D), BF)
    w_key: Any = ((2 * FEAT, D), BF)
    w_value: Any = ((D, WIDE), BF)
    w_out: Any = ((WIDE, D), BF)
    win_k: Any = ((D, WIDE), BF)
    win_v: Any = ((D, WIDE), BF)
    win_q: Any = ((D, WIDE), BF)
    win_out: Any = ((WIDE, D), BF)
    w_gate: Any = ((FF_PAD, D), BF)
    w_up: Any = ((FF_PAD, D), BF)
    w_down: Any = ((FF_PAD, D), BF)


class Saved(NamedTuple):
    normed_one: Any = ((ROWS, D), BF)
    query: Any = ((2, ROWS, 2 * FEAT), BF)
    key: Any = ((2, ROWS, 2 * FEAT), BF)
    value: Any = ((ROWS, WIDE), BF)
    carried: Any = ((2, WIDE, HD), F32)
    carried_norm: Any = ((2, 1, WIDE), F32)
    quotient: Any = ((ROWS, WIDE), F32)
    denominator: Any = ((2, ROWS, 1), F32)
    mixed_lin: Any = ((ROWS, WIDE), BF)
    resid_one: Any = ((OWN, D), F32)
    normed_two: Any = ((ROWS, D), BF)
    query_win: Any = ((ROWS, WIDE), BF)
    keys_all: Any = ((ROWS + WIN, WIDE), BF)
    values_all: Any = ((ROWS + WIN, WIDE), BF)
    probs: Any = ((2, ROWS, TILE), F32)
    mixed_win: Any = ((ROWS, WIDE), BF)
    resid_two: Any = ((OWN, D), F32)
    low_four: Any = ((ROWS, D), BF)
    grad_own: Any = ((OWN, D), F32)
    gain_sum: Any = ((8, D), F32)
    gate_sum: Any = ((4, 4, FF, TILE), BF)
    up_sum: Any = ((4, 4, FF, TILE), BF)
    down_sum: Any = ((4, 4, FF, TILE), BF)
    part_three: Any = ((ROWS, D), BF)


class ForwardWork(NamedTuple):
    part: Any = ((ROWS, D), BF)
    own: Any = ((OWN, D), F32)
    group_col: Any = ((ROWS, TILE), F32)
    tail_flag: Any = ((16, TILE), BF)
    halo_flag: Any = ((16, TILE), BF)
    query_feat: Any = ((2, ROWS, WIDE), BF)
    key_feat: Any = ((2, ROWS, WIDE), BF)
    normed_three: Any = ((ROWS, D), BF)
    hidden_grad: Any = ((ROWS, FF_PAD), F32)
    hidden: Any = ((ROWS, FF_PAD), BF)
    gate_low: Any = ((ROWS, FF_PAD), BF)
    up_low: Any = ((ROWS, FF_PAD), BF)
    flipped: Any = ((FF_PAD, ROWS), BF)


class SeqSum:
    def __init__(self, place, copies, blocks, out, bufs):
        self.place, self.copies, self.blocks, self.out = place, copies, blocks, out
        z, y = place.z, place.y
        quarter = self.quarter = blocks.shape[2] // 4
        ring_y, ring_z = (place.on_y(1), place.on_y(3)), (place.on_z(1), place.on_z(3))

        def pick_one(k, half):
            return blocks.at[:, (y + k) % 4, pl.ds(half * quarter, quarter)]

        def pick_two(k, half):
            return blocks.at[(z + k) % 4, :, pl.ds((2 + half) * quarter, quarter)]

        def pick_three(k, half):
            return blocks.at[(z + k) % 4, y, pl.ds(half * quarter, quarter)]

        def pick_four(k, half):
            return blocks.at[z, (y + k) % 4, pl.ds((2 + half) * quarter, quarter)]

        live = [types.SimpleNamespace() for _ in range(4)]
        self.early = ((ring_y, pick_one, bufs[0:3], live[0]), (ring_z, pick_two, bufs[3:6], live[1]))
        self.late = ((ring_z, pick_three, bufs[6:9], live[2]), (ring_y, pick_four, bufs[9:12], live[3]))

    def begin(self, rings):
        for (right, left), pick, (fwd, direct, comb), live in rings:
            live.fr = self.copies.start(pick(2, 0), fwd.at[0], right)
            live.fl = self.copies.start(pick(2, 1), fwd.at[1], left)
            live.dr = self.copies.start(pick(1, 1), direct.at[1], right)
            live.dl = self.copies.start(pick(3, 0), direct.at[0], left)

    def join(self, rings):
        for (right, left), pick, (fwd, direct, comb), live in rings:
            live.fr.wait_recv()
            block = pick(1, 0)
            block[...] = (block[...].astype(F32) + fwd[0].astype(F32)).astype(BF)
            live.cr = self.copies.start(block, comb.at[0], right)
            live.fl.wait_recv()
            block = pick(3, 1)
            block[...] = (block[...].astype(F32) + fwd[1].astype(F32)).astype(BF)
            live.cl = self.copies.start(block, comb.at[1], left)

    def total(self, ring, half):
        _, pick, (fwd, direct, comb), live = ring
        (live.cr if half == 0 else live.cl).wait_recv()
        total = pick(0, half)[...].astype(F32) + comb[half].astype(F32)
        if direct is None:
            return total
        (live.dl if half == 0 else live.dr).wait_recv()
        return total + direct[half].astype(F32)

    def fold(self, rings):
        for _, pick, (fwd, direct, _), live in rings:
            for copy, block, got in (
                (live.fr, pick(1, 0), fwd.at[0]),
                (live.fl, pick(3, 1), fwd.at[1]),
                (live.dl, pick(0, 0), direct.at[0]),
                (live.dr, pick(0, 1), direct.at[1]),
            ):
                copy.wait_recv()
                block[...] = (block[...].astype(F32) + got[...].astype(F32)).astype(BF)

    def pass_on(self, rings):
        for (right, left), pick, (_, _, comb), live in rings:
            live.cr = self.copies.start(pick(1, 0), comb.at[0], right)
            live.cl = self.copies.start(pick(3, 1), comb.at[1], left)

    def step(self, number):
        if number == 0 and self.early[0][2][1] is None:
            self.pass_on(self.early)
        elif number == 0:
            self.begin(self.early)
        elif number == 1:
            self.join(self.early)
        elif number == 2:
            for ring in self.early:
                for half in range(2):
                    block = ring[1](0, half)
                    block[...] = self.total(ring, half).astype(BF)
            self.begin(self.late)
        elif number == 3:
            self.join(self.late)
        else:
            size = self.quarter
            for half in range(2):
                self.out[pl.ds(half * size, size)] = self.total(self.late[0], half)
                self.out[pl.ds((2 + half) * size, size)] = self.total(self.late[1], half)


def seq_scratch(width):
    early, late = (2, 4, width // 4, TILE), (2, width // 4, TILE)
    return [pltpu.VMEM(early, BF)] * 6 + [pltpu.VMEM(late, BF)] * 6


FOLDED = 2


def folded_scratch():
    late = pltpu.VMEM((2, FF // 4, TILE), BF)
    return [pltpu.VMEM((2, 4, FF // 4, TILE), BF)] * 2 + [late] * 6


def taker(refs):
    refs = list(refs)

    def take(kind):
        return kind(*[refs.pop(0) for _ in kind._fields])

    def some(count):
        return [refs.pop(0) for _ in range(count)]

    return take, some


def vmem(kind):
    return [pltpu.VMEM(*entry) for entry in kind()]


def forward_kernel(*refs):
    take, some = taker(refs)
    inputs, hbm_weights, hbm_saved = take(Inputs), take(Weights), take(Saved)
    weights, saved, work, scan_bufs = take(Weights), take(Saved), take(ForwardWork), take(StateScan)
    bufs = some(7)
    fold_bufs = [some(4) for _ in range(FOLDED)]
    fold_sems = some(2)
    mp_sems, (state_send, state_recv), (halo_send, halo_recv), (local_sems,) = (
        some(2),
        some(2),
        some(2),
        some(1),
    )
    place = Place()
    local = Locals(local_sems)
    loads = []
    for src, dst in zip(hbm_weights[1:], weights[1:]):
        loads.append(local.start(src, dst if src.shape == dst.shape else dst.at[pl.ds(0, FF)]))
    loads = Weights(local.start(hbm_weights.out_grad, weights.out_grad), *loads)
    saves = []

    def save(*pairs):
        for src, dst in pairs:
            saves.append(local.start(src, dst))

    greet(
        [place.peer()]
        + [place.on_x(k) for k in (1, 3)]
        + [place.on_y(k) for k in (1, 2, 3)]
        + [place.on_z(k) for k in (1, 2, 3)]
        + [place.along(1), place.along(15)]
    )
    for ref in (weights.w_gate, weights.w_up, weights.w_down):
        ref[FF:FF_PAD] = jnp.zeros((FF_PAD - FF, D), BF)
    tokens, group_row, group_col = inputs.tokens, inputs.group_row, work.group_col
    first, second, vectors = inputs.first, inputs.second, inputs.vectors
    scale = vectors[2:3]
    normed_one = saved.normed_one

    def norm_rows(i, _):
        rows = rows_at(i * 32, 32)
        normed_one[rows] = normed(tokens[rows].astype(F32), inputs.gain_one[...]).astype(BF)
        return 0

    lax.fori_loop(0, ROWS // 32, norm_rows, 0)
    save((normed_one, hbm_saved.normed_one))
    column(group_row, group_col)
    query, key, value = saved.query, saved.key, saved.value
    for load, weight, held in (
        (loads.w_key, weights.w_key, key),
        (loads.w_query, weights.w_query, query),
    ):
        load.wait()
        held[0], held[1] = halves(dot_nt(normed_one[...], weight[...]))
    loads.w_value.wait()
    value[...] = dot(normed_one[...], weights.w_value[...]).astype(BF)

    last = group_row[0:1, ROWS - 1 : ROWS].astype(F32)
    in_last = (group_col[:, 0:1] == last).astype(F32)
    query_feat, key_feat, mine = work.query_feat, work.key_feat, scan_bufs.mine
    for head in range(2):
        left, right = factors(head, (key[0], key[1]), first, second, vectors)
        feat = (left * right * scale).astype(BF)
        key_feat[head] = feat
        kept = feat.astype(F32) * in_last
        state = dot_tn(kept.astype(BF), value[:, head * HD : (head + 1) * HD])
        mine[head, 0:FEATURES] = state[0:FEATURES].astype(BF)
        mine[head, FEATURES:STATE] = norm_rows_of(jnp.sum(kept, axis=0, keepdims=True)).astype(BF)
    meet(11)
    copies_state = Copies(state_send, state_recv)
    scan = state_scan(place, copies_state, scan_bufs, saved.carried, saved.carried_norm, False)
    next(scan)
    save((query, hbm_saved.query), (key, hbm_saved.key), (value, hbm_saved.value))
    quotient, denominator = saved.quotient, saved.denominator
    for head in range(2):
        left, right = factors(head, (query[0], query[1]), first, second, vectors)
        query_feat[head] = (left * right * scale).astype(BF)
    for tile in range(ROWS // TILE):
        rows, count = pl.ds(tile * TILE, TILE), (tile + 1) * TILE
        kept = kept_pairs(group_col, group_row, tile)
        for head in range(2):
            inner = products(head, (query.at[0], query.at[1]), (key.at[0], key.at[1]), rows, count)
            block = jnp.where(kept, 1.0 + inner * 0.25 + inner * inner * 0.03125, 0.0).astype(BF)
            denominator[head, rows] = jnp.sum(block.astype(F32), axis=1, keepdims=True)
            quotient[rows, head * HD : (head + 1) * HD] = dot(
                block, value[0:count, head * HD : (head + 1) * HD]
            )
        if tile == 1:
            next(scan)
    loads.w_down.wait()
    loads.out_grad.wait()
    work.hidden_grad[...] = dot_nt(weights.out_grad[...], weights.w_down[...])
    for _ in scan:
        pass
    copies_state.finish()
    first_group = group_row[0:1, 0:1].astype(F32)
    incoming = (group_col[:, 0:1] == first_group).astype(F32) * jnp.where(place.seq > 0, 1.0, 0.0)
    carried, carried_norm, mixed_lin = saved.carried, saved.carried_norm, saved.mixed_lin
    save((carried, hbm_saved.carried), (carried_norm, hbm_saved.carried_norm))
    for head in range(2):
        lanes = slice(head * HD, (head + 1) * HD)
        feat = query_feat[head]
        numer = quotient[:, lanes] + incoming * dot(feat, carried[head].astype(BF))
        denom = denominator[head] + incoming * jnp.sum(
            feat.astype(F32) * carried_norm[head], axis=1, keepdims=True
        )
        ratio = numer / denom
        denominator[head] = denom
        quotient[:, lanes] = ratio
        mixed_lin[:, lanes] = ratio.astype(BF)
    save(
        (quotient, hbm_saved.quotient),
        (denominator, hbm_saved.denominator),
        (mixed_lin, hbm_saved.mixed_lin),
    )
    loads.w_out.wait()

    part, own = work.part, work.own
    resid_one, resid_two = saved.resid_one, saved.resid_two
    normed_two, normed_three = saved.normed_two, work.normed_three
    sum_one = MpSum(place, mp_sems, part, normed_two, own, bufs, 0, (3, 0, 1, 2))
    sum_two = MpSum(place, mp_sems, part, normed_three, own, bufs, 1)
    sum_four = MpSum(place, mp_sems, part, saved.low_four, own, bufs)

    def produce_one(j):
        rows = pl.ds(j * CHUNK, CHUNK)
        part[rows] = dot(mixed_lin[rows], weights.w_out[...]).astype(BF)

    def finish_one(j):
        mine = pl.ds(j * PIECE, PIECE)
        rows = own[mine] + tokens[sum_one.own_rows(j)].astype(F32)
        resid_one[mine] = rows
        normed_two[sum_one.own_rows(j)] = normed(rows, inputs.gain_two[...]).astype(BF)

    query_win, keys_all, values_all = saved.query_win, saved.keys_all, saved.values_all
    copies_halo = Copies(halo_send, halo_recv)
    lane = lax.broadcasted_iota(jnp.int32, (1, TILE), 1)
    group_blocks = [group_row[0:1, k * TILE : (k + 1) * TILE].astype(F32) for k in range(4)]
    turned = [pltpu.roll(block, WIN, 1) for block in group_blocks]
    work.tail_flag[...] = jnp.broadcast_to((turned[3] == last).astype(F32), (16, TILE)).astype(BF)
    halo = []

    def ready_one(j):
        rows = pl.ds(j * CHUNK, CHUNK)
        below = pl.ds(WIN + j * CHUNK, CHUNK)
        if j == 3:
            for load in (loads.win_k, loads.win_v, loads.win_q):
                load.wait()
        keys_all[below] = dot(normed_two[rows], weights.win_k[...]).astype(BF)
        values_all[below] = dot(normed_two[rows], weights.win_v[...]).astype(BF)
        if j == 3:
            for ref in (keys_all, values_all):
                halo.append(
                    copies_halo.start(ref.at[pl.ds(ROWS, WIN)], ref.at[pl.ds(0, WIN)], place.along(1))
                )
            halo.append(copies_halo.start(work.tail_flag, work.halo_flag, place.along(1)))
        query_win[rows] = dot(normed_two[rows], weights.win_q[...]).astype(BF)
        if j != 3:
            next(two)

    probs, mixed_win = saved.probs, saved.mixed_win
    tile_row = lax.broadcasted_iota(jnp.int32, (WIN, TILE), 0)
    tile_col = lax.broadcasted_iota(jnp.int32, (WIN, TILE), 1)
    near = (tile_col > tile_row) & (tile_col <= tile_row + WIN)
    score_scale = HD ** (-0.5)

    def window_tile(t):
        rows = pl.ds(t * WIN, WIN)
        if t == 0:
            flag = jnp.where(place.seq > 0, work.halo_flag[0:1].astype(F32), 0.0)
            groups = jnp.where(lane < WIN, jnp.where(flag > 0.5, first_group, -2.0), turned[0])
        elif t % 2 == 1:
            groups = group_blocks[t // 2]
        else:
            groups = jnp.where(lane < WIN, turned[t // 2 - 1], turned[t // 2])
        kept = near & (group_col[rows] == groups)
        for head in range(2):
            lanes = slice(head * HD, (head + 1) * HD)
            scores = dot_nt(query_win[rows, lanes], keys_all[t * WIN : t * WIN + TILE, lanes])
            scores = jnp.where(kept, scores * score_scale, -1e30)
            exp_scores = jnp.exp(scores - jnp.max(scores, axis=1, keepdims=True))
            found = exp_scores / jnp.sum(exp_scores, axis=1, keepdims=True)
            probs[head, rows] = found
            mixed_win[rows, lanes] = dot(
                found.astype(BF), values_all[t * WIN : t * WIN + TILE, lanes]
            ).astype(BF)

    def produce_two(j):
        if j == 0:
            for copy in halo:
                copy.wait_recv()
            loads.win_out.wait()
        window_tile(2 * j)
        window_tile(2 * j + 1)
        rows = pl.ds(j * CHUNK, CHUNK)
        part[rows] = dot(mixed_win[rows], weights.win_out[...]).astype(BF)

    def finish_two(j):
        mine = pl.ds(j * PIECE, PIECE)
        rows = own[mine] + resid_one[mine]
        resid_two[mine] = rows
        normed_three[sum_two.own_rows(j)] = normed(rows, inputs.gain_three[...]).astype(BF)

    w_gate, w_up, w_down, og = weights.w_gate, weights.w_up, weights.w_down, weights.out_grad
    hidden, gate_low, up_low = work.hidden, work.gate_low, work.up_low

    def ready_two(j):
        if j % 2 == 0:
            return
        if j == 1:
            for load in (loads.w_gate, loads.w_up):
                load.wait()
        rows = pl.ds((j - 1) * CHUNK, 2 * CHUNK)
        gate = dot_nt(normed_three[rows], w_gate[...])
        up = dot_nt(normed_three[rows], w_up[...])
        sigmoid = 1.0 / (1.0 + jnp.exp(-gate))
        act, hidden_grad = gate * sigmoid, work.hidden_grad[rows]
        hidden[rows] = (act * up).astype(BF)
        up_low[rows] = (hidden_grad * act).astype(BF)
        gate_low[rows] = (hidden_grad * up * (sigmoid + act * (1.0 - sigmoid))).astype(BF)

    one = sum_one.slots(produce_one, finish_one, ready_one)
    two = sum_two.slots(produce_two, finish_two, ready_two)
    run(one)
    copies_halo.finish()
    save(
        (resid_one, hbm_saved.resid_one),
        (normed_two, hbm_saved.normed_two),
        (query_win, hbm_saved.query_win),
        (keys_all, hbm_saved.keys_all),
        (values_all, hbm_saved.values_all),
    )
    run(two)
    save(
        (probs, hbm_saved.probs), (mixed_win, hbm_saved.mixed_win), (resid_two, hbm_saved.resid_two)
    )

    def input_back(half):
        cols = pl.ds(half * 1024, 1024)
        part[:, cols] = (
            dot(gate_low[...], w_gate[:, cols]) + dot(up_low[...], w_up[:, cols])
        ).astype(BF)

    def project_down(half):
        cols = pl.ds(half * 1024, 1024)
        saved.part_three[:, cols] = dot(hidden[...], w_down[:, cols]).astype(BF)
        if half == 1:
            save((saved.part_three, hbm_saved.part_three))

    def finish_four(j):
        mine, rows = pl.ds(j * PIECE, PIECE), sum_four.own_rows(j)
        total, here = back_through_norm(
            resid_two[mine], og[rows].astype(F32), own[mine], inputs.gain_three[...]
        )
        saved.gain_sum[0:1] = here if j == 0 else saved.gain_sum[0:1] + here
        saved.grad_own[mine] = total
        saved.low_four[rows] = total.astype(BF)

    seq_copies = Copies(*fold_sems)
    folds = []

    def weight_back(number, into, to_hbm, left, right, quarter):
        if quarter == 0:
            work.flipped[...] = left[...].T
        weight_block(into, work.flipped, right, quarter)
        if quarter < 3:
            return
        if number < FOLDED:
            fwd_y, direct_y, fwd_z, direct_z = fold_bufs[number]
            early = [fwd_y, direct_y, None, fwd_z, direct_z, None]
            seq_sum = SeqSum(place, seq_copies, into, None, early + [None] * 6)
            seq_sum.begin(seq_sum.early)
            folds.append((seq_sum, into, to_hbm))
        else:
            save((into, to_hbm))

    blocks = []
    for number, (into, to_hbm, left, right) in enumerate(
        (
            (saved.gate_sum, hbm_saved.gate_sum, gate_low, normed_three),
            (saved.up_sum, hbm_saved.up_sum, up_low, normed_three),
            (saved.down_sum, hbm_saved.down_sum, hidden, og),
        )
    ):
        blocks += [
            functools.partial(weight_back, number, into, to_hbm, left, right, k) for k in range(4)
        ]
    blocks += [functools.partial(project_down, k) for k in range(2)]
    saved.gain_sum[...] = jnp.zeros_like(saved.gain_sum)
    input_back(0)
    input_back(1)
    four = sum_four.slots(lambda j: None, finish_four)
    for _ in four:
        for _ in range(3):
            if blocks:
                blocks.pop(0)()
    save(
        (saved.low_four, hbm_saved.low_four),
        (saved.grad_own, hbm_saved.grad_own),
        (saved.gain_sum, hbm_saved.gain_sum),
    )
    for block in blocks:
        block()
    for seq_sum, into, to_hbm in folds:
        seq_sum.fold(seq_sum.early)
        save((into, to_hbm))
    seq_copies.finish()
    for copy in saves:
        copy.wait()


HBM = pl.BlockSpec(memory_space=pl.ANY)
INSIDE = pl.BlockSpec(memory_space=pltpu.VMEM)


def forward(inputs, weights):
    scratch = vmem(Weights) + vmem(Saved) + vmem(ForwardWork) + vmem(StateScan) + mp_scratch()
    scratch += [pltpu.VMEM((2, 4, FF // 4, TILE), BF)] * (4 * FOLDED) + [dma(8 * FOLDED)] * 2
    scratch += [dma(CHUNKS * PER_CHUNK)] * 2 + [dma(12)] * 2 + [dma(3)] * 2
    scratch += [dma(len(Weights._fields) + len(Saved._fields))]
    return Saved(
        *pl.pallas_call(
            forward_kernel,
            out_shape=[shape(dims, kind) for dims, kind in Saved()],
            in_specs=[INSIDE] * len(inputs) + [HBM] * len(weights),
            out_specs=[HBM] * len(Saved._fields),
            scratch_shapes=scratch,
            compiler_params=pltpu.CompilerParams(
                collective_id=0, has_side_effects=True, vmem_limit_bytes=VMEM_LIMIT
            ),
        )(*inputs, *weights)
    )


class Groups(NamedTuple):
    gate: Any = FF
    up: Any = FF
    down: Any = FF
    win_out: Any = WIDE
    win: Any = 3 * WIDE
    out: Any = WIDE
    lin: Any = WIDE + 4 * FEAT


class BackInputs(NamedTuple):
    group_row: Any
    gain_one: Any
    gain_two: Any
    first: Any
    second: Any
    vectors: Any


class BackHbm(NamedTuple):
    part_three: Any
    low_four: Any
    grad_own: Any
    gain_sum: Any
    tokens: Any
    normed_one: Any
    normed_two: Any
    gate_sum: Any
    up_sum: Any
    down_sum: Any
    w_query: Any
    w_key: Any
    w_value: Any
    w_out: Any
    win_q: Any
    win_k: Any
    win_v: Any
    win_out: Any


SPECS = Saved()


class BackSaved(NamedTuple):
    query: Any = SPECS.query
    key: Any = SPECS.key
    value: Any = SPECS.value
    carried: Any = SPECS.carried
    carried_norm: Any = SPECS.carried_norm
    quotient: Any = SPECS.quotient
    denominator: Any = SPECS.denominator
    mixed_lin: Any = SPECS.mixed_lin
    resid_one: Any = SPECS.resid_one
    query_win: Any = SPECS.query_win
    keys_all: Any = SPECS.keys_all
    values_all: Any = SPECS.values_all
    probs: Any = SPECS.probs
    mixed_win: Any = SPECS.mixed_win
    resid_two: Any = SPECS.resid_two


class BackOuts(NamedTuple):
    tokens_low: Any = ((ROWS, D), BF)
    gain_one: Any = ((1, TILE), F32)
    gain_two: Any = ((1, TILE), F32)
    gain_three: Any = ((1, TILE), F32)
    gate: Any = ((FF, TILE), F32)
    up: Any = ((FF, TILE), F32)
    down: Any = ((FF, TILE), F32)
    win_out: Any = ((WIDE, TILE), F32)
    out: Any = ((WIDE, TILE), F32)
    win_q: Any = ((TILE, WIDE), F32)
    win_k: Any = ((TILE, WIDE), F32)
    win_v: Any = ((TILE, WIDE), F32)
    value: Any = ((TILE, WIDE), F32)
    query: Any = ((2 * FEAT, TILE), F32)
    key: Any = ((2 * FEAT, TILE), F32)
    result: Any = ((ROWS, D), BF)


class BackWork(NamedTuple):
    part: Any = ((ROWS, D), BF)
    other_full: Any = ((ROWS, D), BF)
    own: Any = ((OWN, D), F32)
    grad_own: Any = ((OWN, D), F32)
    token_own: Any = ((OWN, D), BF)
    group_col: Any = ((ROWS, TILE), F32)
    normed_low: Any = ((ROWS, D), BF)
    w_query: Any = ((2 * FEAT, D), BF)
    w_key: Any = ((2 * FEAT, D), BF)
    w_out: Any = ((WIDE, D), BF)
    win_out: Any = ((WIDE, D), BF)
    w_win: Any = ((D, 3 * WIDE), BF)
    mixed_grad: Any = ((ROWS, WIDE), BF)
    keys_sum: Any = ((ROWS + WIN, WIDE), F32)
    values_sum: Any = ((ROWS + WIN, WIDE), F32)
    back_key: Any = ((2, WIN, WIDE), BF)
    back_value: Any = ((2, WIN, WIDE), BF)
    win_grads: Any = ((ROWS, 3 * WIDE), BF)
    flipped: Any = ((3 * WIDE, ROWS), BF)
    query_sum: Any = ((ROWS, 2 * FEAT), F32)
    key_sum: Any = ((ROWS, 2 * FEAT), F32)
    query_low: Any = ((ROWS, 2 * FEAT), BF)
    key_low: Any = ((ROWS, 2 * FEAT), BF)
    state_sum: Any = ((2, WIDE, HD), F32)
    norm_sum: Any = ((2, 1, WIDE), F32)
    gain_sums: Any = ((16, D), F32)
    gain_low: Any = ((16, D), BF)
    gain_z: Any = ((3, 16, 512), BF)
    gain_zz: Any = ((16, 512), BF)
    gain_y: Any = ((3, 16, TILE), BF)
    gain_x: Any = ((16, TILE), BF)
    gain_xx: Any = ((3, 16, TILE), BF)
    gain_p: Any = ((16, TILE), BF)
    gain_pp: Any = ((16, TILE), BF)
    sum_win: Any = ((3 * WIDE, TILE), F32)
    sum_lin: Any = ((WIDE + 4 * FEAT, TILE), F32)
    later: Any = ((2, WIDE, HD), F32)
    later_norm: Any = ((2, 1, WIDE), F32)


def backward_kernel(*refs):
    take, some = taker(refs)
    inputs, hbm, hbm_saved, outs = take(BackInputs), take(BackHbm), take(BackSaved), take(BackOuts)
    saved, blocks, work, scan_bufs = take(BackSaved), take(Groups), take(BackWork), take(StateScan)
    seq_bufs = []
    for number in range(len(Groups._fields)):
        if number < FOLDED:
            comb_y, comb_z, *late = some(8)
            seq_bufs.append([None, None, comb_y, None, None, comb_z] + late)
        else:
            seq_bufs.append(some(12))
    bufs, bufs_three = some(7), some(7)
    mp_sems, three_sems, (seq_send, seq_recv), (few_send, few_recv), (local_sems,) = (
        some(2),
        some(2),
        some(2),
        some(2),
        some(1),
    )
    place = Place()
    z, y = place.z, place.y
    local = Locals(local_sems)
    part, own, other_full, tokens_low = work.part, work.own, work.other_full, outs.tokens_low
    sum_three = MpSum(place, three_sems, part, outs.result, own, bufs_three, hold=True)
    sum_five = MpSum(place, mp_sems, part, other_full, own, bufs)
    sum_six = MpSum(place, mp_sems, part, tokens_low, own, bufs)

    load_part = local.start(hbm.part_three, part)
    load_low = local.start(hbm.low_four, tokens_low)
    load_win_out = local.start(hbm.win_out, work.win_out)
    mlp_loads = [
        local.start(src, dst)
        for src, dst in ((hbm.gate_sum, blocks.gate), (hbm.up_sum, blocks.up), (hbm.down_sum, blocks.down))
    ]
    load_saved = BackSaved(*[local.start(src, dst) for src, dst in zip(hbm_saved, saved)])
    load_win = [
        local.start(src, work.w_win.at[:, pl.ds(k * WIDE, WIDE)])
        for k, src in enumerate((hbm.win_q, hbm.win_k, hbm.win_v))
    ]
    load_grad = local.start(hbm.grad_own, work.grad_own)
    load_gain = local.start(hbm.gain_sum, work.gain_sums.at[pl.ds(0, 8)])
    load_normed = local.start(hbm.normed_two, work.normed_low)
    load_lin = [
        local.start(src, dst)
        for src, dst in ((hbm.w_query, work.w_query), (hbm.w_key, work.w_key), (hbm.w_out, work.w_out))
    ]
    greet(
        [place.peer()]
        + [place.on_x(k) for k in (1, 2, 3)]
        + [place.on_y(k) for k in (1, 2, 3)]
        + [place.on_z(k) for k in (1, 2, 3)]
        + [place.along(1), place.along(15)]
    )
    seq_copies = Copies(seq_send, seq_recv)
    few = Copies(few_send, few_recv)
    finished = Groups(outs.gate, outs.up, outs.down, outs.win_out, work.sum_win, outs.out, work.sum_lin)
    seq_sums = Groups(
        *[
            SeqSum(place, seq_copies, block, out, bufs_here)
            for block, out, bufs_here in zip(blocks, finished, seq_bufs)
        ]
    )
    first, second, vectors = inputs.first, inputs.second, inputs.vectors
    scale = vectors[2:3]
    group_row, group_col = inputs.group_row, work.group_col
    column(group_row, group_col)
    last_group = group_row[0:1, ROWS - 1 : ROWS].astype(F32)
    first_group = group_row[0:1, 0:1].astype(F32)
    in_last = (group_col[:, 0:1] == last_group).astype(F32)
    after_first = jnp.where(place.seq > 0, 1.0, 0.0)
    work.gain_sums[8:16] = jnp.zeros((8, D), F32)

    def finish(mp_sum, number, resid, gain, to, j):
        mine = pl.ds(j * PIECE, PIECE)
        total, here = back_through_norm(
            resid[mine].astype(F32), work.grad_own[mine], own[mine], gain[...]
        )
        work.gain_sums[number : number + 1] += here
        work.grad_own[mine] = total
        to[mp_sum.own_rows(j)] = total.astype(BF)

    mixed_grad, keys_sum, values_sum, win_grads = (
        work.mixed_grad,
        work.keys_sum,
        work.values_sum,
        work.win_grads,
    )
    probs, query_win, keys_all, values_all = (
        saved.probs,
        saved.query_win,
        saved.keys_all,
        saved.values_all,
    )
    score_scale = HD ** (-0.5)
    back = []

    def window_back(t):
        rows, window = pl.ds(t * WIN, WIN), pl.ds(t * WIN, TILE)
        for head in range(2):
            lanes = slice(head * HD, (head + 1) * HD)
            grad_tile, held = mixed_grad[rows, lanes], probs[head, rows]
            probs_grad = dot_nt(grad_tile, values_all[window, lanes])
            score_low = (
                held * (probs_grad - jnp.sum(probs_grad * held, axis=1, keepdims=True))
            ).astype(BF)
            win_grads[rows, lanes] = (dot(score_low, keys_all[window, lanes]) * score_scale).astype(BF)
            for ref, found in (
                (keys_sum, dot_tn(score_low, query_win[rows, lanes]) * score_scale),
                (values_sum, dot_tn(held.astype(BF), grad_tile)),
            ):
                if t == 0:
                    ref[window, lanes] = found
                else:
                    ref[rows, lanes] += found[:WIN]
                    ref[pl.ds(t * WIN + WIN, WIN), lanes] = found[WIN:]
        if t == 0:
            for ref, to_send in ((keys_sum, work.back_key), (values_sum, work.back_value)):
                to_send[0] = ref[0:WIN].astype(BF)
                back.append(few.start(to_send.at[0], to_send.at[1], place.along(15)))

    def produce_five(j):
        rows = pl.ds(j * CHUNK, CHUNK)
        for k, (ref, got) in enumerate(((keys_sum, work.back_key), (values_sum, work.back_value))):
            lanes = slice((k + 1) * WIDE, (k + 2) * WIDE)
            if j < CHUNKS - 1:
                win_grads[rows, lanes] = ref[WIN + j * CHUNK : WIN + (j + 1) * CHUNK].astype(BF)
            else:
                win_grads[j * CHUNK : ROWS - WIN, lanes] = ref[WIN + j * CHUNK : ROWS].astype(BF)
                back[k].wait_recv()
                win_grads[ROWS - WIN : ROWS, lanes] = (
                    ref[ROWS : ROWS + WIN] + got[1].astype(F32)
                ).astype(BF)
        if j % 2 == 0:
            return
        rows = pl.ds((j - 1) * CHUNK, 2 * CHUNK)
        part[rows] = dot_nt(win_grads[rows], work.w_win[...]).astype(BF)

    def finish_five(j):
        if j == 0:
            load_saved.resid_one.wait()
            load_grad.wait()
            load_gain.wait()
        finish(sum_five, 1, saved.resid_one, inputs.gain_two, other_full, j)

    query, key, value, carried = saved.query, saved.key, saved.value, saved.carried
    numer_low, query_sum, key_sum, value_sum, value_low = (
        query_win,
        work.query_sum,
        work.key_sum,
        keys_sum,
        mixed_grad,
    )

    def through_features(head, parts, grad):
        left, right = parts
        scaled = grad * scale
        return dot_nt((scaled * right).astype(BF), first[head]) + dot_nt(
            (scaled * left).astype(BF), second[head]
        )

    def ready_five(j):
        rows, count = pl.ds(j * CHUNK, CHUNK), (j + 1) * CHUNK
        if j == 0:
            for load in load_lin:
                load.wait()
            for load in (
                load_saved.denominator,
                load_saved.quotient,
                load_saved.query,
                load_saved.key,
                load_saved.value,
                load_saved.carried,
                load_saved.carried_norm,
            ):
                load.wait()
        mixed = dot_nt(other_full[rows], work.w_out[...]).astype(BF).astype(F32)
        incoming = (group_col[rows, 0:1] == first_group).astype(F32) * after_first
        kept = kept_pairs(group_col, group_row, j)
        key_new = []
        for head in range(2):
            lanes = slice(head * HD, (head + 1) * HD)
            denom = saved.denominator[head, rows]
            numer = (mixed[:, lanes] / denom).astype(BF)
            numer_low[rows, lanes] = numer
            denom_grad = (
                -jnp.sum(mixed[:, lanes] * saved.quotient[rows, lanes], axis=1, keepdims=True) / denom
            )
            parts = factors(head, (query[0, rows], query[1, rows]), first, second, vectors)
            used = (parts[0] * parts[1] * scale).astype(BF).astype(F32) * incoming
            state = dot_tn(used.astype(BF), numer)
            norm = jnp.sum(used * denom_grad, axis=0, keepdims=True)
            if j == 0:
                work.state_sum[head], work.norm_sum[head] = state, norm
            else:
                work.state_sum[head] += state
                work.norm_sum[head] += norm
            grad = incoming * (
                dot_nt(numer, carried[head].astype(BF)) + denom_grad * saved.carried_norm[head]
            )
            query_new = through_features(head, parts, grad)
            inner = products(head, (query.at[0], query.at[1]), (key.at[0], key.at[1]), rows, count)
            kernel = jnp.where(kept, 1.0 + inner * 0.25 + inner * inner * 0.03125, 0.0).astype(BF)
            grad = dot_nt(numer, value[0:count, lanes]) + denom_grad
            grad = jnp.where(kept, grad, 0.0).astype(BF).astype(F32)
            inner_grad = (grad * (0.25 + inner * 0.0625)).astype(BF)
            query_new = query_new + of_head(dot(inner_grad, key[0, 0:count]), head)
            if head == 0:
                query_sum[rows] = query_new
            else:
                query_sum[rows] += query_new
            key_new.append(of_head(dot_tn(inner_grad, query[0, rows]), head))
            found = dot_tn(kernel, numer)
            if j > 0:
                value_sum[0 : count - CHUNK, lanes] += found[0 : count - CHUNK]
            value_sum[count - CHUNK : count, lanes] = found[count - CHUNK : count]
        found = key_new[0] + key_new[1]
        if j > 0:
            key_sum[0 : count - CHUNK] += found[0 : count - CHUNK]
        key_sum[count - CHUNK : count] = found[count - CHUNK : count]
        if j == CHUNKS - 1:
            for head in range(2):
                scan_bufs.mine[head, 0:FEATURES] = work.state_sum[head, 0:FEATURES].astype(BF)
                scan_bufs.mine[head, FEATURES:STATE] = norm_rows_of(work.norm_sum[head]).astype(BF)

    def weight_task(block, right, quarter):
        weight_block(block, work.flipped, right, quarter)

    def begin(group):
        group.step(0)

    def turn_mixed(ref, load):
        load.wait()
        work.flipped[0:WIDE] = ref[...].T

    def turn_win():
        load_normed.wait()
        for k in range(3):
            rows = slice(k * WIDE, (k + 1) * WIDE)
            work.flipped[rows] = win_grads[:, rows].T

    late_work = [lambda: turn_mixed(saved.mixed_win, load_saved.mixed_win)]
    late_work += [functools.partial(weight_task, blocks.win_out, tokens_low, k) for k in range(4)]
    late_work += [functools.partial(begin, seq_sums.win_out), turn_win]
    late_work += [functools.partial(weight_task, blocks.win, work.normed_low, k) for k in range(4)]
    late_work += [functools.partial(begin, seq_sums.win)]

    def steps(*names):
        for group, number in names:
            group.step(number)

    gate, up, down, win_out, win, out, lin = seq_sums
    def finish_three(j):
        mine = pl.ds(j * PIECE, PIECE)
        outs.result[sum_three.own_rows(j)] = (own[mine] + saved.resid_two[mine]).astype(BF)

    three = sum_three.slots(lambda j: None, finish_three)
    meet(12)
    load_part.wait()
    next(three)
    for load in (load_low, load_win_out):
        load.wait()
    mixed_grad[...] = dot_nt(tokens_low[...], work.win_out[...]).astype(BF)
    for load, group in zip(mlp_loads, (gate, up, down)):
        load.wait()
        group.step(0)
    next(three)
    for load in (load_saved.probs, load_saved.query_win, load_saved.keys_all, load_saved.values_all):
        load.wait()
    load_saved.resid_two.wait()
    for t in range(8):
        window_back(t)
        if t == 4:
            next(three)
    next(three)
    for load in load_win:
        load.wait()
    for j in range(0, CHUNKS, 2):
        produce_five(j)
        produce_five(j + 1)
    five = sum_five.slots(lambda j: None, finish_five, ready_five)
    plans = {2: [(gate, 2)], 3: [(down, 1)], 4: [(up, 2)], 6: [(down, 2)]}
    for slot in five:
        for _ in range(3):
            if late_work:
                late_work.pop(0)()
        steps(*plans.get(slot, ()))
    for block in late_work:
        block()
    scan = state_scan(place, few, scan_bufs, work.later, work.later_norm, True)
    next(scan)
    load_normed_one = local.start(hbm.normed_one, work.normed_low)
    load_value = local.start(hbm.w_value, work.w_win.at[:, pl.ds(0, WIDE)])
    load_token = [
        local.start(hbm.tokens.at[sum_six.own_rows(j)], work.token_own.at[pl.ds(j * PIECE, PIECE)])
        for j in range(CHUNKS)
    ]
    next(three)
    turn_mixed(saved.mixed_lin, load_saved.mixed_lin)
    weight_task(blocks.out, other_full, 0)
    weight_task(blocks.out, other_full, 1)
    next(scan)
    next(three)
    weight_task(blocks.out, other_full, 2)
    weight_task(blocks.out, other_full, 3)
    steps((out, 0), (gate, 3), (win_out, 1))
    for _ in scan:
        pass
    next(three)
    for head in range(2):
        lanes = slice(head * HD, (head + 1) * HD)
        state = work.later[head].astype(BF)
        parts = factors(head, (key[0], key[1]), first, second, vectors)
        feat = (parts[0] * parts[1] * scale).astype(BF)
        grad = in_last * (dot_nt(value[:, lanes], state) + work.later_norm[head])
        key_sum[...] += through_features(head, parts, grad)
        value_sum[0:ROWS, lanes] += in_last * dot(feat, state)
    work.query_low[...] = query_sum[...].astype(BF)
    work.key_low[...] = key_sum[...].astype(BF)
    value_low[...] = value_sum[0:ROWS].astype(BF)
    load_value.wait()

    def produce_six(j):
        rows = pl.ds(j * CHUNK, CHUNK)
        part[rows] = (
            dot_nt(value_low[rows], work.w_win[:, 0:WIDE])
            + dot(work.query_low[rows], work.w_query[...])
            + dot(work.key_low[rows], work.w_key[...])
        ).astype(BF)

    for load in load_token:
        load.wait()

    def finish_six(j):
        finish(sum_six, 2, work.token_own, inputs.gain_one, tokens_low, j)

    def gains():
        work.gain_low[...] = work.gain_sums[...].astype(BF)

        def block(ref, at, size):
            return ref.at[:, pl.ds(pl.multiple_of(at * size, TILE), size)]

        over = [
            few.start(block(work.gain_low, (z + k) % 4, 512), work.gain_z.at[k - 1], place.on_z(k))
            for k in (1, 2, 3)
        ]
        yield
        total = block(work.gain_low, z, 512)[...].astype(F32)
        for k, copy in enumerate(over):
            copy.wait_recv()
            total = total + work.gain_z[k].astype(F32)
        work.gain_zz[...] = total.astype(BF)
        over = [
            few.start(block(work.gain_zz, (y + k) % 4, TILE), work.gain_y.at[k - 1], place.on_y(k))
            for k in (1, 2, 3)
        ]
        yield
        total = block(work.gain_zz, y, TILE)[...].astype(F32)
        for k, copy in enumerate(over):
            copy.wait_recv()
            total = total + work.gain_y[k].astype(F32)
        work.gain_x[...] = total.astype(BF)
        over = [few.start(work.gain_x, work.gain_xx.at[k - 1], place.on_x(k)) for k in (1, 2, 3)]
        yield
        total = work.gain_x[...].astype(F32)
        for k, copy in enumerate(over):
            copy.wait_recv()
            total = total + work.gain_xx[k].astype(F32)
        work.gain_p[...] = total.astype(BF)
        copy = few.start(work.gain_p, work.gain_pp, place.peer())
        yield
        copy.wait_recv()
        total = work.gain_p[...].astype(F32) + work.gain_pp[...].astype(F32)
        for k, ref in enumerate((outs.gain_three, outs.gain_two, outs.gain_one)):
            ref[...] = total[k : k + 1]

    def turn_lin():
        load_normed_one.wait()
        work.flipped[0:WIDE] = value_low[...].T
        for k, ref in enumerate((query_sum, key_sum)):
            at = WIDE + 2 * FEAT * k
            wide = jnp.concatenate([ref[...], jnp.zeros((ROWS, TILE - 2 * FEAT), F32)], axis=1)
            work.flipped[at : at + 2 * FEAT] = wide.T[0 : 2 * FEAT].astype(BF)

    six = sum_six.slots(produce_six, finish_six)
    next(six)
    next(three)
    steps((up, 3), (win, 1))
    turn_lin()
    for k in range(4):
        weight_task(blocks.lin, work.normed_low, k)
    steps((lin, 0))
    plans = {
        1: [(down, 3), (gate, 4), (win_out, 2)],
        2: [(out, 1), (up, 4), (win, 2)],
        3: [(lin, 1), (down, 4)],
        4: [(out, 2), (win_out, 3), (lin, 2)],
        5: [(win, 3), (win_out, 4)],
        6: [(out, 3), (lin, 3), (win, 4)],
    }
    gain_steps = gains()
    for slot in six:
        if slot >= 3:
            next(gain_steps, None)
        steps(*plans.get(slot, ()))
    steps((out, 4), (lin, 4))
    for k, ref in enumerate((outs.win_q, outs.win_k, outs.win_v)):
        ref[...] = work.sum_win[k * WIDE : (k + 1) * WIDE].T
    outs.value[...] = work.sum_lin[0:WIDE].T
    outs.query[...] = work.sum_lin[WIDE : WIDE + 2 * FEAT]
    outs.key[...] = work.sum_lin[WIDE + 2 * FEAT : WIDE + 4 * FEAT]
    for _ in gain_steps:
        pass
    seq_copies.finish()
    few.finish()


def backward(saved, inputs, weights):
    back_inputs = BackInputs(*[getattr(inputs, name) for name in BackInputs._fields])
    hbm = BackHbm(
        part_three=saved.part_three,
        low_four=saved.low_four,
        grad_own=saved.grad_own,
        gain_sum=saved.gain_sum,
        tokens=inputs.tokens,
        normed_one=saved.normed_one,
        normed_two=saved.normed_two,
        gate_sum=saved.gate_sum,
        up_sum=saved.up_sum,
        down_sum=saved.down_sum,
        w_query=weights.w_query,
        w_key=weights.w_key,
        w_value=weights.w_value,
        w_out=weights.w_out,
        win_q=weights.win_q,
        win_k=weights.win_k,
        win_v=weights.win_v,
        win_out=weights.win_out,
    )
    held = BackSaved(*[getattr(saved, name) for name in BackSaved._fields])
    scratch = vmem(BackSaved) + [pltpu.VMEM((4, 4, width, TILE), BF) for width in Groups()]
    scratch += vmem(BackWork) + vmem(StateScan)
    for number, width in enumerate(Groups()):
        scratch += folded_scratch() if number < FOLDED else seq_scratch(width)
    scratch += mp_scratch() * 2
    scratch += [dma(CHUNKS * PER_CHUNK)] * 4 + [dma(24 * len(Groups._fields))] * 2 + [dma(24)] * 2
    scratch += [dma(64)]
    return BackOuts(
        *pl.pallas_call(
            backward_kernel,
            out_shape=[shape(dims, kind) for dims, kind in BackOuts()],
            in_specs=[INSIDE] * len(back_inputs) + [HBM] * (len(hbm) + len(held)),
            out_specs=[INSIDE] * len(BackOuts._fields),
            scratch_shapes=scratch,
            compiler_params=pltpu.CompilerParams(
                collective_id=1, has_side_effects=True, vmem_limit_bytes=VMEM_LIMIT
            ),
        )(*back_inputs, *hbm, *held)
    )


def hand_over_kernel(*refs):
    count = (len(refs) - 2) // 3
    ins, outs, held = refs[:count], refs[count : 2 * count], refs[2 * count : 3 * count]
    wide, sems = refs[3 * count :]
    block = ROWS // 4
    local = Locals(sems)
    parts = [pl.ds(k * block, block) for k in range(4)]
    loads = [local.start(ins[0].at[rows], held[0].at[rows]) for rows in parts]
    others = [local.start(src, dst) for src, dst in zip(ins[1:], held[1:])]
    copies = []
    for load, rows in zip(loads, parts):
        load.wait()
        wide[rows] = held[0][rows].astype(F32)
        copies.append(local.start(wide.at[rows], outs[0].at[rows]))
    for load, src, dst in zip(others, held[1:], outs[1:]):
        load.wait()
        copies.append(local.start(src, dst))
    for copy in copies:
        copy.wait()


def hand_over(arrays):
    kinds = [F32] + [array.dtype for array in arrays[1:]]
    return pl.pallas_call(
        hand_over_kernel,
        out_shape=[shape(array.shape, kind) for array, kind in zip(arrays, kinds)],
        in_specs=[HBM] * len(arrays),
        out_specs=[HBM] * len(arrays),
        scratch_shapes=[pltpu.VMEM(array.shape, array.dtype) for array in arrays]
        + [pltpu.VMEM((ROWS, D), F32), dma(2 * len(arrays) + 6)],
        compiler_params=pltpu.CompilerParams(vmem_limit_bytes=VMEM_LIMIT),
    )(*arrays)


def local(
    tokens,
    group_ids,
    gain_one,
    lin_query,
    lin_key,
    lin_value,
    lin_output,
    gain_two,
    win_query,
    win_key,
    win_value,
    win_output,
    gain_three,
    mlp_gate,
    mlp_up,
    mlp_down,
    out_grad,
):
    first, second, vectors = feature_tables()
    inputs = Inputs(
        tokens=tokens,
        group_row=group_ids.reshape(1, ROWS),
        gain_one=gain_one.reshape(1, D),
        gain_two=gain_two.reshape(1, D),
        gain_three=gain_three.reshape(1, D),
        first=first,
        second=second,
        vectors=vectors,
    )
    weights = Weights(
        out_grad=out_grad,
        w_query=lin_query.T,
        w_key=lin_key.T,
        w_value=lin_value,
        w_out=lin_output,
        win_k=win_key,
        win_v=win_value,
        win_q=win_query,
        win_out=win_output,
        w_gate=mlp_gate.T,
        w_up=mlp_up.T,
        w_down=mlp_down,
    )
    saved = forward(inputs, weights)
    outs = BackOuts(*backward(saved, inputs, weights))
    outs = BackOuts(*hand_over([*outs]))
    return (
        outs.result,
        outs.tokens_low,
        outs.gain_one.reshape(TILE),
        outs.query.T,
        outs.key.T,
        outs.value,
        outs.out,
        outs.gain_two.reshape(TILE),
        outs.win_q,
        outs.win_k,
        outs.win_v,
        outs.win_out,
        outs.gain_three.reshape(TILE),
        outs.gate.T,
        outs.up.T,
        outs.down,
    )


def solution(mesh):
    return jax.shard_map(
        local,
        mesh=mesh,
        in_specs=(
            P("seq", None),
            P("seq"),
            P(),
            P(None, "mp"),
            P(None, "mp"),
            P(None, "mp"),
            P("mp", None),
            P(),
            P(None, "mp"),
            P(None, "mp"),
            P(None, "mp"),
            P("mp", None),
            P(),
            P(None, "mp"),
            P(None, "mp"),
            P("mp", None),
            P("seq", None),
        ),
        out_specs=(
            P("seq", None),
            P("seq", None),
            P("seq"),
            P("seq", "mp"),
            P("seq", "mp"),
            P("seq", "mp"),
            P("mp", "seq"),
            P("seq"),
            P("seq", "mp"),
            P("seq", "mp"),
            P("seq", "mp"),
            P("mp", "seq"),
            P("seq"),
            P("seq", "mp"),
            P("seq", "mp"),
            P("mp", "seq"),
        ),
        check_vma=False,
    )
```

```python
import functools
import types
from typing import Any, NamedTuple

import jax
import jax.numpy as jnp
import numpy as np
from jax import lax
from jax.experimental import pallas as pl
from jax.experimental.pallas import tpu as pltpu
from jax.sharding import PartitionSpec as P

D = 2048
HD = 128
FEAT = 16
WIN = 64
FF = 704
FF_PAD = 768
ROWS = 512
TILE = 128
WIDE = 256
FEATURES = 160
STATE = FEATURES + 16

CHUNKS = 4
CHUNK = ROWS // CHUNKS
HALF = CHUNK // 2
PIECE = CHUNK // 8
OWN = 64
COLS = D // 2
PER_CHUNK = 21

EPSILON = 1e-05
MESH = pl.DeviceIdType.MESH
BF = jnp.bfloat16
F32 = jnp.float32
VMEM_LIMIT = 63 * 1024 * 1024 + 512 * 1024


class Place:
    def __init__(self):
        self.seq = lax.axis_index("seq")
        self.mp = lax.axis_index("mp")
        self.z, self.y = self.seq // 4, self.seq % 4
        self.x, self.core = self.mp // 2, self.mp % 2

    def peer(self):
        return (self.seq, self.x * 2 + (1 - self.core))

    def on_x(self, step):
        return (self.seq, ((self.x + step) % 4) * 2 + self.core)

    def on_y(self, step):
        return (self.z * 4 + (self.y + step) % 4, self.mp)

    def on_z(self, step):
        return (((self.z + step) % 4) * 4 + self.y, self.mp)

    def along(self, step):
        return ((self.seq + step) % 16, self.mp)


class Copies:
    def __init__(self, send_sems, recv_sems):
        self.send_sems, self.recv_sems = send_sems, recv_sems
        self.count, self.started = 0, []

    def start(self, src, dst, device):
        k = self.count
        self.count += 1
        copy = pltpu.make_async_remote_copy(
            src_ref=src,
            dst_ref=dst,
            send_sem=self.send_sems.at[k],
            recv_sem=self.recv_sems.at[k],
            device_id=device,
            device_id_type=MESH,
        )
        copy.start()
        self.started.append(copy)
        return copy

    def finish(self):
        for copy in self.started:
            copy.wait_send()


class Locals:
    def __init__(self, sems):
        self.sems, self.count = sems, 0

    def start(self, src, dst):
        copy = pltpu.make_async_copy(src, dst, self.sems.at[self.count])
        self.count += 1
        copy.start()
        return copy


def greet(devices):
    barrier = pltpu.get_barrier_semaphore()
    for device in devices:
        pl.semaphore_signal(barrier, inc=1, device_id=device, device_id_type=MESH)


def meet(count):
    pl.semaphore_wait(pltpu.get_barrier_semaphore(), count)


def rows_at(start, size):
    return pl.ds(pl.multiple_of(start, 16), size)


def dot(left, right):
    return lax.dot_general(left, right, (((1,), (0,)), ((), ())), preferred_element_type=F32)


def dot_nt(left, right):
    return lax.dot_general(left, right, (((1,), (1,)), ((), ())), preferred_element_type=F32)


def dot_tn(left, right):
    return lax.dot_general(left, right, (((0,), (0,)), ((), ())), preferred_element_type=F32)


def halves(values):
    high = values.astype(BF)
    return high, (values - high.astype(F32)).astype(BF)


class MpSum:
    def __init__(self, place, sems, part, full, own, bufs, lag=(0,) * CHUNKS, order=tuple(range(CHUNKS)), hold=False):
        self.place, self.part, self.full, self.own = place, part, full, own
        self.lag, self.order, self.hold = lag, order, hold
        self.send_sems, self.recv_sems = sems
        (self.from_peer, self.send_opp, self.send_right, self.send_left) = bufs[:4]
        (self.fwd, self.direct, self.comb) = bufs[4:]
        x = place.x
        self.turn = [(x + 2) % 4, (x + 1) % 4, (x + 3) % 4, x]
        self.peer, self.right, self.left = place.peer(), place.on_x(1), place.on_x(3)
        self.live = [types.SimpleNamespace(sent=[]) for _ in range(CHUNKS)]

    def start(self, j, src, dst, device):
        k = j * PER_CHUNK + len(self.live[j].sent)
        copy = pltpu.make_async_remote_copy(
            src_ref=src,
            dst_ref=dst,
            send_sem=self.send_sems.at[k],
            recv_sem=self.recv_sems.at[k],
            device_id=device,
            device_id_type=MESH,
        )
        copy.start()
        self.live[j].sent.append(copy)
        return copy

    def rows(self, j, core, x):
        return rows_at(j * CHUNK + core * HALF + x * PIECE, PIECE)

    def own_rows(self, j):
        return self.rows(j, self.place.core, self.place.x)

    def chip_sum(self, j, slot, low, size):
        cols = pl.ds(low, size)
        return self.part[self.rows(j, self.place.core, self.turn[slot]), cols].astype(
            F32
        ) + self.from_peer[j, slot, :, cols].astype(F32)

    def exchange(self, j):
        self.live[j].ex = [
            self.start(
                j,
                self.part.at[self.rows(j, 1 - self.place.core, at)],
                self.from_peer.at[j, slot],
                self.peer,
            )
            for slot, at in enumerate(self.turn)
        ]

    def first(self, j):
        live = self.live[j]
        low, high = pl.ds(0, COLS), pl.ds(COLS, COLS)
        live.ex[0].wait_recv()
        self.send_opp[j] = self.chip_sum(j, 0, 0, D).astype(BF)
        live.fr = self.start(j, self.send_opp.at[j, :, low], self.fwd.at[j, 0], self.right)
        live.fl = self.start(j, self.send_opp.at[j, :, high], self.fwd.at[j, 1], self.left)
        live.ex[1].wait_recv()
        self.send_right[j, 0] = self.chip_sum(j, 1, COLS, COLS).astype(BF)
        live.dr = self.start(j, self.send_right.at[j, 0], self.direct.at[j, 1], self.right)
        live.ex[2].wait_recv()
        self.send_left[j, 0] = self.chip_sum(j, 2, 0, COLS).astype(BF)
        live.dl = self.start(j, self.send_left.at[j, 0], self.direct.at[j, 0], self.left)

    def second(self, j):
        live = self.live[j]
        live.fr.wait_recv()
        self.send_right[j, 1] = (
            self.chip_sum(j, 1, 0, COLS) + self.fwd[j, 0].astype(F32)
        ).astype(BF)
        live.cr = self.start(j, self.send_right.at[j, 1], self.comb.at[j, 0], self.right)
        live.fl.wait_recv()
        self.send_left[j, 1] = (
            self.chip_sum(j, 2, COLS, COLS) + self.fwd[j, 1].astype(F32)
        ).astype(BF)
        live.cl = self.start(j, self.send_left.at[j, 1], self.comb.at[j, 1], self.left)

    def total(self, j):
        live, mine = self.live[j], pl.ds(j * PIECE, PIECE)
        live.ex[3].wait_recv()
        live.dl.wait_recv()
        live.cr.wait_recv()
        self.own[mine, 0:COLS] = (
            self.chip_sum(j, 3, 0, COLS)
            + self.direct[j, 0].astype(F32)
            + self.comb[j, 0].astype(F32)
        )
        live.dr.wait_recv()
        live.cl.wait_recv()
        self.own[mine, COLS:D] = (
            self.chip_sum(j, 3, COLS, COLS)
            + self.direct[j, 1].astype(F32)
            + self.comb[j, 1].astype(F32)
        )
        for copy in live.ex:
            copy.wait_send()

    def send(self, j, at, low, size, device):
        block = self.full.at[self.rows(j, self.place.core, at), pl.ds(low, size)]
        return self.start(j, block, block, device)

    def spread(self, j):
        live, x = self.live[j], self.place.x
        live.rl = self.send(j, x, 0, COLS, self.right)
        live.lh = self.send(j, x, COLS, COLS, self.left)
        live.rh = self.send(j, x, COLS, COLS, self.right)
        live.ll = self.send(j, x, 0, COLS, self.left)
        live.peers = [self.send(j, x, 0, D, self.peer)]

    def relay(self, j):
        live, x = self.live[j], self.place.x
        live.rl.wait_recv()
        live.gr = self.send(j, (x + 3) % 4, 0, COLS, self.right)
        live.lh.wait_recv()
        live.gl = self.send(j, (x + 1) % 4, COLS, COLS, self.left)
        live.rh.wait_recv()
        live.peers.append(self.send(j, (x + 3) % 4, 0, D, self.peer))
        live.ll.wait_recv()
        live.peers.append(self.send(j, (x + 1) % 4, 0, D, self.peer))

    def last(self, j):
        live, x = self.live[j], self.place.x
        live.gr.wait_recv()
        live.peers.append(self.send(j, (x + 2) % 4, 0, COLS, self.peer))
        live.gl.wait_recv()
        live.peers.append(self.send(j, (x + 2) % 4, COLS, COLS, self.peer))

    def arrived(self, j):
        for copy in self.live[j].peers:
            copy.wait_recv()
        for copy in self.live[j].sent[4:]:
            copy.wait_send()

    def slots(self, produce, finish, ready=None):
        for slot in range(self.lag[-1] + (8 if self.hold else 7)):
            for position, j in enumerate(self.order):
                stage = slot - self.lag[position]
                if self.hold and stage >= 4:
                    if stage == 4:
                        self.spread(j)
                        continue
                    stage -= 1
                if stage == 0:
                    produce(j)
                    self.exchange(j)
                elif stage == 1:
                    self.first(j)
                elif stage == 2:
                    self.second(j)
                elif stage == 3:
                    self.total(j)
                    finish(j)
                    if not self.hold:
                        self.spread(j)
                elif stage == 4:
                    self.relay(j)
                elif stage == 5:
                    self.last(j)
                elif stage == 6:
                    self.arrived(j)
                    if ready is not None:
                        ready(j)
            yield slot


def mp_scratch():
    ring = pltpu.VMEM((CHUNKS, 2, PIECE, COLS), BF)
    return [pltpu.VMEM((CHUNKS, 4, PIECE, D), BF), pltpu.VMEM((CHUNKS, PIECE, D), BF)] + [ring] * 5


def dma(count):
    return pltpu.SemaphoreType.DMA((count,))


def run(slots):
    for _ in slots:
        pass


def norm_rows_of(total):
    row = lax.broadcasted_iota(jnp.int32, (16, TILE), 0)
    return jnp.where(row == 0, total[:, 0:TILE], jnp.where(row == 1, total[:, TILE:WIDE], 0.0))


class StateScan(NamedTuple):
    mine: Any = ((2, STATE, HD), BF)
    early: Any = ((2, 3, STATE, HD), BF)
    sent: Any = ((2, 2, STATE, HD), BF)
    late: Any = ((2, 3, STATE, HD), BF)


def state_scan(place, copies, bufs, states, norms, reverse):
    def counted(position, step):
        at = (position - step + 4) % 4
        reached = at > position if reverse else at < position
        return jnp.where(reached, 1.0, 0.0)

    def wider(step):
        to = (place.y + step) % 4
        return (to < place.y if reverse else to > place.y).astype(jnp.int32)

    def put(head, total):
        states[head, 0:FEATURES] = total[0:FEATURES]
        states[head, FEATURES:WIDE] = jnp.zeros((WIDE - FEATURES, HD), F32)
        norms[head, 0:1, 0:TILE] = total[FEATURES : FEATURES + 1]
        norms[head, 0:1, TILE:WIDE] = total[FEATURES + 1 : FEATURES + 2]

    steps = (1, 2, 3)
    over = [copies.start(bufs.mine.at[0], bufs.early.at[0, k - 1], place.on_y(k)) for k in steps]
    across = [copies.start(bufs.mine.at[1], bufs.early.at[1, k - 1], place.on_z(k)) for k in steps]
    yield
    total, before = bufs.mine[0].astype(F32), jnp.zeros((STATE, HD), F32)
    for k, copy in zip(steps, over):
        copy.wait_recv()
        part = bufs.early[0, k - 1].astype(F32)
        total, before = total + part, before + counted(place.y, k) * part
    bufs.sent[0, 0] = total.astype(BF)
    over = [copies.start(bufs.sent.at[0, 0], bufs.late.at[0, k - 1], place.on_z(k)) for k in steps]
    put(0, before)
    before = jnp.zeros((STATE, HD), F32)
    for k, copy in zip(steps, across):
        copy.wait_recv()
        before = before + counted(place.z, k) * bufs.early[1, k - 1].astype(F32)
    bufs.sent[1, 0] = before.astype(BF)
    bufs.sent[1, 1] = (before + bufs.mine[1].astype(F32)).astype(BF)
    across = [
        copies.start(bufs.sent.at[1, wider(k)], bufs.late.at[1, k - 1], place.on_y(k)) for k in steps
    ]
    put(1, before)
    yield
    for head, sent in enumerate((over, across)):
        total = jnp.zeros((STATE, HD), F32)
        for k, copy in zip(steps, sent):
            copy.wait_recv()
            part = bufs.late[head, k - 1].astype(F32)
            total = total + (counted(place.z, k) * part if head == 0 else part)
        states[head, 0:FEATURES] += total[0:FEATURES]
        norms[head, 0:1, 0:TILE] += total[FEATURES : FEATURES + 1]
        norms[head, 0:1, TILE:WIDE] += total[FEATURES + 1 : FEATURES + 2]
    yield


def feature_tables():
    pairs = [(a, b) for a in range(FEAT) for b in range(a, FEAT)]
    first = np.zeros((2, 2 * FEAT, WIDE), np.float32)
    second = np.zeros((2, 2 * FEAT, WIDE), np.float32)
    vectors = np.zeros((8, WIDE), np.float32)
    vectors[0, 0] = vectors[1, 0] = vectors[2, 0] = 1.0
    for a in range(FEAT):
        vectors[1, 1 + a] = 1.0
        vectors[2, 1 + a] = FEAT ** (-0.25)
        for h in range(2):
            first[h, h * FEAT + a, 1 + a] = 1.0
    for number, (a, b) in enumerate(pairs):
        at = 1 + FEAT + number
        vectors[2, at] = (1.0 if a == b else 2.0**0.5) * (2.0 * FEAT) ** (-0.5)
        for h in range(2):
            first[h, h * FEAT + a, at] = 1.0
            second[h, h * FEAT + b, at] = 1.0
    return jnp.asarray(first, BF), jnp.asarray(second, BF), jnp.asarray(vectors, F32)


def factors(head, values, first, second, vectors):
    high, low = values
    left = dot(high, first[head]) + dot(low, first[head]) + vectors[0:1]
    right = dot(high, second[head]) + dot(low, second[head]) + vectors[1:2]
    return left, right


def of_head(values, head):
    lane = lax.broadcasted_iota(jnp.int32, values.shape, 1)
    return jnp.where((lane >= head * FEAT) & (lane < (head + 1) * FEAT), values, jnp.zeros_like(values))


def products(head, query, key, rows, count):
    high, low = (of_head(part[rows], head) for part in query)
    key_high, key_low = (part[0:count] for part in key)
    return dot_nt(high, key_high) + dot_nt(low, key_high) + dot_nt(high, key_low)


def shape(dims, kind):
    return jax.ShapeDtypeStruct(dims, kind)


def normed(rows, gain):
    factor = lax.rsqrt(jnp.mean(rows * rows, axis=-1, keepdims=True) + EPSILON)
    return rows * factor * gain


def column(group_row, held):
    for k in range(ROWS // TILE):
        block = group_row[0:1, k * TILE : (k + 1) * TILE].astype(F32)
        held[k * TILE : (k + 1) * TILE] = jnp.broadcast_to(block, (TILE, TILE)).T


def kept_pairs(group_col, group_row, tile):
    count = (tile + 1) * TILE
    row = lax.broadcasted_iota(jnp.int32, (TILE, count), 0) + tile * TILE
    col = lax.broadcasted_iota(jnp.int32, (TILE, count), 1)
    groups = group_col[tile * TILE : (tile + 1) * TILE, 0:1]
    return (col <= row) & (groups == group_row[0:1, 0:count].astype(F32))


def weight_block(into, left_t, right, quarter):
    count = into.shape[2]
    block = dot(left_t[0:count], right[:, quarter * 512 : (quarter + 1) * 512]).astype(BF)
    for k in range(4):
        into[quarter, k] = block[:, k * TILE : (k + 1) * TILE]


def back_through_norm(resid, grad, normed_grad, gain):
    factor = lax.rsqrt(jnp.mean(resid * resid, axis=-1, keepdims=True) + EPSILON)
    unit = resid * factor
    scaled = normed_grad * gain
    total = grad + factor * (scaled - unit * jnp.mean(scaled * unit, axis=-1, keepdims=True))
    return total, jnp.sum(normed_grad * unit, axis=0, keepdims=True)


LAG_ONE = (0, 0, 0, 0)
LAG_FIVE = (0, 0, 0, 0)


class Inputs(NamedTuple):
    tokens: Any
    group_row: Any
    gain_one: Any
    gain_two: Any
    gain_three: Any
    first: Any
    second: Any
    vectors: Any


class Weights(NamedTuple):
    out_grad: Any = ((ROWS, D), BF)
    w_query: Any = ((2 * FEAT, D), BF)
    w_key: Any = ((2 * FEAT, D), BF)
    w_value: Any = ((D, WIDE), BF)
    w_out: Any = ((WIDE, D), BF)
    win_k: Any = ((D, WIDE), BF)
    win_v: Any = ((D, WIDE), BF)
    win_q: Any = ((D, WIDE), BF)
    win_out: Any = ((WIDE, D), BF)
    w_gate: Any = ((FF_PAD, D), BF)
    w_up: Any = ((FF_PAD, D), BF)
    w_down: Any = ((FF_PAD, D), BF)


class Saved(NamedTuple):
    normed_one: Any = ((ROWS, D), BF)
    query: Any = ((2, ROWS, 2 * FEAT), BF)
    key: Any = ((2, ROWS, 2 * FEAT), BF)
    value: Any = ((ROWS, WIDE), BF)
    carried: Any = ((2, WIDE, HD), F32)
    carried_norm: Any = ((2, 1, WIDE), F32)
    quotient: Any = ((ROWS, WIDE), F32)
    denominator: Any = ((2, ROWS, 1), F32)
    mixed_lin: Any = ((ROWS, WIDE), BF)
    resid_one: Any = ((OWN, D), F32)
    normed_two: Any = ((ROWS, D), BF)
    query_win: Any = ((ROWS, WIDE), BF)
    keys_all: Any = ((ROWS + WIN, WIDE), BF)
    values_all: Any = ((ROWS + WIN, WIDE), BF)
    probs: Any = ((2, ROWS, TILE), F32)
    mixed_win: Any = ((ROWS, WIDE), BF)
    resid_two: Any = ((OWN, D), F32)
    low_four: Any = ((ROWS, D), BF)
    grad_own: Any = ((OWN, D), F32)
    gain_sum: Any = ((8, D), F32)
    gate_sum: Any = ((4, 4, FF, TILE), BF)
    up_sum: Any = ((4, 4, FF, TILE), BF)
    down_sum: Any = ((4, 4, FF, TILE), BF)
    part_three: Any = ((ROWS, D), BF)


class ForwardWork(NamedTuple):
    part: Any = ((ROWS, D), BF)
    own: Any = ((OWN, D), F32)
    group_col: Any = ((ROWS, TILE), F32)
    tail_flag: Any = ((16, TILE), BF)
    halo_flag: Any = ((16, TILE), BF)
    query_feat: Any = ((2, ROWS, WIDE), BF)
    key_feat: Any = ((2, ROWS, WIDE), BF)
    normed_three: Any = ((ROWS, D), BF)
    hidden_grad: Any = ((ROWS, FF_PAD), F32)
    hidden: Any = ((ROWS, FF_PAD), BF)
    gate_low: Any = ((ROWS, FF_PAD), BF)
    up_low: Any = ((ROWS, FF_PAD), BF)
    flipped: Any = ((FF_PAD, ROWS), BF)


class SeqSum:
    def __init__(self, place, copies, blocks, out, bufs):
        self.place, self.copies, self.blocks, self.out = place, copies, blocks, out
        z, y = place.z, place.y
        quarter = self.quarter = blocks.shape[2] // 4
        ring_y, ring_z = (place.on_y(1), place.on_y(3)), (place.on_z(1), place.on_z(3))

        def pick_one(k, half):
            return blocks.at[:, (y + k) % 4, pl.ds(half * quarter, quarter)]

        def pick_two(k, half):
            return blocks.at[(z + k) % 4, :, pl.ds((2 + half) * quarter, quarter)]

        def pick_three(k, half):
            return blocks.at[(z + k) % 4, y, pl.ds(half * quarter, quarter)]

        def pick_four(k, half):
            return blocks.at[z, (y + k) % 4, pl.ds((2 + half) * quarter, quarter)]

        live = [types.SimpleNamespace() for _ in range(4)]
        self.early = ((ring_y, pick_one, bufs[0:3], live[0]), (ring_z, pick_two, bufs[3:6], live[1]))
        self.late = ((ring_z, pick_three, bufs[6:9], live[2]), (ring_y, pick_four, bufs[9:12], live[3]))

    def begin(self, rings):
        for (right, left), pick, (fwd, direct, comb), live in rings:
            live.fr = self.copies.start(pick(2, 0), fwd.at[0], right)
            live.fl = self.copies.start(pick(2, 1), fwd.at[1], left)
            live.dr = self.copies.start(pick(1, 1), direct.at[1], right)
            live.dl = self.copies.start(pick(3, 0), direct.at[0], left)

    def join(self, rings):
        for (right, left), pick, (fwd, direct, comb), live in rings:
            live.fr.wait_recv()
            block = pick(1, 0)
            block[...] = (block[...].astype(F32) + fwd[0].astype(F32)).astype(BF)
            live.cr = self.copies.start(block, comb.at[0], right)
            live.fl.wait_recv()
            block = pick(3, 1)
            block[...] = (block[...].astype(F32) + fwd[1].astype(F32)).astype(BF)
            live.cl = self.copies.start(block, comb.at[1], left)

    def total(self, ring, half):
        _, pick, (fwd, direct, comb), live = ring
        (live.cr if half == 0 else live.cl).wait_recv()
        total = pick(0, half)[...].astype(F32) + comb[half].astype(F32)
        if direct is None:
            return total
        (live.dl if half == 0 else live.dr).wait_recv()
        return total + direct[half].astype(F32)

    def fold(self, rings):
        for _, pick, (fwd, direct, _), live in rings:
            for copy, block, got in (
                (live.fr, pick(1, 0), fwd.at[0]),
                (live.fl, pick(3, 1), fwd.at[1]),
                (live.dl, pick(0, 0), direct.at[0]),
                (live.dr, pick(0, 1), direct.at[1]),
            ):
                copy.wait_recv()
                block[...] = (block[...].astype(F32) + got[...].astype(F32)).astype(BF)

    def pass_on(self, rings):
        for (right, left), pick, (_, _, comb), live in rings:
            live.cr = self.copies.start(pick(1, 0), comb.at[0], right)
            live.cl = self.copies.start(pick(3, 1), comb.at[1], left)

    def step(self, number):
        if number == 0 and self.early[0][2][1] is None:
            self.pass_on(self.early)
        elif number == 0:
            self.begin(self.early)
        elif number == 1:
            if self.early[0][2][1] is not None:
                self.join(self.early)
        elif number == 2:
            for ring in self.early:
                for half in range(2):
                    block = ring[1](0, half)
                    block[...] = self.total(ring, half).astype(BF)
            self.begin(self.late)
        elif number == 3:
            self.join(self.late)
        else:
            size = self.quarter
            for half in range(2):
                self.out[pl.ds(half * size, size)] = self.total(self.late[0], half)
                self.out[pl.ds((2 + half) * size, size)] = self.total(self.late[1], half)


def seq_scratch(width):
    early, late = (2, 4, width // 4, TILE), (2, width // 4, TILE)
    return [pltpu.VMEM(early, BF)] * 6 + [pltpu.VMEM(late, BF)] * 6


FOLDED = 2


def folded_scratch():
    late = pltpu.VMEM((2, FF // 4, TILE), BF)
    return [pltpu.VMEM((2, 4, FF // 4, TILE), BF)] * 2 + [late] * 6


def taker(refs):
    refs = list(refs)

    def take(kind):
        return kind(*[refs.pop(0) for _ in kind._fields])

    def some(count):
        return [refs.pop(0) for _ in range(count)]

    return take, some


def vmem(kind):
    return [pltpu.VMEM(*entry) for entry in kind()]


def forward_kernel(*refs):
    take, some = taker(refs)
    inputs, hbm_weights, hbm_saved = take(Inputs), take(Weights), take(Saved)
    weights, saved, work, scan_bufs = take(Weights), take(Saved), take(ForwardWork), take(StateScan)
    bufs = some(7)
    fold_bufs = [some(4) for _ in range(FOLDED)]
    fold_sems = some(2)
    mp_sems, (state_send, state_recv), (halo_send, halo_recv), (local_sems,) = (
        some(2),
        some(2),
        some(2),
        some(1),
    )
    place = Place()
    local = Locals(local_sems)
    loads = []
    for src, dst in zip(hbm_weights[1:], weights[1:]):
        loads.append(local.start(src, dst if src.shape == dst.shape else dst.at[pl.ds(0, FF)]))
    loads = Weights(local.start(hbm_weights.out_grad, weights.out_grad), *loads)
    saves = []

    def save(*pairs):
        for src, dst in pairs:
            saves.append(local.start(src, dst))

    greet(
        [place.peer()]
        + [place.on_x(k) for k in (1, 3)]
        + [place.on_y(k) for k in (1, 2, 3)]
        + [place.on_z(k) for k in (1, 2, 3)]
        + [place.along(1), place.along(15)]
    )
    for ref in (weights.w_gate, weights.w_up, weights.w_down):
        ref[FF:FF_PAD] = jnp.zeros((FF_PAD - FF, D), BF)
    tokens, group_row, group_col = inputs.tokens, inputs.group_row, work.group_col
    first, second, vectors = inputs.first, inputs.second, inputs.vectors
    scale = vectors[2:3]
    normed_one = saved.normed_one

    def norm_rows(i, _):
        rows = rows_at(i * 32, 32)
        normed_one[rows] = normed(tokens[rows].astype(F32), inputs.gain_one[...]).astype(BF)
        return 0

    lax.fori_loop(0, ROWS // 32, norm_rows, 0)
    save((normed_one, hbm_saved.normed_one))
    column(group_row, group_col)
    query, key, value = saved.query, saved.key, saved.value
    for load, weight, held in (
        (loads.w_key, weights.w_key, key),
        (loads.w_query, weights.w_query, query),
    ):
        load.wait()
        held[0], held[1] = halves(dot_nt(normed_one[...], weight[...]))
    loads.w_value.wait()
    value[...] = dot(normed_one[...], weights.w_value[...]).astype(BF)

    last = group_row[0:1, ROWS - 1 : ROWS].astype(F32)
    in_last = (group_col[:, 0:1] == last).astype(F32)
    query_feat, key_feat, mine = work.query_feat, work.key_feat, scan_bufs.mine
    for head in range(2):
        left, right = factors(head, (key[0], key[1]), first, second, vectors)
        feat = (left * right * scale).astype(BF)
        key_feat[head] = feat
        kept = feat.astype(F32) * in_last
        state = dot_tn(kept.astype(BF), value[:, head * HD : (head + 1) * HD])
        mine[head, 0:FEATURES] = state[0:FEATURES].astype(BF)
        mine[head, FEATURES:STATE] = norm_rows_of(jnp.sum(kept, axis=0, keepdims=True)).astype(BF)
    meet(11)
    copies_state = Copies(state_send, state_recv)
    scan = state_scan(place, copies_state, scan_bufs, saved.carried, saved.carried_norm, False)
    next(scan)
    save((query, hbm_saved.query), (key, hbm_saved.key), (value, hbm_saved.value))
    quotient, denominator = saved.quotient, saved.denominator
    for head in range(2):
        left, right = factors(head, (query[0], query[1]), first, second, vectors)
        query_feat[head] = (left * right * scale).astype(BF)
    for tile in range(ROWS // TILE):
        rows, count = pl.ds(tile * TILE, TILE), (tile + 1) * TILE
        kept = kept_pairs(group_col, group_row, tile)
        for head in range(2):
            inner = products(head, (query.at[0], query.at[1]), (key.at[0], key.at[1]), rows, count)
            block = jnp.where(kept, 1.0 + inner * 0.25 + inner * inner * 0.03125, 0.0).astype(BF)
            denominator[head, rows] = jnp.sum(block.astype(F32), axis=1, keepdims=True)
            quotient[rows, head * HD : (head + 1) * HD] = dot(
                block, value[0:count, head * HD : (head + 1) * HD]
            )
        if tile == 1:
            next(scan)
    loads.w_down.wait()
    loads.out_grad.wait()
    work.hidden_grad[...] = dot_nt(weights.out_grad[...], weights.w_down[...])
    for _ in scan:
        pass
    copies_state.finish()
    first_group = group_row[0:1, 0:1].astype(F32)
    incoming = (group_col[:, 0:1] == first_group).astype(F32) * jnp.where(place.seq > 0, 1.0, 0.0)
    carried, carried_norm, mixed_lin = saved.carried, saved.carried_norm, saved.mixed_lin
    save((carried, hbm_saved.carried), (carried_norm, hbm_saved.carried_norm))
    for head in range(2):
        lanes = slice(head * HD, (head + 1) * HD)
        feat = query_feat[head]
        numer = quotient[:, lanes] + incoming * dot(feat, carried[head].astype(BF))
        denom = denominator[head] + incoming * jnp.sum(
            feat.astype(F32) * carried_norm[head], axis=1, keepdims=True
        )
        ratio = numer / denom
        denominator[head] = denom
        quotient[:, lanes] = ratio
        mixed_lin[:, lanes] = ratio.astype(BF)
    save(
        (quotient, hbm_saved.quotient),
        (denominator, hbm_saved.denominator),
        (mixed_lin, hbm_saved.mixed_lin),
    )
    loads.w_out.wait()

    part, own = work.part, work.own
    resid_one, resid_two = saved.resid_one, saved.resid_two
    normed_two, normed_three = saved.normed_two, work.normed_three
    sum_one = MpSum(place, mp_sems, part, normed_two, own, bufs, LAG_ONE, (3, 0, 1, 2))
    sum_two = MpSum(place, mp_sems, part, normed_three, own, bufs, (0, 1, 2, 3))
    sum_four = MpSum(place, mp_sems, part, saved.low_four, own, bufs, (0, 0, 2, 2))

    def produce_one(j):
        rows = pl.ds(j * CHUNK, CHUNK)
        part[rows] = dot(mixed_lin[rows], weights.w_out[...]).astype(BF)

    def finish_one(j):
        mine = pl.ds(j * PIECE, PIECE)
        rows = own[mine] + tokens[sum_one.own_rows(j)].astype(F32)
        resid_one[mine] = rows
        normed_two[sum_one.own_rows(j)] = normed(rows, inputs.gain_two[...]).astype(BF)

    query_win, keys_all, values_all = saved.query_win, saved.keys_all, saved.values_all
    copies_halo = Copies(halo_send, halo_recv)
    lane = lax.broadcasted_iota(jnp.int32, (1, TILE), 1)
    group_blocks = [group_row[0:1, k * TILE : (k + 1) * TILE].astype(F32) for k in range(4)]
    turned = [pltpu.roll(block, WIN, 1) for block in group_blocks]
    work.tail_flag[...] = jnp.broadcast_to((turned[3] == last).astype(F32), (16, TILE)).astype(BF)
    halo = []

    def ready_one(j):
        rows = pl.ds(j * CHUNK, CHUNK)
        below = pl.ds(WIN + j * CHUNK, CHUNK)
        if j == 3:
            for load in (loads.win_k, loads.win_v, loads.win_q):
                load.wait()
        keys_all[below] = dot(normed_two[rows], weights.win_k[...]).astype(BF)
        values_all[below] = dot(normed_two[rows], weights.win_v[...]).astype(BF)
        if j == 3:
            for ref in (keys_all, values_all):
                halo.append(
                    copies_halo.start(ref.at[pl.ds(ROWS, WIN)], ref.at[pl.ds(0, WIN)], place.along(1))
                )
            halo.append(copies_halo.start(work.tail_flag, work.halo_flag, place.along(1)))
        query_win[rows] = dot(normed_two[rows], weights.win_q[...]).astype(BF)
        if j != 3:
            next(two)

    probs, mixed_win = saved.probs, saved.mixed_win
    tile_row = lax.broadcasted_iota(jnp.int32, (WIN, TILE), 0)
    tile_col = lax.broadcasted_iota(jnp.int32, (WIN, TILE), 1)
    near = (tile_col > tile_row) & (tile_col <= tile_row + WIN)
    score_scale = HD ** (-0.5)

    def window_tile(t):
        rows = pl.ds(t * WIN, WIN)
        if t == 0:
            flag = jnp.where(place.seq > 0, work.halo_flag[0:1].astype(F32), 0.0)
            groups = jnp.where(lane < WIN, jnp.where(flag > 0.5, first_group, -2.0), turned[0])
        elif t % 2 == 1:
            groups = group_blocks[t // 2]
        else:
            groups = jnp.where(lane < WIN, turned[t // 2 - 1], turned[t // 2])
        kept = near & (group_col[rows] == groups)
        for head in range(2):
            lanes = slice(head * HD, (head + 1) * HD)
            scores = dot_nt(query_win[rows, lanes], keys_all[t * WIN : t * WIN + TILE, lanes])
            scores = jnp.where(kept, scores * score_scale, -1e30)
            exp_scores = jnp.exp(scores - jnp.max(scores, axis=1, keepdims=True))
            found = exp_scores / jnp.sum(exp_scores, axis=1, keepdims=True)
            probs[head, rows] = found
            mixed_win[rows, lanes] = dot(
                found.astype(BF), values_all[t * WIN : t * WIN + TILE, lanes]
            ).astype(BF)

    def produce_two(j):
        if j == 0:
            for copy in halo:
                copy.wait_recv()
            loads.win_out.wait()
        window_tile(2 * j)
        window_tile(2 * j + 1)
        rows = pl.ds(j * CHUNK, CHUNK)
        part[rows] = dot(mixed_win[rows], weights.win_out[...]).astype(BF)

    def finish_two(j):
        mine = pl.ds(j * PIECE, PIECE)
        rows = own[mine] + resid_one[mine]
        resid_two[mine] = rows
        normed_three[sum_two.own_rows(j)] = normed(rows, inputs.gain_three[...]).astype(BF)

    w_gate, w_up, w_down, og = weights.w_gate, weights.w_up, weights.w_down, weights.out_grad
    hidden, gate_low, up_low = work.hidden, work.gate_low, work.up_low

    def ready_two(j):
        if j % 2 == 0:
            return
        if j == 1:
            for load in (loads.w_gate, loads.w_up):
                load.wait()
        rows = pl.ds((j - 1) * CHUNK, 2 * CHUNK)
        gate = dot_nt(normed_three[rows], w_gate[...])
        up = dot_nt(normed_three[rows], w_up[...])
        sigmoid = 1.0 / (1.0 + jnp.exp(-gate))
        act, hidden_grad = gate * sigmoid, work.hidden_grad[rows]
        hidden[rows] = (act * up).astype(BF)
        up_low[rows] = (hidden_grad * act).astype(BF)
        gate_low[rows] = (hidden_grad * up * (sigmoid + act * (1.0 - sigmoid))).astype(BF)
        part[rows] = (dot(gate_low[rows], w_gate[...]) + dot(up_low[rows], w_up[...])).astype(BF)
        next(four)

    one = sum_one.slots(produce_one, finish_one, ready_one)
    two = sum_two.slots(produce_two, finish_two, ready_two)
    def finish_four(j):
        mine, rows = pl.ds(j * PIECE, PIECE), sum_four.own_rows(j)
        total, here = back_through_norm(
            resid_two[mine], og[rows].astype(F32), own[mine], inputs.gain_three[...]
        )
        saved.gain_sum[0:1] += here
        saved.grad_own[mine] = total
        saved.low_four[rows] = total.astype(BF)

    four = sum_four.slots(lambda j: None, finish_four)
    saved.gain_sum[...] = jnp.zeros_like(saved.gain_sum)
    run(one)
    copies_halo.finish()
    save(
        (resid_one, hbm_saved.resid_one),
        (normed_two, hbm_saved.normed_two),
        (query_win, hbm_saved.query_win),
        (keys_all, hbm_saved.keys_all),
        (values_all, hbm_saved.values_all),
    )
    for slot in two:
        if slot == 8:
            next(four)
    save(
        (probs, hbm_saved.probs), (mixed_win, hbm_saved.mixed_win), (resid_two, hbm_saved.resid_two)
    )

    def project_down(half):
        cols = pl.ds(half * 1024, 1024)
        saved.part_three[:, cols] = dot(hidden[...], w_down[:, cols]).astype(BF)
        if half == 1:
            save((saved.part_three, hbm_saved.part_three))

    seq_copies = Copies(*fold_sems)
    folds = []

    def weight_back(number, into, to_hbm, left, right, quarter):
        if quarter == 0:
            work.flipped[...] = left[...].T
        weight_block(into, work.flipped, right, quarter)
        if quarter < 3:
            return
        if number < FOLDED:
            fwd_y, direct_y, fwd_z, direct_z = fold_bufs[number]
            early = [fwd_y, direct_y, None, fwd_z, direct_z, None]
            seq_sum = SeqSum(place, seq_copies, into, None, early + [None] * 6)
            seq_sum.begin(seq_sum.early)
            folds.append((seq_sum, into, to_hbm))
        else:
            save((into, to_hbm))

    blocks = []
    for number, (into, to_hbm, left, right) in enumerate(
        (
            (saved.gate_sum, hbm_saved.gate_sum, gate_low, normed_three),
            (saved.up_sum, hbm_saved.up_sum, up_low, normed_three),
            (saved.down_sum, hbm_saved.down_sum, hidden, og),
        )
    ):
        blocks += [
            functools.partial(weight_back, number, into, to_hbm, left, right, k) for k in range(4)
        ]
    blocks += [functools.partial(project_down, k) for k in range(2)]
    for _ in four:
        for _ in range(3):
            if blocks:
                blocks.pop(0)()
    save(
        (saved.low_four, hbm_saved.low_four),
        (saved.grad_own, hbm_saved.grad_own),
        (saved.gain_sum, hbm_saved.gain_sum),
    )
    for block in blocks:
        block()
    for seq_sum, into, to_hbm in folds:
        seq_sum.fold(seq_sum.early)
        save((into, to_hbm))
    seq_copies.finish()
    for copy in saves:
        copy.wait()


HBM = pl.BlockSpec(memory_space=pl.ANY)
INSIDE = pl.BlockSpec(memory_space=pltpu.VMEM)


def forward(inputs, weights):
    scratch = vmem(Weights) + vmem(Saved) + vmem(ForwardWork) + vmem(StateScan) + mp_scratch()
    scratch += [pltpu.VMEM((2, 4, FF // 4, TILE), BF)] * (4 * FOLDED) + [dma(8 * FOLDED)] * 2
    scratch += [dma(CHUNKS * PER_CHUNK)] * 2 + [dma(12)] * 2 + [dma(3)] * 2
    scratch += [dma(len(Weights._fields) + len(Saved._fields))]
    return Saved(
        *pl.pallas_call(
            forward_kernel,
            out_shape=[shape(dims, kind) for dims, kind in Saved()],
            in_specs=[INSIDE] * len(inputs) + [HBM] * len(weights),
            out_specs=[HBM] * len(Saved._fields),
            scratch_shapes=scratch,
            compiler_params=pltpu.CompilerParams(
                collective_id=0, has_side_effects=True, vmem_limit_bytes=VMEM_LIMIT
            ),
        )(*inputs, *weights)
    )


class Groups(NamedTuple):
    gate: Any = FF
    up: Any = FF
    down: Any = FF
    win_out: Any = WIDE
    win: Any = 3 * WIDE
    out: Any = WIDE
    lin: Any = WIDE + 4 * FEAT


class BackInputs(NamedTuple):
    group_row: Any
    gain_one: Any
    gain_two: Any
    first: Any
    second: Any
    vectors: Any


class BackHbm(NamedTuple):
    part_three: Any
    low_four: Any
    grad_own: Any
    gain_sum: Any
    tokens: Any
    normed_one: Any
    normed_two: Any
    gate_sum: Any
    up_sum: Any
    down_sum: Any
    w_query: Any
    w_key: Any
    w_value: Any
    w_out: Any
    win_q: Any
    win_k: Any
    win_v: Any
    win_out: Any


SPECS = Saved()


class BackSaved(NamedTuple):
    query: Any = SPECS.query
    key: Any = SPECS.key
    value: Any = SPECS.value
    carried: Any = SPECS.carried
    carried_norm: Any = SPECS.carried_norm
    quotient: Any = SPECS.quotient
    denominator: Any = SPECS.denominator
    mixed_lin: Any = SPECS.mixed_lin
    resid_one: Any = SPECS.resid_one
    query_win: Any = SPECS.query_win
    keys_all: Any = SPECS.keys_all
    values_all: Any = SPECS.values_all
    probs: Any = SPECS.probs
    mixed_win: Any = SPECS.mixed_win
    resid_two: Any = SPECS.resid_two


class BackOuts(NamedTuple):
    tokens_low: Any = ((ROWS, D), BF)
    gain_one: Any = ((1, TILE), F32)
    gain_two: Any = ((1, TILE), F32)
    gain_three: Any = ((1, TILE), F32)
    gate: Any = ((FF, TILE), F32)
    up: Any = ((FF, TILE), F32)
    down: Any = ((FF, TILE), F32)
    win_out: Any = ((WIDE, TILE), F32)
    out: Any = ((WIDE, TILE), F32)
    win_q: Any = ((TILE, WIDE), F32)
    win_k: Any = ((TILE, WIDE), F32)
    win_v: Any = ((TILE, WIDE), F32)
    value: Any = ((TILE, WIDE), F32)
    query: Any = ((2 * FEAT, TILE), F32)
    key: Any = ((2 * FEAT, TILE), F32)
    result: Any = ((ROWS, D), BF)


class BackWork(NamedTuple):
    part: Any = ((ROWS, D), BF)
    other_full: Any = ((ROWS, D), BF)
    own: Any = ((OWN, D), F32)
    grad_own: Any = ((OWN, D), F32)
    token_own: Any = ((OWN, D), BF)
    group_col: Any = ((ROWS, TILE), F32)
    normed_low: Any = ((ROWS, D), BF)
    w_query: Any = ((2 * FEAT, D), BF)
    w_key: Any = ((2 * FEAT, D), BF)
    w_out: Any = ((WIDE, D), BF)
    win_out: Any = ((WIDE, D), BF)
    w_win: Any = ((D, 3 * WIDE), BF)
    mixed_grad: Any = ((ROWS, WIDE), BF)
    keys_sum: Any = ((ROWS + WIN, WIDE), F32)
    values_sum: Any = ((ROWS + WIN, WIDE), F32)
    back_key: Any = ((2, WIN, WIDE), BF)
    back_value: Any = ((2, WIN, WIDE), BF)
    win_grads: Any = ((ROWS, 3 * WIDE), BF)
    flipped: Any = ((3 * WIDE, ROWS), BF)
    denom_grad: Any = ((2, ROWS, 1), F32)
    query_sum: Any = ((ROWS, 2 * FEAT), F32)
    key_sum: Any = ((ROWS, 2 * FEAT), F32)
    query_low: Any = ((ROWS, 2 * FEAT), BF)
    key_low: Any = ((ROWS, 2 * FEAT), BF)
    state_sum: Any = ((2, WIDE, HD), F32)
    norm_sum: Any = ((2, 1, WIDE), F32)
    gain_sums: Any = ((16, D), F32)
    gain_low: Any = ((16, D), BF)
    gain_z: Any = ((3, 16, 512), BF)
    gain_zz: Any = ((16, 512), BF)
    gain_y: Any = ((3, 16, TILE), BF)
    gain_x: Any = ((16, TILE), BF)
    gain_xx: Any = ((3, 16, TILE), BF)
    gain_p: Any = ((16, TILE), BF)
    gain_pp: Any = ((16, TILE), BF)
    sum_win: Any = ((3 * WIDE, TILE), F32)
    sum_lin: Any = ((WIDE + 4 * FEAT, TILE), F32)
    later: Any = ((2, WIDE, HD), F32)
    later_norm: Any = ((2, 1, WIDE), F32)


def backward_kernel(*refs):
    take, some = taker(refs)
    inputs, hbm, hbm_saved, outs = take(BackInputs), take(BackHbm), take(BackSaved), take(BackOuts)
    saved, blocks, work, scan_bufs = take(BackSaved), take(Groups), take(BackWork), take(StateScan)
    seq_bufs = []
    for number in range(len(Groups._fields)):
        if number < FOLDED:
            comb_y, comb_z, *late = some(8)
            seq_bufs.append([None, None, comb_y, None, None, comb_z] + late)
        else:
            seq_bufs.append(some(12))
    bufs, bufs_three = some(7), some(7)
    mp_sems, three_sems, (seq_send, seq_recv), (few_send, few_recv), (local_sems,) = (
        some(2),
        some(2),
        some(2),
        some(2),
        some(1),
    )
    place = Place()
    z, y = place.z, place.y
    local = Locals(local_sems)
    part, own, other_full, tokens_low = work.part, work.own, work.other_full, outs.tokens_low
    sum_three = MpSum(place, three_sems, part, outs.result, own, bufs_three, hold=True)
    sum_five = MpSum(place, mp_sems, part, other_full, own, bufs, LAG_FIVE)
    sum_six = MpSum(place, mp_sems, part, tokens_low, own, bufs)

    load_part = local.start(hbm.part_three, part)
    load_low = local.start(hbm.low_four, tokens_low)
    load_win_out = local.start(hbm.win_out, work.win_out)
    mlp_loads = [
        local.start(src, dst)
        for src, dst in ((hbm.gate_sum, blocks.gate), (hbm.up_sum, blocks.up), (hbm.down_sum, blocks.down))
    ]
    load_saved = BackSaved(*[local.start(src, dst) for src, dst in zip(hbm_saved, saved)])
    load_win = [
        local.start(src, work.w_win.at[:, pl.ds(k * WIDE, WIDE)])
        for k, src in enumerate((hbm.win_q, hbm.win_k, hbm.win_v))
    ]
    load_grad = local.start(hbm.grad_own, work.grad_own)
    load_gain = local.start(hbm.gain_sum, work.gain_sums.at[pl.ds(0, 8)])
    load_normed = local.start(hbm.normed_two, work.normed_low)
    load_lin = [
        local.start(src, dst)
        for src, dst in ((hbm.w_query, work.w_query), (hbm.w_key, work.w_key), (hbm.w_out, work.w_out))
    ]
    greet(
        [place.peer()]
        + [place.on_x(k) for k in (1, 2, 3)]
        + [place.on_y(k) for k in (1, 2, 3)]
        + [place.on_z(k) for k in (1, 2, 3)]
        + [place.along(1), place.along(15)]
    )
    seq_copies = Copies(seq_send, seq_recv)
    few = Copies(few_send, few_recv)
    finished = Groups(outs.gate, outs.up, outs.down, outs.win_out, work.sum_win, outs.out, work.sum_lin)
    seq_sums = Groups(
        *[
            SeqSum(place, seq_copies, block, out, bufs_here)
            for block, out, bufs_here in zip(blocks, finished, seq_bufs)
        ]
    )
    first, second, vectors = inputs.first, inputs.second, inputs.vectors
    scale = vectors[2:3]
    group_row, group_col = inputs.group_row, work.group_col
    column(group_row, group_col)
    last_group = group_row[0:1, ROWS - 1 : ROWS].astype(F32)
    first_group = group_row[0:1, 0:1].astype(F32)
    in_last = (group_col[:, 0:1] == last_group).astype(F32)
    after_first = jnp.where(place.seq > 0, 1.0, 0.0)
    work.gain_sums[8:16] = jnp.zeros((8, D), F32)

    def finish(mp_sum, number, resid, gain, to, j):
        mine = pl.ds(j * PIECE, PIECE)
        total, here = back_through_norm(
            resid[mine].astype(F32), work.grad_own[mine], own[mine], gain[...]
        )
        work.gain_sums[number : number + 1] += here
        work.grad_own[mine] = total
        to[mp_sum.own_rows(j)] = total.astype(BF)

    mixed_grad, keys_sum, values_sum, win_grads = (
        work.mixed_grad,
        work.keys_sum,
        work.values_sum,
        work.win_grads,
    )
    probs, query_win, keys_all, values_all = (
        saved.probs,
        saved.query_win,
        saved.keys_all,
        saved.values_all,
    )
    score_scale = HD ** (-0.5)
    back = []

    def window_back(t):
        rows, window = pl.ds(t * WIN, WIN), pl.ds(t * WIN, TILE)
        for head in range(2):
            lanes = slice(head * HD, (head + 1) * HD)
            grad_tile, held = mixed_grad[rows, lanes], probs[head, rows]
            probs_grad = dot_nt(grad_tile, values_all[window, lanes])
            score_low = (
                held * (probs_grad - jnp.sum(probs_grad * held, axis=1, keepdims=True))
            ).astype(BF)
            win_grads[rows, lanes] = (dot(score_low, keys_all[window, lanes]) * score_scale).astype(BF)
            for ref, found in (
                (keys_sum, dot_tn(score_low, query_win[rows, lanes]) * score_scale),
                (values_sum, dot_tn(held.astype(BF), grad_tile)),
            ):
                if t == 0:
                    ref[window, lanes] = found
                else:
                    ref[rows, lanes] += found[:WIN]
                    ref[pl.ds(t * WIN + WIN, WIN), lanes] = found[WIN:]
        if t == 0:
            for ref, to_send in ((keys_sum, work.back_key), (values_sum, work.back_value)):
                to_send[0] = ref[0:WIN].astype(BF)
                back.append(few.start(to_send.at[0], to_send.at[1], place.along(15)))

    def produce_five(j):
        rows = pl.ds(j * CHUNK, CHUNK)
        for k, (ref, got) in enumerate(((keys_sum, work.back_key), (values_sum, work.back_value))):
            lanes = slice((k + 1) * WIDE, (k + 2) * WIDE)
            if j < CHUNKS - 1:
                win_grads[rows, lanes] = ref[WIN + j * CHUNK : WIN + (j + 1) * CHUNK].astype(BF)
            else:
                win_grads[j * CHUNK : ROWS - WIN, lanes] = ref[WIN + j * CHUNK : ROWS].astype(BF)
                back[k].wait_recv()
                win_grads[ROWS - WIN : ROWS, lanes] = (
                    ref[ROWS : ROWS + WIN] + got[1].astype(F32)
                ).astype(BF)
        if j % 2 == 0:
            return
        rows = pl.ds((j - 1) * CHUNK, 2 * CHUNK)
        part[rows] = dot_nt(win_grads[rows], work.w_win[...]).astype(BF)

    def finish_five(j):
        if j == 0:
            load_saved.resid_one.wait()
            load_grad.wait()
            load_gain.wait()
        finish(sum_five, 1, saved.resid_one, inputs.gain_two, other_full, j)

    query, key, value, carried = saved.query, saved.key, saved.value, saved.carried
    numer_low, query_sum, key_sum, value_sum, value_low = (
        query_win,
        work.query_sum,
        work.key_sum,
        keys_sum,
        mixed_grad,
    )

    def through_features(head, parts, grad):
        left, right = parts
        scaled = grad * scale
        return dot_nt((scaled * right).astype(BF), first[head]) + dot_nt(
            (scaled * left).astype(BF), second[head]
        )

    def ready_five(j):
        rows = pl.ds(j * CHUNK, CHUNK)
        if j == 0:
            for load in load_lin:
                load.wait()
            for load in (
                load_saved.denominator,
                load_saved.quotient,
                load_saved.query,
                load_saved.key,
                load_saved.value,
                load_saved.carried,
                load_saved.carried_norm,
            ):
                load.wait()
        mixed = dot_nt(other_full[rows], work.w_out[...]).astype(BF).astype(F32)
        incoming = (group_col[rows, 0:1] == first_group).astype(F32) * after_first
        for head in range(2):
            lanes = slice(head * HD, (head + 1) * HD)
            denom = saved.denominator[head, rows]
            numer = (mixed[:, lanes] / denom).astype(BF)
            numer_low[rows, lanes] = numer
            denom_grad = (
                -jnp.sum(mixed[:, lanes] * saved.quotient[rows, lanes], axis=1, keepdims=True) / denom
            )
            work.denom_grad[head, rows] = denom_grad
            parts = factors(head, (query[0, rows], query[1, rows]), first, second, vectors)
            used = (parts[0] * parts[1] * scale).astype(BF).astype(F32) * incoming
            state = dot_tn(used.astype(BF), numer)
            norm = jnp.sum(used * denom_grad, axis=0, keepdims=True)
            if j == 0:
                work.state_sum[head], work.norm_sum[head] = state, norm
            else:
                work.state_sum[head] += state
                work.norm_sum[head] += norm
        if j == CHUNKS - 1:
            for head in range(2):
                scan_bufs.mine[head, 0:FEATURES] = work.state_sum[head, 0:FEATURES].astype(BF)
                scan_bufs.mine[head, FEATURES:STATE] = norm_rows_of(work.norm_sum[head]).astype(BF)

    def within(j):
        rows, count = pl.ds(j * CHUNK, CHUNK), (j + 1) * CHUNK
        incoming = (group_col[rows, 0:1] == first_group).astype(F32) * after_first
        kept = kept_pairs(group_col, group_row, j)
        key_new = []
        for head in range(2):
            lanes = slice(head * HD, (head + 1) * HD)
            numer, denom_grad = numer_low[rows, lanes], work.denom_grad[head, rows]
            parts = factors(head, (query[0, rows], query[1, rows]), first, second, vectors)
            grad = incoming * (
                dot_nt(numer, carried[head].astype(BF)) + denom_grad * saved.carried_norm[head]
            )
            query_new = through_features(head, parts, grad)
            inner = products(head, (query.at[0], query.at[1]), (key.at[0], key.at[1]), rows, count)
            kernel = jnp.where(kept, 1.0 + inner * 0.25 + inner * inner * 0.03125, 0.0).astype(BF)
            grad = dot_nt(numer, value[0:count, lanes]) + denom_grad
            grad = jnp.where(kept, grad, 0.0).astype(BF).astype(F32)
            inner_grad = (grad * (0.25 + inner * 0.0625)).astype(BF)
            query_new = query_new + of_head(dot(inner_grad, key[0, 0:count]), head)
            if head == 0:
                query_sum[rows] = query_new
            else:
                query_sum[rows] += query_new
            key_new.append(of_head(dot_tn(inner_grad, query[0, rows]), head))
            found = dot_tn(kernel, numer)
            if j > 0:
                value_sum[0 : count - CHUNK, lanes] += found[0 : count - CHUNK]
            value_sum[count - CHUNK : count, lanes] = found[count - CHUNK : count]
        found = key_new[0] + key_new[1]
        if j > 0:
            key_sum[0 : count - CHUNK] += found[0 : count - CHUNK]
        key_sum[count - CHUNK : count] = found[count - CHUNK : count]

    def weight_task(block, right, quarter):
        weight_block(block, work.flipped, right, quarter)

    def begin(group):
        group.step(0)

    def turn_mixed(ref, load):
        load.wait()
        work.flipped[0:WIDE] = ref[...].T

    def turn_win():
        load_normed.wait()
        for k in range(3):
            rows = slice(k * WIDE, (k + 1) * WIDE)
            work.flipped[rows] = win_grads[:, rows].T

    late_work = [lambda: turn_mixed(saved.mixed_win, load_saved.mixed_win)]
    late_work += [functools.partial(weight_task, blocks.win_out, tokens_low, k) for k in range(4)]
    late_work += [functools.partial(begin, seq_sums.win_out), turn_win]
    late_work += [functools.partial(weight_task, blocks.win, work.normed_low, k) for k in range(4)]
    late_work += [functools.partial(begin, seq_sums.win)]

    def steps(*names):
        for group, number in names:
            group.step(number)

    gate, up, down, win_out, win, out, lin = seq_sums
    def finish_three(j):
        mine = pl.ds(j * PIECE, PIECE)
        outs.result[sum_three.own_rows(j)] = (own[mine] + saved.resid_two[mine]).astype(BF)

    three = sum_three.slots(lambda j: None, finish_three)
    meet(12)
    load_part.wait()
    next(three)
    for load in (load_low, load_win_out):
        load.wait()
    mixed_grad[...] = dot_nt(tokens_low[...], work.win_out[...]).astype(BF)
    for load, group in zip(mlp_loads, (gate, up, down)):
        load.wait()
        group.step(0)
    next(three)
    for load in (load_saved.probs, load_saved.query_win, load_saved.keys_all, load_saved.values_all):
        load.wait()
    load_saved.resid_two.wait()
    for t in range(8):
        window_back(t)
        if t == 4:
            next(three)
    next(three)
    for load in load_win:
        load.wait()
    for j in range(0, CHUNKS, 2):
        produce_five(j)
        produce_five(j + 1)
    five = sum_five.slots(lambda j: None, finish_five, ready_five)
    plans = {2: [(gate, 2)], 3: [(down, 1)], 4: [(up, 2)], 6: [(down, 2)]}
    for slot in five:
        for _ in range(3):
            if late_work:
                late_work.pop(0)()
        steps(*plans.get(slot, ()))
    for block in late_work:
        block()
    scan = state_scan(place, few, scan_bufs, work.later, work.later_norm, True)
    next(scan)
    load_normed_one = local.start(hbm.normed_one, work.normed_low)
    load_value = local.start(hbm.w_value, work.w_win.at[:, pl.ds(0, WIDE)])
    load_token = [
        local.start(hbm.tokens.at[sum_six.own_rows(j)], work.token_own.at[pl.ds(j * PIECE, PIECE)])
        for j in range(CHUNKS)
    ]
    next(three)
    turn_mixed(saved.mixed_lin, load_saved.mixed_lin)
    for k in range(4):
        weight_task(blocks.out, other_full, k)
    steps((out, 0), (gate, 3))
    within(0)
    next(scan)
    next(three)
    within(1)
    steps((win_out, 1))
    within(2)
    within(3)
    for _ in scan:
        pass
    next(three)
    for head in range(2):
        lanes = slice(head * HD, (head + 1) * HD)
        state = work.later[head].astype(BF)
        parts = factors(head, (key[0], key[1]), first, second, vectors)
        feat = (parts[0] * parts[1] * scale).astype(BF)
        grad = in_last * (dot_nt(value[:, lanes], state) + work.later_norm[head])
        key_sum[...] += through_features(head, parts, grad)
        value_sum[0:ROWS, lanes] += in_last * dot(feat, state)
    work.query_low[...] = query_sum[...].astype(BF)
    work.key_low[...] = key_sum[...].astype(BF)
    value_low[...] = value_sum[0:ROWS].astype(BF)
    load_value.wait()

    def produce_six(j):
        rows = pl.ds(j * CHUNK, CHUNK)
        part[rows] = (
            dot_nt(value_low[rows], work.w_win[:, 0:WIDE])
            + dot(work.query_low[rows], work.w_query[...])
            + dot(work.key_low[rows], work.w_key[...])
        ).astype(BF)

    for load in load_token:
        load.wait()

    def finish_six(j):
        finish(sum_six, 2, work.token_own, inputs.gain_one, tokens_low, j)

    def gains():
        work.gain_low[...] = work.gain_sums[...].astype(BF)

        def block(ref, at, size):
            return ref.at[:, pl.ds(pl.multiple_of(at * size, TILE), size)]

        over = [
            few.start(block(work.gain_low, (z + k) % 4, 512), work.gain_z.at[k - 1], place.on_z(k))
            for k in (1, 2, 3)
        ]
        yield
        total = block(work.gain_low, z, 512)[...].astype(F32)
        for k, copy in enumerate(over):
            copy.wait_recv()
            total = total + work.gain_z[k].astype(F32)
        work.gain_zz[...] = total.astype(BF)
        over = [
            few.start(block(work.gain_zz, (y + k) % 4, TILE), work.gain_y.at[k - 1], place.on_y(k))
            for k in (1, 2, 3)
        ]
        yield
        total = block(work.gain_zz, y, TILE)[...].astype(F32)
        for k, copy in enumerate(over):
            copy.wait_recv()
            total = total + work.gain_y[k].astype(F32)
        work.gain_x[...] = total.astype(BF)
        over = [few.start(work.gain_x, work.gain_xx.at[k - 1], place.on_x(k)) for k in (1, 2, 3)]
        yield
        total = work.gain_x[...].astype(F32)
        for k, copy in enumerate(over):
            copy.wait_recv()
            total = total + work.gain_xx[k].astype(F32)
        work.gain_p[...] = total.astype(BF)
        copy = few.start(work.gain_p, work.gain_pp, place.peer())
        yield
        copy.wait_recv()
        total = work.gain_p[...].astype(F32) + work.gain_pp[...].astype(F32)
        for k, ref in enumerate((outs.gain_three, outs.gain_two, outs.gain_one)):
            ref[...] = total[k : k + 1]

    def turn_lin():
        load_normed_one.wait()
        work.flipped[0:WIDE] = value_low[...].T
        for k, ref in enumerate((query_sum, key_sum)):
            at = WIDE + 2 * FEAT * k
            wide = jnp.concatenate([ref[...], jnp.zeros((ROWS, TILE - 2 * FEAT), F32)], axis=1)
            work.flipped[at : at + 2 * FEAT] = wide.T[0 : 2 * FEAT].astype(BF)

    six = sum_six.slots(produce_six, finish_six)
    next(six)
    next(three)
    steps((up, 3), (win, 1))
    turn_lin()
    for k in range(4):
        weight_task(blocks.lin, work.normed_low, k)
    steps((lin, 0))
    plans = {
        1: [(out, 1), (down, 3), (win_out, 2)],
        2: [(gate, 4), (up, 4), (win, 2)],
        3: [(lin, 1), (out, 2), (down, 4)],
        4: [(lin, 2), (win_out, 3)],
        5: [(win, 3), (out, 3), (lin, 3)],
        6: [(win_out, 4), (win, 4), (out, 4)],
    }
    gain_steps = gains()
    for slot in six:
        if slot >= 3:
            next(gain_steps, None)
        steps(*plans.get(slot, ()))
    steps((lin, 4))
    for k, ref in enumerate((outs.win_q, outs.win_k, outs.win_v)):
        ref[...] = work.sum_win[k * WIDE : (k + 1) * WIDE].T
    outs.value[...] = work.sum_lin[0:WIDE].T
    outs.query[...] = work.sum_lin[WIDE : WIDE + 2 * FEAT]
    outs.key[...] = work.sum_lin[WIDE + 2 * FEAT : WIDE + 4 * FEAT]
    for _ in gain_steps:
        pass
    seq_copies.finish()
    few.finish()


def backward(saved, inputs, weights):
    back_inputs = BackInputs(*[getattr(inputs, name) for name in BackInputs._fields])
    hbm = BackHbm(
        part_three=saved.part_three,
        low_four=saved.low_four,
        grad_own=saved.grad_own,
        gain_sum=saved.gain_sum,
        tokens=inputs.tokens,
        normed_one=saved.normed_one,
        normed_two=saved.normed_two,
        gate_sum=saved.gate_sum,
        up_sum=saved.up_sum,
        down_sum=saved.down_sum,
        w_query=weights.w_query,
        w_key=weights.w_key,
        w_value=weights.w_value,
        w_out=weights.w_out,
        win_q=weights.win_q,
        win_k=weights.win_k,
        win_v=weights.win_v,
        win_out=weights.win_out,
    )
    held = BackSaved(*[getattr(saved, name) for name in BackSaved._fields])
    scratch = vmem(BackSaved) + [pltpu.VMEM((4, 4, width, TILE), BF) for width in Groups()]
    scratch += vmem(BackWork) + vmem(StateScan)
    for number, width in enumerate(Groups()):
        scratch += folded_scratch() if number < FOLDED else seq_scratch(width)
    scratch += mp_scratch() * 2
    scratch += [dma(CHUNKS * PER_CHUNK)] * 4 + [dma(24 * len(Groups._fields))] * 2 + [dma(24)] * 2
    scratch += [dma(64)]
    return BackOuts(
        *pl.pallas_call(
            backward_kernel,
            out_shape=[shape(dims, kind) for dims, kind in BackOuts()],
            in_specs=[INSIDE] * len(back_inputs) + [HBM] * (len(hbm) + len(held)),
            out_specs=[INSIDE] * len(BackOuts._fields),
            scratch_shapes=scratch,
            compiler_params=pltpu.CompilerParams(
                collective_id=1, has_side_effects=True, vmem_limit_bytes=VMEM_LIMIT
            ),
        )(*back_inputs, *hbm, *held)
    )


def hand_over_kernel(*refs):
    count = (len(refs) - 2) // 3
    ins, outs, held = refs[:count], refs[count : 2 * count], refs[2 * count : 3 * count]
    wide, sems = refs[3 * count :]
    block = ROWS // 4
    local = Locals(sems)
    parts = [pl.ds(k * block, block) for k in range(4)]
    loads = [local.start(ins[0].at[rows], held[0].at[rows]) for rows in parts]
    others = [local.start(src, dst) for src, dst in zip(ins[1:], held[1:])]
    copies = []
    for load, rows in zip(loads, parts):
        load.wait()
        wide[rows] = held[0][rows].astype(F32)
        copies.append(local.start(wide.at[rows], outs[0].at[rows]))
    for load, src, dst in zip(others, held[1:], outs[1:]):
        load.wait()
        copies.append(local.start(src, dst))
    for copy in copies:
        copy.wait()


def hand_over(arrays):
    kinds = [F32] + [array.dtype for array in arrays[1:]]
    return pl.pallas_call(
        hand_over_kernel,
        out_shape=[shape(array.shape, kind) for array, kind in zip(arrays, kinds)],
        in_specs=[HBM] * len(arrays),
        out_specs=[HBM] * len(arrays),
        scratch_shapes=[pltpu.VMEM(array.shape, array.dtype) for array in arrays]
        + [pltpu.VMEM((ROWS, D), F32), dma(2 * len(arrays) + 6)],
        compiler_params=pltpu.CompilerParams(vmem_limit_bytes=VMEM_LIMIT),
    )(*arrays)


def local(
    tokens,
    group_ids,
    gain_one,
    lin_query,
    lin_key,
    lin_value,
    lin_output,
    gain_two,
    win_query,
    win_key,
    win_value,
    win_output,
    gain_three,
    mlp_gate,
    mlp_up,
    mlp_down,
    out_grad,
):
    first, second, vectors = feature_tables()
    inputs = Inputs(
        tokens=tokens,
        group_row=group_ids.reshape(1, ROWS),
        gain_one=gain_one.reshape(1, D),
        gain_two=gain_two.reshape(1, D),
        gain_three=gain_three.reshape(1, D),
        first=first,
        second=second,
        vectors=vectors,
    )
    weights = Weights(
        out_grad=out_grad,
        w_query=lin_query.T,
        w_key=lin_key.T,
        w_value=lin_value,
        w_out=lin_output,
        win_k=win_key,
        win_v=win_value,
        win_q=win_query,
        win_out=win_output,
        w_gate=mlp_gate.T,
        w_up=mlp_up.T,
        w_down=mlp_down,
    )
    saved = forward(inputs, weights)
    outs = BackOuts(*backward(saved, inputs, weights))
    outs = BackOuts(*hand_over([*outs]))
    return (
        outs.result,
        outs.tokens_low,
        outs.gain_one.reshape(TILE),
        outs.query.T,
        outs.key.T,
        outs.value,
        outs.out,
        outs.gain_two.reshape(TILE),
        outs.win_q,
        outs.win_k,
        outs.win_v,
        outs.win_out,
        outs.gain_three.reshape(TILE),
        outs.gate.T,
        outs.up.T,
        outs.down,
    )


def solution(mesh):
    return jax.shard_map(
        local,
        mesh=mesh,
        in_specs=(
            P("seq", None),
            P("seq"),
            P(),
            P(None, "mp"),
            P(None, "mp"),
            P(None, "mp"),
            P("mp", None),
            P(),
            P(None, "mp"),
            P(None, "mp"),
            P(None, "mp"),
            P("mp", None),
            P(),
            P(None, "mp"),
            P(None, "mp"),
            P("mp", None),
            P("seq", None),
        ),
        out_specs=(
            P("seq", None),
            P("seq", None),
            P("seq"),
            P("seq", "mp"),
            P("seq", "mp"),
            P("seq", "mp"),
            P("mp", "seq"),
            P("seq"),
            P("seq", "mp"),
            P("seq", "mp"),
            P("seq", "mp"),
            P("mp", "seq"),
            P("seq"),
            P("seq", "mp"),
            P("seq", "mp"),
            P("mp", "seq"),
        ),
        check_vma=False,
    )
```

```python
import functools
import types
from typing import Any, NamedTuple

import jax
import jax.numpy as jnp
import numpy as np
from jax import lax
from jax.experimental import pallas as pl
from jax.experimental.pallas import tpu as pltpu
from jax.sharding import PartitionSpec as P

D = 2048
HD = 128
FEAT = 16
WIN = 64
FF = 704
FF_PAD = 768
ROWS = 512
TILE = 128
WIDE = 256
FEATURES = 160
STATE = FEATURES + 16

CHUNKS = 4
CHUNK = ROWS // CHUNKS
HALF = CHUNK // 2
PIECE = CHUNK // 8
OWN = 64
COLS = D // 2
PER_CHUNK = 21

EPSILON = 1e-05
MESH = pl.DeviceIdType.MESH
BF = jnp.bfloat16
F32 = jnp.float32
VMEM_LIMIT = 63 * 1024 * 1024 + 512 * 1024


class Place:
    def __init__(self):
        self.seq = lax.axis_index("seq")
        self.mp = lax.axis_index("mp")
        self.z, self.y = self.seq // 4, self.seq % 4
        self.x, self.core = self.mp // 2, self.mp % 2

    def peer(self):
        return (self.seq, self.x * 2 + (1 - self.core))

    def on_x(self, step):
        return (self.seq, ((self.x + step) % 4) * 2 + self.core)

    def on_y(self, step):
        return (self.z * 4 + (self.y + step) % 4, self.mp)

    def on_z(self, step):
        return (((self.z + step) % 4) * 4 + self.y, self.mp)

    def along(self, step):
        return ((self.seq + step) % 16, self.mp)


class Copies:
    def __init__(self, send_sems, recv_sems):
        self.send_sems, self.recv_sems = send_sems, recv_sems
        self.count, self.started = 0, []

    def start(self, src, dst, device):
        k = self.count
        self.count += 1
        copy = pltpu.make_async_remote_copy(
            src_ref=src,
            dst_ref=dst,
            send_sem=self.send_sems.at[k],
            recv_sem=self.recv_sems.at[k],
            device_id=device,
            device_id_type=MESH,
        )
        copy.start()
        self.started.append(copy)
        return copy

    def finish(self):
        for copy in self.started:
            copy.wait_send()


class Locals:
    def __init__(self, sems):
        self.sems, self.count = sems, 0

    def start(self, src, dst):
        copy = pltpu.make_async_copy(src, dst, self.sems.at[self.count])
        self.count += 1
        copy.start()
        return copy


def greet(devices):
    barrier = pltpu.get_barrier_semaphore()
    for device in devices:
        pl.semaphore_signal(barrier, inc=1, device_id=device, device_id_type=MESH)


def meet(count):
    pl.semaphore_wait(pltpu.get_barrier_semaphore(), count)


def rows_at(start, size):
    return pl.ds(pl.multiple_of(start, 16), size)


def dot(left, right):
    return lax.dot_general(left, right, (((1,), (0,)), ((), ())), preferred_element_type=F32)


def dot_nt(left, right):
    return lax.dot_general(left, right, (((1,), (1,)), ((), ())), preferred_element_type=F32)


def dot_tn(left, right):
    return lax.dot_general(left, right, (((0,), (0,)), ((), ())), preferred_element_type=F32)


def halves(values):
    high = values.astype(BF)
    return high, (values - high.astype(F32)).astype(BF)


class MpSum:
    def __init__(self, place, sems, part, full, own, bufs, lag=(0,) * CHUNKS, order=tuple(range(CHUNKS)), hold=False):
        self.place, self.part, self.full, self.own = place, part, full, own
        self.lag, self.order, self.hold = lag, order, hold
        self.send_sems, self.recv_sems = sems
        (self.from_peer, self.send_opp, self.send_right, self.send_left) = bufs[:4]
        (self.fwd, self.direct, self.comb) = bufs[4:]
        x = place.x
        self.turn = [(x + 2) % 4, (x + 1) % 4, (x + 3) % 4, x]
        self.peer, self.right, self.left = place.peer(), place.on_x(1), place.on_x(3)
        self.live = [types.SimpleNamespace(sent=[]) for _ in range(CHUNKS)]

    def start(self, j, src, dst, device):
        k = j * PER_CHUNK + len(self.live[j].sent)
        copy = pltpu.make_async_remote_copy(
            src_ref=src,
            dst_ref=dst,
            send_sem=self.send_sems.at[k],
            recv_sem=self.recv_sems.at[k],
            device_id=device,
            device_id_type=MESH,
        )
        copy.start()
        self.live[j].sent.append(copy)
        return copy

    def rows(self, j, core, x):
        return rows_at(j * CHUNK + core * HALF + x * PIECE, PIECE)

    def own_rows(self, j):
        return self.rows(j, self.place.core, self.place.x)

    def chip_sum(self, j, slot, low, size):
        cols = pl.ds(low, size)
        return self.part[self.rows(j, self.place.core, self.turn[slot]), cols].astype(
            F32
        ) + self.from_peer[j, slot, :, cols].astype(F32)

    def exchange(self, j):
        self.live[j].ex = [
            self.start(
                j,
                self.part.at[self.rows(j, 1 - self.place.core, at)],
                self.from_peer.at[j, slot],
                self.peer,
            )
            for slot, at in enumerate(self.turn)
        ]

    def first(self, j):
        live = self.live[j]
        low, high = pl.ds(0, COLS), pl.ds(COLS, COLS)
        live.ex[0].wait_recv()
        self.send_opp[j] = self.chip_sum(j, 0, 0, D).astype(BF)
        live.fr = self.start(j, self.send_opp.at[j, :, low], self.fwd.at[j, 0], self.right)
        live.fl = self.start(j, self.send_opp.at[j, :, high], self.fwd.at[j, 1], self.left)
        live.ex[1].wait_recv()
        self.send_right[j, 0] = self.chip_sum(j, 1, COLS, COLS).astype(BF)
        live.dr = self.start(j, self.send_right.at[j, 0], self.direct.at[j, 1], self.right)
        live.ex[2].wait_recv()
        self.send_left[j, 0] = self.chip_sum(j, 2, 0, COLS).astype(BF)
        live.dl = self.start(j, self.send_left.at[j, 0], self.direct.at[j, 0], self.left)

    def second(self, j):
        live = self.live[j]
        live.fr.wait_recv()
        self.send_right[j, 1] = (
            self.chip_sum(j, 1, 0, COLS) + self.fwd[j, 0].astype(F32)
        ).astype(BF)
        live.cr = self.start(j, self.send_right.at[j, 1], self.comb.at[j, 0], self.right)
        live.fl.wait_recv()
        self.send_left[j, 1] = (
            self.chip_sum(j, 2, COLS, COLS) + self.fwd[j, 1].astype(F32)
        ).astype(BF)
        live.cl = self.start(j, self.send_left.at[j, 1], self.comb.at[j, 1], self.left)

    def total(self, j):
        live, mine = self.live[j], pl.ds(j * PIECE, PIECE)
        live.ex[3].wait_recv()
        live.dl.wait_recv()
        live.cr.wait_recv()
        self.own[mine, 0:COLS] = (
            self.chip_sum(j, 3, 0, COLS)
            + self.direct[j, 0].astype(F32)
            + self.comb[j, 0].astype(F32)
        )
        live.dr.wait_recv()
        live.cl.wait_recv()
        self.own[mine, COLS:D] = (
            self.chip_sum(j, 3, COLS, COLS)
            + self.direct[j, 1].astype(F32)
            + self.comb[j, 1].astype(F32)
        )
        for copy in live.ex:
            copy.wait_send()

    def send(self, j, at, low, size, device):
        block = self.full.at[self.rows(j, self.place.core, at), pl.ds(low, size)]
        return self.start(j, block, block, device)

    def spread(self, j):
        live, x = self.live[j], self.place.x
        live.rl = self.send(j, x, 0, COLS, self.right)
        live.lh = self.send(j, x, COLS, COLS, self.left)
        live.rh = self.send(j, x, COLS, COLS, self.right)
        live.ll = self.send(j, x, 0, COLS, self.left)
        live.peers = [self.send(j, x, 0, D, self.peer)]

    def relay(self, j):
        live, x = self.live[j], self.place.x
        live.rl.wait_recv()
        live.gr = self.send(j, (x + 3) % 4, 0, COLS, self.right)
        live.lh.wait_recv()
        live.gl = self.send(j, (x + 1) % 4, COLS, COLS, self.left)
        live.rh.wait_recv()
        live.peers.append(self.send(j, (x + 3) % 4, 0, D, self.peer))
        live.ll.wait_recv()
        live.peers.append(self.send(j, (x + 1) % 4, 0, D, self.peer))

    def last(self, j):
        live, x = self.live[j], self.place.x
        live.gr.wait_recv()
        live.peers.append(self.send(j, (x + 2) % 4, 0, COLS, self.peer))
        live.gl.wait_recv()
        live.peers.append(self.send(j, (x + 2) % 4, COLS, COLS, self.peer))

    def arrived(self, j):
        for copy in self.live[j].peers:
            copy.wait_recv()
        for copy in self.live[j].sent[4:]:
            copy.wait_send()

    def slots(self, produce, finish, ready=None):
        for slot in range(self.lag[-1] + (8 if self.hold else 7)):
            for position, j in enumerate(self.order):
                stage = slot - self.lag[position]
                if self.hold and stage >= 4:
                    if stage == 4:
                        self.spread(j)
                        continue
                    stage -= 1
                if stage == 0:
                    produce(j)
                    self.exchange(j)
                elif stage == 1:
                    self.first(j)
                elif stage == 2:
                    self.second(j)
                elif stage == 3:
                    self.total(j)
                    finish(j)
                    if not self.hold:
                        self.spread(j)
                elif stage == 4:
                    self.relay(j)
                elif stage == 5:
                    self.last(j)
                elif stage == 6:
                    self.arrived(j)
                    if ready is not None:
                        ready(j)
            yield slot


def mp_scratch():
    ring = pltpu.VMEM((CHUNKS, 2, PIECE, COLS), BF)
    return [pltpu.VMEM((CHUNKS, 4, PIECE, D), BF), pltpu.VMEM((CHUNKS, PIECE, D), BF)] + [ring] * 5


def dma(count):
    return pltpu.SemaphoreType.DMA((count,))


def run(slots):
    for _ in slots:
        pass


def norm_rows_of(total):
    row = lax.broadcasted_iota(jnp.int32, (16, TILE), 0)
    return jnp.where(row == 0, total[:, 0:TILE], jnp.where(row == 1, total[:, TILE:WIDE], 0.0))


class StateScan(NamedTuple):
    mine: Any = ((2, STATE, HD), BF)
    early: Any = ((2, 3, STATE, HD), BF)
    sent: Any = ((2, 2, STATE, HD), BF)
    late: Any = ((2, 3, STATE, HD), BF)


def state_scan(place, copies, bufs, states, norms, reverse):
    def counted(position, step):
        at = (position - step + 4) % 4
        reached = at > position if reverse else at < position
        return jnp.where(reached, 1.0, 0.0)

    def wider(step):
        to = (place.y + step) % 4
        return (to < place.y if reverse else to > place.y).astype(jnp.int32)

    def put(head, total):
        states[head, 0:FEATURES] = total[0:FEATURES]
        states[head, FEATURES:WIDE] = jnp.zeros((WIDE - FEATURES, HD), F32)
        norms[head, 0:1, 0:TILE] = total[FEATURES : FEATURES + 1]
        norms[head, 0:1, TILE:WIDE] = total[FEATURES + 1 : FEATURES + 2]

    steps = (1, 2, 3)
    over = [copies.start(bufs.mine.at[0], bufs.early.at[0, k - 1], place.on_y(k)) for k in steps]
    across = [copies.start(bufs.mine.at[1], bufs.early.at[1, k - 1], place.on_z(k)) for k in steps]
    yield
    total, before = bufs.mine[0].astype(F32), jnp.zeros((STATE, HD), F32)
    for k, copy in zip(steps, over):
        copy.wait_recv()
        part = bufs.early[0, k - 1].astype(F32)
        total, before = total + part, before + counted(place.y, k) * part
    bufs.sent[0, 0] = total.astype(BF)
    over = [copies.start(bufs.sent.at[0, 0], bufs.late.at[0, k - 1], place.on_z(k)) for k in steps]
    put(0, before)
    before = jnp.zeros((STATE, HD), F32)
    for k, copy in zip(steps, across):
        copy.wait_recv()
        before = before + counted(place.z, k) * bufs.early[1, k - 1].astype(F32)
    bufs.sent[1, 0] = before.astype(BF)
    bufs.sent[1, 1] = (before + bufs.mine[1].astype(F32)).astype(BF)
    across = [
        copies.start(bufs.sent.at[1, wider(k)], bufs.late.at[1, k - 1], place.on_y(k)) for k in steps
    ]
    put(1, before)
    yield
    for head, sent in enumerate((over, across)):
        total = jnp.zeros((STATE, HD), F32)
        for k, copy in zip(steps, sent):
            copy.wait_recv()
            part = bufs.late[head, k - 1].astype(F32)
            total = total + (counted(place.z, k) * part if head == 0 else part)
        states[head, 0:FEATURES] += total[0:FEATURES]
        norms[head, 0:1, 0:TILE] += total[FEATURES : FEATURES + 1]
        norms[head, 0:1, TILE:WIDE] += total[FEATURES + 1 : FEATURES + 2]
    yield


def feature_tables():
    pairs = [(a, b) for a in range(FEAT) for b in range(a, FEAT)]
    first = np.zeros((2, 2 * FEAT, WIDE), np.float32)
    second = np.zeros((2, 2 * FEAT, WIDE), np.float32)
    vectors = np.zeros((8, WIDE), np.float32)
    vectors[0, 0] = vectors[1, 0] = vectors[2, 0] = 1.0
    for a in range(FEAT):
        vectors[1, 1 + a] = 1.0
        vectors[2, 1 + a] = FEAT ** (-0.25)
        for h in range(2):
            first[h, h * FEAT + a, 1 + a] = 1.0
    for number, (a, b) in enumerate(pairs):
        at = 1 + FEAT + number
        vectors[2, at] = (1.0 if a == b else 2.0**0.5) * (2.0 * FEAT) ** (-0.5)
        for h in range(2):
            first[h, h * FEAT + a, at] = 1.0
            second[h, h * FEAT + b, at] = 1.0
    return jnp.asarray(first, BF), jnp.asarray(second, BF), jnp.asarray(vectors, F32)


def factors(head, values, first, second, vectors):
    high, low = values
    left = dot(high, first[head]) + dot(low, first[head]) + vectors[0:1]
    right = dot(high, second[head]) + dot(low, second[head]) + vectors[1:2]
    return left, right


def of_head(values, head):
    lane = lax.broadcasted_iota(jnp.int32, values.shape, 1)
    return jnp.where((lane >= head * FEAT) & (lane < (head + 1) * FEAT), values, jnp.zeros_like(values))


def products(head, query, key, rows, count):
    high, low = (of_head(part[rows], head) for part in query)
    key_high, key_low = (part[0:count] for part in key)
    return dot_nt(high, key_high) + dot_nt(low, key_high) + dot_nt(high, key_low)


def shape(dims, kind):
    return jax.ShapeDtypeStruct(dims, kind)


def normed(rows, gain):
    factor = lax.rsqrt(jnp.mean(rows * rows, axis=-1, keepdims=True) + EPSILON)
    return rows * factor * gain


def column(group_row, held):
    for k in range(ROWS // TILE):
        block = group_row[0:1, k * TILE : (k + 1) * TILE].astype(F32)
        held[k * TILE : (k + 1) * TILE] = jnp.broadcast_to(block, (TILE, TILE)).T


def kept_pairs(group_col, group_row, tile):
    count = (tile + 1) * TILE
    row = lax.broadcasted_iota(jnp.int32, (TILE, count), 0) + tile * TILE
    col = lax.broadcasted_iota(jnp.int32, (TILE, count), 1)
    groups = group_col[tile * TILE : (tile + 1) * TILE, 0:1]
    return (col <= row) & (groups == group_row[0:1, 0:count].astype(F32))


def weight_block(into, left_t, right, quarter):
    count = into.shape[2]
    block = dot(left_t[0:count], right[:, quarter * 512 : (quarter + 1) * 512]).astype(BF)
    for k in range(4):
        into[quarter, k] = block[:, k * TILE : (k + 1) * TILE]


def back_through_norm(resid, grad, normed_grad, gain):
    factor = lax.rsqrt(jnp.mean(resid * resid, axis=-1, keepdims=True) + EPSILON)
    unit = resid * factor
    scaled = normed_grad * gain
    total = grad + factor * (scaled - unit * jnp.mean(scaled * unit, axis=-1, keepdims=True))
    return total, jnp.sum(normed_grad * unit, axis=0, keepdims=True)


LAG_ONE = (0, 0, 0, 0)
LAG_FIVE = (0, 0, 0, 0)


class Inputs(NamedTuple):
    tokens: Any
    group_row: Any
    gain_one: Any
    gain_two: Any
    gain_three: Any
    first: Any
    second: Any
    vectors: Any


class Weights(NamedTuple):
    out_grad: Any = ((ROWS, D), BF)
    w_query: Any = ((2 * FEAT, D), BF)
    w_key: Any = ((2 * FEAT, D), BF)
    w_value: Any = ((D, WIDE), BF)
    w_out: Any = ((WIDE, D), BF)
    win_k: Any = ((D, WIDE), BF)
    win_v: Any = ((D, WIDE), BF)
    win_q: Any = ((D, WIDE), BF)
    win_out: Any = ((WIDE, D), BF)
    w_gate: Any = ((FF_PAD, D), BF)
    w_up: Any = ((FF_PAD, D), BF)
    w_down: Any = ((FF_PAD, D), BF)


class Saved(NamedTuple):
    normed_one: Any = ((ROWS, D), BF)
    query: Any = ((2, ROWS, 2 * FEAT), BF)
    key: Any = ((2, ROWS, 2 * FEAT), BF)
    value: Any = ((ROWS, WIDE), BF)
    carried: Any = ((2, WIDE, HD), F32)
    carried_norm: Any = ((2, 1, WIDE), F32)
    quotient: Any = ((ROWS, WIDE), F32)
    denominator: Any = ((2, ROWS, 1), F32)
    mixed_lin: Any = ((ROWS, WIDE), BF)
    resid_one: Any = ((OWN, D), F32)
    normed_two: Any = ((ROWS, D), BF)
    query_win: Any = ((ROWS, WIDE), BF)
    keys_all: Any = ((ROWS + WIN, WIDE), BF)
    values_all: Any = ((ROWS + WIN, WIDE), BF)
    probs: Any = ((2, ROWS, TILE), F32)
    mixed_win: Any = ((ROWS, WIDE), BF)
    resid_two: Any = ((OWN, D), F32)
    low_four: Any = ((ROWS, D), BF)
    grad_own: Any = ((OWN, D), F32)
    gain_sum: Any = ((8, D), F32)
    gate_sum: Any = ((4, 4, FF, TILE), BF)
    up_sum: Any = ((4, 4, FF, TILE), BF)
    down_sum: Any = ((4, 4, FF, TILE), BF)
    part_three: Any = ((ROWS, D), BF)


class ForwardWork(NamedTuple):
    part: Any = ((ROWS, D), BF)
    own: Any = ((OWN, D), F32)
    group_col: Any = ((ROWS, TILE), F32)
    tail_flag: Any = ((16, TILE), BF)
    halo_flag: Any = ((16, TILE), BF)
    query_feat: Any = ((2, ROWS, WIDE), BF)
    key_feat: Any = ((2, ROWS, WIDE), BF)
    normed_three: Any = ((ROWS, D), BF)
    hidden_grad: Any = ((ROWS, FF_PAD), F32)
    hidden: Any = ((ROWS, FF_PAD), BF)
    gate_low: Any = ((ROWS, FF_PAD), BF)
    up_low: Any = ((ROWS, FF_PAD), BF)
    flipped: Any = ((FF_PAD, ROWS), BF)


class SeqSum:
    def __init__(self, place, copies, blocks, out, bufs):
        self.place, self.copies, self.blocks, self.out = place, copies, blocks, out
        z, y = place.z, place.y
        quarter = self.quarter = blocks.shape[2] // 4
        ring_y, ring_z = (place.on_y(1), place.on_y(3)), (place.on_z(1), place.on_z(3))

        def pick_one(k, half):
            return blocks.at[:, (y + k) % 4, pl.ds(half * quarter, quarter)]

        def pick_two(k, half):
            return blocks.at[(z + k) % 4, :, pl.ds((2 + half) * quarter, quarter)]

        def pick_three(k, half):
            return blocks.at[(z + k) % 4, y, pl.ds(half * quarter, quarter)]

        def pick_four(k, half):
            return blocks.at[z, (y + k) % 4, pl.ds((2 + half) * quarter, quarter)]

        live = [types.SimpleNamespace() for _ in range(4)]
        self.early = ((ring_y, pick_one, bufs[0:3], live[0]), (ring_z, pick_two, bufs[3:6], live[1]))
        self.late = ((ring_z, pick_three, bufs[6:9], live[2]), (ring_y, pick_four, bufs[9:12], live[3]))

    def begin(self, rings):
        for (right, left), pick, (fwd, direct, comb), live in rings:
            live.fr = self.copies.start(pick(2, 0), fwd.at[0], right)
            live.fl = self.copies.start(pick(2, 1), fwd.at[1], left)
            live.dr = self.copies.start(pick(1, 1), direct.at[1], right)
            live.dl = self.copies.start(pick(3, 0), direct.at[0], left)

    def join(self, rings):
        for (right, left), pick, (fwd, direct, comb), live in rings:
            live.fr.wait_recv()
            block = pick(1, 0)
            block[...] = (block[...].astype(F32) + fwd[0].astype(F32)).astype(BF)
            live.cr = self.copies.start(block, comb.at[0], right)
            live.fl.wait_recv()
            block = pick(3, 1)
            block[...] = (block[...].astype(F32) + fwd[1].astype(F32)).astype(BF)
            live.cl = self.copies.start(block, comb.at[1], left)

    def total(self, ring, half):
        _, pick, (fwd, direct, comb), live = ring
        (live.cr if half == 0 else live.cl).wait_recv()
        total = pick(0, half)[...].astype(F32) + comb[half].astype(F32)
        if direct is None:
            return total
        (live.dl if half == 0 else live.dr).wait_recv()
        return total + direct[half].astype(F32)

    def fold(self, rings):
        for _, pick, (fwd, direct, _), live in rings:
            for copy, block, got in (
                (live.fr, pick(1, 0), fwd.at[0]),
                (live.fl, pick(3, 1), fwd.at[1]),
                (live.dl, pick(0, 0), direct.at[0]),
                (live.dr, pick(0, 1), direct.at[1]),
            ):
                copy.wait_recv()
                block[...] = (block[...].astype(F32) + got[...].astype(F32)).astype(BF)

    def pass_on(self, rings):
        for (right, left), pick, (_, _, comb), live in rings:
            live.cr = self.copies.start(pick(1, 0), comb.at[0], right)
            live.cl = self.copies.start(pick(3, 1), comb.at[1], left)

    def step(self, number):
        if number == 0 and self.early[0][2][1] is None:
            self.pass_on(self.early)
        elif number == 0:
            self.begin(self.early)
        elif number == 1:
            if self.early[0][2][1] is not None:
                self.join(self.early)
        elif number == 2:
            for ring in self.early:
                for half in range(2):
                    block = ring[1](0, half)
                    block[...] = self.total(ring, half).astype(BF)
            self.begin(self.late)
        elif number == 3:
            self.join(self.late)
        else:
            size = self.quarter
            for half in range(2):
                self.out[pl.ds(half * size, size)] = self.total(self.late[0], half)
                self.out[pl.ds((2 + half) * size, size)] = self.total(self.late[1], half)


def seq_scratch(width):
    early, late = (2, 4, width // 4, TILE), (2, width // 4, TILE)
    return [pltpu.VMEM(early, BF)] * 6 + [pltpu.VMEM(late, BF)] * 6


FOLDED = 2


def folded_scratch():
    late = pltpu.VMEM((2, FF // 4, TILE), BF)
    return [pltpu.VMEM((2, 4, FF // 4, TILE), BF)] * 2 + [late] * 6


def taker(refs):
    refs = list(refs)

    def take(kind):
        return kind(*[refs.pop(0) for _ in kind._fields])

    def some(count):
        return [refs.pop(0) for _ in range(count)]

    return take, some


def vmem(kind):
    return [pltpu.VMEM(*entry) for entry in kind()]


def forward_kernel(*refs):
    take, some = taker(refs)
    inputs, hbm_weights, hbm_saved = take(Inputs), take(Weights), take(Saved)
    weights, saved, work, scan_bufs = take(Weights), take(Saved), take(ForwardWork), take(StateScan)
    bufs = some(7)
    fold_bufs = [some(4) for _ in range(FOLDED)]
    fold_sems = some(2)
    mp_sems, (state_send, state_recv), (halo_send, halo_recv), (local_sems,) = (
        some(2),
        some(2),
        some(2),
        some(1),
    )
    place = Place()
    local = Locals(local_sems)
    loads = []
    for src, dst in zip(hbm_weights[1:], weights[1:]):
        loads.append(local.start(src, dst if src.shape == dst.shape else dst.at[pl.ds(0, FF)]))
    loads = Weights(local.start(hbm_weights.out_grad, weights.out_grad), *loads)
    saves = []

    def save(*pairs):
        for src, dst in pairs:
            saves.append(local.start(src, dst))

    greet(
        [place.peer()]
        + [place.on_x(k) for k in (1, 3)]
        + [place.on_y(k) for k in (1, 2, 3)]
        + [place.on_z(k) for k in (1, 2, 3)]
        + [place.along(1), place.along(15)]
    )
    for ref in (weights.w_gate, weights.w_up, weights.w_down):
        ref[FF:FF_PAD] = jnp.zeros((FF_PAD - FF, D), BF)
    tokens, group_row, group_col = inputs.tokens, inputs.group_row, work.group_col
    first, second, vectors = inputs.first, inputs.second, inputs.vectors
    scale = vectors[2:3]
    normed_one = saved.normed_one

    def norm_rows(i, _):
        rows = rows_at(i * 32, 32)
        normed_one[rows] = normed(tokens[rows].astype(F32), inputs.gain_one[...]).astype(BF)
        return 0

    lax.fori_loop(0, ROWS // 32, norm_rows, 0, unroll=4)
    save((normed_one, hbm_saved.normed_one))
    column(group_row, group_col)
    query, key, value = saved.query, saved.key, saved.value
    for load, weight, held in (
        (loads.w_key, weights.w_key, key),
        (loads.w_query, weights.w_query, query),
    ):
        load.wait()
        held[0], held[1] = halves(dot_nt(normed_one[...], weight[...]))
    loads.w_value.wait()
    value[...] = dot(normed_one[...], weights.w_value[...]).astype(BF)

    last = group_row[0:1, ROWS - 1 : ROWS].astype(F32)
    in_last = (group_col[:, 0:1] == last).astype(F32)
    query_feat, key_feat, mine = work.query_feat, work.key_feat, scan_bufs.mine
    for head in range(2):
        left, right = factors(head, (key[0], key[1]), first, second, vectors)
        feat = (left * right * scale).astype(BF)
        key_feat[head] = feat
        kept = feat.astype(F32) * in_last
        state = dot_tn(kept.astype(BF), value[:, head * HD : (head + 1) * HD])
        mine[head, 0:FEATURES] = state[0:FEATURES].astype(BF)
        mine[head, FEATURES:STATE] = norm_rows_of(jnp.sum(kept, axis=0, keepdims=True)).astype(BF)
    meet(11)
    copies_state = Copies(state_send, state_recv)
    scan = state_scan(place, copies_state, scan_bufs, saved.carried, saved.carried_norm, False)
    next(scan)
    save((query, hbm_saved.query), (key, hbm_saved.key), (value, hbm_saved.value))
    quotient, denominator = saved.quotient, saved.denominator
    for head in range(2):
        left, right = factors(head, (query[0], query[1]), first, second, vectors)
        query_feat[head] = (left * right * scale).astype(BF)
    for tile in range(ROWS // TILE):
        rows, count = pl.ds(tile * TILE, TILE), (tile + 1) * TILE
        kept = kept_pairs(group_col, group_row, tile)
        for head in range(2):
            inner = products(head, (query.at[0], query.at[1]), (key.at[0], key.at[1]), rows, count)
            block = jnp.where(kept, 1.0 + inner * 0.25 + inner * inner * 0.03125, 0.0).astype(BF)
            denominator[head, rows] = jnp.sum(block.astype(F32), axis=1, keepdims=True)
            quotient[rows, head * HD : (head + 1) * HD] = dot(
                block, value[0:count, head * HD : (head + 1) * HD]
            )
        if tile == 1:
            next(scan)
    loads.w_down.wait()
    loads.out_grad.wait()
    work.hidden_grad[...] = dot_nt(weights.out_grad[...], weights.w_down[...])
    for _ in scan:
        pass
    copies_state.finish()
    first_group = group_row[0:1, 0:1].astype(F32)
    incoming = (group_col[:, 0:1] == first_group).astype(F32) * jnp.where(place.seq > 0, 1.0, 0.0)
    carried, carried_norm, mixed_lin = saved.carried, saved.carried_norm, saved.mixed_lin
    save((carried, hbm_saved.carried), (carried_norm, hbm_saved.carried_norm))
    for head in range(2):
        lanes = slice(head * HD, (head + 1) * HD)
        feat = query_feat[head]
        numer = quotient[:, lanes] + incoming * dot(feat, carried[head].astype(BF))
        denom = denominator[head] + incoming * jnp.sum(
            feat.astype(F32) * carried_norm[head], axis=1, keepdims=True
        )
        ratio = numer / denom
        denominator[head] = denom
        quotient[:, lanes] = ratio
        mixed_lin[:, lanes] = ratio.astype(BF)
    save(
        (quotient, hbm_saved.quotient),
        (denominator, hbm_saved.denominator),
        (mixed_lin, hbm_saved.mixed_lin),
    )
    loads.w_out.wait()

    part, own = work.part, work.own
    resid_one, resid_two = saved.resid_one, saved.resid_two
    normed_two, normed_three = saved.normed_two, work.normed_three
    sum_one = MpSum(place, mp_sems, part, normed_two, own, bufs, LAG_ONE, (3, 0, 1, 2))
    sum_two = MpSum(place, mp_sems, part, normed_three, own, bufs, (0, 1, 2, 3))
    sum_four = MpSum(place, mp_sems, part, saved.low_four, own, bufs, (0, 0, 2, 2))

    def produce_one(j):
        rows = pl.ds(j * CHUNK, CHUNK)
        part[rows] = dot(mixed_lin[rows], weights.w_out[...]).astype(BF)

    def finish_one(j):
        mine = pl.ds(j * PIECE, PIECE)
        rows = own[mine] + tokens[sum_one.own_rows(j)].astype(F32)
        resid_one[mine] = rows
        normed_two[sum_one.own_rows(j)] = normed(rows, inputs.gain_two[...]).astype(BF)

    query_win, keys_all, values_all = saved.query_win, saved.keys_all, saved.values_all
    copies_halo = Copies(halo_send, halo_recv)
    lane = lax.broadcasted_iota(jnp.int32, (1, TILE), 1)
    group_blocks = [group_row[0:1, k * TILE : (k + 1) * TILE].astype(F32) for k in range(4)]
    turned = [pltpu.roll(block, WIN, 1) for block in group_blocks]
    work.tail_flag[...] = jnp.broadcast_to((turned[3] == last).astype(F32), (16, TILE)).astype(BF)
    halo = []

    def ready_one(j):
        rows = pl.ds(j * CHUNK, CHUNK)
        below = pl.ds(WIN + j * CHUNK, CHUNK)
        if j == 3:
            for load in (loads.win_k, loads.win_v, loads.win_q):
                load.wait()
        keys_all[below] = dot(normed_two[rows], weights.win_k[...]).astype(BF)
        values_all[below] = dot(normed_two[rows], weights.win_v[...]).astype(BF)
        if j == 3:
            for ref in (keys_all, values_all):
                halo.append(
                    copies_halo.start(ref.at[pl.ds(ROWS, WIN)], ref.at[pl.ds(0, WIN)], place.along(1))
                )
            halo.append(copies_halo.start(work.tail_flag, work.halo_flag, place.along(1)))
        query_win[rows] = dot(normed_two[rows], weights.win_q[...]).astype(BF)
        if j != 3:
            next(two)

    probs, mixed_win = saved.probs, saved.mixed_win
    tile_row = lax.broadcasted_iota(jnp.int32, (WIN, TILE), 0)
    tile_col = lax.broadcasted_iota(jnp.int32, (WIN, TILE), 1)
    near = (tile_col > tile_row) & (tile_col <= tile_row + WIN)
    score_scale = HD ** (-0.5)

    def window_tile(t):
        rows = pl.ds(t * WIN, WIN)
        if t == 0:
            flag = jnp.where(place.seq > 0, work.halo_flag[0:1].astype(F32), 0.0)
            groups = jnp.where(lane < WIN, jnp.where(flag > 0.5, first_group, -2.0), turned[0])
        elif t % 2 == 1:
            groups = group_blocks[t // 2]
        else:
            groups = jnp.where(lane < WIN, turned[t // 2 - 1], turned[t // 2])
        kept = near & (group_col[rows] == groups)
        for head in range(2):
            lanes = slice(head * HD, (head + 1) * HD)
            scores = dot_nt(query_win[rows, lanes], keys_all[t * WIN : t * WIN + TILE, lanes])
            scores = jnp.where(kept, scores * score_scale, -1e30)
            exp_scores = jnp.exp(scores - jnp.max(scores, axis=1, keepdims=True))
            found = exp_scores / jnp.sum(exp_scores, axis=1, keepdims=True)
            probs[head, rows] = found
            mixed_win[rows, lanes] = dot(
                found.astype(BF), values_all[t * WIN : t * WIN + TILE, lanes]
            ).astype(BF)

    def produce_two(j):
        if j == 0:
            for copy in halo:
                copy.wait_recv()
            loads.win_out.wait()
        window_tile(2 * j)
        window_tile(2 * j + 1)
        rows = pl.ds(j * CHUNK, CHUNK)
        part[rows] = dot(mixed_win[rows], weights.win_out[...]).astype(BF)

    def finish_two(j):
        mine = pl.ds(j * PIECE, PIECE)
        rows = own[mine] + resid_one[mine]
        resid_two[mine] = rows
        normed_three[sum_two.own_rows(j)] = normed(rows, inputs.gain_three[...]).astype(BF)

    w_gate, w_up, w_down, og = weights.w_gate, weights.w_up, weights.w_down, weights.out_grad
    hidden, gate_low, up_low = work.hidden, work.gate_low, work.up_low

    def ready_two(j):
        if j % 2 == 0:
            return
        if j == 1:
            for load in (loads.w_gate, loads.w_up):
                load.wait()
        rows = pl.ds((j - 1) * CHUNK, 2 * CHUNK)
        gate = dot_nt(normed_three[rows], w_gate[...])
        up = dot_nt(normed_three[rows], w_up[...])
        sigmoid = 1.0 / (1.0 + jnp.exp(-gate))
        act, hidden_grad = gate * sigmoid, work.hidden_grad[rows]
        hidden[rows] = (act * up).astype(BF)
        up_low[rows] = (hidden_grad * act).astype(BF)
        gate_low[rows] = (hidden_grad * up * (sigmoid + act * (1.0 - sigmoid))).astype(BF)
        part[rows] = (dot(gate_low[rows], w_gate[...]) + dot(up_low[rows], w_up[...])).astype(BF)
        next(four)

    one = sum_one.slots(produce_one, finish_one, ready_one)
    two = sum_two.slots(produce_two, finish_two, ready_two)
    def finish_four(j):
        mine, rows = pl.ds(j * PIECE, PIECE), sum_four.own_rows(j)
        total, here = back_through_norm(
            resid_two[mine], og[rows].astype(F32), own[mine], inputs.gain_three[...]
        )
        saved.gain_sum[0:1] += here
        saved.grad_own[mine] = total
        saved.low_four[rows] = total.astype(BF)

    four = sum_four.slots(lambda j: None, finish_four)
    saved.gain_sum[...] = jnp.zeros_like(saved.gain_sum)
    run(one)
    copies_halo.finish()
    save(
        (resid_one, hbm_saved.resid_one),
        (normed_two, hbm_saved.normed_two),
        (query_win, hbm_saved.query_win),
        (keys_all, hbm_saved.keys_all),
        (values_all, hbm_saved.values_all),
    )
    for slot in two:
        if slot == 8:
            next(four)
    save(
        (probs, hbm_saved.probs), (mixed_win, hbm_saved.mixed_win), (resid_two, hbm_saved.resid_two)
    )

    def project_down(half):
        cols = pl.ds(half * 1024, 1024)
        saved.part_three[:, cols] = dot(hidden[...], w_down[:, cols]).astype(BF)
        if half == 1:
            save((saved.part_three, hbm_saved.part_three))

    seq_copies = Copies(*fold_sems)
    folds = []

    def weight_back(number, into, to_hbm, left, right, quarter):
        if quarter == 0:
            work.flipped[...] = left[...].T
        weight_block(into, work.flipped, right, quarter)
        if quarter < 3:
            return
        if number < FOLDED:
            fwd_y, direct_y, fwd_z, direct_z = fold_bufs[number]
            early = [fwd_y, direct_y, None, fwd_z, direct_z, None]
            seq_sum = SeqSum(place, seq_copies, into, None, early + [None] * 6)
            seq_sum.begin(seq_sum.early)
            folds.append((seq_sum, into, to_hbm))
        else:
            save((into, to_hbm))

    blocks = []
    for number, (into, to_hbm, left, right) in enumerate(
        (
            (saved.gate_sum, hbm_saved.gate_sum, gate_low, normed_three),
            (saved.up_sum, hbm_saved.up_sum, up_low, normed_three),
            (saved.down_sum, hbm_saved.down_sum, hidden, og),
        )
    ):
        blocks += [
            functools.partial(weight_back, number, into, to_hbm, left, right, k) for k in range(4)
        ]
    blocks += [functools.partial(project_down, k) for k in range(2)]
    for _ in four:
        for _ in range(3):
            if blocks:
                blocks.pop(0)()
    save(
        (saved.low_four, hbm_saved.low_four),
        (saved.grad_own, hbm_saved.grad_own),
        (saved.gain_sum, hbm_saved.gain_sum),
    )
    for block in blocks:
        block()
    for seq_sum, into, to_hbm in folds:
        seq_sum.fold(seq_sum.early)
        save((into, to_hbm))
    seq_copies.finish()
    for copy in saves:
        copy.wait()


HBM = pl.BlockSpec(memory_space=pl.ANY)
INSIDE = pl.BlockSpec(memory_space=pltpu.VMEM)


def forward(inputs, weights):
    scratch = vmem(Weights) + vmem(Saved) + vmem(ForwardWork) + vmem(StateScan) + mp_scratch()
    scratch += [pltpu.VMEM((2, 4, FF // 4, TILE), BF)] * (4 * FOLDED) + [dma(8 * FOLDED)] * 2
    scratch += [dma(CHUNKS * PER_CHUNK)] * 2 + [dma(12)] * 2 + [dma(3)] * 2
    scratch += [dma(len(Weights._fields) + len(Saved._fields))]
    return Saved(
        *pl.pallas_call(
            forward_kernel,
            out_shape=[shape(dims, kind) for dims, kind in Saved()],
            in_specs=[INSIDE] * len(inputs) + [HBM] * len(weights),
            out_specs=[HBM] * len(Saved._fields),
            scratch_shapes=scratch,
            compiler_params=pltpu.CompilerParams(
                collective_id=0, has_side_effects=True, vmem_limit_bytes=VMEM_LIMIT
            ),
        )(*inputs, *weights)
    )


class Groups(NamedTuple):
    gate: Any = FF
    up: Any = FF
    down: Any = FF
    win_out: Any = WIDE
    win: Any = 3 * WIDE
    out: Any = WIDE
    lin: Any = WIDE + 4 * FEAT


class BackInputs(NamedTuple):
    group_row: Any
    gain_one: Any
    gain_two: Any
    first: Any
    second: Any
    vectors: Any


class BackHbm(NamedTuple):
    part_three: Any
    low_four: Any
    grad_own: Any
    gain_sum: Any
    tokens: Any
    normed_one: Any
    normed_two: Any
    gate_sum: Any
    up_sum: Any
    down_sum: Any
    w_query: Any
    w_key: Any
    w_value: Any
    w_out: Any
    win_q: Any
    win_k: Any
    win_v: Any
    win_out: Any


SPECS = Saved()


class BackSaved(NamedTuple):
    query: Any = SPECS.query
    key: Any = SPECS.key
    value: Any = SPECS.value
    carried: Any = SPECS.carried
    carried_norm: Any = SPECS.carried_norm
    quotient: Any = SPECS.quotient
    denominator: Any = SPECS.denominator
    mixed_lin: Any = SPECS.mixed_lin
    resid_one: Any = SPECS.resid_one
    query_win: Any = SPECS.query_win
    keys_all: Any = SPECS.keys_all
    values_all: Any = SPECS.values_all
    probs: Any = SPECS.probs
    mixed_win: Any = SPECS.mixed_win
    resid_two: Any = SPECS.resid_two


class BackOuts(NamedTuple):
    tokens_low: Any = ((ROWS, D), BF)
    gain_one: Any = ((1, TILE), F32)
    gain_two: Any = ((1, TILE), F32)
    gain_three: Any = ((1, TILE), F32)
    gate: Any = ((FF, TILE), F32)
    up: Any = ((FF, TILE), F32)
    down: Any = ((FF, TILE), F32)
    win_out: Any = ((WIDE, TILE), F32)
    out: Any = ((WIDE, TILE), F32)
    win_q: Any = ((TILE, WIDE), F32)
    win_k: Any = ((TILE, WIDE), F32)
    win_v: Any = ((TILE, WIDE), F32)
    value: Any = ((TILE, WIDE), F32)
    query: Any = ((2 * FEAT, TILE), F32)
    key: Any = ((2 * FEAT, TILE), F32)
    result: Any = ((ROWS, D), BF)


class BackWork(NamedTuple):
    part: Any = ((ROWS, D), BF)
    other_full: Any = ((ROWS, D), BF)
    own: Any = ((OWN, D), F32)
    grad_own: Any = ((OWN, D), F32)
    token_own: Any = ((OWN, D), BF)
    group_col: Any = ((ROWS, TILE), F32)
    normed_low: Any = ((ROWS, D), BF)
    w_query: Any = ((2 * FEAT, D), BF)
    w_key: Any = ((2 * FEAT, D), BF)
    w_out: Any = ((WIDE, D), BF)
    win_out: Any = ((WIDE, D), BF)
    w_win: Any = ((D, 3 * WIDE), BF)
    mixed_grad: Any = ((ROWS, WIDE), BF)
    keys_sum: Any = ((ROWS + WIN, WIDE), F32)
    values_sum: Any = ((ROWS + WIN, WIDE), F32)
    back_key: Any = ((2, WIN, WIDE), BF)
    back_value: Any = ((2, WIN, WIDE), BF)
    win_grads: Any = ((ROWS, 3 * WIDE), BF)
    flipped: Any = ((3 * WIDE, ROWS), BF)
    denom_grad: Any = ((2, ROWS, 1), F32)
    query_sum: Any = ((ROWS, 2 * FEAT), F32)
    key_sum: Any = ((ROWS, 2 * FEAT), F32)
    query_low: Any = ((ROWS, 2 * FEAT), BF)
    key_low: Any = ((ROWS, 2 * FEAT), BF)
    state_sum: Any = ((2, WIDE, HD), F32)
    norm_sum: Any = ((2, 1, WIDE), F32)
    gain_sums: Any = ((16, D), F32)
    gain_low: Any = ((16, D), BF)
    gain_z: Any = ((3, 16, 512), BF)
    gain_zz: Any = ((16, 512), BF)
    gain_y: Any = ((3, 16, TILE), BF)
    gain_x: Any = ((16, TILE), BF)
    gain_xx: Any = ((3, 16, TILE), BF)
    gain_p: Any = ((16, TILE), BF)
    gain_pp: Any = ((16, TILE), BF)
    sum_win: Any = ((3 * WIDE, TILE), F32)
    sum_lin: Any = ((WIDE + 4 * FEAT, TILE), F32)
    later: Any = ((2, WIDE, HD), F32)
    later_norm: Any = ((2, 1, WIDE), F32)


def backward_kernel(*refs):
    take, some = taker(refs)
    inputs, hbm, hbm_saved, outs = take(BackInputs), take(BackHbm), take(BackSaved), take(BackOuts)
    saved, blocks, work, scan_bufs = take(BackSaved), take(Groups), take(BackWork), take(StateScan)
    seq_bufs = []
    for number in range(len(Groups._fields)):
        if number < FOLDED:
            comb_y, comb_z, *late = some(8)
            seq_bufs.append([None, None, comb_y, None, None, comb_z] + late)
        else:
            seq_bufs.append(some(12))
    bufs, bufs_three = some(7), some(7)
    mp_sems, three_sems, (seq_send, seq_recv), (few_send, few_recv), (local_sems,) = (
        some(2),
        some(2),
        some(2),
        some(2),
        some(1),
    )
    place = Place()
    z, y = place.z, place.y
    local = Locals(local_sems)
    part, own, other_full, tokens_low = work.part, work.own, work.other_full, outs.tokens_low
    sum_three = MpSum(place, three_sems, part, outs.result, own, bufs_three, hold=True)
    sum_five = MpSum(place, mp_sems, part, other_full, own, bufs, LAG_FIVE)
    sum_six = MpSum(place, mp_sems, part, tokens_low, own, bufs)

    load_part = local.start(hbm.part_three, part)
    load_low = local.start(hbm.low_four, tokens_low)
    load_win_out = local.start(hbm.win_out, work.win_out)
    mlp_loads = [
        local.start(src, dst)
        for src, dst in ((hbm.gate_sum, blocks.gate), (hbm.up_sum, blocks.up), (hbm.down_sum, blocks.down))
    ]
    load_saved = BackSaved(*[local.start(src, dst) for src, dst in zip(hbm_saved, saved)])
    load_win = [
        local.start(src, work.w_win.at[:, pl.ds(k * WIDE, WIDE)])
        for k, src in enumerate((hbm.win_q, hbm.win_k, hbm.win_v))
    ]
    load_grad = local.start(hbm.grad_own, work.grad_own)
    load_gain = local.start(hbm.gain_sum, work.gain_sums.at[pl.ds(0, 8)])
    load_normed = local.start(hbm.normed_two, work.normed_low)
    load_lin = [
        local.start(src, dst)
        for src, dst in ((hbm.w_query, work.w_query), (hbm.w_key, work.w_key), (hbm.w_out, work.w_out))
    ]
    greet(
        [place.peer()]
        + [place.on_x(k) for k in (1, 2, 3)]
        + [place.on_y(k) for k in (1, 2, 3)]
        + [place.on_z(k) for k in (1, 2, 3)]
        + [place.along(1), place.along(15)]
    )
    seq_copies = Copies(seq_send, seq_recv)
    few = Copies(few_send, few_recv)
    finished = Groups(outs.gate, outs.up, outs.down, outs.win_out, work.sum_win, outs.out, work.sum_lin)
    seq_sums = Groups(
        *[
            SeqSum(place, seq_copies, block, out, bufs_here)
            for block, out, bufs_here in zip(blocks, finished, seq_bufs)
        ]
    )
    first, second, vectors = inputs.first, inputs.second, inputs.vectors
    scale = vectors[2:3]
    group_row, group_col = inputs.group_row, work.group_col
    column(group_row, group_col)
    last_group = group_row[0:1, ROWS - 1 : ROWS].astype(F32)
    first_group = group_row[0:1, 0:1].astype(F32)
    in_last = (group_col[:, 0:1] == last_group).astype(F32)
    after_first = jnp.where(place.seq > 0, 1.0, 0.0)
    work.gain_sums[8:16] = jnp.zeros((8, D), F32)

    def finish(mp_sum, number, resid, gain, to, j):
        mine = pl.ds(j * PIECE, PIECE)
        total, here = back_through_norm(
            resid[mine].astype(F32), work.grad_own[mine], own[mine], gain[...]
        )
        work.gain_sums[number : number + 1] += here
        work.grad_own[mine] = total
        to[mp_sum.own_rows(j)] = total.astype(BF)

    mixed_grad, keys_sum, values_sum, win_grads = (
        work.mixed_grad,
        work.keys_sum,
        work.values_sum,
        work.win_grads,
    )
    probs, query_win, keys_all, values_all = (
        saved.probs,
        saved.query_win,
        saved.keys_all,
        saved.values_all,
    )
    score_scale = HD ** (-0.5)
    back = []

    def window_back(t):
        rows, window = pl.ds(t * WIN, WIN), pl.ds(t * WIN, TILE)
        for head in range(2):
            lanes = slice(head * HD, (head + 1) * HD)
            grad_tile, held = mixed_grad[rows, lanes], probs[head, rows]
            probs_grad = dot_nt(grad_tile, values_all[window, lanes])
            score_low = (
                held * (probs_grad - jnp.sum(probs_grad * held, axis=1, keepdims=True))
            ).astype(BF)
            win_grads[rows, lanes] = (dot(score_low, keys_all[window, lanes]) * score_scale).astype(BF)
            for ref, found in (
                (keys_sum, dot_tn(score_low, query_win[rows, lanes]) * score_scale),
                (values_sum, dot_tn(held.astype(BF), grad_tile)),
            ):
                if t == 0:
                    ref[window, lanes] = found
                else:
                    ref[rows, lanes] += found[:WIN]
                    ref[pl.ds(t * WIN + WIN, WIN), lanes] = found[WIN:]
        if t == 0:
            for ref, to_send in ((keys_sum, work.back_key), (values_sum, work.back_value)):
                to_send[0] = ref[0:WIN].astype(BF)
                back.append(few.start(to_send.at[0], to_send.at[1], place.along(15)))

    def produce_five(j):
        rows = pl.ds(j * CHUNK, CHUNK)
        for k, (ref, got) in enumerate(((keys_sum, work.back_key), (values_sum, work.back_value))):
            lanes = slice((k + 1) * WIDE, (k + 2) * WIDE)
            if j < CHUNKS - 1:
                win_grads[rows, lanes] = ref[WIN + j * CHUNK : WIN + (j + 1) * CHUNK].astype(BF)
            else:
                win_grads[j * CHUNK : ROWS - WIN, lanes] = ref[WIN + j * CHUNK : ROWS].astype(BF)
                back[k].wait_recv()
                win_grads[ROWS - WIN : ROWS, lanes] = (
                    ref[ROWS : ROWS + WIN] + got[1].astype(F32)
                ).astype(BF)
        if j % 2 == 0:
            return
        rows = pl.ds((j - 1) * CHUNK, 2 * CHUNK)
        part[rows] = dot_nt(win_grads[rows], work.w_win[...]).astype(BF)

    def finish_five(j):
        if j == 0:
            load_saved.resid_one.wait()
            load_grad.wait()
            load_gain.wait()
        finish(sum_five, 1, saved.resid_one, inputs.gain_two, other_full, j)

    query, key, value, carried = saved.query, saved.key, saved.value, saved.carried
    numer_low, query_sum, key_sum, value_sum, value_low = (
        query_win,
        work.query_sum,
        work.key_sum,
        keys_sum,
        mixed_grad,
    )

    def through_features(head, parts, grad):
        left, right = parts
        scaled = grad * scale
        return dot_nt((scaled * right).astype(BF), first[head]) + dot_nt(
            (scaled * left).astype(BF), second[head]
        )

    def ready_five(j):
        rows = pl.ds(j * CHUNK, CHUNK)
        if j == 0:
            for load in load_lin:
                load.wait()
            for load in (
                load_saved.denominator,
                load_saved.quotient,
                load_saved.query,
                load_saved.key,
                load_saved.value,
                load_saved.carried,
                load_saved.carried_norm,
            ):
                load.wait()
        mixed = dot_nt(other_full[rows], work.w_out[...]).astype(BF).astype(F32)
        incoming = (group_col[rows, 0:1] == first_group).astype(F32) * after_first
        for head in range(2):
            lanes = slice(head * HD, (head + 1) * HD)
            denom = saved.denominator[head, rows]
            numer = (mixed[:, lanes] / denom).astype(BF)
            numer_low[rows, lanes] = numer
            denom_grad = (
                -jnp.sum(mixed[:, lanes] * saved.quotient[rows, lanes], axis=1, keepdims=True) / denom
            )
            work.denom_grad[head, rows] = denom_grad
            parts = factors(head, (query[0, rows], query[1, rows]), first, second, vectors)
            used = (parts[0] * parts[1] * scale).astype(BF).astype(F32) * incoming
            state = dot_tn(used.astype(BF), numer)
            norm = jnp.sum(used * denom_grad, axis=0, keepdims=True)
            if j == 0:
                work.state_sum[head], work.norm_sum[head] = state, norm
            else:
                work.state_sum[head] += state
                work.norm_sum[head] += norm
        if j == CHUNKS - 1:
            for head in range(2):
                scan_bufs.mine[head, 0:FEATURES] = work.state_sum[head, 0:FEATURES].astype(BF)
                scan_bufs.mine[head, FEATURES:STATE] = norm_rows_of(work.norm_sum[head]).astype(BF)

    def within(j):
        rows, count = pl.ds(j * CHUNK, CHUNK), (j + 1) * CHUNK
        incoming = (group_col[rows, 0:1] == first_group).astype(F32) * after_first
        kept = kept_pairs(group_col, group_row, j)
        key_new = []
        for head in range(2):
            lanes = slice(head * HD, (head + 1) * HD)
            numer, denom_grad = numer_low[rows, lanes], work.denom_grad[head, rows]
            parts = factors(head, (query[0, rows], query[1, rows]), first, second, vectors)
            grad = incoming * (
                dot_nt(numer, carried[head].astype(BF)) + denom_grad * saved.carried_norm[head]
            )
            query_new = through_features(head, parts, grad)
            inner = products(head, (query.at[0], query.at[1]), (key.at[0], key.at[1]), rows, count)
            kernel = jnp.where(kept, 1.0 + inner * 0.25 + inner * inner * 0.03125, 0.0).astype(BF)
            grad = dot_nt(numer, value[0:count, lanes]) + denom_grad
            grad = jnp.where(kept, grad, 0.0).astype(BF).astype(F32)
            inner_grad = (grad * (0.25 + inner * 0.0625)).astype(BF)
            query_new = query_new + of_head(dot(inner_grad, key[0, 0:count]), head)
            if head == 0:
                query_sum[rows] = query_new
            else:
                query_sum[rows] += query_new
            key_new.append(of_head(dot_tn(inner_grad, query[0, rows]), head))
            found = dot_tn(kernel, numer)
            if j > 0:
                value_sum[0 : count - CHUNK, lanes] += found[0 : count - CHUNK]
            value_sum[count - CHUNK : count, lanes] = found[count - CHUNK : count]
        found = key_new[0] + key_new[1]
        if j > 0:
            key_sum[0 : count - CHUNK] += found[0 : count - CHUNK]
        key_sum[count - CHUNK : count] = found[count - CHUNK : count]

    def weight_task(block, right, quarter):
        weight_block(block, work.flipped, right, quarter)

    def begin(group):
        group.step(0)

    def turn_mixed(ref, load):
        load.wait()
        work.flipped[0:WIDE] = ref[...].T

    def turn_win():
        load_normed.wait()
        for k in range(3):
            rows = slice(k * WIDE, (k + 1) * WIDE)
            work.flipped[rows] = win_grads[:, rows].T

    late_work = [lambda: turn_mixed(saved.mixed_win, load_saved.mixed_win)]
    late_work += [functools.partial(weight_task, blocks.win_out, tokens_low, k) for k in range(4)]
    late_work += [functools.partial(begin, seq_sums.win_out), turn_win]
    late_work += [functools.partial(weight_task, blocks.win, work.normed_low, k) for k in range(4)]
    late_work += [functools.partial(begin, seq_sums.win)]

    def steps(*names):
        for group, number in names:
            group.step(number)

    gate, up, down, win_out, win, out, lin = seq_sums
    def finish_three(j):
        mine = pl.ds(j * PIECE, PIECE)
        outs.result[sum_three.own_rows(j)] = (own[mine] + saved.resid_two[mine]).astype(BF)

    three = sum_three.slots(lambda j: None, finish_three)
    meet(12)
    load_part.wait()
    next(three)
    for load in (load_low, load_win_out):
        load.wait()
    mixed_grad[...] = dot_nt(tokens_low[...], work.win_out[...]).astype(BF)
    for load, group in zip(mlp_loads, (gate, up, down)):
        load.wait()
        group.step(0)
    next(three)
    for load in (load_saved.probs, load_saved.query_win, load_saved.keys_all, load_saved.values_all):
        load.wait()
    load_saved.resid_two.wait()
    for t in range(8):
        window_back(t)
        if t == 4:
            next(three)
    next(three)
    for load in load_win:
        load.wait()
    for j in range(0, CHUNKS, 2):
        produce_five(j)
        produce_five(j + 1)
    five = sum_five.slots(lambda j: None, finish_five, ready_five)
    plans = {2: [(gate, 2)], 3: [(down, 1)], 4: [(up, 2)], 6: [(down, 2)]}
    for slot in five:
        for _ in range(3):
            if late_work:
                late_work.pop(0)()
        steps(*plans.get(slot, ()))
    for block in late_work:
        block()
    scan = state_scan(place, few, scan_bufs, work.later, work.later_norm, True)
    next(scan)
    load_normed_one = local.start(hbm.normed_one, work.normed_low)
    load_value = local.start(hbm.w_value, work.w_win.at[:, pl.ds(0, WIDE)])
    load_token = [
        local.start(hbm.tokens.at[sum_six.own_rows(j)], work.token_own.at[pl.ds(j * PIECE, PIECE)])
        for j in range(CHUNKS)
    ]
    next(three)
    turn_mixed(saved.mixed_lin, load_saved.mixed_lin)
    for k in range(4):
        weight_task(blocks.out, other_full, k)
    steps((out, 0), (gate, 3))
    within(0)
    next(scan)
    next(three)
    within(1)
    steps((win_out, 1))
    within(2)
    within(3)
    for _ in scan:
        pass
    next(three)
    for head in range(2):
        lanes = slice(head * HD, (head + 1) * HD)
        state = work.later[head].astype(BF)
        parts = factors(head, (key[0], key[1]), first, second, vectors)
        feat = (parts[0] * parts[1] * scale).astype(BF)
        grad = in_last * (dot_nt(value[:, lanes], state) + work.later_norm[head])
        key_sum[...] += through_features(head, parts, grad)
        value_sum[0:ROWS, lanes] += in_last * dot(feat, state)
    work.query_low[...] = query_sum[...].astype(BF)
    work.key_low[...] = key_sum[...].astype(BF)
    value_low[...] = value_sum[0:ROWS].astype(BF)
    load_value.wait()

    def produce_six(j):
        rows = pl.ds(j * CHUNK, CHUNK)
        part[rows] = (
            dot_nt(value_low[rows], work.w_win[:, 0:WIDE])
            + dot(work.query_low[rows], work.w_query[...])
            + dot(work.key_low[rows], work.w_key[...])
        ).astype(BF)

    for load in load_token:
        load.wait()

    def finish_six(j):
        finish(sum_six, 2, work.token_own, inputs.gain_one, tokens_low, j)

    def gains():
        work.gain_low[...] = work.gain_sums[...].astype(BF)

        def block(ref, at, size):
            return ref.at[:, pl.ds(pl.multiple_of(at * size, TILE), size)]

        over = [
            few.start(block(work.gain_low, (z + k) % 4, 512), work.gain_z.at[k - 1], place.on_z(k))
            for k in (1, 2, 3)
        ]
        yield
        total = block(work.gain_low, z, 512)[...].astype(F32)
        for k, copy in enumerate(over):
            copy.wait_recv()
            total = total + work.gain_z[k].astype(F32)
        work.gain_zz[...] = total.astype(BF)
        over = [
            few.start(block(work.gain_zz, (y + k) % 4, TILE), work.gain_y.at[k - 1], place.on_y(k))
            for k in (1, 2, 3)
        ]
        yield
        total = block(work.gain_zz, y, TILE)[...].astype(F32)
        for k, copy in enumerate(over):
            copy.wait_recv()
            total = total + work.gain_y[k].astype(F32)
        work.gain_x[...] = total.astype(BF)
        over = [few.start(work.gain_x, work.gain_xx.at[k - 1], place.on_x(k)) for k in (1, 2, 3)]
        yield
        total = work.gain_x[...].astype(F32)
        for k, copy in enumerate(over):
            copy.wait_recv()
            total = total + work.gain_xx[k].astype(F32)
        work.gain_p[...] = total.astype(BF)
        copy = few.start(work.gain_p, work.gain_pp, place.peer())
        yield
        copy.wait_recv()
        total = work.gain_p[...].astype(F32) + work.gain_pp[...].astype(F32)
        for k, ref in enumerate((outs.gain_three, outs.gain_two, outs.gain_one)):
            ref[...] = total[k : k + 1]

    def turn_lin():
        load_normed_one.wait()
        work.flipped[0:WIDE] = value_low[...].T
        for k, ref in enumerate((query_sum, key_sum)):
            at = WIDE + 2 * FEAT * k
            wide = jnp.concatenate([ref[...], jnp.zeros((ROWS, TILE - 2 * FEAT), F32)], axis=1)
            work.flipped[at : at + 2 * FEAT] = wide.T[0 : 2 * FEAT].astype(BF)

    six = sum_six.slots(produce_six, finish_six)
    next(six)
    next(three)
    steps((up, 3), (win, 1))
    turn_lin()
    for k in range(4):
        weight_task(blocks.lin, work.normed_low, k)
    steps((lin, 0))
    plans = {
        1: [(out, 1), (down, 3), (win_out, 2)],
        2: [(gate, 4), (up, 4), (win, 2)],
        3: [(lin, 1), (out, 2), (down, 4)],
        4: [(lin, 2), (win_out, 3)],
        5: [(win, 3), (out, 3), (lin, 3)],
        6: [(win_out, 4), (win, 4), (out, 4)],
    }
    gain_steps = gains()
    for slot in six:
        if slot >= 3:
            next(gain_steps, None)
        steps(*plans.get(slot, ()))
    steps((lin, 4))
    for k, ref in enumerate((outs.win_q, outs.win_k, outs.win_v)):
        ref[...] = work.sum_win[k * WIDE : (k + 1) * WIDE].T
    outs.value[...] = work.sum_lin[0:WIDE].T
    outs.query[...] = work.sum_lin[WIDE : WIDE + 2 * FEAT]
    outs.key[...] = work.sum_lin[WIDE + 2 * FEAT : WIDE + 4 * FEAT]
    for _ in gain_steps:
        pass
    seq_copies.finish()
    few.finish()


def backward(saved, inputs, weights):
    back_inputs = BackInputs(*[getattr(inputs, name) for name in BackInputs._fields])
    hbm = BackHbm(
        part_three=saved.part_three,
        low_four=saved.low_four,
        grad_own=saved.grad_own,
        gain_sum=saved.gain_sum,
        tokens=inputs.tokens,
        normed_one=saved.normed_one,
        normed_two=saved.normed_two,
        gate_sum=saved.gate_sum,
        up_sum=saved.up_sum,
        down_sum=saved.down_sum,
        w_query=weights.w_query,
        w_key=weights.w_key,
        w_value=weights.w_value,
        w_out=weights.w_out,
        win_q=weights.win_q,
        win_k=weights.win_k,
        win_v=weights.win_v,
        win_out=weights.win_out,
    )
    held = BackSaved(*[getattr(saved, name) for name in BackSaved._fields])
    scratch = vmem(BackSaved) + [pltpu.VMEM((4, 4, width, TILE), BF) for width in Groups()]
    scratch += vmem(BackWork) + vmem(StateScan)
    for number, width in enumerate(Groups()):
        scratch += folded_scratch() if number < FOLDED else seq_scratch(width)
    scratch += mp_scratch() * 2
    scratch += [dma(CHUNKS * PER_CHUNK)] * 4 + [dma(24 * len(Groups._fields))] * 2 + [dma(24)] * 2
    scratch += [dma(64)]
    return BackOuts(
        *pl.pallas_call(
            backward_kernel,
            out_shape=[shape(dims, kind) for dims, kind in BackOuts()],
            in_specs=[INSIDE] * len(back_inputs) + [HBM] * (len(hbm) + len(held)),
            out_specs=[INSIDE] * len(BackOuts._fields),
            scratch_shapes=scratch,
            compiler_params=pltpu.CompilerParams(
                collective_id=1, has_side_effects=True, vmem_limit_bytes=VMEM_LIMIT
            ),
        )(*back_inputs, *hbm, *held)
    )


def hand_over_kernel(*refs):
    count = (len(refs) - 2) // 3
    ins, outs, held = refs[:count], refs[count : 2 * count], refs[2 * count : 3 * count]
    wide, sems = refs[3 * count :]
    block = ROWS // 4
    local = Locals(sems)
    parts = [pl.ds(k * block, block) for k in range(4)]
    loads = [local.start(ins[0].at[rows], held[0].at[rows]) for rows in parts]
    others = [local.start(src, dst) for src, dst in zip(ins[1:], held[1:])]
    copies = []
    for load, rows in zip(loads, parts):
        load.wait()
        wide[rows] = held[0][rows].astype(F32)
        copies.append(local.start(wide.at[rows], outs[0].at[rows]))
    for load, src, dst in zip(others, held[1:], outs[1:]):
        load.wait()
        copies.append(local.start(src, dst))
    for copy in copies:
        copy.wait()


def hand_over(arrays):
    kinds = [F32] + [array.dtype for array in arrays[1:]]
    return pl.pallas_call(
        hand_over_kernel,
        out_shape=[shape(array.shape, kind) for array, kind in zip(arrays, kinds)],
        in_specs=[HBM] * len(arrays),
        out_specs=[HBM] * len(arrays),
        scratch_shapes=[pltpu.VMEM(array.shape, array.dtype) for array in arrays]
        + [pltpu.VMEM((ROWS, D), F32), dma(2 * len(arrays) + 6)],
        compiler_params=pltpu.CompilerParams(vmem_limit_bytes=VMEM_LIMIT),
    )(*arrays)


def local(
    tokens,
    group_ids,
    gain_one,
    lin_query,
    lin_key,
    lin_value,
    lin_output,
    gain_two,
    win_query,
    win_key,
    win_value,
    win_output,
    gain_three,
    mlp_gate,
    mlp_up,
    mlp_down,
    out_grad,
):
    first, second, vectors = feature_tables()
    inputs = Inputs(
        tokens=tokens,
        group_row=group_ids.reshape(1, ROWS),
        gain_one=gain_one.reshape(1, D),
        gain_two=gain_two.reshape(1, D),
        gain_three=gain_three.reshape(1, D),
        first=first,
        second=second,
        vectors=vectors,
    )
    weights = Weights(
        out_grad=out_grad,
        w_query=lin_query.T,
        w_key=lin_key.T,
        w_value=lin_value,
        w_out=lin_output,
        win_k=win_key,
        win_v=win_value,
        win_q=win_query,
        win_out=win_output,
        w_gate=mlp_gate.T,
        w_up=mlp_up.T,
        w_down=mlp_down,
    )
    saved = forward(inputs, weights)
    outs = BackOuts(*backward(saved, inputs, weights))
    outs = BackOuts(*hand_over([*outs]))
    return (
        outs.result,
        outs.tokens_low,
        outs.gain_one.reshape(TILE),
        outs.query.T,
        outs.key.T,
        outs.value,
        outs.out,
        outs.gain_two.reshape(TILE),
        outs.win_q,
        outs.win_k,
        outs.win_v,
        outs.win_out,
        outs.gain_three.reshape(TILE),
        outs.gate.T,
        outs.up.T,
        outs.down,
    )


def solution(mesh):
    return jax.shard_map(
        local,
        mesh=mesh,
        in_specs=(
            P("seq", None),
            P("seq"),
            P(),
            P(None, "mp"),
            P(None, "mp"),
            P(None, "mp"),
            P("mp", None),
            P(),
            P(None, "mp"),
            P(None, "mp"),
            P(None, "mp"),
            P("mp", None),
            P(),
            P(None, "mp"),
            P(None, "mp"),
            P("mp", None),
            P("seq", None),
        ),
        out_specs=(
            P("seq", None),
            P("seq", None),
            P("seq"),
            P("seq", "mp"),
            P("seq", "mp"),
            P("seq", "mp"),
            P("mp", "seq"),
            P("seq"),
            P("seq", "mp"),
            P("seq", "mp"),
            P("seq", "mp"),
            P("mp", "seq"),
            P("seq"),
            P("seq", "mp"),
            P("seq", "mp"),
            P("mp", "seq"),
        ),
        check_vma=False,
    )
```

```python
import functools
import types
from typing import Any, NamedTuple

import jax
import jax.numpy as jnp
import numpy as np
from jax import lax
from jax.experimental import pallas as pl
from jax.experimental.pallas import tpu as pltpu
from jax.sharding import PartitionSpec as P

D = 2048
HD = 128
FEAT = 16
WIN = 64
FF = 704
FF_PAD = 768
ROWS = 512
TILE = 128
WIDE = 256
FEATURES = 160
STATE = FEATURES + 16

CHUNKS = 4
CHUNK = ROWS // CHUNKS
HALF = CHUNK // 2
PIECE = CHUNK // 8
OWN = 64
COLS = D // 2
PER_CHUNK = 21

EPSILON = 1e-05
MESH = pl.DeviceIdType.MESH
BF = jnp.bfloat16
F32 = jnp.float32
VMEM_LIMIT = 63 * 1024 * 1024 + 512 * 1024


class Place:
    def __init__(self):
        self.seq = lax.axis_index("seq")
        self.mp = lax.axis_index("mp")
        self.z, self.y = self.seq // 4, self.seq % 4
        self.x, self.core = self.mp // 2, self.mp % 2

    def peer(self):
        return (self.seq, self.x * 2 + (1 - self.core))

    def on_x(self, step):
        return (self.seq, ((self.x + step) % 4) * 2 + self.core)

    def on_y(self, step):
        return (self.z * 4 + (self.y + step) % 4, self.mp)

    def on_z(self, step):
        return (((self.z + step) % 4) * 4 + self.y, self.mp)

    def along(self, step):
        return ((self.seq + step) % 16, self.mp)


class Copies:
    def __init__(self, send_sems, recv_sems):
        self.send_sems, self.recv_sems = send_sems, recv_sems
        self.count, self.started = 0, []

    def start(self, src, dst, device):
        k = self.count
        self.count += 1
        copy = pltpu.make_async_remote_copy(
            src_ref=src,
            dst_ref=dst,
            send_sem=self.send_sems.at[k],
            recv_sem=self.recv_sems.at[k],
            device_id=device,
            device_id_type=MESH,
        )
        copy.start()
        self.started.append(copy)
        return copy

    def finish(self):
        for copy in self.started:
            copy.wait_send()


class Locals:
    def __init__(self, sems):
        self.sems, self.count = sems, 0

    def start(self, src, dst):
        copy = pltpu.make_async_copy(src, dst, self.sems.at[self.count])
        self.count += 1
        copy.start()
        return copy


def greet(devices):
    barrier = pltpu.get_barrier_semaphore()
    for device in devices:
        pl.semaphore_signal(barrier, inc=1, device_id=device, device_id_type=MESH)


def meet(count):
    pl.semaphore_wait(pltpu.get_barrier_semaphore(), count)


def rows_at(start, size):
    return pl.ds(pl.multiple_of(start, 16), size)


def dot(left, right):
    return lax.dot_general(left, right, (((1,), (0,)), ((), ())), preferred_element_type=F32)


def dot_nt(left, right):
    return lax.dot_general(left, right, (((1,), (1,)), ((), ())), preferred_element_type=F32)


def dot_tn(left, right):
    return lax.dot_general(left, right, (((0,), (0,)), ((), ())), preferred_element_type=F32)


def halves(values):
    high = values.astype(BF)
    return high, (values - high.astype(F32)).astype(BF)


class MpSum:
    def __init__(self, place, sems, part, full, own, bufs, lag=(0,) * CHUNKS, order=tuple(range(CHUNKS)), hold=False):
        self.place, self.part, self.full, self.own = place, part, full, own
        self.lag, self.order, self.hold = lag, order, hold
        self.send_sems, self.recv_sems = sems
        (self.from_peer, self.send_opp, self.send_right, self.send_left) = bufs[:4]
        (self.fwd, self.direct, self.comb) = bufs[4:]
        x = place.x
        self.turn = [(x + 2) % 4, (x + 1) % 4, (x + 3) % 4, x]
        self.peer, self.right, self.left = place.peer(), place.on_x(1), place.on_x(3)
        self.live = [types.SimpleNamespace(sent=[]) for _ in range(CHUNKS)]

    def start(self, j, src, dst, device):
        k = j * PER_CHUNK + len(self.live[j].sent)
        copy = pltpu.make_async_remote_copy(
            src_ref=src,
            dst_ref=dst,
            send_sem=self.send_sems.at[k],
            recv_sem=self.recv_sems.at[k],
            device_id=device,
            device_id_type=MESH,
        )
        copy.start()
        self.live[j].sent.append(copy)
        return copy

    def rows(self, j, core, x):
        return rows_at(j * CHUNK + core * HALF + x * PIECE, PIECE)

    def own_rows(self, j):
        return self.rows(j, self.place.core, self.place.x)

    def chip_sum(self, j, slot, low, size):
        cols = pl.ds(low, size)
        return self.part[self.rows(j, self.place.core, self.turn[slot]), cols].astype(
            F32
        ) + self.from_peer[j, slot, :, cols].astype(F32)

    def exchange(self, j):
        self.live[j].ex = [
            self.start(
                j,
                self.part.at[self.rows(j, 1 - self.place.core, at)],
                self.from_peer.at[j, slot],
                self.peer,
            )
            for slot, at in enumerate(self.turn)
        ]

    def first(self, j):
        live = self.live[j]
        low, high = pl.ds(0, COLS), pl.ds(COLS, COLS)
        live.ex[0].wait_recv()
        self.send_opp[j] = self.chip_sum(j, 0, 0, D).astype(BF)
        live.fr = self.start(j, self.send_opp.at[j, :, low], self.fwd.at[j, 0], self.right)
        live.fl = self.start(j, self.send_opp.at[j, :, high], self.fwd.at[j, 1], self.left)
        live.ex[1].wait_recv()
        self.send_right[j, 0] = self.chip_sum(j, 1, COLS, COLS).astype(BF)
        live.dr = self.start(j, self.send_right.at[j, 0], self.direct.at[j, 1], self.right)
        live.ex[2].wait_recv()
        self.send_left[j, 0] = self.chip_sum(j, 2, 0, COLS).astype(BF)
        live.dl = self.start(j, self.send_left.at[j, 0], self.direct.at[j, 0], self.left)

    def second(self, j):
        live = self.live[j]
        live.fr.wait_recv()
        self.send_right[j, 1] = (
            self.chip_sum(j, 1, 0, COLS) + self.fwd[j, 0].astype(F32)
        ).astype(BF)
        live.cr = self.start(j, self.send_right.at[j, 1], self.comb.at[j, 0], self.right)
        live.fl.wait_recv()
        self.send_left[j, 1] = (
            self.chip_sum(j, 2, COLS, COLS) + self.fwd[j, 1].astype(F32)
        ).astype(BF)
        live.cl = self.start(j, self.send_left.at[j, 1], self.comb.at[j, 1], self.left)

    def total(self, j):
        live, mine = self.live[j], pl.ds(j * PIECE, PIECE)
        live.ex[3].wait_recv()
        live.dl.wait_recv()
        live.cr.wait_recv()
        self.own[mine, 0:COLS] = (
            self.chip_sum(j, 3, 0, COLS)
            + self.direct[j, 0].astype(F32)
            + self.comb[j, 0].astype(F32)
        )
        live.dr.wait_recv()
        live.cl.wait_recv()
        self.own[mine, COLS:D] = (
            self.chip_sum(j, 3, COLS, COLS)
            + self.direct[j, 1].astype(F32)
            + self.comb[j, 1].astype(F32)
        )
        for copy in live.ex:
            copy.wait_send()

    def send(self, j, at, low, size, device):
        block = self.full.at[self.rows(j, self.place.core, at), pl.ds(low, size)]
        return self.start(j, block, block, device)

    def spread(self, j):
        live, x = self.live[j], self.place.x
        live.rl = self.send(j, x, 0, COLS, self.right)
        live.lh = self.send(j, x, COLS, COLS, self.left)
        live.rh = self.send(j, x, COLS, COLS, self.right)
        live.ll = self.send(j, x, 0, COLS, self.left)
        live.peers = [self.send(j, x, 0, D, self.peer)]

    def relay(self, j):
        live, x = self.live[j], self.place.x
        live.rl.wait_recv()
        live.gr = self.send(j, (x + 3) % 4, 0, COLS, self.right)
        live.lh.wait_recv()
        live.gl = self.send(j, (x + 1) % 4, COLS, COLS, self.left)
        live.rh.wait_recv()
        live.peers.append(self.send(j, (x + 3) % 4, 0, D, self.peer))
        live.ll.wait_recv()
        live.peers.append(self.send(j, (x + 1) % 4, 0, D, self.peer))

    def last(self, j):
        live, x = self.live[j], self.place.x
        live.gr.wait_recv()
        live.peers.append(self.send(j, (x + 2) % 4, 0, COLS, self.peer))
        live.gl.wait_recv()
        live.peers.append(self.send(j, (x + 2) % 4, COLS, COLS, self.peer))

    def arrived(self, j):
        for copy in self.live[j].peers:
            copy.wait_recv()
        for copy in self.live[j].sent[4:]:
            copy.wait_send()

    def slots(self, produce, finish, ready=None):
        for slot in range(self.lag[-1] + (8 if self.hold else 7)):
            for position, j in enumerate(self.order):
                stage = slot - self.lag[position]
                if self.hold and stage >= 4:
                    if stage == 4:
                        self.spread(j)
                        continue
                    stage -= 1
                if stage == 0:
                    produce(j)
                    self.exchange(j)
                elif stage == 1:
                    self.first(j)
                elif stage == 2:
                    self.second(j)
                elif stage == 3:
                    self.total(j)
                    finish(j)
                    if not self.hold:
                        self.spread(j)
                elif stage == 4:
                    self.relay(j)
                elif stage == 5:
                    self.last(j)
                elif stage == 6:
                    self.arrived(j)
                    if ready is not None:
                        ready(j)
            yield slot


def mp_scratch():
    ring = pltpu.VMEM((CHUNKS, 2, PIECE, COLS), BF)
    return [pltpu.VMEM((CHUNKS, 4, PIECE, D), BF), pltpu.VMEM((CHUNKS, PIECE, D), BF)] + [ring] * 5


def dma(count):
    return pltpu.SemaphoreType.DMA((count,))


def run(slots):
    for _ in slots:
        pass


def norm_rows_of(total):
    row = lax.broadcasted_iota(jnp.int32, (16, TILE), 0)
    return jnp.where(row == 0, total[:, 0:TILE], jnp.where(row == 1, total[:, TILE:WIDE], 0.0))


class StateScan(NamedTuple):
    mine: Any = ((2, STATE, HD), BF)
    early: Any = ((2, 3, STATE, HD), BF)
    sent: Any = ((2, 2, STATE, HD), BF)
    late: Any = ((2, 3, STATE, HD), BF)


def state_scan(place, copies, bufs, states, norms, reverse):
    def counted(position, step):
        at = (position - step + 4) % 4
        reached = at > position if reverse else at < position
        return jnp.where(reached, 1.0, 0.0)

    def wider(step):
        to = (place.y + step) % 4
        return (to < place.y if reverse else to > place.y).astype(jnp.int32)

    def put(head, total):
        states[head, 0:FEATURES] = total[0:FEATURES]
        states[head, FEATURES:WIDE] = jnp.zeros((WIDE - FEATURES, HD), F32)
        norms[head, 0:1, 0:TILE] = total[FEATURES : FEATURES + 1]
        norms[head, 0:1, TILE:WIDE] = total[FEATURES + 1 : FEATURES + 2]

    steps = (1, 2, 3)
    over = [copies.start(bufs.mine.at[0], bufs.early.at[0, k - 1], place.on_y(k)) for k in steps]
    across = [copies.start(bufs.mine.at[1], bufs.early.at[1, k - 1], place.on_z(k)) for k in steps]
    yield
    total, before = bufs.mine[0].astype(F32), jnp.zeros((STATE, HD), F32)
    for k, copy in zip(steps, over):
        copy.wait_recv()
        part = bufs.early[0, k - 1].astype(F32)
        total, before = total + part, before + counted(place.y, k) * part
    bufs.sent[0, 0] = total.astype(BF)
    over = [copies.start(bufs.sent.at[0, 0], bufs.late.at[0, k - 1], place.on_z(k)) for k in steps]
    put(0, before)
    before = jnp.zeros((STATE, HD), F32)
    for k, copy in zip(steps, across):
        copy.wait_recv()
        before = before + counted(place.z, k) * bufs.early[1, k - 1].astype(F32)
    bufs.sent[1, 0] = before.astype(BF)
    bufs.sent[1, 1] = (before + bufs.mine[1].astype(F32)).astype(BF)
    across = [
        copies.start(bufs.sent.at[1, wider(k)], bufs.late.at[1, k - 1], place.on_y(k)) for k in steps
    ]
    put(1, before)
    yield
    for head, sent in enumerate((over, across)):
        total = jnp.zeros((STATE, HD), F32)
        for k, copy in zip(steps, sent):
            copy.wait_recv()
            part = bufs.late[head, k - 1].astype(F32)
            total = total + (counted(place.z, k) * part if head == 0 else part)
        states[head, 0:FEATURES] += total[0:FEATURES]
        norms[head, 0:1, 0:TILE] += total[FEATURES : FEATURES + 1]
        norms[head, 0:1, TILE:WIDE] += total[FEATURES + 1 : FEATURES + 2]
    yield


def feature_tables():
    pairs = [(a, b) for a in range(FEAT) for b in range(a, FEAT)]
    first = np.zeros((2, 2 * FEAT, WIDE), np.float32)
    second = np.zeros((2, 2 * FEAT, WIDE), np.float32)
    vectors = np.zeros((8, WIDE), np.float32)
    vectors[0, 0] = vectors[1, 0] = vectors[2, 0] = 1.0
    for a in range(FEAT):
        vectors[1, 1 + a] = 1.0
        vectors[2, 1 + a] = FEAT ** (-0.25)
        for h in range(2):
            first[h, h * FEAT + a, 1 + a] = 1.0
    for number, (a, b) in enumerate(pairs):
        at = 1 + FEAT + number
        vectors[2, at] = (1.0 if a == b else 2.0**0.5) * (2.0 * FEAT) ** (-0.5)
        for h in range(2):
            first[h, h * FEAT + a, at] = 1.0
            second[h, h * FEAT + b, at] = 1.0
    return jnp.asarray(first, BF), jnp.asarray(second, BF), jnp.asarray(vectors, F32)


def factors(head, values, first, second, vectors):
    high, low = values
    left = dot(high, first[head]) + dot(low, first[head]) + vectors[0:1]
    right = dot(high, second[head]) + dot(low, second[head]) + vectors[1:2]
    return left, right


def of_head(values, head):
    lane = lax.broadcasted_iota(jnp.int32, values.shape, 1)
    return jnp.where((lane >= head * FEAT) & (lane < (head + 1) * FEAT), values, jnp.zeros_like(values))


def products(head, query, key, rows, count):
    high, low = (of_head(part[rows], head) for part in query)
    key_high, key_low = (part[0:count] for part in key)
    return dot_nt(high, key_high) + dot_nt(low, key_high) + dot_nt(high, key_low)


def shape(dims, kind):
    return jax.ShapeDtypeStruct(dims, kind)


def normed(rows, gain):
    factor = lax.rsqrt(jnp.mean(rows * rows, axis=-1, keepdims=True) + EPSILON)
    return rows * factor * gain


def column(group_row, held):
    for k in range(ROWS // TILE):
        block = group_row[0:1, k * TILE : (k + 1) * TILE].astype(F32)
        held[k * TILE : (k + 1) * TILE] = jnp.broadcast_to(block, (TILE, TILE)).T


def kept_pairs(group_col, group_row, tile):
    count = (tile + 1) * TILE
    row = lax.broadcasted_iota(jnp.int32, (TILE, count), 0) + tile * TILE
    col = lax.broadcasted_iota(jnp.int32, (TILE, count), 1)
    groups = group_col[tile * TILE : (tile + 1) * TILE, 0:1]
    return (col <= row) & (groups == group_row[0:1, 0:count].astype(F32))


def weight_block(into, left_t, right, quarter):
    count = into.shape[2]
    block = dot(left_t[0:count], right[:, quarter * 512 : (quarter + 1) * 512]).astype(BF)
    for k in range(4):
        into[quarter, k] = block[:, k * TILE : (k + 1) * TILE]


def back_through_norm(resid, grad, normed_grad, gain):
    factor = lax.rsqrt(jnp.mean(resid * resid, axis=-1, keepdims=True) + EPSILON)
    unit = resid * factor
    scaled = normed_grad * gain
    total = grad + factor * (scaled - unit * jnp.mean(scaled * unit, axis=-1, keepdims=True))
    return total, jnp.sum(normed_grad * unit, axis=0, keepdims=True)


LAG_ONE = (0, 0, 0, 0)
LAG_FIVE = (0, 0, 0, 0)


class Inputs(NamedTuple):
    tokens: Any
    group_row: Any
    gain_one: Any
    gain_two: Any
    gain_three: Any
    first: Any
    second: Any
    vectors: Any


class Weights(NamedTuple):
    out_grad: Any = ((ROWS, D), BF)
    w_query: Any = ((2 * FEAT, D), BF)
    w_key: Any = ((2 * FEAT, D), BF)
    w_value: Any = ((D, WIDE), BF)
    w_out: Any = ((WIDE, D), BF)
    win_k: Any = ((D, WIDE), BF)
    win_v: Any = ((D, WIDE), BF)
    win_q: Any = ((D, WIDE), BF)
    win_out: Any = ((WIDE, D), BF)
    w_gate: Any = ((FF_PAD, D), BF)
    w_up: Any = ((FF_PAD, D), BF)
    w_down: Any = ((FF_PAD, D), BF)


class Saved(NamedTuple):
    normed_one: Any = ((ROWS, D), BF)
    query: Any = ((2, ROWS, 2 * FEAT), BF)
    key: Any = ((2, ROWS, 2 * FEAT), BF)
    value: Any = ((ROWS, WIDE), BF)
    carried: Any = ((2, WIDE, HD), F32)
    carried_norm: Any = ((2, 1, WIDE), F32)
    quotient: Any = ((ROWS, WIDE), F32)
    denominator: Any = ((2, ROWS, 1), F32)
    mixed_lin: Any = ((ROWS, WIDE), BF)
    resid_one: Any = ((OWN, D), F32)
    normed_two: Any = ((ROWS, D), BF)
    query_win: Any = ((ROWS, WIDE), BF)
    keys_all: Any = ((ROWS + WIN, WIDE), BF)
    values_all: Any = ((ROWS + WIN, WIDE), BF)
    probs: Any = ((2, ROWS, TILE), F32)
    mixed_win: Any = ((ROWS, WIDE), BF)
    resid_two: Any = ((OWN, D), F32)
    low_four: Any = ((ROWS, D), BF)
    grad_own: Any = ((OWN, D), F32)
    gain_sum: Any = ((8, D), F32)
    gate_sum: Any = ((4, 4, FF, TILE), BF)
    up_sum: Any = ((4, 4, FF, TILE), BF)
    down_sum: Any = ((4, 4, FF, TILE), BF)
    part_three: Any = ((ROWS, D), BF)


class ForwardWork(NamedTuple):
    part: Any = ((ROWS, D), BF)
    own: Any = ((OWN, D), F32)
    group_col: Any = ((ROWS, TILE), F32)
    tail_flag: Any = ((16, TILE), BF)
    halo_flag: Any = ((16, TILE), BF)
    query_feat: Any = ((2, ROWS, WIDE), BF)
    key_feat: Any = ((2, ROWS, WIDE), BF)
    normed_three: Any = ((ROWS, D), BF)
    hidden_grad: Any = ((ROWS, FF_PAD), F32)
    hidden: Any = ((ROWS, FF_PAD), BF)
    gate_low: Any = ((ROWS, FF_PAD), BF)
    up_low: Any = ((ROWS, FF_PAD), BF)
    flipped: Any = ((FF_PAD, ROWS), BF)


class SeqSum:
    def __init__(self, place, copies, blocks, out, bufs):
        self.place, self.copies, self.blocks, self.out = place, copies, blocks, out
        z, y = place.z, place.y
        quarter = self.quarter = blocks.shape[2] // 4
        ring_y, ring_z = (place.on_y(1), place.on_y(3)), (place.on_z(1), place.on_z(3))

        def pick_one(k, half):
            return blocks.at[:, (y + k) % 4, pl.ds(half * quarter, quarter)]

        def pick_two(k, half):
            return blocks.at[(z + k) % 4, :, pl.ds((2 + half) * quarter, quarter)]

        def pick_three(k, half):
            return blocks.at[(z + k) % 4, y, pl.ds(half * quarter, quarter)]

        def pick_four(k, half):
            return blocks.at[z, (y + k) % 4, pl.ds((2 + half) * quarter, quarter)]

        live = [types.SimpleNamespace() for _ in range(4)]
        self.early = ((ring_y, pick_one, bufs[0:3], live[0]), (ring_z, pick_two, bufs[3:6], live[1]))
        self.late = ((ring_z, pick_three, bufs[6:9], live[2]), (ring_y, pick_four, bufs[9:12], live[3]))

    def begin(self, rings):
        for (right, left), pick, (fwd, direct, comb), live in rings:
            live.fr = self.copies.start(pick(2, 0), fwd.at[0], right)
            live.fl = self.copies.start(pick(2, 1), fwd.at[1], left)
            live.dr = self.copies.start(pick(1, 1), direct.at[1], right)
            live.dl = self.copies.start(pick(3, 0), direct.at[0], left)

    def join(self, rings):
        for (right, left), pick, (fwd, direct, comb), live in rings:
            live.fr.wait_recv()
            block = pick(1, 0)
            block[...] = (block[...].astype(F32) + fwd[0].astype(F32)).astype(BF)
            live.cr = self.copies.start(block, comb.at[0], right)
            live.fl.wait_recv()
            block = pick(3, 1)
            block[...] = (block[...].astype(F32) + fwd[1].astype(F32)).astype(BF)
            live.cl = self.copies.start(block, comb.at[1], left)

    def total(self, ring, half):
        _, pick, (fwd, direct, comb), live = ring
        (live.cr if half == 0 else live.cl).wait_recv()
        total = pick(0, half)[...].astype(F32) + comb[half].astype(F32)
        if direct is None:
            return total
        (live.dl if half == 0 else live.dr).wait_recv()
        return total + direct[half].astype(F32)

    def fold(self, rings):
        for _, pick, (fwd, direct, _), live in rings:
            for copy, block, got in (
                (live.fr, pick(1, 0), fwd.at[0]),
                (live.fl, pick(3, 1), fwd.at[1]),
                (live.dl, pick(0, 0), direct.at[0]),
                (live.dr, pick(0, 1), direct.at[1]),
            ):
                copy.wait_recv()
                block[...] = (block[...].astype(F32) + got[...].astype(F32)).astype(BF)

    def pass_on(self, rings):
        for (right, left), pick, (_, _, comb), live in rings:
            live.cr = self.copies.start(pick(1, 0), comb.at[0], right)
            live.cl = self.copies.start(pick(3, 1), comb.at[1], left)

    def step(self, number):
        if number == 0 and self.early[0][2][1] is None:
            self.pass_on(self.early)
        elif number == 0:
            self.begin(self.early)
        elif number == 1:
            if self.early[0][2][1] is not None:
                self.join(self.early)
        elif number == 2:
            for ring in self.early:
                for half in range(2):
                    block = ring[1](0, half)
                    block[...] = self.total(ring, half).astype(BF)
            self.begin(self.late)
        elif number == 3:
            self.join(self.late)
        else:
            size = self.quarter
            for half in range(2):
                self.out[pl.ds(half * size, size)] = self.total(self.late[0], half)
                self.out[pl.ds((2 + half) * size, size)] = self.total(self.late[1], half)


def seq_scratch(width):
    early, late = (2, 4, width // 4, TILE), (2, width // 4, TILE)
    return [pltpu.VMEM(early, BF)] * 6 + [pltpu.VMEM(late, BF)] * 6


FOLDED = 2


def folded_scratch():
    late = pltpu.VMEM((2, FF // 4, TILE), BF)
    return [pltpu.VMEM((2, 4, FF // 4, TILE), BF)] * 2 + [late] * 6


def taker(refs):
    refs = list(refs)

    def take(kind):
        return kind(*[refs.pop(0) for _ in kind._fields])

    def some(count):
        return [refs.pop(0) for _ in range(count)]

    return take, some


def vmem(kind):
    return [pltpu.VMEM(*entry) for entry in kind()]


def forward_kernel(*refs):
    take, some = taker(refs)
    inputs, hbm_weights, hbm_saved = take(Inputs), take(Weights), take(Saved)
    weights, saved, work, scan_bufs = take(Weights), take(Saved), take(ForwardWork), take(StateScan)
    bufs = some(7)
    fold_bufs = [some(4) for _ in range(FOLDED)]
    fold_sems = some(2)
    mp_sems, (state_send, state_recv), (halo_send, halo_recv), (local_sems,) = (
        some(2),
        some(2),
        some(2),
        some(1),
    )
    place = Place()
    local = Locals(local_sems)
    loads = []
    for src, dst in zip(hbm_weights[1:], weights[1:]):
        loads.append(local.start(src, dst if src.shape == dst.shape else dst.at[pl.ds(0, FF)]))
    loads = Weights(local.start(hbm_weights.out_grad, weights.out_grad), *loads)
    saves = []

    def save(*pairs):
        for src, dst in pairs:
            saves.append(local.start(src, dst))

    greet(
        [place.peer()]
        + [place.on_x(k) for k in (1, 3)]
        + [place.on_y(k) for k in (1, 2, 3)]
        + [place.on_z(k) for k in (1, 2, 3)]
        + [place.along(1), place.along(15)]
    )
    for ref in (weights.w_gate, weights.w_up, weights.w_down):
        ref[FF:FF_PAD] = jnp.zeros((FF_PAD - FF, D), BF)
    tokens, group_row, group_col = inputs.tokens, inputs.group_row, work.group_col
    first, second, vectors = inputs.first, inputs.second, inputs.vectors
    scale = vectors[2:3]
    normed_one = saved.normed_one

    def norm_rows(i, _):
        rows = rows_at(i * 32, 32)
        normed_one[rows] = normed(tokens[rows].astype(F32), inputs.gain_one[...]).astype(BF)
        return 0

    lax.fori_loop(0, ROWS // 32, norm_rows, 0)
    save((normed_one, hbm_saved.normed_one))
    column(group_row, group_col)
    query, key, value = saved.query, saved.key, saved.value
    for load, weight, held in (
        (loads.w_key, weights.w_key, key),
        (loads.w_query, weights.w_query, query),
    ):
        load.wait()
        held[0], held[1] = halves(dot_nt(normed_one[...], weight[...]))
    loads.w_value.wait()
    value[...] = dot(normed_one[...], weights.w_value[...]).astype(BF)

    last = group_row[0:1, ROWS - 1 : ROWS].astype(F32)
    in_last = (group_col[:, 0:1] == last).astype(F32)
    query_feat, key_feat, mine = work.query_feat, work.key_feat, scan_bufs.mine
    for head in range(2):
        left, right = factors(head, (key[0], key[1]), first, second, vectors)
        feat = (left * right * scale).astype(BF)
        key_feat[head] = feat
        kept = feat.astype(F32) * in_last
        state = dot_tn(kept.astype(BF), value[:, head * HD : (head + 1) * HD])
        mine[head, 0:FEATURES] = state[0:FEATURES].astype(BF)
        mine[head, FEATURES:STATE] = norm_rows_of(jnp.sum(kept, axis=0, keepdims=True)).astype(BF)
    meet(11)
    copies_state = Copies(state_send, state_recv)
    scan = state_scan(place, copies_state, scan_bufs, saved.carried, saved.carried_norm, False)
    next(scan)
    save((query, hbm_saved.query), (key, hbm_saved.key), (value, hbm_saved.value))
    quotient, denominator = saved.quotient, saved.denominator
    for head in range(2):
        left, right = factors(head, (query[0], query[1]), first, second, vectors)
        query_feat[head] = (left * right * scale).astype(BF)
    for tile in range(ROWS // TILE):
        rows, count = pl.ds(tile * TILE, TILE), (tile + 1) * TILE
        kept = kept_pairs(group_col, group_row, tile)
        for head in range(2):
            inner = products(head, (query.at[0], query.at[1]), (key.at[0], key.at[1]), rows, count)
            block = jnp.where(kept, 1.0 + inner * 0.25 + inner * inner * 0.03125, 0.0).astype(BF)
            denominator[head, rows] = jnp.sum(block.astype(F32), axis=1, keepdims=True)
            quotient[rows, head * HD : (head + 1) * HD] = dot(
                block, value[0:count, head * HD : (head + 1) * HD]
            )
        if tile == 1:
            next(scan)
    loads.w_down.wait()
    loads.out_grad.wait()
    work.hidden_grad[...] = dot_nt(weights.out_grad[...], weights.w_down[...])
    for _ in scan:
        pass
    copies_state.finish()
    first_group = group_row[0:1, 0:1].astype(F32)
    incoming = (group_col[:, 0:1] == first_group).astype(F32) * jnp.where(place.seq > 0, 1.0, 0.0)
    carried, carried_norm, mixed_lin = saved.carried, saved.carried_norm, saved.mixed_lin
    save((carried, hbm_saved.carried), (carried_norm, hbm_saved.carried_norm))
    for head in range(2):
        lanes = slice(head * HD, (head + 1) * HD)
        feat = query_feat[head]
        numer = quotient[:, lanes] + incoming * dot(feat, carried[head].astype(BF))
        denom = denominator[head] + incoming * jnp.sum(
            feat.astype(F32) * carried_norm[head], axis=1, keepdims=True
        )
        ratio = numer / denom
        denominator[head] = denom
        quotient[:, lanes] = ratio
        mixed_lin[:, lanes] = ratio.astype(BF)
    save(
        (quotient, hbm_saved.quotient),
        (denominator, hbm_saved.denominator),
        (mixed_lin, hbm_saved.mixed_lin),
    )
    loads.w_out.wait()

    part, own = work.part, work.own
    resid_one, resid_two = saved.resid_one, saved.resid_two
    normed_two, normed_three = saved.normed_two, work.normed_three
    sum_one = MpSum(place, mp_sems, part, normed_two, own, bufs, LAG_ONE, (3, 0, 1, 2))
    sum_two = MpSum(place, mp_sems, part, normed_three, own, bufs, (0, 1, 2, 3))
    sum_four = MpSum(place, mp_sems, part, saved.low_four, own, bufs, (0, 0, 2, 2))

    def produce_one(j):
        rows = pl.ds(j * CHUNK, CHUNK)
        part[rows] = dot(mixed_lin[rows], weights.w_out[...]).astype(BF)

    def finish_one(j):
        mine = pl.ds(j * PIECE, PIECE)
        rows = own[mine] + tokens[sum_one.own_rows(j)].astype(F32)
        resid_one[mine] = rows
        normed_two[sum_one.own_rows(j)] = normed(rows, inputs.gain_two[...]).astype(BF)

    query_win, keys_all, values_all = saved.query_win, saved.keys_all, saved.values_all
    copies_halo = Copies(halo_send, halo_recv)
    lane = lax.broadcasted_iota(jnp.int32, (1, TILE), 1)
    group_blocks = [group_row[0:1, k * TILE : (k + 1) * TILE].astype(F32) for k in range(4)]
    turned = [pltpu.roll(block, WIN, 1) for block in group_blocks]
    work.tail_flag[...] = jnp.broadcast_to((turned[3] == last).astype(F32), (16, TILE)).astype(BF)
    halo = []

    def ready_one(j):
        rows = pl.ds(j * CHUNK, CHUNK)
        below = pl.ds(WIN + j * CHUNK, CHUNK)
        if j == 3:
            for load in (loads.win_k, loads.win_v, loads.win_q):
                load.wait()
        keys_all[below] = dot(normed_two[rows], weights.win_k[...]).astype(BF)
        values_all[below] = dot(normed_two[rows], weights.win_v[...]).astype(BF)
        if j == 3:
            for ref in (keys_all, values_all):
                halo.append(
                    copies_halo.start(ref.at[pl.ds(ROWS, WIN)], ref.at[pl.ds(0, WIN)], place.along(1))
                )
            halo.append(copies_halo.start(work.tail_flag, work.halo_flag, place.along(1)))
        query_win[rows] = dot(normed_two[rows], weights.win_q[...]).astype(BF)
        if j != 3:
            next(two)

    probs, mixed_win = saved.probs, saved.mixed_win
    tile_row = lax.broadcasted_iota(jnp.int32, (WIN, TILE), 0)
    tile_col = lax.broadcasted_iota(jnp.int32, (WIN, TILE), 1)
    near = (tile_col > tile_row) & (tile_col <= tile_row + WIN)
    score_scale = HD ** (-0.5)

    def window_tile(t):
        rows = pl.ds(t * WIN, WIN)
        if t == 0:
            flag = jnp.where(place.seq > 0, work.halo_flag[0:1].astype(F32), 0.0)
            groups = jnp.where(lane < WIN, jnp.where(flag > 0.5, first_group, -2.0), turned[0])
        elif t % 2 == 1:
            groups = group_blocks[t // 2]
        else:
            groups = jnp.where(lane < WIN, turned[t // 2 - 1], turned[t // 2])
        kept = near & (group_col[rows] == groups)
        for head in range(2):
            lanes = slice(head * HD, (head + 1) * HD)
            scores = dot_nt(query_win[rows, lanes], keys_all[t * WIN : t * WIN + TILE, lanes])
            scores = jnp.where(kept, scores * score_scale, -1e30)
            exp_scores = jnp.exp(scores - jnp.max(scores, axis=1, keepdims=True))
            found = exp_scores / jnp.sum(exp_scores, axis=1, keepdims=True)
            probs[head, rows] = found
            mixed_win[rows, lanes] = dot(
                found.astype(BF), values_all[t * WIN : t * WIN + TILE, lanes]
            ).astype(BF)

    def produce_two(j):
        if j == 0:
            for copy in halo:
                copy.wait_recv()
            loads.win_out.wait()
        window_tile(2 * j)
        window_tile(2 * j + 1)
        rows = pl.ds(j * CHUNK, CHUNK)
        part[rows] = dot(mixed_win[rows], weights.win_out[...]).astype(BF)

    def finish_two(j):
        mine = pl.ds(j * PIECE, PIECE)
        rows = own[mine] + resid_one[mine]
        resid_two[mine] = rows
        normed_three[sum_two.own_rows(j)] = normed(rows, inputs.gain_three[...]).astype(BF)

    w_gate, w_up, w_down, og = weights.w_gate, weights.w_up, weights.w_down, weights.out_grad
    hidden, gate_low, up_low = work.hidden, work.gate_low, work.up_low

    def ready_two(j):
        if j % 2 == 0:
            return
        if j == 1:
            for load in (loads.w_gate, loads.w_up):
                load.wait()
        rows = pl.ds((j - 1) * CHUNK, 2 * CHUNK)
        gate = dot_nt(normed_three[rows], w_gate[...])
        up = dot_nt(normed_three[rows], w_up[...])
        sigmoid = 1.0 / (1.0 + jnp.exp(-gate))
        act, hidden_grad = gate * sigmoid, work.hidden_grad[rows]
        hidden[rows] = (act * up).astype(BF)
        up_low[rows] = (hidden_grad * act).astype(BF)
        gate_low[rows] = (hidden_grad * up * (sigmoid + act * (1.0 - sigmoid))).astype(BF)
        part[rows] = (dot(gate_low[rows], w_gate[...]) + dot(up_low[rows], w_up[...])).astype(BF)
        next(four)

    one = sum_one.slots(produce_one, finish_one, ready_one)
    two = sum_two.slots(produce_two, finish_two, ready_two)
    def finish_four(j):
        mine, rows = pl.ds(j * PIECE, PIECE), sum_four.own_rows(j)
        total, here = back_through_norm(
            resid_two[mine], og[rows].astype(F32), own[mine], inputs.gain_three[...]
        )
        saved.gain_sum[0:1] += here
        saved.grad_own[mine] = total
        saved.low_four[rows] = total.astype(BF)

    four = sum_four.slots(lambda j: None, finish_four)
    saved.gain_sum[...] = jnp.zeros_like(saved.gain_sum)
    run(one)
    copies_halo.finish()
    save(
        (resid_one, hbm_saved.resid_one),
        (normed_two, hbm_saved.normed_two),
        (query_win, hbm_saved.query_win),
        (keys_all, hbm_saved.keys_all),
        (values_all, hbm_saved.values_all),
    )
    for slot in two:
        if slot == 8:
            next(four)
    save(
        (probs, hbm_saved.probs), (mixed_win, hbm_saved.mixed_win), (resid_two, hbm_saved.resid_two)
    )

    def project_down(half):
        cols = pl.ds(half * 1024, 1024)
        saved.part_three[:, cols] = dot(hidden[...], w_down[:, cols]).astype(BF)
        if half == 1:
            save((saved.part_three, hbm_saved.part_three))

    seq_copies = Copies(*fold_sems)
    folds = []

    def weight_back(number, into, to_hbm, left, right, quarter):
        if quarter == 0:
            work.flipped[...] = left[...].T
        weight_block(into, work.flipped, right, quarter)
        if quarter < 3:
            return
        if number < FOLDED:
            fwd_y, direct_y, fwd_z, direct_z = fold_bufs[number]
            early = [fwd_y, direct_y, None, fwd_z, direct_z, None]
            seq_sum = SeqSum(place, seq_copies, into, None, early + [None] * 6)
            seq_sum.begin(seq_sum.early)
            folds.append((seq_sum, into, to_hbm))
        else:
            save((into, to_hbm))

    blocks = []
    for number, (into, to_hbm, left, right) in enumerate(
        (
            (saved.gate_sum, hbm_saved.gate_sum, gate_low, normed_three),
            (saved.up_sum, hbm_saved.up_sum, up_low, normed_three),
            (saved.down_sum, hbm_saved.down_sum, hidden, og),
        )
    ):
        blocks += [
            functools.partial(weight_back, number, into, to_hbm, left, right, k) for k in range(4)
        ]
    blocks += [functools.partial(project_down, k) for k in range(2)]
    for _ in four:
        for _ in range(4):
            if blocks:
                blocks.pop(0)()
    save(
        (saved.low_four, hbm_saved.low_four),
        (saved.grad_own, hbm_saved.grad_own),
        (saved.gain_sum, hbm_saved.gain_sum),
    )
    for block in blocks:
        block()
    for seq_sum, into, to_hbm in folds:
        seq_sum.fold(seq_sum.early)
        save((into, to_hbm))
    seq_copies.finish()
    for copy in saves:
        copy.wait()


HBM = pl.BlockSpec(memory_space=pl.ANY)
INSIDE = pl.BlockSpec(memory_space=pltpu.VMEM)


def forward(inputs, weights):
    scratch = vmem(Weights) + vmem(Saved) + vmem(ForwardWork) + vmem(StateScan) + mp_scratch()
    scratch += [pltpu.VMEM((2, 4, FF // 4, TILE), BF)] * (4 * FOLDED) + [dma(8 * FOLDED)] * 2
    scratch += [dma(CHUNKS * PER_CHUNK)] * 2 + [dma(12)] * 2 + [dma(3)] * 2
    scratch += [dma(len(Weights._fields) + len(Saved._fields))]
    return Saved(
        *pl.pallas_call(
            forward_kernel,
            out_shape=[shape(dims, kind) for dims, kind in Saved()],
            in_specs=[INSIDE] * len(inputs) + [HBM] * len(weights),
            out_specs=[HBM] * len(Saved._fields),
            scratch_shapes=scratch,
            compiler_params=pltpu.CompilerParams(
                collective_id=0, has_side_effects=True, vmem_limit_bytes=VMEM_LIMIT
            ),
        )(*inputs, *weights)
    )


class Groups(NamedTuple):
    gate: Any = FF
    up: Any = FF
    down: Any = FF
    win_out: Any = WIDE
    win: Any = 3 * WIDE
    out: Any = WIDE
    lin: Any = WIDE + 4 * FEAT


class BackInputs(NamedTuple):
    group_row: Any
    gain_one: Any
    gain_two: Any
    first: Any
    second: Any
    vectors: Any


class BackHbm(NamedTuple):
    part_three: Any
    low_four: Any
    grad_own: Any
    gain_sum: Any
    tokens: Any
    normed_one: Any
    normed_two: Any
    gate_sum: Any
    up_sum: Any
    down_sum: Any
    w_query: Any
    w_key: Any
    w_value: Any
    w_out: Any
    win_q: Any
    win_k: Any
    win_v: Any
    win_out: Any


SPECS = Saved()


class BackSaved(NamedTuple):
    query: Any = SPECS.query
    key: Any = SPECS.key
    value: Any = SPECS.value
    carried: Any = SPECS.carried
    carried_norm: Any = SPECS.carried_norm
    quotient: Any = SPECS.quotient
    denominator: Any = SPECS.denominator
    mixed_lin: Any = SPECS.mixed_lin
    resid_one: Any = SPECS.resid_one
    query_win: Any = SPECS.query_win
    keys_all: Any = SPECS.keys_all
    values_all: Any = SPECS.values_all
    probs: Any = SPECS.probs
    mixed_win: Any = SPECS.mixed_win
    resid_two: Any = SPECS.resid_two


class BackOuts(NamedTuple):
    tokens_low: Any = ((ROWS, D), BF)
    gain_one: Any = ((1, TILE), F32)
    gain_two: Any = ((1, TILE), F32)
    gain_three: Any = ((1, TILE), F32)
    gate: Any = ((FF, TILE), F32)
    up: Any = ((FF, TILE), F32)
    down: Any = ((FF, TILE), F32)
    win_out: Any = ((WIDE, TILE), F32)
    out: Any = ((WIDE, TILE), F32)
    win_q: Any = ((TILE, WIDE), F32)
    win_k: Any = ((TILE, WIDE), F32)
    win_v: Any = ((TILE, WIDE), F32)
    value: Any = ((TILE, WIDE), F32)
    query: Any = ((2 * FEAT, TILE), F32)
    key: Any = ((2 * FEAT, TILE), F32)
    result: Any = ((ROWS, D), BF)


class BackWork(NamedTuple):
    part: Any = ((ROWS, D), BF)
    other_full: Any = ((ROWS, D), BF)
    own: Any = ((OWN, D), F32)
    grad_own: Any = ((OWN, D), F32)
    token_own: Any = ((OWN, D), BF)
    group_col: Any = ((ROWS, TILE), F32)
    normed_low: Any = ((ROWS, D), BF)
    w_query: Any = ((2 * FEAT, D), BF)
    w_key: Any = ((2 * FEAT, D), BF)
    w_out: Any = ((WIDE, D), BF)
    win_out: Any = ((WIDE, D), BF)
    w_win: Any = ((D, 3 * WIDE), BF)
    mixed_grad: Any = ((ROWS, WIDE), BF)
    keys_sum: Any = ((ROWS + WIN, WIDE), F32)
    values_sum: Any = ((ROWS + WIN, WIDE), F32)
    back_key: Any = ((2, WIN, WIDE), BF)
    back_value: Any = ((2, WIN, WIDE), BF)
    win_grads: Any = ((ROWS, 3 * WIDE), BF)
    flipped: Any = ((3 * WIDE, ROWS), BF)
    denom_grad: Any = ((2, ROWS, 1), F32)
    query_sum: Any = ((ROWS, 2 * FEAT), F32)
    key_sum: Any = ((ROWS, 2 * FEAT), F32)
    query_low: Any = ((ROWS, 2 * FEAT), BF)
    key_low: Any = ((ROWS, 2 * FEAT), BF)
    state_sum: Any = ((2, WIDE, HD), F32)
    norm_sum: Any = ((2, 1, WIDE), F32)
    gain_sums: Any = ((16, D), F32)
    gain_low: Any = ((16, D), BF)
    gain_z: Any = ((3, 16, 512), BF)
    gain_zz: Any = ((16, 512), BF)
    gain_y: Any = ((3, 16, TILE), BF)
    gain_x: Any = ((16, TILE), BF)
    gain_xx: Any = ((3, 16, TILE), BF)
    gain_p: Any = ((16, TILE), BF)
    gain_pp: Any = ((16, TILE), BF)
    sum_win: Any = ((3 * WIDE, TILE), F32)
    sum_lin: Any = ((WIDE + 4 * FEAT, TILE), F32)
    later: Any = ((2, WIDE, HD), F32)
    later_norm: Any = ((2, 1, WIDE), F32)


def backward_kernel(*refs):
    take, some = taker(refs)
    inputs, hbm, hbm_saved, outs = take(BackInputs), take(BackHbm), take(BackSaved), take(BackOuts)
    saved, blocks, work, scan_bufs = take(BackSaved), take(Groups), take(BackWork), take(StateScan)
    seq_bufs = []
    for number in range(len(Groups._fields)):
        if number < FOLDED:
            comb_y, comb_z, *late = some(8)
            seq_bufs.append([None, None, comb_y, None, None, comb_z] + late)
        else:
            seq_bufs.append(some(12))
    bufs, bufs_three = some(7), some(7)
    mp_sems, three_sems, (seq_send, seq_recv), (few_send, few_recv), (local_sems,) = (
        some(2),
        some(2),
        some(2),
        some(2),
        some(1),
    )
    place = Place()
    z, y = place.z, place.y
    local = Locals(local_sems)
    part, own, other_full, tokens_low = work.part, work.own, work.other_full, outs.tokens_low
    sum_three = MpSum(place, three_sems, part, outs.result, own, bufs_three, hold=True)
    sum_five = MpSum(place, mp_sems, part, other_full, own, bufs, LAG_FIVE)
    sum_six = MpSum(place, mp_sems, part, tokens_low, own, bufs)

    load_part = local.start(hbm.part_three, part)
    load_low = local.start(hbm.low_four, tokens_low)
    load_win_out = local.start(hbm.win_out, work.win_out)
    mlp_loads = [
        local.start(src, dst)
        for src, dst in ((hbm.gate_sum, blocks.gate), (hbm.up_sum, blocks.up), (hbm.down_sum, blocks.down))
    ]
    load_saved = BackSaved(*[local.start(src, dst) for src, dst in zip(hbm_saved, saved)])
    load_win = [
        local.start(src, work.w_win.at[:, pl.ds(k * WIDE, WIDE)])
        for k, src in enumerate((hbm.win_q, hbm.win_k, hbm.win_v))
    ]
    load_grad = local.start(hbm.grad_own, work.grad_own)
    load_gain = local.start(hbm.gain_sum, work.gain_sums.at[pl.ds(0, 8)])
    load_normed = local.start(hbm.normed_two, work.normed_low)
    load_lin = [
        local.start(src, dst)
        for src, dst in ((hbm.w_query, work.w_query), (hbm.w_key, work.w_key), (hbm.w_out, work.w_out))
    ]
    greet(
        [place.peer()]
        + [place.on_x(k) for k in (1, 2, 3)]
        + [place.on_y(k) for k in (1, 2, 3)]
        + [place.on_z(k) for k in (1, 2, 3)]
        + [place.along(1), place.along(15)]
    )
    seq_copies = Copies(seq_send, seq_recv)
    few = Copies(few_send, few_recv)
    finished = Groups(outs.gate, outs.up, outs.down, outs.win_out, work.sum_win, outs.out, work.sum_lin)
    seq_sums = Groups(
        *[
            SeqSum(place, seq_copies, block, out, bufs_here)
            for block, out, bufs_here in zip(blocks, finished, seq_bufs)
        ]
    )
    first, second, vectors = inputs.first, inputs.second, inputs.vectors
    scale = vectors[2:3]
    group_row, group_col = inputs.group_row, work.group_col
    column(group_row, group_col)
    last_group = group_row[0:1, ROWS - 1 : ROWS].astype(F32)
    first_group = group_row[0:1, 0:1].astype(F32)
    in_last = (group_col[:, 0:1] == last_group).astype(F32)
    after_first = jnp.where(place.seq > 0, 1.0, 0.0)
    work.gain_sums[8:16] = jnp.zeros((8, D), F32)

    def finish(mp_sum, number, resid, gain, to, j):
        mine = pl.ds(j * PIECE, PIECE)
        total, here = back_through_norm(
            resid[mine].astype(F32), work.grad_own[mine], own[mine], gain[...]
        )
        work.gain_sums[number : number + 1] += here
        work.grad_own[mine] = total
        to[mp_sum.own_rows(j)] = total.astype(BF)

    mixed_grad, keys_sum, values_sum, win_grads = (
        work.mixed_grad,
        work.keys_sum,
        work.values_sum,
        work.win_grads,
    )
    probs, query_win, keys_all, values_all = (
        saved.probs,
        saved.query_win,
        saved.keys_all,
        saved.values_all,
    )
    score_scale = HD ** (-0.5)
    back = []

    def window_back(t):
        rows, window = pl.ds(t * WIN, WIN), pl.ds(t * WIN, TILE)
        for head in range(2):
            lanes = slice(head * HD, (head + 1) * HD)
            grad_tile, held = mixed_grad[rows, lanes], probs[head, rows]
            probs_grad = dot_nt(grad_tile, values_all[window, lanes])
            score_low = (
                held * (probs_grad - jnp.sum(probs_grad * held, axis=1, keepdims=True))
            ).astype(BF)
            win_grads[rows, lanes] = (dot(score_low, keys_all[window, lanes]) * score_scale).astype(BF)
            for ref, found in (
                (keys_sum, dot_tn(score_low, query_win[rows, lanes]) * score_scale),
                (values_sum, dot_tn(held.astype(BF), grad_tile)),
            ):
                if t == 0:
                    ref[window, lanes] = found
                else:
                    ref[rows, lanes] += found[:WIN]
                    ref[pl.ds(t * WIN + WIN, WIN), lanes] = found[WIN:]
        if t == 0:
            for ref, to_send in ((keys_sum, work.back_key), (values_sum, work.back_value)):
                to_send[0] = ref[0:WIN].astype(BF)
                back.append(few.start(to_send.at[0], to_send.at[1], place.along(15)))

    def produce_five(j):
        rows = pl.ds(j * CHUNK, CHUNK)
        for k, (ref, got) in enumerate(((keys_sum, work.back_key), (values_sum, work.back_value))):
            lanes = slice((k + 1) * WIDE, (k + 2) * WIDE)
            if j < CHUNKS - 1:
                win_grads[rows, lanes] = ref[WIN + j * CHUNK : WIN + (j + 1) * CHUNK].astype(BF)
            else:
                win_grads[j * CHUNK : ROWS - WIN, lanes] = ref[WIN + j * CHUNK : ROWS].astype(BF)
                back[k].wait_recv()
                win_grads[ROWS - WIN : ROWS, lanes] = (
                    ref[ROWS : ROWS + WIN] + got[1].astype(F32)
                ).astype(BF)
        if j % 2 == 0:
            return
        rows = pl.ds((j - 1) * CHUNK, 2 * CHUNK)
        part[rows] = dot_nt(win_grads[rows], work.w_win[...]).astype(BF)

    def finish_five(j):
        if j == 0:
            load_saved.resid_one.wait()
            load_grad.wait()
            load_gain.wait()
        finish(sum_five, 1, saved.resid_one, inputs.gain_two, other_full, j)

    query, key, value, carried = saved.query, saved.key, saved.value, saved.carried
    numer_low, query_sum, key_sum, value_sum, value_low = (
        query_win,
        work.query_sum,
        work.key_sum,
        keys_sum,
        mixed_grad,
    )

    def through_features(head, parts, grad):
        left, right = parts
        scaled = grad * scale
        return dot_nt((scaled * right).astype(BF), first[head]) + dot_nt(
            (scaled * left).astype(BF), second[head]
        )

    def ready_five(j):
        rows = pl.ds(j * CHUNK, CHUNK)
        if j == 0:
            for load in load_lin:
                load.wait()
            for load in (
                load_saved.denominator,
                load_saved.quotient,
                load_saved.query,
                load_saved.key,
                load_saved.value,
                load_saved.carried,
                load_saved.carried_norm,
            ):
                load.wait()
        mixed = dot_nt(other_full[rows], work.w_out[...]).astype(BF).astype(F32)
        incoming = (group_col[rows, 0:1] == first_group).astype(F32) * after_first
        for head in range(2):
            lanes = slice(head * HD, (head + 1) * HD)
            denom = saved.denominator[head, rows]
            numer = (mixed[:, lanes] / denom).astype(BF)
            numer_low[rows, lanes] = numer
            denom_grad = (
                -jnp.sum(mixed[:, lanes] * saved.quotient[rows, lanes], axis=1, keepdims=True) / denom
            )
            work.denom_grad[head, rows] = denom_grad
            parts = factors(head, (query[0, rows], query[1, rows]), first, second, vectors)
            used = (parts[0] * parts[1] * scale).astype(BF).astype(F32) * incoming
            state = dot_tn(used.astype(BF), numer)
            norm = jnp.sum(used * denom_grad, axis=0, keepdims=True)
            if j == 0:
                work.state_sum[head], work.norm_sum[head] = state, norm
            else:
                work.state_sum[head] += state
                work.norm_sum[head] += norm
        if j == CHUNKS - 1:
            for head in range(2):
                scan_bufs.mine[head, 0:FEATURES] = work.state_sum[head, 0:FEATURES].astype(BF)
                scan_bufs.mine[head, FEATURES:STATE] = norm_rows_of(work.norm_sum[head]).astype(BF)

    def within(j):
        rows, count = pl.ds(j * CHUNK, CHUNK), (j + 1) * CHUNK
        incoming = (group_col[rows, 0:1] == first_group).astype(F32) * after_first
        kept = kept_pairs(group_col, group_row, j)
        key_new = []
        for head in range(2):
            lanes = slice(head * HD, (head + 1) * HD)
            numer, denom_grad = numer_low[rows, lanes], work.denom_grad[head, rows]
            parts = factors(head, (query[0, rows], query[1, rows]), first, second, vectors)
            grad = incoming * (
                dot_nt(numer, carried[head].astype(BF)) + denom_grad * saved.carried_norm[head]
            )
            query_new = through_features(head, parts, grad)
            inner = products(head, (query.at[0], query.at[1]), (key.at[0], key.at[1]), rows, count)
            kernel = jnp.where(kept, 1.0 + inner * 0.25 + inner * inner * 0.03125, 0.0).astype(BF)
            grad = dot_nt(numer, value[0:count, lanes]) + denom_grad
            grad = jnp.where(kept, grad, 0.0).astype(BF).astype(F32)
            inner_grad = (grad * (0.25 + inner * 0.0625)).astype(BF)
            query_new = query_new + of_head(dot(inner_grad, key[0, 0:count]), head)
            if head == 0:
                query_sum[rows] = query_new
            else:
                query_sum[rows] += query_new
            key_new.append(of_head(dot_tn(inner_grad, query[0, rows]), head))
            found = dot_tn(kernel, numer)
            if j > 0:
                value_sum[0 : count - CHUNK, lanes] += found[0 : count - CHUNK]
            value_sum[count - CHUNK : count, lanes] = found[count - CHUNK : count]
        found = key_new[0] + key_new[1]
        if j > 0:
            key_sum[0 : count - CHUNK] += found[0 : count - CHUNK]
        key_sum[count - CHUNK : count] = found[count - CHUNK : count]

    def weight_task(block, right, quarter):
        weight_block(block, work.flipped, right, quarter)

    def begin(group):
        group.step(0)

    def turn_mixed(ref, load):
        load.wait()
        work.flipped[0:WIDE] = ref[...].T

    def turn_win():
        load_normed.wait()
        for k in range(3):
            rows = slice(k * WIDE, (k + 1) * WIDE)
            work.flipped[rows] = win_grads[:, rows].T

    late_work = [lambda: turn_mixed(saved.mixed_win, load_saved.mixed_win)]
    late_work += [functools.partial(weight_task, blocks.win_out, tokens_low, k) for k in range(4)]
    late_work += [functools.partial(begin, seq_sums.win_out), turn_win]
    late_work += [functools.partial(weight_task, blocks.win, work.normed_low, k) for k in range(4)]
    late_work += [functools.partial(begin, seq_sums.win)]

    def steps(*names):
        for group, number in names:
            group.step(number)

    gate, up, down, win_out, win, out, lin = seq_sums
    def finish_three(j):
        mine = pl.ds(j * PIECE, PIECE)
        outs.result[sum_three.own_rows(j)] = (own[mine] + saved.resid_two[mine]).astype(BF)

    three = sum_three.slots(lambda j: None, finish_three)
    meet(12)
    load_part.wait()
    next(three)
    for load in (load_low, load_win_out):
        load.wait()
    mixed_grad[...] = dot_nt(tokens_low[...], work.win_out[...]).astype(BF)
    for load, group in zip(mlp_loads, (gate, up, down)):
        load.wait()
        group.step(0)
    next(three)
    for load in (load_saved.probs, load_saved.query_win, load_saved.keys_all, load_saved.values_all):
        load.wait()
    load_saved.resid_two.wait()
    for t in range(8):
        window_back(t)
        if t == 4:
            next(three)
    next(three)
    for load in load_win:
        load.wait()
    for j in range(0, CHUNKS, 2):
        produce_five(j)
        produce_five(j + 1)
    five = sum_five.slots(lambda j: None, finish_five, ready_five)
    plans = {2: [(gate, 2)], 3: [(down, 1)], 4: [(up, 2)], 6: [(down, 2)]}
    for slot in five:
        for _ in range(3):
            if late_work:
                late_work.pop(0)()
        steps(*plans.get(slot, ()))
    for block in late_work:
        block()
    scan = state_scan(place, few, scan_bufs, work.later, work.later_norm, True)
    next(scan)
    load_normed_one = local.start(hbm.normed_one, work.normed_low)
    load_value = local.start(hbm.w_value, work.w_win.at[:, pl.ds(0, WIDE)])
    load_token = [
        local.start(hbm.tokens.at[sum_six.own_rows(j)], work.token_own.at[pl.ds(j * PIECE, PIECE)])
        for j in range(CHUNKS)
    ]
    next(three)
    turn_mixed(saved.mixed_lin, load_saved.mixed_lin)
    for k in range(4):
        weight_task(blocks.out, other_full, k)
    steps((out, 0), (gate, 3))
    within(0)
    next(scan)
    next(three)
    within(1)
    steps((win_out, 1))
    within(2)
    within(3)
    for _ in scan:
        pass
    next(three)
    for head in range(2):
        lanes = slice(head * HD, (head + 1) * HD)
        state = work.later[head].astype(BF)
        parts = factors(head, (key[0], key[1]), first, second, vectors)
        feat = (parts[0] * parts[1] * scale).astype(BF)
        grad = in_last * (dot_nt(value[:, lanes], state) + work.later_norm[head])
        key_sum[...] += through_features(head, parts, grad)
        value_sum[0:ROWS, lanes] += in_last * dot(feat, state)
    work.query_low[...] = query_sum[...].astype(BF)
    work.key_low[...] = key_sum[...].astype(BF)
    value_low[...] = value_sum[0:ROWS].astype(BF)
    load_value.wait()

    def produce_six(j):
        rows = pl.ds(j * CHUNK, CHUNK)
        part[rows] = (
            dot_nt(value_low[rows], work.w_win[:, 0:WIDE])
            + dot(work.query_low[rows], work.w_query[...])
            + dot(work.key_low[rows], work.w_key[...])
        ).astype(BF)

    for load in load_token:
        load.wait()

    def finish_six(j):
        finish(sum_six, 2, work.token_own, inputs.gain_one, tokens_low, j)

    def gains():
        work.gain_low[...] = work.gain_sums[...].astype(BF)

        def block(ref, at, size):
            return ref.at[:, pl.ds(pl.multiple_of(at * size, TILE), size)]

        over = [
            few.start(block(work.gain_low, (z + k) % 4, 512), work.gain_z.at[k - 1], place.on_z(k))
            for k in (1, 2, 3)
        ]
        yield
        total = block(work.gain_low, z, 512)[...].astype(F32)
        for k, copy in enumerate(over):
            copy.wait_recv()
            total = total + work.gain_z[k].astype(F32)
        work.gain_zz[...] = total.astype(BF)
        over = [
            few.start(block(work.gain_zz, (y + k) % 4, TILE), work.gain_y.at[k - 1], place.on_y(k))
            for k in (1, 2, 3)
        ]
        yield
        total = block(work.gain_zz, y, TILE)[...].astype(F32)
        for k, copy in enumerate(over):
            copy.wait_recv()
            total = total + work.gain_y[k].astype(F32)
        work.gain_x[...] = total.astype(BF)
        over = [few.start(work.gain_x, work.gain_xx.at[k - 1], place.on_x(k)) for k in (1, 2, 3)]
        yield
        total = work.gain_x[...].astype(F32)
        for k, copy in enumerate(over):
            copy.wait_recv()
            total = total + work.gain_xx[k].astype(F32)
        work.gain_p[...] = total.astype(BF)
        copy = few.start(work.gain_p, work.gain_pp, place.peer())
        yield
        copy.wait_recv()
        total = work.gain_p[...].astype(F32) + work.gain_pp[...].astype(F32)
        for k, ref in enumerate((outs.gain_three, outs.gain_two, outs.gain_one)):
            ref[...] = total[k : k + 1]

    def turn_lin():
        load_normed_one.wait()
        work.flipped[0:WIDE] = value_low[...].T
        for k, ref in enumerate((query_sum, key_sum)):
            at = WIDE + 2 * FEAT * k
            wide = jnp.concatenate([ref[...], jnp.zeros((ROWS, TILE - 2 * FEAT), F32)], axis=1)
            work.flipped[at : at + 2 * FEAT] = wide.T[0 : 2 * FEAT].astype(BF)

    six = sum_six.slots(produce_six, finish_six)
    next(six)
    next(three)
    steps((up, 3), (win, 1))
    turn_lin()
    for k in range(4):
        weight_task(blocks.lin, work.normed_low, k)
    steps((lin, 0))
    plans = {
        1: [(out, 1), (down, 3), (win_out, 2)],
        2: [(gate, 4), (up, 4), (win, 2)],
        3: [(lin, 1), (out, 2), (down, 4)],
        4: [(lin, 2), (win_out, 3)],
        5: [(win, 3), (out, 3), (lin, 3)],
        6: [(win_out, 4), (win, 4), (out, 4)],
    }
    gain_steps = gains()
    for slot in six:
        if slot >= 3:
            next(gain_steps, None)
        steps(*plans.get(slot, ()))
    steps((lin, 4))
    for k, ref in enumerate((outs.win_q, outs.win_k, outs.win_v)):
        ref[...] = work.sum_win[k * WIDE : (k + 1) * WIDE].T
    outs.value[...] = work.sum_lin[0:WIDE].T
    outs.query[...] = work.sum_lin[WIDE : WIDE + 2 * FEAT]
    outs.key[...] = work.sum_lin[WIDE + 2 * FEAT : WIDE + 4 * FEAT]
    for _ in gain_steps:
        pass
    seq_copies.finish()
    few.finish()


def backward(saved, inputs, weights):
    back_inputs = BackInputs(*[getattr(inputs, name) for name in BackInputs._fields])
    hbm = BackHbm(
        part_three=saved.part_three,
        low_four=saved.low_four,
        grad_own=saved.grad_own,
        gain_sum=saved.gain_sum,
        tokens=inputs.tokens,
        normed_one=saved.normed_one,
        normed_two=saved.normed_two,
        gate_sum=saved.gate_sum,
        up_sum=saved.up_sum,
        down_sum=saved.down_sum,
        w_query=weights.w_query,
        w_key=weights.w_key,
        w_value=weights.w_value,
        w_out=weights.w_out,
        win_q=weights.win_q,
        win_k=weights.win_k,
        win_v=weights.win_v,
        win_out=weights.win_out,
    )
    held = BackSaved(*[getattr(saved, name) for name in BackSaved._fields])
    scratch = vmem(BackSaved) + [pltpu.VMEM((4, 4, width, TILE), BF) for width in Groups()]
    scratch += vmem(BackWork) + vmem(StateScan)
    for number, width in enumerate(Groups()):
        scratch += folded_scratch() if number < FOLDED else seq_scratch(width)
    scratch += mp_scratch() * 2
    scratch += [dma(CHUNKS * PER_CHUNK)] * 4 + [dma(24 * len(Groups._fields))] * 2 + [dma(24)] * 2
    scratch += [dma(64)]
    return BackOuts(
        *pl.pallas_call(
            backward_kernel,
            out_shape=[shape(dims, kind) for dims, kind in BackOuts()],
            in_specs=[INSIDE] * len(back_inputs) + [HBM] * (len(hbm) + len(held)),
            out_specs=[INSIDE] * len(BackOuts._fields),
            scratch_shapes=scratch,
            compiler_params=pltpu.CompilerParams(
                collective_id=1, has_side_effects=True, vmem_limit_bytes=VMEM_LIMIT
            ),
        )(*back_inputs, *hbm, *held)
    )


def hand_over_kernel(*refs):
    count = (len(refs) - 2) // 3
    ins, outs, held = refs[:count], refs[count : 2 * count], refs[2 * count : 3 * count]
    wide, sems = refs[3 * count :]
    block = ROWS // 4
    local = Locals(sems)
    parts = [pl.ds(k * block, block) for k in range(4)]
    loads = [local.start(ins[0].at[rows], held[0].at[rows]) for rows in parts]
    others = [local.start(src, dst) for src, dst in zip(ins[1:], held[1:])]
    copies = []
    for load, rows in zip(loads, parts):
        load.wait()
        wide[rows] = held[0][rows].astype(F32)
        copies.append(local.start(wide.at[rows], outs[0].at[rows]))
    for load, src, dst in zip(others, held[1:], outs[1:]):
        load.wait()
        copies.append(local.start(src, dst))
    for copy in copies:
        copy.wait()


def hand_over(arrays):
    kinds = [F32] + [array.dtype for array in arrays[1:]]
    return pl.pallas_call(
        hand_over_kernel,
        out_shape=[shape(array.shape, kind) for array, kind in zip(arrays, kinds)],
        in_specs=[HBM] * len(arrays),
        out_specs=[HBM] * len(arrays),
        scratch_shapes=[pltpu.VMEM(array.shape, array.dtype) for array in arrays]
        + [pltpu.VMEM((ROWS, D), F32), dma(2 * len(arrays) + 6)],
        compiler_params=pltpu.CompilerParams(vmem_limit_bytes=VMEM_LIMIT),
    )(*arrays)


def local(
    tokens,
    group_ids,
    gain_one,
    lin_query,
    lin_key,
    lin_value,
    lin_output,
    gain_two,
    win_query,
    win_key,
    win_value,
    win_output,
    gain_three,
    mlp_gate,
    mlp_up,
    mlp_down,
    out_grad,
):
    first, second, vectors = feature_tables()
    inputs = Inputs(
        tokens=tokens,
        group_row=group_ids.reshape(1, ROWS),
        gain_one=gain_one.reshape(1, D),
        gain_two=gain_two.reshape(1, D),
        gain_three=gain_three.reshape(1, D),
        first=first,
        second=second,
        vectors=vectors,
    )
    weights = Weights(
        out_grad=out_grad,
        w_query=lin_query.T,
        w_key=lin_key.T,
        w_value=lin_value,
        w_out=lin_output,
        win_k=win_key,
        win_v=win_value,
        win_q=win_query,
        win_out=win_output,
        w_gate=mlp_gate.T,
        w_up=mlp_up.T,
        w_down=mlp_down,
    )
    saved = forward(inputs, weights)
    outs = BackOuts(*backward(saved, inputs, weights))
    outs = BackOuts(*hand_over([*outs]))
    return (
        outs.result,
        outs.tokens_low,
        outs.gain_one.reshape(TILE),
        outs.query.T,
        outs.key.T,
        outs.value,
        outs.out,
        outs.gain_two.reshape(TILE),
        outs.win_q,
        outs.win_k,
        outs.win_v,
        outs.win_out,
        outs.gain_three.reshape(TILE),
        outs.gate.T,
        outs.up.T,
        outs.down,
    )


def solution(mesh):
    return jax.shard_map(
        local,
        mesh=mesh,
        in_specs=(
            P("seq", None),
            P("seq"),
            P(),
            P(None, "mp"),
            P(None, "mp"),
            P(None, "mp"),
            P("mp", None),
            P(),
            P(None, "mp"),
            P(None, "mp"),
            P(None, "mp"),
            P("mp", None),
            P(),
            P(None, "mp"),
            P(None, "mp"),
            P("mp", None),
            P("seq", None),
        ),
        out_specs=(
            P("seq", None),
            P("seq", None),
            P("seq"),
            P("seq", "mp"),
            P("seq", "mp"),
            P("seq", "mp"),
            P("mp", "seq"),
            P("seq"),
            P("seq", "mp"),
            P("seq", "mp"),
            P("seq", "mp"),
            P("mp", "seq"),
            P("seq"),
            P("seq", "mp"),
            P("seq", "mp"),
            P("mp", "seq"),
        ),
        check_vma=False,
    )
```
